32 devices in a mesh: dp: 8 (over z, y), head: 4 (over x, core).
Axes of the slice: x: 2, y: 2, z: 4, core: 2. Of those that a mesh axis runs over, the one named last changes fastest.
Arguments:
- block_input_rows: bfloat16 [32, 1024, 1024], P('dp', 'head'), may hold values from -6 to 6
- document_starts: int32 [32, 1024], P('dp'), may hold values from 0 to 1023, as said below
- counted_mask: int32 [32, 1024], P('dp', 'head'), may hold values from 0 to 1
- output_gradient: bfloat16 [32, 1024, 1024], P('dp', 'head'), may hold values from -6 to 6
- first_norm_gain: bfloat16 [1024], replicated, may hold values from 0.099609375 to 1.8984375
- first_norm_bias: bfloat16 [1024], replicated, may hold values from -4 to 4
- query_key_value_weight: bfloat16 [1024, 3072], replicated, may hold values from -0.1875 to 0.1875
- query_down_weight: bfloat16 [1024, 4], replicated, may hold values from -0.1875 to 0.1875
- query_up_weight: bfloat16 [4, 1024], replicated, may hold values from -0.75 to 0.75
- value_down_weight: bfloat16 [1024, 4], replicated, may hold values from -0.1875 to 0.1875
- value_up_weight: bfloat16 [4, 1024], replicated, may hold values from -0.75 to 0.75
- attention_out_weight: bfloat16 [1024, 1024], replicated, may hold values from -0.75 to 0.75
- second_norm_gain: bfloat16 [1024], replicated, may hold values from 0.099609375 to 1.8984375
- second_norm_bias: bfloat16 [1024], replicated, may hold values from -4 to 4
- feed_input_weight: bfloat16 [1024, 4096], replicated, may hold values from -0.1875 to 0.1875
- feed_input_bias: bfloat16 [4096], replicated, may hold values from -6 to 6
- feed_output_weight: bfloat16 [4096, 1024], replicated, may hold values from -0.09375 to 0.09375
Outputs:
- output: bfloat16 [32, 1024, 1024], P('dp', 'head')
- input_grad: bfloat16 [32, 1024, 1024], P('dp', 'head')
- grad_lora_aq: float32 [1024, 4], replicated
- grad_lora_bq: float32 [4, 1024], replicated
- grad_lora_av: float32 [1024, 4], replicated
- grad_lora_bv: float32 [4, 1024], replicated
- rms_values: float32 [2], replicated
The draws below stay inside these ranges and needn't reach their ends.
Inputs may be any that keep to these rules, and one draw needn't show every extreme that they name: `document_starts`: within each slot a token's id is the position of the first token of its document, so ids never fall along the slot. In each aligned group of 4 slots one slot, drawn from the seed, is a single document; in every other slot the last token is a document of its own.
All inputs are finite; a program needn't handle non-finite values.
Results may differ from the reference program's by a relative error of at most 0.013.
Values may be sent and summed in bfloat16 or wider, within the bound.
A program may use at most 192 MiB of HBM per device.

```python
import jax
import jax.numpy as jnp
from jax import lax

MODEL_WIDTH = 1024
H = 16
FF = 4096
ADAPTER_RANK = 4
SLOT_TOKENS = 1024
SLOTS_PER_SHARD = 4
HD = 64
TOTAL_SLOTS = 32


def draw_document_starts(key, part):
    key = jax.random.fold_in(key, 11)
    first_random_key, second_random_key = jax.random.split(key)
    places = jnp.arange(SLOT_TOKENS)[None, :]
    mark_flags = jax.random.randint(first_random_key, (TOTAL_SLOTS, SLOT_TOKENS), 0, max(SLOT_TOKENS // 4, 2)) == 0
    starts = mark_flags | (places == 0) | (places == SLOT_TOKENS - 1)
    picked_value = jax.random.randint(second_random_key, (TOTAL_SLOTS // SLOTS_PER_SHARD,), 0, SLOTS_PER_SHARD)
    slot_position = jnp.arange(TOTAL_SLOTS)
    single = slot_position % SLOTS_PER_SHARD == jnp.repeat(picked_value, SLOTS_PER_SHARD)
    starts = jnp.where(single[:, None], places == 0, starts)
    labels = lax.cummax(jnp.where(starts, places, 0).astype(jnp.int32), axis=1)
    return labels.astype(jnp.int32)


def draw_counted_mask(key, part):
    key = jax.random.fold_in(key, 23)
    raw_sample = jax.random.randint(key, (TOTAL_SLOTS, SLOT_TOKENS), 0, 100)
    slot_portion = jnp.arange(TOTAL_SLOTS)[:, None] * 100 // TOTAL_SLOTS
    place_share = jnp.arange(SLOT_TOKENS)[None, :] * 100 // SLOT_TOKENS
    limit_value = 15 + (slot_portion + place_share) * 35 // 100
    return (raw_sample < limit_value).astype(jnp.int32)


def block_levels(rng, dims, pieces, smallest, largest):
    factor_of = 1.0
    for axis_at, blocks in pieces:
        heights = jax.random.uniform(jax.random.fold_in(jax.random.fold_in(rng, 6), axis_at), (blocks,), jnp.float32, smallest / len(pieces), largest / len(pieces))
        factor_of = factor_of * jnp.repeat(jnp.exp(heights), dims[axis_at] // blocks).reshape((-1,) + (1,) * (len(dims) - 1 - axis_at))
    return factor_of


def noise(rng, shape, deviation, limit, pieces=(), dtype=jnp.bfloat16):
    drawn = deviation * jax.random.normal(rng, shape, jnp.float32)
    if pieces:
        drawn = drawn * block_levels(rng, shape, pieces, -0.22, 0.18)
    return jnp.clip(drawn, -limit, limit).astype(dtype)


def setup_inputs(seed: int = 0) -> dict:
    seeds = jax.random.split(jax.random.key(seed), 18)
    return {
        "block_input_rows": noise(seeds[0], (TOTAL_SLOTS, SLOT_TOKENS, MODEL_WIDTH), 1.0, 6.0, ((0, 8), (1, 4))),
        "document_starts": draw_document_starts(jax.random.fold_in(seeds[17], 71), 0),
        "counted_mask": draw_counted_mask(jax.random.fold_in(seeds[17], 71), 0),
        "output_gradient": noise(seeds[3], (TOTAL_SLOTS, SLOT_TOKENS, MODEL_WIDTH), 1.0, 6.0, ((0, 8), (1, 4))),
        "first_norm_gain": jnp.clip(1.0 + 0.18 * jax.random.normal(seeds[4], (MODEL_WIDTH,), jnp.float32), 0.099609375, 1.8984375).astype(jnp.bfloat16),
        "first_norm_bias": noise(seeds[5], (MODEL_WIDTH,), 0.3, 4.0),
        "query_key_value_weight": noise(seeds[6], (MODEL_WIDTH, 3 * MODEL_WIDTH), MODEL_WIDTH ** -0.5, 0.1875),
        "query_down_weight": noise(seeds[7], (MODEL_WIDTH, ADAPTER_RANK), MODEL_WIDTH ** -0.5, 0.1875),
        "query_up_weight": noise(seeds[8], (ADAPTER_RANK, MODEL_WIDTH), 0.05, 0.75),
        "value_down_weight": noise(seeds[9], (MODEL_WIDTH, ADAPTER_RANK), MODEL_WIDTH ** -0.5, 0.1875),
        "value_up_weight": noise(seeds[10], (ADAPTER_RANK, MODEL_WIDTH), 0.05, 0.75),
        "attention_out_weight": noise(seeds[11], (MODEL_WIDTH, MODEL_WIDTH), (MODEL_WIDTH // 16) ** -0.5, 0.75),
        "second_norm_gain": jnp.clip(1.0 + 0.18 * jax.random.normal(seeds[12], (MODEL_WIDTH,), jnp.float32), 0.099609375, 1.8984375).astype(jnp.bfloat16),
        "second_norm_bias": noise(seeds[13], (MODEL_WIDTH,), 0.3, 4.0),
        "feed_input_weight": noise(seeds[14], (MODEL_WIDTH, FF), MODEL_WIDTH ** -0.5, 0.1875),
        "feed_input_bias": noise(seeds[15], (FF,), 0.5, 6.0),
        "feed_output_weight": noise(seeds[16], (FF, MODEL_WIDTH), FF ** -0.5, 0.09375),
    }


EPSILON = 1e-05
ADAPTER_SCALE = 8.0
NEGATIVE = -1e+30
HIGHEST = lax.Precision.HIGHEST

@jax.custom_vjp
def low(v):
    return lax.optimization_barrier(v.astype(jnp.bfloat16)).astype(jnp.float32)

@jax.custom_vjp
def low_back(v):
    return v

def low_keep(v):
    return (low(v), None)

def low_pass(kept, grad):
    return (grad,)

def back_keep(v):
    return (v, None)

def back_low(kept, grad):
    return (low(grad),)
low.defvjp(low_keep, low_pass)
low_back.defvjp(back_keep, back_low)

def both_rounded(matrix):
    return low_back(low(matrix))

def product_result(left, right):
    return jnp.dot(left, right, precision=HIGHEST)

def norm_rows(matrix, gain_vec, shift_vec):
    center = matrix - lax.optimization_barrier(jnp.mean(matrix, axis=-1, keepdims=True))
    variance = lax.optimization_barrier(jnp.mean(center * center, axis=-1, keepdims=True))
    return center * lax.rsqrt(variance + EPSILON) * gain_vec + shift_vec

def slot_forward(inputs, query_down, query_up_result, value_down, value_up_result, segments, frozen):
    gain_one, shift_one, query_key_value_weight, attention_out_weight, gain_two, shift_two, feed_input_weight, feed_input_bias, feed_output_weight = frozen
    normed_rows = low(norm_rows(inputs, gain_one, shift_one))
    query_low_rank = both_rounded(product_result(normed_rows, query_down))
    value_low_rank = both_rounded(product_result(normed_rows, value_down))
    projected_rows = product_result(normed_rows, query_key_value_weight)
    query_rows = both_rounded(projected_rows[:, :MODEL_WIDTH] + ADAPTER_SCALE * product_result(query_low_rank, query_up_result))
    key_rows = both_rounded(projected_rows[:, MODEL_WIDTH:2 * MODEL_WIDTH])
    value_matrix = both_rounded(projected_rows[:, 2 * MODEL_WIDTH:] + ADAPTER_SCALE * product_result(value_low_rank, value_up_result))
    head_shape = (SLOT_TOKENS, H, HD)
    scores = jnp.einsum('qhd,khd->hqk', query_rows.reshape(head_shape), key_rows.reshape(head_shape), precision=HIGHEST) * HD ** (-0.5)
    scores = low_back(scores)
    places = jnp.arange(SLOT_TOKENS)
    allowed = (segments[:, None] == segments[None, :]) & (places[None, :] <= places[:, None])
    scores = jnp.where(allowed[None], scores, NEGATIVE)
    weights = low(jax.nn.softmax(scores, axis=-1))
    context = jnp.einsum('hqk,khd->qhd', weights, value_matrix.reshape(head_shape), precision=HIGHEST)
    context = both_rounded(context.reshape(SLOT_TOKENS, MODEL_WIDTH))
    branch = low_back(product_result(context, attention_out_weight))
    hidden_state = inputs + branch
    normed_two = low(norm_rows(hidden_state, gain_two, shift_two))
    before = low_back(product_result(normed_two, feed_input_weight) + feed_input_bias)
    activated = low(jax.nn.gelu(before, approximate=True))
    feed_out = product_result(activated, feed_output_weight)
    return (hidden_state + feed_out, (branch, feed_out))

def reference(block_input_rows, document_starts, counted_mask, output_gradient, first_norm_gain, first_norm_bias, query_key_value_weight, query_down_weight, query_up_weight, value_down_weight, value_up_weight, attention_out_weight, second_norm_gain, second_norm_bias, feed_input_weight, feed_input_bias, feed_output_weight):
    frozen = tuple((element_item.astype(jnp.float32) for element_item in (first_norm_gain, first_norm_bias, query_key_value_weight, attention_out_weight, second_norm_gain, second_norm_bias, feed_input_weight, feed_input_bias, feed_output_weight)))
    adapter_params = tuple((element_item.astype(jnp.float32) for element_item in (query_down_weight, query_up_weight, value_down_weight, value_up_weight)))

    def slot_step(totals, inputs_now):
        slot_input, slot_grad, segments, valid_rows = inputs_now

        def forward_fn(inputs, query_down, query_up_result, value_down, value_up_result):
            return slot_forward(inputs, query_down, query_up_result, value_down, value_up_result, segments, frozen)
        output, pullback, extras = jax.vjp(forward_fn, slot_input.astype(jnp.float32), adapter_params[0], adapter_params[1], adapter_params[2], adapter_params[3], has_aux=True)
        gradients = pullback(slot_grad.astype(jnp.float32))
        branch, feed_out = extras
        row_weight = valid_rows.astype(jnp.float32)[:, None]
        square_sums = jnp.stack([jnp.sum(row_weight * output * output), jnp.sum(row_weight * (branch * branch + feed_out * feed_out)), jnp.sum(valid_rows.astype(jnp.float32))])
        new_totals = (totals[0] + gradients[1], totals[1] + gradients[2], totals[2] + gradients[3], totals[3] + gradients[4], totals[4] + square_sums)
        return (new_totals, (output.astype(jnp.bfloat16), gradients[0].astype(jnp.bfloat16)))
    initial = (jnp.zeros((MODEL_WIDTH, ADAPTER_RANK), jnp.float32), jnp.zeros((ADAPTER_RANK, MODEL_WIDTH), jnp.float32), jnp.zeros((MODEL_WIDTH, ADAPTER_RANK), jnp.float32), jnp.zeros((ADAPTER_RANK, MODEL_WIDTH), jnp.float32), jnp.zeros((3,), jnp.float32))
    totals, stacked = lax.scan(slot_step, initial, (block_input_rows, output_gradient, document_starts, counted_mask))
    outputs, input_grads = stacked
    token_count = jnp.maximum(totals[4][2], 1.0)
    rms_values = jnp.stack([jnp.sqrt(totals[4][0] / (token_count * MODEL_WIDTH)), jnp.sqrt(totals[4][1] / (2.0 * token_count * MODEL_WIDTH))])
    return (outputs, input_grads, totals[0], totals[1], totals[2], totals[3], rms_values)
```

```python
import functools

import jax
import jax.numpy as jnp
from jax import lax
from jax.experimental import pallas as pl
from jax.experimental.pallas import tpu as pltpu
from jax.sharding import PartitionSpec as P

H = 16


EPSILON = 1e-05
ADAPTER_SCALE = 8.0
NEGATIVE = -1e30


def as_sent(x):

    def short(part):
        return part.astype(jnp.bfloat16) if part.dtype == jnp.float32 else part

    return jax.tree.map(short, x)


def norm_rows(matrix, gain_vec, shift_vec):
    center = matrix - jnp.mean(matrix, axis=-1, keepdims=True)
    variance = jnp.mean(center * center, axis=-1, keepdims=True)
    return center * lax.rsqrt(variance + EPSILON) * gain_vec + shift_vec


def norm_back(matrix, gain_vec, shift_vec, incoming):
    pullback = jax.vjp(lambda element_item: norm_rows(element_item, gain_vec, shift_vec), matrix)[1]
    return pullback(incoming)[0]


def gelu_tanh(matrix):
    return jax.nn.gelu(matrix, approximate=True)


def plain_product(left, right):
    return jnp.dot(left, right, preferred_element_type=jnp.float32)


def last_product(left, right):
    return lax.dot_general(
        left, right, (((1,), (1,)), ((), ())), preferred_element_type=jnp.float32
    )


def first_product(left, right):
    return lax.dot_general(
        left, right, (((0,), (0,)), ((), ())), preferred_element_type=jnp.float32
    )


def masked_scores(query_block, key_slot, segments, row_start, row_end, score_scale):
    places = jnp.arange(row_end)
    allowed = (segments[row_start:row_end, None] == segments[None, :row_end]) & (
        places[None, :] <= places[row_start:row_end, None]
    )
    scores = (
        jnp.einsum(
            "qhd,khd->hqk", query_block, key_slot[:row_end], preferred_element_type=jnp.float32
        )
        * score_scale
    )
    return jnp.where(allowed[None], scores, NEGATIVE)


def attend_slot(query_slot, key_slot, value_slot, segments, block_rows, score_scale):
    length = query_slot.shape[0]
    outputs_list = []
    logsum_list = []
    for block_index in range(length // block_rows):
        row_start = block_index * block_rows
        row_end = row_start + block_rows
        scores = masked_scores(
            query_slot[row_start:row_end], key_slot, segments, row_start, row_end, score_scale
        )
        row_max = jnp.max(scores, axis=-1, keepdims=True)
        exponent = jnp.exp(scores - row_max)
        row_total = jnp.sum(exponent, axis=-1, keepdims=True)
        probability = (exponent / row_total).astype(jnp.bfloat16)
        context = jnp.einsum(
            "hqk,khd->qhd", probability, value_slot[:row_end], preferred_element_type=jnp.float32
        )
        outputs_list.append(context.astype(jnp.bfloat16))
        logsum_list.append((row_max + jnp.log(row_total))[..., 0])
    return (jnp.concatenate(outputs_list, 0), jnp.concatenate(logsum_list, 1))


def attend_back(
    query_slot, key_slot, value_slot, grad_slot, logsum, segments, block_rows, score_scale
):
    length = query_slot.shape[0]
    key_grad = jnp.zeros(key_slot.shape, jnp.float32)
    value_gradient = jnp.zeros(value_slot.shape, jnp.float32)
    query_parts = []
    for block_index in range(length // block_rows):
        row_start = block_index * block_rows
        row_end = row_start + block_rows
        query_block = query_slot[row_start:row_end]
        grad_block = grad_slot[row_start:row_end]
        scores = masked_scores(query_block, key_slot, segments, row_start, row_end, score_scale)
        probability = jnp.exp(scores - logsum[:, row_start:row_end, None])
        prob_grad = jnp.einsum(
            "qhd,khd->hqk", grad_block, value_slot[:row_end], preferred_element_type=jnp.float32
        )
        inner_sum = jnp.sum(probability * prob_grad, axis=-1, keepdims=True)
        score_grad = (probability * (prob_grad - inner_sum)).astype(jnp.bfloat16)
        query_parts.append(
            jnp.einsum(
                "hqk,khd->qhd", score_grad, key_slot[:row_end], preferred_element_type=jnp.float32
            )
            * score_scale
        )
        key_grad = key_grad.at[:row_end].add(
            jnp.einsum("hqk,qhd->khd", score_grad, query_block, preferred_element_type=jnp.float32)
            * score_scale
        )
        value_gradient = value_gradient.at[:row_end].add(
            jnp.einsum(
                "hqk,qhd->khd",
                probability.astype(jnp.bfloat16),
                grad_block,
                preferred_element_type=jnp.float32,
            )
        )
    query_gradient = jnp.concatenate(query_parts, 0)
    return (
        query_gradient.astype(jnp.bfloat16),
        key_grad.astype(jnp.bfloat16),
        value_gradient.astype(jnp.bfloat16),
    )


def shards(
    block_input_rows,
    document_starts,
    counted_mask,
    output_gradient,
    first_norm_gain,
    first_norm_bias,
    query_key_value_weight,
    query_down_weight,
    query_up_weight,
    value_down_weight,
    value_up_weight,
    attention_out_weight,
    second_norm_gain,
    second_norm_bias,
    feed_input_weight,
    feed_input_bias,
    feed_output_weight,
):
    slot_count, local_len, row_width = block_input_rows.shape
    groups = lax.axis_size("head")
    full_len = local_len * groups
    head_size = row_width // H
    heads_here = H // groups
    row_count = slot_count * local_len
    block_rows = min(512, full_len)
    score_scale = head_size ** (-0.5)
    gain_one = first_norm_gain.astype(jnp.float32)
    shift_one = first_norm_bias.astype(jnp.float32)
    gain_two = second_norm_gain.astype(jnp.float32)
    shift_two = second_norm_bias.astype(jnp.float32)
    fc_bias = feed_input_bias.astype(jnp.float32)
    local_shape = (slot_count, local_len, row_width)
    split_shape = (slot_count, full_len, heads_here, head_size)
    merged_shape = (slot_count, full_len, heads_here * head_size)
    flat_in = block_input_rows.reshape(row_count, row_width).astype(jnp.float32)
    normed_rows = norm_rows(flat_in, gain_one, shift_one).astype(jnp.bfloat16)
    query_low_rank = plain_product(normed_rows, query_down_weight).astype(jnp.bfloat16)
    value_low_rank = plain_product(normed_rows, value_down_weight).astype(jnp.bfloat16)
    projected_rows = plain_product(normed_rows, query_key_value_weight)
    query_rows = (
        projected_rows[:, :row_width]
        + ADAPTER_SCALE * plain_product(query_low_rank, query_up_weight)
    ).astype(jnp.bfloat16)
    key_rows = projected_rows[:, row_width : 2 * row_width].astype(jnp.bfloat16)
    value_matrix = (
        projected_rows[:, 2 * row_width :]
        + ADAPTER_SCALE * plain_product(value_low_rank, value_up_weight)
    ).astype(jnp.bfloat16)
    head_query, head_key, head_value = (
        lax.all_to_all(
            query_rows.reshape(local_shape), "head", split_axis=2, concat_axis=1, tiled=True
        ),
        lax.all_to_all(
            key_rows.reshape(local_shape), "head", split_axis=2, concat_axis=1, tiled=True
        ),
        lax.all_to_all(
            value_matrix.reshape(local_shape), "head", split_axis=2, concat_axis=1, tiled=True
        ),
    )
    head_query = head_query.reshape(split_shape)
    head_key = head_key.reshape(split_shape)
    head_value = head_value.reshape(split_shape)

    def slot_fn(packed):
        return attend_slot(packed[0], packed[1], packed[2], packed[3], block_rows, score_scale)

    context_heads, logsum = lax.map(slot_fn, (head_query, head_key, head_value, document_starts))
    context_local = lax.all_to_all(
        as_sent(context_heads.reshape(merged_shape)),
        "head",
        split_axis=1,
        concat_axis=2,
        tiled=True,
    )
    context_flat = context_local.reshape(row_count, row_width)
    branch = plain_product(context_flat, attention_out_weight)
    hidden_state = flat_in + branch
    normed_two = norm_rows(hidden_state, gain_two, shift_two).astype(jnp.bfloat16)
    before = plain_product(normed_two, feed_input_weight) + fc_bias
    activated = gelu_tanh(before).astype(jnp.bfloat16)
    feed_out = plain_product(activated, feed_output_weight)
    result = hidden_state + feed_out
    output = result.astype(jnp.bfloat16).reshape(block_input_rows.shape)
    valid_rows = counted_mask.reshape(row_count).astype(jnp.float32)[:, None]
    square_sums = jnp.stack(
        [
            jnp.sum(valid_rows * result * result),
            jnp.sum(valid_rows * (branch * branch + feed_out * feed_out)),
            jnp.sum(valid_rows),
        ]
    )
    grad_flat = output_gradient.reshape(row_count, row_width)
    act_grad = last_product(grad_flat, feed_output_weight)
    gelu_pull = jax.vjp(gelu_tanh, before)[1]
    before_grad = gelu_pull(act_grad)[0].astype(jnp.bfloat16)
    normed_two_grad = last_product(before_grad, feed_input_weight)
    hidden_grad = grad_flat.astype(jnp.float32) + norm_back(
        hidden_state, gain_two, shift_two, normed_two_grad
    )
    branch_grad = hidden_grad.astype(jnp.bfloat16)
    context_grad = last_product(branch_grad, attention_out_weight).astype(jnp.bfloat16)
    grad_heads = lax.all_to_all(
        context_grad.reshape(local_shape), "head", split_axis=2, concat_axis=1, tiled=True
    ).reshape(split_shape)

    def back_fn(packed):
        return attend_back(
            packed[0],
            packed[1],
            packed[2],
            packed[3],
            packed[4],
            packed[5],
            block_rows,
            score_scale,
        )

    query_gradient, key_grad, value_gradient = lax.map(
        back_fn, (head_query, head_key, head_value, grad_heads, logsum, document_starts)
    )
    query_gradient, key_grad, value_gradient = (
        lax.all_to_all(
            as_sent(query_gradient.reshape(merged_shape)),
            "head",
            split_axis=1,
            concat_axis=2,
            tiled=True,
        ),
        lax.all_to_all(
            as_sent(key_grad.reshape(merged_shape)), "head", split_axis=1, concat_axis=2, tiled=True
        ),
        lax.all_to_all(
            as_sent(value_gradient.reshape(merged_shape)),
            "head",
            split_axis=1,
            concat_axis=2,
            tiled=True,
        ),
    )
    query_gradient = query_gradient.reshape(row_count, row_width)
    key_grad = key_grad.reshape(row_count, row_width)
    value_gradient = value_gradient.reshape(row_count, row_width)
    query_low_gradient = (ADAPTER_SCALE * last_product(query_gradient, query_up_weight)).astype(
        jnp.bfloat16
    )
    value_low_gradient = (ADAPTER_SCALE * last_product(value_gradient, value_up_weight)).astype(
        jnp.bfloat16
    )
    joined_grads = jnp.concatenate([query_gradient, key_grad, value_gradient], axis=1)
    normed_grad = (
        last_product(joined_grads, query_key_value_weight)
        + last_product(query_low_gradient, query_down_weight)
        + last_product(value_low_gradient, value_down_weight)
    )
    input_grad = hidden_grad + norm_back(flat_in, gain_one, shift_one, normed_grad)
    down_query = first_product(normed_rows, query_low_gradient)
    lifted_query = ADAPTER_SCALE * first_product(query_low_rank, query_gradient)
    down_value = first_product(normed_rows, value_low_gradient)
    lifted_value = ADAPTER_SCALE * first_product(value_low_rank, value_gradient)
    totals = lax.psum(
        (down_query, lifted_query, down_value, lifted_value, square_sums), ("dp", "head")
    )
    token_count = jnp.maximum(totals[4][2], 1.0)
    rms_values = jnp.stack(
        [
            jnp.sqrt(totals[4][0] / (token_count * row_width)),
            jnp.sqrt(totals[4][1] / (2.0 * token_count * row_width)),
        ]
    )
    return (
        output,
        input_grad.astype(jnp.bfloat16).reshape(block_input_rows.shape),
        totals[0],
        totals[1],
        totals[2],
        totals[3],
        rms_values,
    )


LOG2E = 1.4426950408889634
LN2 = 0.6931471805599453
TILE = 256
GROUP = 256
bf16 = jnp.bfloat16
f32 = jnp.float32
NT = (((1,), (1,)), ((), ()))
NN = (((1,), (0,)), ((), ()))
TN = (((0,), (0,)), ((), ()))
MESH = pl.DeviceIdType.MESH
MIB = 2**20


def dg(left, right, dims):
    return lax.dot_general(left, right, dims, preferred_element_type=f32)


def resident(shape):
    zeros = (0,) * len(shape)
    return pl.BlockSpec(shape, lambda *_: zeros, pipeline_mode=pl.Buffered(1))


def params(mib):
    return pltpu.CompilerParams(
        vmem_limit_bytes=mib * MIB, dimension_semantics=("arbitrary",)
    )


def norm_stats(rows):
    center = rows - jnp.mean(rows, axis=-1, keepdims=True)
    rs = lax.rsqrt(jnp.mean(center * center, axis=-1, keepdims=True) + EPSILON)
    return center * rs, rs


def norm_grad(unit, rs, gain, incoming):
    t = incoming * gain
    return (
        t - jnp.mean(t, axis=-1, keepdims=True) - unit * jnp.mean(t * unit, axis=-1, keepdims=True)
    ) * rs


def qkv_kernel(x_ref, gain_ref, shift_ref, w_ref, down_ref, upq_ref, upv_ref, qkv_ref, normed_ref, low_ref):
    width = x_ref.shape[-1]
    unit, _ = norm_stats(x_ref[0].astype(f32))
    normed = (unit * gain_ref[...] + shift_ref[...]).astype(bf16)
    normed_ref[...] = normed
    low = dg(normed, down_ref[...], NN).astype(bf16)
    low_ref[...] = low
    head_size = width // H
    scale = head_size**-0.5 * LOG2E
    step = 512
    for at in range(0, width, step):
        part = dg(normed, w_ref[:, at : at + step], NN)
        part = part + ADAPTER_SCALE * dg(low, upq_ref[:, at : at + step], NN)
        qkv_ref[:, at : at + step] = (part * scale).astype(bf16)
    for at in range(width, 2 * width, step):
        qkv_ref[:, at : at + step] = dg(normed, w_ref[:, at : at + step], NN).astype(bf16)
    for at in range(0, width, step):
        part = dg(normed, w_ref[:, 2 * width + at : 2 * width + at + step], NN)
        part = part + ADAPTER_SCALE * dg(low, upv_ref[:, at : at + step], NN)
        qkv_ref[:, 2 * width + at : 2 * width + at + step] = part.astype(bf16)


def project(x, gain, shift, w, down, upq, upv):
    blocks, tile, width = x.shape
    rows = blocks * tile
    ranks = down.shape[1]
    return pl.pallas_call(
        qkv_kernel,
        grid=(blocks,),
        in_specs=[
            pl.BlockSpec((1, tile, width), lambda i: (i, 0, 0)),
            resident((1, width)),
            resident((1, width)),
            resident(w.shape),
            resident(down.shape),
            resident(upq.shape),
            resident(upv.shape),
        ],
        out_specs=[
            pl.BlockSpec((tile, 3 * width), lambda i: (i, 0)),
            pl.BlockSpec((tile, width), lambda i: (i, 0)),
            pl.BlockSpec((tile, ranks), lambda i: (i, 0)),
        ],
        out_shape=[
            jax.ShapeDtypeStruct((rows, 3 * width), bf16),
            jax.ShapeDtypeStruct((rows, width), bf16),
            jax.ShapeDtypeStruct((rows, ranks), bf16),
        ],
        compiler_params=params(40),
        cost_estimate=pl.CostEstimate(flops=2 * rows * width * 3 * width, bytes_accessed=20 * MIB, transcendentals=0),
        name="project",
    )(x, gain, shift, w, down, upq, upv)


def head_masks(x, heads, size):
    lane = lax.broadcasted_iota(jnp.int32, x.shape, 1)
    return [
        jnp.where((lane >= size * h) & (lane < size * (h + 1)), x, jnp.zeros_like(x))
        for h in range(heads)
    ]


def merge_heads(stacked, heads, size):
    rows = stacked.shape[0] // heads
    out = stacked[:rows]
    lane = lax.broadcasted_iota(jnp.int32, out.shape, 1)
    for h in range(1, heads):
        out = jnp.where(lane >= size * h, stacked[h * rows : (h + 1) * rows], out)
    return out


def attend_kernel(start_ref, q_ref, k_ref, v_ref, o_ref, p_ref, s_sc, bias_sc, *, size, strip):
    length = q_ref.shape[0]
    heads = q_ref.shape[1] // size
    blocks = length // TILE

    @pl.when(pl.program_id(0) == 0)
    def _():
        for i in range(blocks):
            n = (i + 1) * TILE
            for r in range(i * TILE, n, strip):
                keys = lax.broadcasted_iota(jnp.int32, (strip, n), 1)
                rows = lax.broadcasted_iota(jnp.int32, (strip, n), 0) + r
                allowed = (keys >= start_ref[r : r + strip, :]) & (keys <= rows)
                bias_sc[r : r + strip, 0:n] = jnp.where(allowed, 0.0, NEGATIVE)

    def scores(i):
        masked = jnp.concatenate(head_masks(q_ref[i * TILE : (i + 1) * TILE, :], heads, size), 0)
        for j in range(i + 1):
            s_sc[i % 2, :, j * TILE : (j + 1) * TILE] = dg(masked, k_ref[j * TILE : (j + 1) * TILE, :], NT)

    def soft(i):
        n = (i + 1) * TILE
        for r in range(0, TILE, strip):
            for h in range(heads):
                at = h * TILE + r
                s = s_sc[i % 2, at : at + strip, 0:n] + bias_sc[i * TILE + r : i * TILE + r + strip, 0:n]
                e = jnp.exp2(s - jnp.max(s, axis=1, keepdims=True))
                total = jnp.sum(e, axis=1, keepdims=True)
                p_ref[h, i * TILE + r : i * TILE + r + strip, 0:n] = (e * (1.0 / total)).astype(bf16)

    def mix(i):
        n = (i + 1) * TILE
        probs = p_ref[:, i * TILE : n, 0:n].reshape(heads * TILE, n)
        o_ref[i * TILE : n, :] = merge_heads(dg(probs, v_ref[0:n, :], NN), heads, size).astype(bf16)

    for t in range(blocks + 2):
        if t < blocks:
            scores(t)
        if 0 <= t - 1 < blocks:
            soft(t - 1)
        if 0 <= t - 2 < blocks:
            mix(t - 2)


def attend(starts, qkv, size):
    length, wide = qkv.shape
    width = wide // 3
    groups = width // GROUP
    per = GROUP // size
    return pl.pallas_call(
        functools.partial(attend_kernel, size=size, strip=32),
        grid=(groups,),
        in_specs=[
            resident((length, 1)),
            pl.BlockSpec((length, GROUP), lambda g: (0, g)),
            pl.BlockSpec((length, GROUP), lambda g: (0, g + groups)),
            pl.BlockSpec((length, GROUP), lambda g: (0, g + 2 * groups)),
        ],
        out_specs=[
            pl.BlockSpec((length, GROUP), lambda g: (0, g)),
            pl.BlockSpec((per, length, length), lambda g: (g, 0, 0)),
        ],
        out_shape=[
            jax.ShapeDtypeStruct((length, width), bf16),
            jax.ShapeDtypeStruct((per * groups, length, length), bf16),
        ],
        scratch_shapes=[
            pltpu.VMEM((2, per * TILE, length), f32),
            pltpu.VMEM((length, length), f32),
        ],
        compiler_params=params(48),
        cost_estimate=pl.CostEstimate(flops=20 * 10**9, bytes_accessed=40 * MIB, transcendentals=0),
        name="attend",
    )(starts, qkv, qkv, qkv)


def attend_back_kernel(q_ref, k_ref, v_ref, g_ref, o_ref, p_ref, dq_ref, dk_ref, dv_ref, dp_sc, ds_sc, dk_sc, dv_sc, *, size, strip):
    length = q_ref.shape[0]
    heads = q_ref.shape[1] // size
    blocks = length // TILE
    scale = size**-0.5

    def stack(ref, i):
        return jnp.concatenate(head_masks(ref[i * TILE : (i + 1) * TILE, :], heads, size), 0)

    def prob_grads(i):
        masked = stack(g_ref, i)
        for j in range(i + 1):
            dp_sc[i % 2, :, j * TILE : (j + 1) * TILE] = dg(masked, v_ref[j * TILE : (j + 1) * TILE, :], NT)

    def score_grads(i):
        n = (i + 1) * TILE
        both = g_ref[i * TILE : n, :].astype(f32) * o_ref[i * TILE : n, :].astype(f32)
        for h in range(heads):
            for r in range(0, TILE, strip):
                at = h * TILE + r
                inner = jnp.sum(both[r : r + strip, size * h : size * (h + 1)], axis=1, keepdims=True)
                prob = p_ref[h, i * TILE + r : i * TILE + r + strip, 0:n].astype(f32)
                ds_sc[i % 2, at : at + strip, 0:n] = (prob * (dp_sc[i % 2, at : at + strip, 0:n] - inner)).astype(bf16)

    def products(i):
        n = (i + 1) * TILE
        dq = merge_heads(dg(ds_sc[i % 2, :, 0:n], k_ref[0:n, :], NN), heads, size)
        dq_ref[i * TILE : n, :] = (dq * scale).astype(bf16)
        grad4 = stack(g_ref, i)
        query4 = stack(q_ref, i)
        for j in range(i + 1):
            at = slice(j * TILE, (j + 1) * TILE)
            dv = dg(p_ref[:, i * TILE : n, at].reshape(heads * TILE, TILE), grad4, TN)
            dk = dg(ds_sc[i % 2, :, at], query4, TN)
            if i == j:
                dv_sc[at] = dv
                dk_sc[at] = dk
            else:
                dv_sc[at] += dv
                dk_sc[at] += dk

    for t in range(blocks + 2):
        if t < blocks:
            prob_grads(t)
        if 0 <= t - 1 < blocks:
            score_grads(t - 1)
        if 0 <= t - 2 < blocks:
            products(t - 2)
    dk_ref[...] = (dk_sc[...] * LN2).astype(bf16)
    dv_ref[...] = dv_sc[...].astype(bf16)


def attend_back_slot(qkv, grad, context, probs, size):
    length, wide = qkv.shape
    width = wide // 3
    groups = width // GROUP
    per = GROUP // size
    part = pl.BlockSpec((length, GROUP), lambda g: (0, g))
    return pl.pallas_call(
        functools.partial(attend_back_kernel, size=size, strip=32),
        grid=(groups,),
        in_specs=[
            part,
            pl.BlockSpec((length, GROUP), lambda g: (0, g + groups)),
            pl.BlockSpec((length, GROUP), lambda g: (0, g + 2 * groups)),
            part,
            part,
            pl.BlockSpec((per, length, length), lambda g: (g, 0, 0)),
        ],
        out_specs=[part] * 3,
        out_shape=[jax.ShapeDtypeStruct((length, width), bf16)] * 3,
        scratch_shapes=[
            pltpu.VMEM((2, per * TILE, length), f32),
            pltpu.VMEM((2, per * TILE, length), bf16),
            pltpu.VMEM((length, GROUP), f32),
            pltpu.VMEM((length, GROUP), f32),
        ],
        compiler_params=params(56),
        cost_estimate=pl.CostEstimate(flops=30 * 10**9, bytes_accessed=45 * MIB, transcendentals=0),
        name="attend_back",
    )(qkv, qkv, qkv, grad, context, probs)


def feed_kernel(
    x_ref, y_ref, ctx_ref, mask_ref, wo_ref, gain_ref, shift_ref, wi_ref, bias_ref, wf_ref,
    out_ref, hg_ref, cg_ref, sums_ref, fwd_sc, bwd_sc,
):
    width = x_ref.shape[-1]
    hidden_units = wi_ref.shape[1]
    branch = dg(ctx_ref[...], wo_ref[...], NN)
    hidden = x_ref[0].astype(f32) + branch
    unit, rs = norm_stats(hidden)
    gain = gain_ref[...]
    normed = (unit * gain + shift_ref[...]).astype(bf16)
    dy = y_ref[0]
    step = 512
    c0 = 0.7978845608028654
    c1 = c0 * 0.044715
    for at in range(0, hidden_units, step):
        v = dg(normed, wi_ref[:, at : at + step], NN) + bias_ref[:, at : at + step]
        act_grad = dg(dy, wf_ref[at : at + step, :], NT)
        square = v * v
        half = 0.5 * jnp.tanh(v * (c0 + c1 * square)) + 0.5
        act = v * half
        slope = half + act * (1.0 - half) * (2.0 * c0 + 6.0 * c1 * square)
        fwd_sc[:, at : at + step] = act.astype(bf16)
        bwd_sc[:, at : at + step] = (slope * act_grad).astype(bf16)
    feed = dg(fwd_sc[...], wf_ref[...], NN)
    result = hidden + feed
    out_ref[0] = result.astype(bf16)
    valid = mask_ref[...]
    one = jnp.sum(valid * (result * result))
    two = jnp.sum(valid * (branch * branch + feed * feed))
    count = jnp.sum(valid)
    row = lax.broadcasted_iota(jnp.int32, sums_ref.shape, 0)
    col = lax.broadcasted_iota(jnp.int32, sums_ref.shape, 1)
    mine = jnp.where(col == 0, one, jnp.where(col == 1, two, jnp.where(col == 2, count, 0.0)))
    mine = jnp.where(row == 0, mine, 0.0)

    @pl.when(pl.program_id(0) == 0)
    def _():
        sums_ref[...] = mine

    @pl.when(pl.program_id(0) > 0)
    def _():
        sums_ref[...] += mine

    normed_grad = dg(bwd_sc[...], wi_ref[...], NT)
    hidden_grad = dy.astype(f32) + norm_grad(unit, rs, gain, normed_grad)
    low = hidden_grad.astype(bf16)
    hg_ref[...] = low
    cg_ref[...] = dg(low, wo_ref[...], NT).astype(bf16)


def feed(x, dy, context, mask, wo, gain, shift, wi, bias, wf):
    blocks, tile, width = x.shape
    rows = blocks * tile
    units = wi.shape[1]
    slab = pl.BlockSpec((1, tile, width), lambda i: (i, 0, 0))
    flat = pl.BlockSpec((tile, width), lambda i: (i, 0))
    return pl.pallas_call(
        feed_kernel,
        grid=(blocks,),
        in_specs=[
            slab, slab, flat,
            pl.BlockSpec((tile, 1), lambda i: (i, 0)),
            resident(wo.shape), resident((1, width)), resident((1, width)),
            resident(wi.shape), resident((1, units)), resident(wf.shape),
        ],
        out_specs=[slab, flat, flat, pl.BlockSpec((8, width), lambda i: (0, 0))],
        out_shape=[
            jax.ShapeDtypeStruct(x.shape, bf16),
            jax.ShapeDtypeStruct((rows, width), bf16),
            jax.ShapeDtypeStruct((rows, width), bf16),
            jax.ShapeDtypeStruct((8, width), f32),
        ],
        scratch_shapes=[pltpu.VMEM((tile, units), bf16), pltpu.VMEM((tile, units), bf16)],
        compiler_params=params(60),
        cost_estimate=pl.CostEstimate(flops=2 * rows * width * (4 * units + 2 * width), bytes_accessed=30 * MIB, transcendentals=0),
        name="feed",
    )(x, dy, context, mask, wo, gain, shift, wi, bias, wf)


def qkv_back_kernel(
    x_ref, hg_ref, dq_ref, dk_ref, dv_ref, normed_ref, low_ref, gain_ref, w_ref, down_ref, upq_ref, upv_ref, sums_ref,
    out_ref, grads_ref,
):
    width = x_ref.shape[-1]
    ranks = down_ref.shape[1]
    half = ranks // 2
    dq, dk, dv = dq_ref[...], dk_ref[...], dv_ref[...]
    low_grad = (ADAPTER_SCALE * (dg(dq, upq_ref[...], NT) + dg(dv, upv_ref[...], NT))).astype(bf16)
    normed_grad = (
        dg(dq, w_ref[:, :width], NT)
        + dg(dk, w_ref[:, width : 2 * width], NT)
        + dg(dv, w_ref[:, 2 * width :], NT)
        + dg(low_grad, down_ref[...], NT)
    )
    unit, rs = norm_stats(x_ref[0].astype(f32))
    out_ref[0] = (hg_ref[...].astype(f32) + norm_grad(unit, rs, gain_ref[...], normed_grad)).astype(bf16)
    downs = dg(low_grad, normed_ref[...], TN)
    low = low_ref[...]
    ups_q = ADAPTER_SCALE * dg(low, dq, TN)[:half]
    ups_v = ADAPTER_SCALE * dg(low, dv, TN)[half:]
    mine = jnp.concatenate([downs, ups_q, ups_v], 0)

    @pl.when(pl.program_id(0) == 0)
    def _():
        grads_ref[0 : 2 * ranks] = mine
        grads_ref[2 * ranks :] = sums_ref[...]

    @pl.when(pl.program_id(0) > 0)
    def _():
        grads_ref[0 : 2 * ranks] += mine


def project_back(x, hidden_grad, dq, dk, dv, normed, low, gain, w, down, upq, upv, sums):
    blocks, tile, width = x.shape
    ranks = down.shape[1]
    slab = pl.BlockSpec((1, tile, width), lambda i: (i, 0, 0))
    flat = pl.BlockSpec((tile, width), lambda i: (i, 0))
    return pl.pallas_call(
        qkv_back_kernel,
        grid=(blocks,),
        in_specs=[
            slab, flat, flat, flat, flat, flat,
            pl.BlockSpec((tile, ranks), lambda i: (i, 0)),
            resident((1, width)), resident(w.shape), resident(down.shape), resident(upq.shape), resident(upv.shape),
            resident(sums.shape),
        ],
        out_specs=[slab, pl.BlockSpec((2 * ranks + 8, width), lambda i: (0, 0))],
        out_shape=[
            jax.ShapeDtypeStruct(x.shape, bf16),
            jax.ShapeDtypeStruct((2 * ranks + 8, width), f32),
        ],
        compiler_params=params(40),
        cost_estimate=pl.CostEstimate(flops=2 * blocks * tile * width * 3 * width, bytes_accessed=20 * MIB, transcendentals=0),
        name="project_back",
    )(x, hidden_grad, dq, dk, dv, normed, low, gain, w, down, upq, upv, sums)


def swap_slabs(me, group, count, refs, send_sem, recv_sem, local_sem):
    copies = []
    for a, (src, dst) in enumerate(refs):
        local = pltpu.make_async_copy(src.at[me], dst.at[me], local_sem.at[a])
        local.start()
        copies.append(local)
    order = [k for k in range(count - 1, 0, -1)]
    for a, (src, dst) in enumerate(refs):
        for k in order:
            peer = lax.rem(me + k, count)
            copy = pltpu.make_async_remote_copy(
                src_ref=src.at[peer],
                dst_ref=dst.at[me],
                send_sem=send_sem.at[a, k],
                recv_sem=recv_sem.at[a, k],
                device_id=(group, peer),
                device_id_type=MESH,
            )
            copy.start()
            copies.append(copy)
    return copies


def entry_barrier(peers):
    barrier = pltpu.get_barrier_semaphore()
    for peer in peers:
        pl.semaphore_signal(barrier, inc=1, device_id=peer, device_id_type=MESH)
    pl.semaphore_wait(barrier, len(peers))


def arrive_kernel(x_ref, mask_ref, xs_ref, masks_ref, send_sem, recv_sem, local_sem):
    count = x_ref.shape[0]
    group, me = lax.axis_index("dp"), lax.axis_index("head")
    entry_barrier([(group, lax.rem(me + k, count)) for k in range(1, count)])
    for copy in swap_slabs(me, group, count, [(x_ref, xs_ref), (mask_ref, masks_ref)], send_sem, recv_sem, local_sem):
        copy.wait()


def arrive(x, mask):
    count = x.shape[0]
    anywhere = pl.BlockSpec(memory_space=pl.ANY)
    return pl.pallas_call(
        arrive_kernel,
        in_specs=[anywhere] * 2,
        out_specs=[anywhere] * 2,
        out_shape=[jax.ShapeDtypeStruct(x.shape, x.dtype), jax.ShapeDtypeStruct(mask.shape, mask.dtype)],
        scratch_shapes=[
            pltpu.SemaphoreType.DMA((2, count)),
            pltpu.SemaphoreType.DMA((2, count)),
            pltpu.SemaphoreType.DMA((2,)),
        ],
        compiler_params=pltpu.CompilerParams(collective_id=0, has_side_effects=True),
        name="arrive",
    )(x, mask)


def leave_kernel(x_ref, part_ref, xs_ref, total_ref, sums, heard, send_sem, recv_sem, local_sem, sum_send, sum_recv, *, sizes):
    count = x_ref.shape[0]
    group, me = lax.axis_index("dp"), lax.axis_index("head")
    swaps = []
    step = 1
    while step < sizes[1]:
        swaps.append((group, me ^ step))
        step *= 2
    step = 1
    while step < sizes[0]:
        swaps.append((group ^ step, me))
        step *= 2
    entry_barrier([(group, lax.rem(me + k, count)) for k in range(1, count)] + swaps[count.bit_length() - 1 :])
    copies = swap_slabs(me, group, count, [(x_ref, xs_ref)], send_sem, recv_sem, local_sem)
    sums[0] = part_ref[...]
    for at, peer in enumerate(swaps):
        copy = pltpu.make_async_remote_copy(
            src_ref=sums.at[at],
            dst_ref=heard.at[at],
            send_sem=sum_send.at[at],
            recv_sem=sum_recv.at[at],
            device_id=peer,
            device_id_type=MESH,
        )
        copy.start()
        copy.wait()
        if at + 1 < len(swaps):
            sums[at + 1] = sums[at] + heard[at]
        else:
            total_ref[...] = sums[at] + heard[at]
    for copy in copies:
        copy.wait()


def leave(x, part, sizes):
    count = x.shape[0]
    steps = (sizes[0].bit_length() - 1) + (sizes[1].bit_length() - 1)
    anywhere = pl.BlockSpec(memory_space=pl.ANY)
    inside = pl.BlockSpec(memory_space=pltpu.VMEM)
    return pl.pallas_call(
        functools.partial(leave_kernel, sizes=sizes),
        in_specs=[anywhere, inside],
        out_specs=[anywhere, inside],
        out_shape=[jax.ShapeDtypeStruct(x.shape, x.dtype), jax.ShapeDtypeStruct(part.shape, f32)],
        scratch_shapes=[
            pltpu.VMEM((steps,) + part.shape, f32),
            pltpu.VMEM((steps,) + part.shape, f32),
            pltpu.SemaphoreType.DMA((1, count)),
            pltpu.SemaphoreType.DMA((1, count)),
            pltpu.SemaphoreType.DMA((1,)),
            pltpu.SemaphoreType.DMA((steps,)),
            pltpu.SemaphoreType.DMA((steps,)),
        ],
        compiler_params=pltpu.CompilerParams(collective_id=1, has_side_effects=True),
        name="leave",
    )(x, part)


def permuted(x, me, count):
    parts = [lax.dynamic_index_in_dim(x, me, 0, keepdims=False)]
    for k in range(1, count):
        mine = lax.dynamic_index_in_dim(x, lax.rem(me + k, count), 0, keepdims=False)
        parts.append(lax.ppermute(mine, "head", [(d, (d + k) % count) for d in range(count)]))
    out = x
    for k in range(count):
        out = lax.dynamic_update_index_in_dim(out, parts[k], lax.rem(me + count - k, count), 0)
    return out


def whole_slots(
    block_input_rows,
    document_starts,
    counted_mask,
    output_gradient,
    first_norm_gain,
    first_norm_bias,
    query_key_value_weight,
    query_down_weight,
    query_up_weight,
    value_down_weight,
    value_up_weight,
    attention_out_weight,
    second_norm_gain,
    second_norm_bias,
    feed_input_weight,
    feed_input_bias,
    feed_output_weight,
):
    slots, local_len, width = block_input_rows.shape
    sizes = (lax.axis_size("dp"), lax.axis_size("head"))
    length = local_len * slots
    size = width // H
    rank = query_down_weight.shape[1]
    me = lax.axis_index("head")

    def row(v):
        return v.astype(f32).reshape(1, -1)

    starts = lax.dynamic_index_in_dim(document_starts, me, 0, keepdims=False).reshape(length, 1)
    down = jnp.concatenate([query_down_weight, value_down_weight], 1)
    blank = jnp.zeros_like(query_up_weight)
    upq = jnp.concatenate([query_up_weight, blank], 0)
    upv = jnp.concatenate([blank, value_up_weight], 0)
    mask8 = jnp.broadcast_to(counted_mask.astype(f32)[:, None, :], (slots, 8, local_len))
    gain_one = row(first_norm_gain)

    x, masks = arrive(block_input_rows, mask8)
    dy = permuted(output_gradient, me, slots)
    mask = masks[:, 0, :].reshape(length, 1)
    qkv, normed, low = project(x, gain_one, row(first_norm_bias), query_key_value_weight, down, upq, upv)
    context, probs = attend(starts, qkv, size)
    out, hidden_grad, context_grad, sums = feed(
        x, dy, context, mask, attention_out_weight, row(second_norm_gain), row(second_norm_bias),
        feed_input_weight, row(feed_input_bias), feed_output_weight,
    )
    output = permuted(out, me, slots)
    dq, dk, dv = attend_back_slot(qkv, context_grad, context, probs, size)
    grad, grads = project_back(
        x, hidden_grad, dq, dk, dv, normed, low, gain_one, query_key_value_weight, down, upq, upv, sums
    )
    input_grad, total = leave(grad, grads, sizes)
    count = jnp.maximum(total[4 * rank, 2], 1.0)
    rms_values = jnp.stack(
        [
            jnp.sqrt(total[4 * rank, 0] / (count * width)),
            jnp.sqrt(total[4 * rank, 1] / (2.0 * count * width)),
        ]
    )
    return (
        output,
        input_grad,
        total[0:rank].T,
        total[2 * rank : 3 * rank],
        total[rank : 2 * rank].T,
        total[3 * rank : 4 * rank],
        rms_values,
    )


def body(*args):
    same = args[0].shape[0] == lax.axis_size("head")
    return whole_slots(*args) if same else shards(*args)


def solution(mesh):
    return jax.shard_map(
        body,
        mesh=mesh,
        in_specs=(
            P("dp", "head", None),
            P("dp", None),
            P("dp", "head"),
            P("dp", "head", None),
            P(),
            P(),
            P(),
            P(),
            P(),
            P(),
            P(),
            P(),
            P(),
            P(),
            P(),
            P(),
            P(),
        ),
        out_specs=(P("dp", "head", None), P("dp", "head", None), P(), P(), P(), P(), P()),
        check_vma=False,
    )
```

```python
import functools

import jax
import jax.numpy as jnp
from jax import lax
from jax.experimental import pallas as pl
from jax.experimental.pallas import tpu as pltpu
from jax.sharding import PartitionSpec as P

H = 16


EPSILON = 1e-05
ADAPTER_SCALE = 8.0
NEGATIVE = -1e30


def as_sent(x):

    def short(part):
        return part.astype(jnp.bfloat16) if part.dtype == jnp.float32 else part

    return jax.tree.map(short, x)


def norm_rows(matrix, gain_vec, shift_vec):
    center = matrix - jnp.mean(matrix, axis=-1, keepdims=True)
    variance = jnp.mean(center * center, axis=-1, keepdims=True)
    return center * lax.rsqrt(variance + EPSILON) * gain_vec + shift_vec


def norm_back(matrix, gain_vec, shift_vec, incoming):
    pullback = jax.vjp(lambda element_item: norm_rows(element_item, gain_vec, shift_vec), matrix)[1]
    return pullback(incoming)[0]


def gelu_tanh(matrix):
    return jax.nn.gelu(matrix, approximate=True)


def plain_product(left, right):
    return jnp.dot(left, right, preferred_element_type=jnp.float32)


def last_product(left, right):
    return lax.dot_general(
        left, right, (((1,), (1,)), ((), ())), preferred_element_type=jnp.float32
    )


def first_product(left, right):
    return lax.dot_general(
        left, right, (((0,), (0,)), ((), ())), preferred_element_type=jnp.float32
    )


def masked_scores(query_block, key_slot, segments, row_start, row_end, score_scale):
    places = jnp.arange(row_end)
    allowed = (segments[row_start:row_end, None] == segments[None, :row_end]) & (
        places[None, :] <= places[row_start:row_end, None]
    )
    scores = (
        jnp.einsum(
            "qhd,khd->hqk", query_block, key_slot[:row_end], preferred_element_type=jnp.float32
        )
        * score_scale
    )
    return jnp.where(allowed[None], scores, NEGATIVE)


def attend_slot(query_slot, key_slot, value_slot, segments, block_rows, score_scale):
    length = query_slot.shape[0]
    outputs_list = []
    logsum_list = []
    for block_index in range(length // block_rows):
        row_start = block_index * block_rows
        row_end = row_start + block_rows
        scores = masked_scores(
            query_slot[row_start:row_end], key_slot, segments, row_start, row_end, score_scale
        )
        row_max = jnp.max(scores, axis=-1, keepdims=True)
        exponent = jnp.exp(scores - row_max)
        row_total = jnp.sum(exponent, axis=-1, keepdims=True)
        probability = (exponent / row_total).astype(jnp.bfloat16)
        context = jnp.einsum(
            "hqk,khd->qhd", probability, value_slot[:row_end], preferred_element_type=jnp.float32
        )
        outputs_list.append(context.astype(jnp.bfloat16))
        logsum_list.append((row_max + jnp.log(row_total))[..., 0])
    return (jnp.concatenate(outputs_list, 0), jnp.concatenate(logsum_list, 1))


def attend_back(
    query_slot, key_slot, value_slot, grad_slot, logsum, segments, block_rows, score_scale
):
    length = query_slot.shape[0]
    key_grad = jnp.zeros(key_slot.shape, jnp.float32)
    value_gradient = jnp.zeros(value_slot.shape, jnp.float32)
    query_parts = []
    for block_index in range(length // block_rows):
        row_start = block_index * block_rows
        row_end = row_start + block_rows
        query_block = query_slot[row_start:row_end]
        grad_block = grad_slot[row_start:row_end]
        scores = masked_scores(query_block, key_slot, segments, row_start, row_end, score_scale)
        probability = jnp.exp(scores - logsum[:, row_start:row_end, None])
        prob_grad = jnp.einsum(
            "qhd,khd->hqk", grad_block, value_slot[:row_end], preferred_element_type=jnp.float32
        )
        inner_sum = jnp.sum(probability * prob_grad, axis=-1, keepdims=True)
        score_grad = (probability * (prob_grad - inner_sum)).astype(jnp.bfloat16)
        query_parts.append(
            jnp.einsum(
                "hqk,khd->qhd", score_grad, key_slot[:row_end], preferred_element_type=jnp.float32
            )
            * score_scale
        )
        key_grad = key_grad.at[:row_end].add(
            jnp.einsum("hqk,qhd->khd", score_grad, query_block, preferred_element_type=jnp.float32)
            * score_scale
        )
        value_gradient = value_gradient.at[:row_end].add(
            jnp.einsum(
                "hqk,qhd->khd",
                probability.astype(jnp.bfloat16),
                grad_block,
                preferred_element_type=jnp.float32,
            )
        )
    query_gradient = jnp.concatenate(query_parts, 0)
    return (
        query_gradient.astype(jnp.bfloat16),
        key_grad.astype(jnp.bfloat16),
        value_gradient.astype(jnp.bfloat16),
    )


def shards(
    block_input_rows,
    document_starts,
    counted_mask,
    output_gradient,
    first_norm_gain,
    first_norm_bias,
    query_key_value_weight,
    query_down_weight,
    query_up_weight,
    value_down_weight,
    value_up_weight,
    attention_out_weight,
    second_norm_gain,
    second_norm_bias,
    feed_input_weight,
    feed_input_bias,
    feed_output_weight,
):
    slot_count, local_len, row_width = block_input_rows.shape
    groups = lax.axis_size("head")
    full_len = local_len * groups
    head_size = row_width // H
    heads_here = H // groups
    row_count = slot_count * local_len
    block_rows = min(512, full_len)
    score_scale = head_size ** (-0.5)
    gain_one = first_norm_gain.astype(jnp.float32)
    shift_one = first_norm_bias.astype(jnp.float32)
    gain_two = second_norm_gain.astype(jnp.float32)
    shift_two = second_norm_bias.astype(jnp.float32)
    fc_bias = feed_input_bias.astype(jnp.float32)
    local_shape = (slot_count, local_len, row_width)
    split_shape = (slot_count, full_len, heads_here, head_size)
    merged_shape = (slot_count, full_len, heads_here * head_size)
    flat_in = block_input_rows.reshape(row_count, row_width).astype(jnp.float32)
    normed_rows = norm_rows(flat_in, gain_one, shift_one).astype(jnp.bfloat16)
    query_low_rank = plain_product(normed_rows, query_down_weight).astype(jnp.bfloat16)
    value_low_rank = plain_product(normed_rows, value_down_weight).astype(jnp.bfloat16)
    projected_rows = plain_product(normed_rows, query_key_value_weight)
    query_rows = (
        projected_rows[:, :row_width]
        + ADAPTER_SCALE * plain_product(query_low_rank, query_up_weight)
    ).astype(jnp.bfloat16)
    key_rows = projected_rows[:, row_width : 2 * row_width].astype(jnp.bfloat16)
    value_matrix = (
        projected_rows[:, 2 * row_width :]
        + ADAPTER_SCALE * plain_product(value_low_rank, value_up_weight)
    ).astype(jnp.bfloat16)
    head_query, head_key, head_value = (
        lax.all_to_all(
            query_rows.reshape(local_shape), "head", split_axis=2, concat_axis=1, tiled=True
        ),
        lax.all_to_all(
            key_rows.reshape(local_shape), "head", split_axis=2, concat_axis=1, tiled=True
        ),
        lax.all_to_all(
            value_matrix.reshape(local_shape), "head", split_axis=2, concat_axis=1, tiled=True
        ),
    )
    head_query = head_query.reshape(split_shape)
    head_key = head_key.reshape(split_shape)
    head_value = head_value.reshape(split_shape)

    def slot_fn(packed):
        return attend_slot(packed[0], packed[1], packed[2], packed[3], block_rows, score_scale)

    context_heads, logsum = lax.map(slot_fn, (head_query, head_key, head_value, document_starts))
    context_local = lax.all_to_all(
        as_sent(context_heads.reshape(merged_shape)),
        "head",
        split_axis=1,
        concat_axis=2,
        tiled=True,
    )
    context_flat = context_local.reshape(row_count, row_width)
    branch = plain_product(context_flat, attention_out_weight)
    hidden_state = flat_in + branch
    normed_two = norm_rows(hidden_state, gain_two, shift_two).astype(jnp.bfloat16)
    before = plain_product(normed_two, feed_input_weight) + fc_bias
    activated = gelu_tanh(before).astype(jnp.bfloat16)
    feed_out = plain_product(activated, feed_output_weight)
    result = hidden_state + feed_out
    output = result.astype(jnp.bfloat16).reshape(block_input_rows.shape)
    valid_rows = counted_mask.reshape(row_count).astype(jnp.float32)[:, None]
    square_sums = jnp.stack(
        [
            jnp.sum(valid_rows * result * result),
            jnp.sum(valid_rows * (branch * branch + feed_out * feed_out)),
            jnp.sum(valid_rows),
        ]
    )
    grad_flat = output_gradient.reshape(row_count, row_width)
    act_grad = last_product(grad_flat, feed_output_weight)
    gelu_pull = jax.vjp(gelu_tanh, before)[1]
    before_grad = gelu_pull(act_grad)[0].astype(jnp.bfloat16)
    normed_two_grad = last_product(before_grad, feed_input_weight)
    hidden_grad = grad_flat.astype(jnp.float32) + norm_back(
        hidden_state, gain_two, shift_two, normed_two_grad
    )
    branch_grad = hidden_grad.astype(jnp.bfloat16)
    context_grad = last_product(branch_grad, attention_out_weight).astype(jnp.bfloat16)
    grad_heads = lax.all_to_all(
        context_grad.reshape(local_shape), "head", split_axis=2, concat_axis=1, tiled=True
    ).reshape(split_shape)

    def back_fn(packed):
        return attend_back(
            packed[0],
            packed[1],
            packed[2],
            packed[3],
            packed[4],
            packed[5],
            block_rows,
            score_scale,
        )

    query_gradient, key_grad, value_gradient = lax.map(
        back_fn, (head_query, head_key, head_value, grad_heads, logsum, document_starts)
    )
    query_gradient, key_grad, value_gradient = (
        lax.all_to_all(
            as_sent(query_gradient.reshape(merged_shape)),
            "head",
            split_axis=1,
            concat_axis=2,
            tiled=True,
        ),
        lax.all_to_all(
            as_sent(key_grad.reshape(merged_shape)), "head", split_axis=1, concat_axis=2, tiled=True
        ),
        lax.all_to_all(
            as_sent(value_gradient.reshape(merged_shape)),
            "head",
            split_axis=1,
            concat_axis=2,
            tiled=True,
        ),
    )
    query_gradient = query_gradient.reshape(row_count, row_width)
    key_grad = key_grad.reshape(row_count, row_width)
    value_gradient = value_gradient.reshape(row_count, row_width)
    query_low_gradient = (ADAPTER_SCALE * last_product(query_gradient, query_up_weight)).astype(
        jnp.bfloat16
    )
    value_low_gradient = (ADAPTER_SCALE * last_product(value_gradient, value_up_weight)).astype(
        jnp.bfloat16
    )
    joined_grads = jnp.concatenate([query_gradient, key_grad, value_gradient], axis=1)
    normed_grad = (
        last_product(joined_grads, query_key_value_weight)
        + last_product(query_low_gradient, query_down_weight)
        + last_product(value_low_gradient, value_down_weight)
    )
    input_grad = hidden_grad + norm_back(flat_in, gain_one, shift_one, normed_grad)
    down_query = first_product(normed_rows, query_low_gradient)
    lifted_query = ADAPTER_SCALE * first_product(query_low_rank, query_gradient)
    down_value = first_product(normed_rows, value_low_gradient)
    lifted_value = ADAPTER_SCALE * first_product(value_low_rank, value_gradient)
    totals = lax.psum(
        (down_query, lifted_query, down_value, lifted_value, square_sums), ("dp", "head")
    )
    token_count = jnp.maximum(totals[4][2], 1.0)
    rms_values = jnp.stack(
        [
            jnp.sqrt(totals[4][0] / (token_count * row_width)),
            jnp.sqrt(totals[4][1] / (2.0 * token_count * row_width)),
        ]
    )
    return (
        output,
        input_grad.astype(jnp.bfloat16).reshape(block_input_rows.shape),
        totals[0],
        totals[1],
        totals[2],
        totals[3],
        rms_values,
    )


LOG2E = 1.4426950408889634
LN2 = 0.6931471805599453
TILE = 256
GROUP = 256
bf16 = jnp.bfloat16
f32 = jnp.float32
NT = (((1,), (1,)), ((), ()))
NN = (((1,), (0,)), ((), ()))
TN = (((0,), (0,)), ((), ()))
MESH = pl.DeviceIdType.MESH
MIB = 2**20


def dg(left, right, dims):
    return lax.dot_general(left, right, dims, preferred_element_type=f32)


def resident(shape):
    zeros = (0,) * len(shape)
    return pl.BlockSpec(shape, lambda *_: zeros, pipeline_mode=pl.Buffered(1))


def params(mib):
    return pltpu.CompilerParams(
        vmem_limit_bytes=mib * MIB, dimension_semantics=("arbitrary",)
    )


def norm_stats(rows):
    center = rows - jnp.mean(rows, axis=-1, keepdims=True)
    rs = lax.rsqrt(jnp.mean(center * center, axis=-1, keepdims=True) + EPSILON)
    return center * rs, rs


def norm_grad(unit, rs, gain, incoming):
    t = incoming * gain
    return (
        t - jnp.mean(t, axis=-1, keepdims=True) - unit * jnp.mean(t * unit, axis=-1, keepdims=True)
    ) * rs


def head_masks(x, heads, size):
    lane = lax.broadcasted_iota(jnp.int32, x.shape, 1)
    return [
        jnp.where((lane >= size * h) & (lane < size * (h + 1)), x, jnp.zeros_like(x))
        for h in range(heads)
    ]


def merge_heads(stacked, heads, size):
    rows = stacked.shape[0] // heads
    out = stacked[:rows]
    lane = lax.broadcasted_iota(jnp.int32, out.shape, 1)
    for h in range(1, heads):
        out = jnp.where(lane >= size * h, stacked[h * rows : (h + 1) * rows], out)
    return out


def column(line):
    return jnp.broadcast_to(line, (128, line.shape[1])).T


def entry_signal(peers):
    barrier = pltpu.get_barrier_semaphore()
    for peer in peers:
        pl.semaphore_signal(barrier, inc=1, device_id=peer, device_id_type=MESH)


def entry_wait(count):
    pl.semaphore_wait(pltpu.get_barrier_semaphore(), count)


def remote(src, dst, send_sem, recv_sem, peer):
    return pltpu.make_async_remote_copy(
        src_ref=src, dst_ref=dst, send_sem=send_sem, recv_sem=recv_sem, device_id=peer, device_id_type=MESH
    )


ANY = pl.BlockSpec(memory_space=pl.ANY)
VMEM = pl.BlockSpec(memory_space=pltpu.VMEM)


def attention_group(q_ref, k_ref, v_ref, o_ref, p_ref, s_sc, bias_sc, size, strip):
    length = q_ref.shape[0]
    heads = q_ref.shape[1] // size
    blocks = length // TILE

    def scores(i):
        masked = jnp.concatenate(head_masks(q_ref[i * TILE : (i + 1) * TILE, :], heads, size), 0)
        for j in range(i + 1):
            s_sc[i % 2, :, j * TILE : (j + 1) * TILE] = dg(masked, k_ref[j * TILE : (j + 1) * TILE, :], NT)

    def soft(i):
        n = (i + 1) * TILE
        for r in range(0, TILE, strip):
            for h in range(heads):
                at = h * TILE + r
                s = s_sc[i % 2, at : at + strip, 0:n] + bias_sc[i * TILE + r : i * TILE + r + strip, 0:n]
                e = jnp.exp2(s - jnp.max(s, axis=1, keepdims=True))
                total = jnp.sum(e, axis=1, keepdims=True)
                p_ref[h, i * TILE + r : i * TILE + r + strip, 0:n] = (e * (1.0 / total)).astype(bf16)

    def mix(i):
        n = (i + 1) * TILE
        probs = p_ref[:, i * TILE : n, 0:n].reshape(heads * TILE, n)
        o_ref[i * TILE : n, :] = merge_heads(dg(probs, v_ref[0:n, :], NN), heads, size).astype(bf16)

    for t in range(blocks + 2):
        if t < blocks:
            scores(t)
        if 0 <= t - 1 < blocks:
            soft(t - 1)
        if 0 <= t - 2 < blocks:
            mix(t - 2)


def open_kernel(
    x_ref, dy_ref, mask_ref, w_ref, start_ref, gain_ref, shift_ref, down_ref, upq_ref, upv_ref,
    xs_ref, dys_ref, masks_ref, qkv_ref, ctx_ref, p_ref,
    x_sc, w_sc, qkv_sc, s_sc, bias_sc,
    x_send, x_recv, y_send, y_recv, m_send, m_recv, local_sem,
    *, size, strip,
):
    slots, tile, width = x_ref.shape
    length = slots * tile
    half = length // 2
    groups = width // GROUP
    step = pl.program_id(0)
    group, me = lax.axis_index("dp"), lax.axis_index("head")
    mine = lax.rem(me, 2)
    near = me - mine
    far = slots // 2 - near
    beside = near + 1 - mine
    across = (far + mine, far + 1 - mine)
    peers = [(group, p) for p in (beside,) + across]

    def x_copy(k):
        return remote(x_ref.at[peers[k][1]], x_sc.at[me], x_send.at[k], x_recv.at[k], peers[k])

    def y_copy(k):
        return remote(dy_ref.at[peers[k][1]], dys_ref.at[me], y_send.at[k], y_recv.at[k], peers[k])

    def m_copy(k):
        return remote(mask_ref.at[peers[k][1]], masks_ref.at[me], m_send.at[k], m_recv.at[k], peers[k])

    def own_x():
        return pltpu.make_async_copy(x_ref.at[me], x_sc.at[me], local_sem.at[0])

    def own_y():
        return pltpu.make_async_copy(dy_ref.at[me], dys_ref.at[me], local_sem.at[1])

    def own_m():
        return pltpu.make_async_copy(mask_ref.at[me], masks_ref.at[me], local_sem.at[2])

    def weight():
        return pltpu.make_async_copy(w_ref, w_sc, local_sem.at[3])

    def save_x():
        return pltpu.make_async_copy(x_sc, xs_ref, local_sem.at[4])

    def save_qkv():
        return pltpu.make_async_copy(qkv_sc, qkv_ref, local_sem.at[5])

    def project(first):
        rows = x_sc[pl.ds(first, 2)].reshape(half, width).astype(f32)
        unit, _ = norm_stats(rows)
        normed = (unit * gain_ref[...] + shift_ref[...]).astype(bf16)
        low = dg(normed, down_ref[...], NN).astype(bf16)
        scale = size**-0.5 * LOG2E
        here = pl.ds(pl.multiple_of(first * tile, tile), half)
        wide = 512
        for at in range(0, 3 * width, wide):
            cols = slice(at, at + wide)
            part = dg(normed, w_sc[:, cols], NN)
            if at < width:
                part = (part + ADAPTER_SCALE * dg(low, upq_ref[:, cols], NN)) * scale
            if at >= 2 * width:
                part = part + ADAPTER_SCALE * dg(low, upv_ref[:, at - 2 * width : at - 2 * width + wide], NN)
            qkv_sc[here, cols] = part.astype(bf16)

    @pl.when(step == 0)
    def _():
        entry_signal(peers)
        own_x().start()
        weight().start()
        entry_wait(len(peers))
        for k in (1, 2, 0):
            x_copy(k).start()
        for k in range(3):
            m_copy(k).start()
        own_m().start()
        own_y().start()
        for i in range(length // TILE):
            n = (i + 1) * TILE
            first_key = column(start_ref[:, i * TILE : n])
            for r in range(0, TILE, strip):
                keys = lax.broadcasted_iota(jnp.int32, (strip, n), 1)
                rows = lax.broadcasted_iota(jnp.int32, (strip, n), 0) + (i * TILE + r)
                allowed = (keys >= first_key[r : r + strip, 0:1]) & (keys <= rows)
                bias_sc[i * TILE + r : i * TILE + r + strip, 0:n] = jnp.where(allowed, 0.0, NEGATIVE)
        own_x().wait()
        x_copy(0).wait_recv()
        weight().wait()
        project(near)

    @pl.when(step == 1)
    def _():
        for k in (1, 2):
            x_copy(k).wait()
        for k in (1, 2, 0):
            y_copy(k).start()
        save_x().start()
        project(far)
        save_qkv().start()

    @pl.when(step >= 2)
    def _():
        g = step - 2

        def part(third):
            return qkv_sc.at[:, pl.ds(pl.multiple_of(third * width + g * GROUP, GROUP), GROUP)]

        attention_group(part(0), part(1), part(2), ctx_ref, p_ref, s_sc, bias_sc, size, strip)

    @pl.when(step == groups + 1)
    def _():
        x_copy(0).wait_send()
        for k in range(3):
            y_copy(k).wait()
            m_copy(k).wait()
        own_m().wait()
        own_y().wait()
        save_x().wait()
        save_qkv().wait()


def opening(x, dy, mask, w, start, gain, shift, down, upq, upv, size):
    slots, tile, width = x.shape
    length = slots * tile
    groups = width // GROUP
    per = GROUP // size
    dma = pltpu.SemaphoreType.DMA
    return pl.pallas_call(
        functools.partial(open_kernel, size=size, strip=32),
        grid=(groups + 2,),
        in_specs=[ANY] * 4 + [
            resident(start.shape), resident(gain.shape), resident(shift.shape),
            resident(down.shape), resident(upq.shape), resident(upv.shape),
        ],
        out_specs=[ANY] * 4 + [
            pl.BlockSpec((length, GROUP), lambda t: (0, jnp.maximum(t - 2, 0))),
            pl.BlockSpec((per, length, length), lambda t: (jnp.maximum(t - 2, 0), 0, 0)),
        ],
        out_shape=[
            jax.ShapeDtypeStruct(x.shape, bf16),
            jax.ShapeDtypeStruct(x.shape, bf16),
            jax.ShapeDtypeStruct(mask.shape, f32),
            jax.ShapeDtypeStruct((length, 3 * width), bf16),
            jax.ShapeDtypeStruct((length, width), bf16),
            jax.ShapeDtypeStruct((per * groups, length, length), bf16),
        ],
        scratch_shapes=[
            pltpu.VMEM(x.shape, bf16),
            pltpu.VMEM(w.shape, bf16),
            pltpu.VMEM((length, 3 * width), bf16),
            pltpu.VMEM((2, per * TILE, length), f32),
            pltpu.VMEM((length, length), f32),
            dma((3,)), dma((3,)), dma((3,)), dma((3,)), dma((3,)), dma((3,)), dma((6,)),
        ],
        compiler_params=pltpu.CompilerParams(
            collective_id=0, has_side_effects=True, vmem_limit_bytes=60 * MIB, dimension_semantics=("arbitrary",)
        ),
        name="opening",
    )(x, dy, mask, w, start, gain, shift, down, upq, upv)


def feed_kernel(
    x_ref, y_ref, ctx_ref, mask_ref, wo_hbm, wi_hbm, wf_hbm, gain_ref, shift_ref, bias_ref,
    out_ref, hg_ref, cg_ref, sums_ref, wo_ref, wi_ref, wf_ref, fwd_sc, bwd_sc, sem,
    *, step,
):
    blocks, tile, width = x_ref.shape
    rows = blocks * tile
    hidden_units = wi_ref.shape[1]
    chunks = hidden_units // step
    first = pl.program_id(0) == 0

    def load_o():
        return pltpu.make_async_copy(wo_hbm, wo_ref, sem.at[2 * chunks])

    def load_i(c):
        cols = pl.ds(c * step, step)
        return pltpu.make_async_copy(wi_hbm.at[:, cols], wi_ref.at[:, cols], sem.at[2 * c])

    def load_f(c):
        cols = pl.ds(c * step, step)
        return pltpu.make_async_copy(wf_hbm.at[cols, :], wf_ref.at[cols, :], sem.at[2 * c + 1])

    @pl.when(first)
    def _():
        load_o().start()
        for c in range(chunks):
            load_i(c).start()
            load_f(c).start()
        load_o().wait()

    branch = dg(ctx_ref[...], wo_ref[...], NN)
    hidden = x_ref[...].reshape(rows, width).astype(f32) + branch
    unit, rs = norm_stats(hidden)
    gain = gain_ref[...]
    normed = (unit * gain + shift_ref[...]).astype(bf16)
    dy = y_ref[...].reshape(rows, width)
    c0 = 0.7978845608028654
    c1 = c0 * 0.044715
    for c in range(chunks):

        @pl.when(first)
        def _():
            load_i(c).wait()
            load_f(c).wait()

        at = c * step
        v = dg(normed, wi_ref[:, at : at + step], NN) + bias_ref[:, at : at + step]
        act_grad = dg(dy, wf_ref[at : at + step, :], NT)
        square = v * v
        half = 0.5 * jnp.tanh(v * (c0 + c1 * square)) + 0.5
        act = v * half
        slope = half + act * (1.0 - half) * (2.0 * c0 + 6.0 * c1 * square)
        fwd_sc[:, at : at + step] = act.astype(bf16)
        bwd_sc[:, at : at + step] = (slope * act_grad).astype(bf16)
    feed = dg(fwd_sc[...], wf_ref[...], NN)
    result = hidden + feed
    out_ref[...] = result.astype(bf16).reshape(out_ref.shape)
    valid = jnp.concatenate([column(mask_ref[b, 0:1, :])[:, 0:1] for b in range(blocks)], 0)
    one = jnp.sum(valid * (result * result))
    two = jnp.sum(valid * (branch * branch + feed * feed))
    count = jnp.sum(valid)
    row = lax.broadcasted_iota(jnp.int32, sums_ref.shape, 0)
    col = lax.broadcasted_iota(jnp.int32, sums_ref.shape, 1)
    mine = jnp.where(col == 0, one, jnp.where(col == 1, two, jnp.where(col == 2, count, 0.0)))
    mine = jnp.where(row == 0, mine, 0.0)

    @pl.when(first)
    def _():
        sums_ref[...] = mine

    @pl.when(jnp.logical_not(first))
    def _():
        sums_ref[...] += mine

    normed_grad = dg(bwd_sc[...], wi_ref[...], NT)
    hidden_grad = dy.astype(f32) + norm_grad(unit, rs, gain, normed_grad)
    low = hidden_grad.astype(bf16)
    hg_ref[...] = low
    cg_ref[...] = dg(low, wo_ref[...], NT).astype(bf16)


def feed(x, dy, context, mask, wo, gain, shift, wi, bias, wf):
    slots, tile, width = x.shape
    rows = slots * tile
    units = wi.shape[1]
    each = 1
    step = 512
    slab = pl.BlockSpec((each, tile, width), lambda i: (i, 0, 0))
    flat = pl.BlockSpec((each * tile, width), lambda i: (i, 0))
    return pl.pallas_call(
        functools.partial(feed_kernel, step=step),
        grid=(slots // each,),
        in_specs=[
            slab, slab, flat,
            pl.BlockSpec((each,) + mask.shape[1:], lambda i: (i, 0, 0)),
            ANY, ANY, ANY, resident((1, width)), resident((1, width)), resident((1, units)),
        ],
        out_specs=[slab, flat, flat, pl.BlockSpec((8, width), lambda i: (0, 0))],
        out_shape=[
            jax.ShapeDtypeStruct(x.shape, bf16),
            jax.ShapeDtypeStruct((rows, width), bf16),
            jax.ShapeDtypeStruct((rows, width), bf16),
            jax.ShapeDtypeStruct((8, width), f32),
        ],
        scratch_shapes=[
            pltpu.VMEM(wo.shape, bf16), pltpu.VMEM(wi.shape, bf16), pltpu.VMEM(wf.shape, bf16),
            pltpu.VMEM((each * tile, units), bf16), pltpu.VMEM((each * tile, units), bf16),
            pltpu.SemaphoreType.DMA((2 * (units // step) + 1,)),
        ],
        compiler_params=params(60),
        name="feed",
    )(x, dy, context, mask, wo, wi, wf, gain, shift, bias)


def attend_back_kernel(
    q_ref, k_ref, v_ref, g_ref, o_ref, p_ref, res_ref,
    dq_ref, dk_ref, dv_ref, out_ref,
    dp_sc, ds_sc, dk_sc, dv_sc, send, recv, local_sem,
    *, size, strip,
):
    length = q_ref.shape[0]
    heads = q_ref.shape[1] // size
    blocks = length // TILE
    scale = size**-0.5
    slots = res_ref.shape[0]
    group, me = lax.axis_index("dp"), lax.axis_index("head")
    peers = [(group, lax.rem(me + k, slots)) for k in range(1, slots)]
    grid_step = pl.program_id(0)

    def copy(k):
        return remote(res_ref.at[peers[k][1]], out_ref.at[me], send.at[k], recv.at[k], peers[k])

    def own():
        return pltpu.make_async_copy(res_ref.at[me], out_ref.at[me], local_sem)

    @pl.when(grid_step == 0)
    def _():
        entry_signal(peers)
        own().start()

    @pl.when(grid_step == 1)
    def _():
        entry_wait(len(peers))
        for k in range(len(peers)):
            copy(k).start()

    def stack(ref, i):
        return jnp.concatenate(head_masks(ref[i * TILE : (i + 1) * TILE, :], heads, size), 0)

    def prob_grads(i):
        masked = stack(g_ref, i)
        for j in range(i + 1):
            dp_sc[i % 2, :, j * TILE : (j + 1) * TILE] = dg(masked, v_ref[j * TILE : (j + 1) * TILE, :], NT)

    def score_grads(i):
        n = (i + 1) * TILE
        both = g_ref[i * TILE : n, :].astype(f32) * o_ref[i * TILE : n, :].astype(f32)
        for h in range(heads):
            for r in range(0, TILE, strip):
                at = h * TILE + r
                inner = jnp.sum(both[r : r + strip, size * h : size * (h + 1)], axis=1, keepdims=True)
                prob = p_ref[h, i * TILE + r : i * TILE + r + strip, 0:n].astype(f32)
                ds_sc[i % 2, at : at + strip, 0:n] = (prob * (dp_sc[i % 2, at : at + strip, 0:n] - inner)).astype(bf16)

    def products(i):
        n = (i + 1) * TILE
        dq = merge_heads(dg(ds_sc[i % 2, :, 0:n], k_ref[0:n, :], NN), heads, size)
        dq_ref[i * TILE : n, :] = (dq * scale).astype(bf16)
        grad4 = stack(g_ref, i)
        query4 = stack(q_ref, i)
        for j in range(i + 1):
            at = slice(j * TILE, (j + 1) * TILE)
            dv = dg(p_ref[:, i * TILE : n, at].reshape(heads * TILE, TILE), grad4, TN)
            dk = dg(ds_sc[i % 2, :, at], query4, TN)
            if i == j:
                dv_sc[at] = dv
                dk_sc[at] = dk
            else:
                dv_sc[at] += dv
                dk_sc[at] += dk

    for t in range(blocks + 2):
        if t < blocks:
            prob_grads(t)
        if 0 <= t - 1 < blocks:
            score_grads(t - 1)
        if 0 <= t - 2 < blocks:
            products(t - 2)
    dk_ref[...] = (dk_sc[...] * LN2).astype(bf16)
    dv_ref[...] = dv_sc[...].astype(bf16)

    @pl.when(grid_step == pl.num_programs(0) - 1)
    def _():
        own().wait()
        for k in range(len(peers)):
            copy(k).wait()


def attend_back_slot(qkv, grad, context, probs, result, size):
    length, wide = qkv.shape
    width = wide // 3
    groups = width // GROUP
    per = GROUP // size
    slots = result.shape[0]
    part = pl.BlockSpec((length, GROUP), lambda g: (0, g))
    dma = pltpu.SemaphoreType.DMA
    return pl.pallas_call(
        functools.partial(attend_back_kernel, size=size, strip=32),
        grid=(groups,),
        in_specs=[
            part,
            pl.BlockSpec((length, GROUP), lambda g: (0, g + groups)),
            pl.BlockSpec((length, GROUP), lambda g: (0, g + 2 * groups)),
            part,
            part,
            pl.BlockSpec((per, length, length), lambda g: (g, 0, 0)),
            ANY,
        ],
        out_specs=[part] * 3 + [ANY],
        out_shape=[jax.ShapeDtypeStruct((length, width), bf16)] * 3 + [jax.ShapeDtypeStruct(result.shape, bf16)],
        scratch_shapes=[
            pltpu.VMEM((2, per * TILE, length), f32),
            pltpu.VMEM((2, per * TILE, length), bf16),
            pltpu.VMEM((length, GROUP), f32),
            pltpu.VMEM((length, GROUP), f32),
            dma((slots - 1,)), dma((slots - 1,)), dma,
        ],
        compiler_params=pltpu.CompilerParams(
            collective_id=1, has_side_effects=True, vmem_limit_bytes=60 * MIB, dimension_semantics=("arbitrary",)
        ),
        name="attend_back",
    )(qkv, qkv, qkv, grad, context, probs, result)


def close_kernel(
    x_hbm, hg_hbm, dq_hbm, dk_hbm, dv_hbm, w_hbm, gain_ref, shift_ref, down_ref, upq_ref, upv_ref, sums_ref,
    out_ref, total_ref,
    x_sc, hg_sc, dq_sc, dk_sc, dv_sc, w_sc, res_sc, sums, heard,
    load_sem, send, recv, local_sem, sum_send, sum_recv,
    *, sizes,
):
    slots, tile, width = x_sc.shape
    ranks = down_ref.shape[1]
    half = ranks // 2
    group, me = lax.axis_index("dp"), lax.axis_index("head")
    mine = lax.rem(me, 2)
    near = me - mine
    far = slots // 2 - near
    beside = near + 1 - mine
    order = [far + mine, far + 1 - mine, beside, me]
    peers = [(group, p) for p in order[:3]]
    swaps = [(group, beside), (group, far + mine)]
    span = 1
    while span < sizes[0]:
        swaps.append((group ^ span, me))
        span *= 2

    entry_signal(peers + swaps[2:])
    arrays = [(x_hbm, x_sc), (hg_hbm, hg_sc), (dq_hbm, dq_sc), (dk_hbm, dk_sc), (dv_hbm, dv_sc)]

    def load(t, a):
        src, dst = arrays[a]
        return pltpu.make_async_copy(src.at[order[t]], dst.at[order[t]], load_sem.at[t, a])

    def weight():
        return pltpu.make_async_copy(w_hbm, w_sc, local_sem.at[0])

    weight().start()
    for t in range(slots):
        for a in range(len(arrays)):
            load(t, a).start()

    def adapters(t):
        s = order[t]
        low_grad = (ADAPTER_SCALE * (dg(dq_sc[s], upq_ref[...], NT) + dg(dv_sc[s], upv_ref[...], NT))).astype(bf16)
        unit, rs = norm_stats(x_sc[s].astype(f32))
        normed = (unit * gain_ref[...] + shift_ref[...]).astype(bf16)
        low = dg(normed, down_ref[...], NN).astype(bf16)
        downs = dg(low_grad, normed, TN)
        ups_q = ADAPTER_SCALE * dg(low, dq_sc[s], TN)[:half]
        ups_v = ADAPTER_SCALE * dg(low, dv_sc[s], TN)[half:]
        part = jnp.concatenate([downs, ups_q, ups_v], 0)
        if t == 0:
            sums[0, 0 : 2 * ranks] = part
            sums[0, 2 * ranks :] = sums_ref[...]
        else:
            sums[0, 0 : 2 * ranks] += part
        return low_grad, unit, rs

    def block(t, low_grad, unit, rs):
        s = order[t]
        normed_grad = (
            dg(dq_sc[s], w_sc[:, :width], NT)
            + dg(dk_sc[s], w_sc[:, width : 2 * width], NT)
            + dg(dv_sc[s], w_sc[:, 2 * width :], NT)
            + dg(low_grad, down_ref[...], NT)
        )
        res_sc[t] = (hg_sc[s].astype(f32) + norm_grad(unit, rs, gain_ref[...], normed_grad)).astype(bf16)

    def give(t):
        return remote(res_sc.at[t], out_ref.at[me], send.at[t], recv.at[t], peers[t])

    def keep():
        return pltpu.make_async_copy(res_sc.at[slots - 1], out_ref.at[me], local_sem.at[1])

    def share(at):
        return remote(sums.at[at], heard.at[at], sum_send.at[at], sum_recv.at[at], swaps[at])

    def add(at):
        share(at).wait()
        if at + 1 < len(swaps):
            sums[at + 1] = sums[at] + heard[at]
            share(at + 1).start()
        else:
            total_ref[...] = sums[at] + heard[at]

    kept = []
    for t in range(slots):
        for a in range(len(arrays)):
            load(t, a).wait()
        kept.append(adapters(t))
    entry_wait(len(peers) + len(swaps) - 2)
    share(0).start()
    weight().wait()
    block(0, *kept[0])
    add(0)
    give(0).start()
    block(1, *kept[1])
    give(1).start()
    add(1)
    block(2, *kept[2])
    give(2).start()
    add(2)
    block(3, *kept[3])
    keep().start()
    for at in range(3, len(swaps)):
        add(at)
    keep().wait()
    for t in range(slots - 1):
        give(t).wait()


def closing(x, hidden_grad, dq, dk, dv, w, gain, shift, down, upq, upv, sums, sizes):
    slots, tile, width = x.shape
    ranks = down.shape[1]
    steps = 2 + (sizes[0].bit_length() - 1)
    total = (2 * ranks + 8, width)
    slabs = [pltpu.VMEM(x.shape, bf16)] * 5
    dma = pltpu.SemaphoreType.DMA
    fold = lambda a: a.reshape(x.shape)
    return pl.pallas_call(
        functools.partial(close_kernel, sizes=sizes),
        in_specs=[ANY] * 6 + [VMEM] * 6,
        out_specs=[ANY, VMEM],
        out_shape=[jax.ShapeDtypeStruct(x.shape, bf16), jax.ShapeDtypeStruct(total, f32)],
        scratch_shapes=slabs + [
            pltpu.VMEM(w.shape, bf16),
            pltpu.VMEM(x.shape, bf16),
            pltpu.VMEM((steps,) + total, f32),
            pltpu.VMEM((steps,) + total, f32),
            dma((slots, 5)), dma((slots - 1,)), dma((slots - 1,)), dma((2,)), dma((steps,)), dma((steps,)),
        ],
        compiler_params=pltpu.CompilerParams(collective_id=2, has_side_effects=True, vmem_limit_bytes=60 * MIB),
        name="closing",
    )(x, fold(hidden_grad), fold(dq), fold(dk), fold(dv), w, gain, shift, down, upq, upv, sums)


def finish_kernel(total_ref, aq_ref, bq_ref, av_ref, bv_ref, rms_ref):
    rank, width = aq_ref.shape
    aq_ref[...] = total_ref[0:rank]
    av_ref[...] = total_ref[rank : 2 * rank]
    bq_ref[...] = total_ref[2 * rank : 3 * rank]
    bv_ref[...] = total_ref[3 * rank : 4 * rank]
    line = total_ref[4 * rank : 4 * rank + 1, 0:128]
    lane = lax.broadcasted_iota(jnp.int32, line.shape, 1)
    count = jnp.maximum(jnp.sum(jnp.where(lane == 2, line, 0.0)), 1.0)
    rms_ref[...] = jnp.sqrt(line / (jnp.where(lane == 0, 1.0, 2.0) * count * width))


def finish(total, rank):
    width = total.shape[1]
    small = jax.ShapeDtypeStruct((rank, width), f32)
    return pl.pallas_call(
        finish_kernel,
        in_specs=[VMEM],
        out_specs=[VMEM] * 5,
        out_shape=[small] * 4 + [jax.ShapeDtypeStruct((1, 128), f32)],
        name="finish",
    )(total)


def whole_slots(
    block_input_rows,
    document_starts,
    counted_mask,
    output_gradient,
    first_norm_gain,
    first_norm_bias,
    query_key_value_weight,
    query_down_weight,
    query_up_weight,
    value_down_weight,
    value_up_weight,
    attention_out_weight,
    second_norm_gain,
    second_norm_bias,
    feed_input_weight,
    feed_input_bias,
    feed_output_weight,
):
    slots, local_len, width = block_input_rows.shape
    sizes = (lax.axis_size("dp"), lax.axis_size("head"))
    length = local_len * slots
    size = width // H
    rank = query_down_weight.shape[1]
    me = lax.axis_index("head")

    def row(v):
        return v.astype(f32).reshape(1, -1)

    starts = lax.dynamic_slice_in_dim(document_starts, me, 1, 0)
    down = jnp.concatenate([query_down_weight, value_down_weight], 1)
    blank = jnp.zeros_like(query_up_weight)
    upq = jnp.concatenate([query_up_weight, blank], 0)
    upv = jnp.concatenate([blank, value_up_weight], 0)
    mask8 = jnp.broadcast_to(counted_mask.astype(f32)[:, None, :], (slots, 8, local_len))
    gain_one = row(first_norm_gain)
    shift_one = row(first_norm_bias)

    x, dy, mask, qkv, context, probs = opening(
        block_input_rows, output_gradient, mask8, query_key_value_weight, starts, gain_one, shift_one,
        down, upq, upv, size,
    )
    out, hidden_grad, context_grad, sums = feed(
        x, dy, context, mask, attention_out_weight, row(second_norm_gain), row(second_norm_bias),
        feed_input_weight, row(feed_input_bias), feed_output_weight,
    )
    dq, dk, dv, output = attend_back_slot(qkv, context_grad, context, probs, out, size)
    input_grad, total = closing(
        x, hidden_grad, dq, dk, dv, query_key_value_weight, gain_one, shift_one, down, upq, upv, sums, sizes
    )
    grad_aq, grad_bq, grad_av, grad_bv, rms = finish(total, rank)
    return output, input_grad, grad_aq.T, grad_bq, grad_av.T, grad_bv, rms[0, :2]


def body(*args):
    same = args[0].shape[0] == lax.axis_size("head")
    return whole_slots(*args) if same else shards(*args)


def solution(mesh):
    return jax.shard_map(
        body,
        mesh=mesh,
        in_specs=(
            P("dp", "head", None),
            P("dp", None),
            P("dp", "head"),
            P("dp", "head", None),
            P(),
            P(),
            P(),
            P(),
            P(),
            P(),
            P(),
            P(),
            P(),
            P(),
            P(),
            P(),
            P(),
        ),
        out_specs=(P("dp", "head", None), P("dp", "head", None), P(), P(), P(), P(), P()),
        check_vma=False,
    )
```

```python
import functools

import jax
import jax.numpy as jnp
from jax import lax
from jax.experimental import pallas as pl
from jax.experimental.pallas import tpu as pltpu
from jax.sharding import PartitionSpec as P

H = 16


EPSILON = 1e-05
ADAPTER_SCALE = 8.0
NEGATIVE = -1e30


def as_sent(x):

    def short(part):
        return part.astype(jnp.bfloat16) if part.dtype == jnp.float32 else part

    return jax.tree.map(short, x)


def norm_rows(matrix, gain_vec, shift_vec):
    center = matrix - jnp.mean(matrix, axis=-1, keepdims=True)
    variance = jnp.mean(center * center, axis=-1, keepdims=True)
    return center * lax.rsqrt(variance + EPSILON) * gain_vec + shift_vec


def norm_back(matrix, gain_vec, shift_vec, incoming):
    pullback = jax.vjp(lambda element_item: norm_rows(element_item, gain_vec, shift_vec), matrix)[1]
    return pullback(incoming)[0]


def gelu_tanh(matrix):
    return jax.nn.gelu(matrix, approximate=True)


def plain_product(left, right):
    return jnp.dot(left, right, preferred_element_type=jnp.float32)


def last_product(left, right):
    return lax.dot_general(
        left, right, (((1,), (1,)), ((), ())), preferred_element_type=jnp.float32
    )


def first_product(left, right):
    return lax.dot_general(
        left, right, (((0,), (0,)), ((), ())), preferred_element_type=jnp.float32
    )


def masked_scores(query_block, key_slot, segments, row_start, row_end, score_scale):
    places = jnp.arange(row_end)
    allowed = (segments[row_start:row_end, None] == segments[None, :row_end]) & (
        places[None, :] <= places[row_start:row_end, None]
    )
    scores = (
        jnp.einsum(
            "qhd,khd->hqk", query_block, key_slot[:row_end], preferred_element_type=jnp.float32
        )
        * score_scale
    )
    return jnp.where(allowed[None], scores, NEGATIVE)


def attend_slot(query_slot, key_slot, value_slot, segments, block_rows, score_scale):
    length = query_slot.shape[0]
    outputs_list = []
    logsum_list = []
    for block_index in range(length // block_rows):
        row_start = block_index * block_rows
        row_end = row_start + block_rows
        scores = masked_scores(
            query_slot[row_start:row_end], key_slot, segments, row_start, row_end, score_scale
        )
        row_max = jnp.max(scores, axis=-1, keepdims=True)
        exponent = jnp.exp(scores - row_max)
        row_total = jnp.sum(exponent, axis=-1, keepdims=True)
        probability = (exponent / row_total).astype(jnp.bfloat16)
        context = jnp.einsum(
            "hqk,khd->qhd", probability, value_slot[:row_end], preferred_element_type=jnp.float32
        )
        outputs_list.append(context.astype(jnp.bfloat16))
        logsum_list.append((row_max + jnp.log(row_total))[..., 0])
    return (jnp.concatenate(outputs_list, 0), jnp.concatenate(logsum_list, 1))


def attend_back(
    query_slot, key_slot, value_slot, grad_slot, logsum, segments, block_rows, score_scale
):
    length = query_slot.shape[0]
    key_grad = jnp.zeros(key_slot.shape, jnp.float32)
    value_gradient = jnp.zeros(value_slot.shape, jnp.float32)
    query_parts = []
    for block_index in range(length // block_rows):
        row_start = block_index * block_rows
        row_end = row_start + block_rows
        query_block = query_slot[row_start:row_end]
        grad_block = grad_slot[row_start:row_end]
        scores = masked_scores(query_block, key_slot, segments, row_start, row_end, score_scale)
        probability = jnp.exp(scores - logsum[:, row_start:row_end, None])
        prob_grad = jnp.einsum(
            "qhd,khd->hqk", grad_block, value_slot[:row_end], preferred_element_type=jnp.float32
        )
        inner_sum = jnp.sum(probability * prob_grad, axis=-1, keepdims=True)
        score_grad = (probability * (prob_grad - inner_sum)).astype(jnp.bfloat16)
        query_parts.append(
            jnp.einsum(
                "hqk,khd->qhd", score_grad, key_slot[:row_end], preferred_element_type=jnp.float32
            )
            * score_scale
        )
        key_grad = key_grad.at[:row_end].add(
            jnp.einsum("hqk,qhd->khd", score_grad, query_block, preferred_element_type=jnp.float32)
            * score_scale
        )
        value_gradient = value_gradient.at[:row_end].add(
            jnp.einsum(
                "hqk,qhd->khd",
                probability.astype(jnp.bfloat16),
                grad_block,
                preferred_element_type=jnp.float32,
            )
        )
    query_gradient = jnp.concatenate(query_parts, 0)
    return (
        query_gradient.astype(jnp.bfloat16),
        key_grad.astype(jnp.bfloat16),
        value_gradient.astype(jnp.bfloat16),
    )


def shards(
    block_input_rows,
    document_starts,
    counted_mask,
    output_gradient,
    first_norm_gain,
    first_norm_bias,
    query_key_value_weight,
    query_down_weight,
    query_up_weight,
    value_down_weight,
    value_up_weight,
    attention_out_weight,
    second_norm_gain,
    second_norm_bias,
    feed_input_weight,
    feed_input_bias,
    feed_output_weight,
):
    slot_count, local_len, row_width = block_input_rows.shape
    groups = lax.axis_size("head")
    full_len = local_len * groups
    head_size = row_width // H
    heads_here = H // groups
    row_count = slot_count * local_len
    block_rows = min(512, full_len)
    score_scale = head_size ** (-0.5)
    gain_one = first_norm_gain.astype(jnp.float32)
    shift_one = first_norm_bias.astype(jnp.float32)
    gain_two = second_norm_gain.astype(jnp.float32)
    shift_two = second_norm_bias.astype(jnp.float32)
    fc_bias = feed_input_bias.astype(jnp.float32)
    local_shape = (slot_count, local_len, row_width)
    split_shape = (slot_count, full_len, heads_here, head_size)
    merged_shape = (slot_count, full_len, heads_here * head_size)
    flat_in = block_input_rows.reshape(row_count, row_width).astype(jnp.float32)
    normed_rows = norm_rows(flat_in, gain_one, shift_one).astype(jnp.bfloat16)
    query_low_rank = plain_product(normed_rows, query_down_weight).astype(jnp.bfloat16)
    value_low_rank = plain_product(normed_rows, value_down_weight).astype(jnp.bfloat16)
    projected_rows = plain_product(normed_rows, query_key_value_weight)
    query_rows = (
        projected_rows[:, :row_width]
        + ADAPTER_SCALE * plain_product(query_low_rank, query_up_weight)
    ).astype(jnp.bfloat16)
    key_rows = projected_rows[:, row_width : 2 * row_width].astype(jnp.bfloat16)
    value_matrix = (
        projected_rows[:, 2 * row_width :]
        + ADAPTER_SCALE * plain_product(value_low_rank, value_up_weight)
    ).astype(jnp.bfloat16)
    head_query, head_key, head_value = (
        lax.all_to_all(
            query_rows.reshape(local_shape), "head", split_axis=2, concat_axis=1, tiled=True
        ),
        lax.all_to_all(
            key_rows.reshape(local_shape), "head", split_axis=2, concat_axis=1, tiled=True
        ),
        lax.all_to_all(
            value_matrix.reshape(local_shape), "head", split_axis=2, concat_axis=1, tiled=True
        ),
    )
    head_query = head_query.reshape(split_shape)
    head_key = head_key.reshape(split_shape)
    head_value = head_value.reshape(split_shape)

    def slot_fn(packed):
        return attend_slot(packed[0], packed[1], packed[2], packed[3], block_rows, score_scale)

    context_heads, logsum = lax.map(slot_fn, (head_query, head_key, head_value, document_starts))
    context_local = lax.all_to_all(
        as_sent(context_heads.reshape(merged_shape)),
        "head",
        split_axis=1,
        concat_axis=2,
        tiled=True,
    )
    context_flat = context_local.reshape(row_count, row_width)
    branch = plain_product(context_flat, attention_out_weight)
    hidden_state = flat_in + branch
    normed_two = norm_rows(hidden_state, gain_two, shift_two).astype(jnp.bfloat16)
    before = plain_product(normed_two, feed_input_weight) + fc_bias
    activated = gelu_tanh(before).astype(jnp.bfloat16)
    feed_out = plain_product(activated, feed_output_weight)
    result = hidden_state + feed_out
    output = result.astype(jnp.bfloat16).reshape(block_input_rows.shape)
    valid_rows = counted_mask.reshape(row_count).astype(jnp.float32)[:, None]
    square_sums = jnp.stack(
        [
            jnp.sum(valid_rows * result * result),
            jnp.sum(valid_rows * (branch * branch + feed_out * feed_out)),
            jnp.sum(valid_rows),
        ]
    )
    grad_flat = output_gradient.reshape(row_count, row_width)
    act_grad = last_product(grad_flat, feed_output_weight)
    gelu_pull = jax.vjp(gelu_tanh, before)[1]
    before_grad = gelu_pull(act_grad)[0].astype(jnp.bfloat16)
    normed_two_grad = last_product(before_grad, feed_input_weight)
    hidden_grad = grad_flat.astype(jnp.float32) + norm_back(
        hidden_state, gain_two, shift_two, normed_two_grad
    )
    branch_grad = hidden_grad.astype(jnp.bfloat16)
    context_grad = last_product(branch_grad, attention_out_weight).astype(jnp.bfloat16)
    grad_heads = lax.all_to_all(
        context_grad.reshape(local_shape), "head", split_axis=2, concat_axis=1, tiled=True
    ).reshape(split_shape)

    def back_fn(packed):
        return attend_back(
            packed[0],
            packed[1],
            packed[2],
            packed[3],
            packed[4],
            packed[5],
            block_rows,
            score_scale,
        )

    query_gradient, key_grad, value_gradient = lax.map(
        back_fn, (head_query, head_key, head_value, grad_heads, logsum, document_starts)
    )
    query_gradient, key_grad, value_gradient = (
        lax.all_to_all(
            as_sent(query_gradient.reshape(merged_shape)),
            "head",
            split_axis=1,
            concat_axis=2,
            tiled=True,
        ),
        lax.all_to_all(
            as_sent(key_grad.reshape(merged_shape)), "head", split_axis=1, concat_axis=2, tiled=True
        ),
        lax.all_to_all(
            as_sent(value_gradient.reshape(merged_shape)),
            "head",
            split_axis=1,
            concat_axis=2,
            tiled=True,
        ),
    )
    query_gradient = query_gradient.reshape(row_count, row_width)
    key_grad = key_grad.reshape(row_count, row_width)
    value_gradient = value_gradient.reshape(row_count, row_width)
    query_low_gradient = (ADAPTER_SCALE * last_product(query_gradient, query_up_weight)).astype(
        jnp.bfloat16
    )
    value_low_gradient = (ADAPTER_SCALE * last_product(value_gradient, value_up_weight)).astype(
        jnp.bfloat16
    )
    joined_grads = jnp.concatenate([query_gradient, key_grad, value_gradient], axis=1)
    normed_grad = (
        last_product(joined_grads, query_key_value_weight)
        + last_product(query_low_gradient, query_down_weight)
        + last_product(value_low_gradient, value_down_weight)
    )
    input_grad = hidden_grad + norm_back(flat_in, gain_one, shift_one, normed_grad)
    down_query = first_product(normed_rows, query_low_gradient)
    lifted_query = ADAPTER_SCALE * first_product(query_low_rank, query_gradient)
    down_value = first_product(normed_rows, value_low_gradient)
    lifted_value = ADAPTER_SCALE * first_product(value_low_rank, value_gradient)
    totals = lax.psum(
        (down_query, lifted_query, down_value, lifted_value, square_sums), ("dp", "head")
    )
    token_count = jnp.maximum(totals[4][2], 1.0)
    rms_values = jnp.stack(
        [
            jnp.sqrt(totals[4][0] / (token_count * row_width)),
            jnp.sqrt(totals[4][1] / (2.0 * token_count * row_width)),
        ]
    )
    return (
        output,
        input_grad.astype(jnp.bfloat16).reshape(block_input_rows.shape),
        totals[0],
        totals[1],
        totals[2],
        totals[3],
        rms_values,
    )


LOG2E = 1.4426950408889634
LN2 = 0.6931471805599453
TILE = 256
GROUP = 256
bf16 = jnp.bfloat16
f32 = jnp.float32
NT = (((1,), (1,)), ((), ()))
NN = (((1,), (0,)), ((), ()))
TN = (((0,), (0,)), ((), ()))
MESH = pl.DeviceIdType.MESH
MIB = 2**20


def dg(left, right, dims):
    return lax.dot_general(left, right, dims, preferred_element_type=f32)


def resident(shape):
    zeros = (0,) * len(shape)
    return pl.BlockSpec(shape, lambda *_: zeros, pipeline_mode=pl.Buffered(1))


def params(mib):
    return pltpu.CompilerParams(
        vmem_limit_bytes=mib * MIB, dimension_semantics=("arbitrary",)
    )


def norm_stats(rows):
    center = rows - jnp.mean(rows, axis=-1, keepdims=True)
    rs = lax.rsqrt(jnp.mean(center * center, axis=-1, keepdims=True) + EPSILON)
    return center * rs, rs


def norm_grad(unit, rs, gain, incoming):
    t = incoming * gain
    return (
        t - jnp.mean(t, axis=-1, keepdims=True) - unit * jnp.mean(t * unit, axis=-1, keepdims=True)
    ) * rs


def head_masks(x, heads, size):
    lane = lax.broadcasted_iota(jnp.int32, x.shape, 1)
    return [
        jnp.where((lane >= size * h) & (lane < size * (h + 1)), x, jnp.zeros_like(x))
        for h in range(heads)
    ]


def merge_heads(stacked, heads, size):
    rows = stacked.shape[0] // heads
    out = stacked[:rows]
    lane = lax.broadcasted_iota(jnp.int32, out.shape, 1)
    for h in range(1, heads):
        out = jnp.where(lane >= size * h, stacked[h * rows : (h + 1) * rows], out)
    return out


def column(line):
    return jnp.broadcast_to(line, (128, line.shape[1])).T


def entry_signal(peers):
    barrier = pltpu.get_barrier_semaphore()
    for peer in peers:
        pl.semaphore_signal(barrier, inc=1, device_id=peer, device_id_type=MESH)


def entry_wait(count):
    pl.semaphore_wait(pltpu.get_barrier_semaphore(), count)


def remote(src, dst, send_sem, recv_sem, peer):
    return pltpu.make_async_remote_copy(
        src_ref=src, dst_ref=dst, send_sem=send_sem, recv_sem=recv_sem, device_id=peer, device_id_type=MESH
    )


ANY = pl.BlockSpec(memory_space=pl.ANY)
VMEM = pl.BlockSpec(memory_space=pltpu.VMEM)


def attention_group(q_ref, k_ref, v_ref, o_ref, p_ref, s_sc, bias_sc, size, strip):
    length = q_ref.shape[0]
    heads = q_ref.shape[1] // size
    blocks = length // TILE

    def scores(i):
        masked = jnp.concatenate(head_masks(q_ref[i * TILE : (i + 1) * TILE, :], heads, size), 0)
        for j in range(i + 1):
            s_sc[i % 2, :, j * TILE : (j + 1) * TILE] = dg(masked, k_ref[j * TILE : (j + 1) * TILE, :], NT)

    def soft(i):
        n = (i + 1) * TILE
        for r in range(0, TILE, strip):
            for h in range(heads):
                at = h * TILE + r
                s = s_sc[i % 2, at : at + strip, 0:n] + bias_sc[i * TILE + r : i * TILE + r + strip, 0:n]
                e = jnp.exp2(s - jnp.max(s, axis=1, keepdims=True))
                total = jnp.sum(e, axis=1, keepdims=True)
                p_ref[h, i * TILE + r : i * TILE + r + strip, 0:n] = (e * (1.0 / total)).astype(bf16)

    def mix(i):
        n = (i + 1) * TILE
        probs = p_ref[:, i * TILE : n, 0:n].reshape(heads * TILE, n)
        o_ref[i * TILE : n, :] = merge_heads(dg(probs, v_ref[0:n, :], NN), heads, size).astype(bf16)

    for t in range(blocks + 2):
        if t < blocks:
            scores(t)
        if 0 <= t - 1 < blocks:
            soft(t - 1)
        if 0 <= t - 2 < blocks:
            mix(t - 2)


def line(ref):
    return ref[...].astype(f32).reshape(1, -1)


def open_kernel(
    x_ref, dy_ref, w_ref, mask_ref, start_ref, gain_ref, shift_ref, downq_ref, downv_ref, upq_ref, upv_ref,
    xs_ref, dys_ref, masks_ref, normed_ref, qkv_ref, ctx_ref, p_ref,
    x_sc, w_sc, mask_sc, normed_sc, qkv_sc, s_sc, bias_sc, first_sc,
    x_send, x_recv, y_send, y_recv, m_send, m_recv, local_sem,
    *, size, strip,
):
    slots, tile, width = x_ref.shape
    length = slots * tile
    half = length // 2
    groups = width // GROUP
    step = pl.program_id(0)
    group, me = lax.axis_index("dp"), lax.axis_index("head")
    mine = lax.rem(me, 2)
    near = me - mine
    far = slots // 2 - near
    beside = near + 1 - mine
    across = (far + mine, far + 1 - mine)
    peers = [(group, p) for p in (beside,) + across]

    def x_copy(k):
        return remote(x_ref.at[peers[k][1]], x_sc.at[me], x_send.at[k], x_recv.at[k], peers[k])

    def y_copy(k):
        return remote(dy_ref.at[peers[k][1]], dys_ref.at[me], y_send.at[k], y_recv.at[k], peers[k])

    def m_copy(k):
        return remote(mask_sc.at[peers[k][1]], masks_ref.at[me], m_send.at[k], m_recv.at[k], peers[k])

    def own_x():
        return pltpu.make_async_copy(x_ref.at[me], x_sc.at[me], local_sem.at[0])

    def own_y():
        return pltpu.make_async_copy(dy_ref.at[me], dys_ref.at[me], local_sem.at[1])

    def own_m():
        return pltpu.make_async_copy(mask_sc.at[me], masks_ref.at[me], local_sem.at[2])

    def weight():
        return pltpu.make_async_copy(w_ref, w_sc, local_sem.at[3])

    def save_x():
        return pltpu.make_async_copy(x_sc, xs_ref, local_sem.at[4])

    def save_normed():
        return pltpu.make_async_copy(normed_sc, normed_ref, local_sem.at[5])

    def save_qkv():
        return pltpu.make_async_copy(qkv_sc, qkv_ref, local_sem.at[6])

    @pl.when(step == 0)
    def _():
        entry_signal(peers)
        own_x().start()
        weight().start()
        own_y().start()
        for s in range(slots):
            mask_sc[s] = jnp.broadcast_to(mask_ref[s : s + 1, :].astype(f32), mask_sc.shape[1:])
        own_m().start()
        entry_wait(len(peers))
        for k in (1, 2, 0):
            x_copy(k).start()
        for k in range(3):
            m_copy(k).start()
        first_sc[...] = column(start_ref[pl.ds(me, 1), :])

        def bias(i, carry):
            here = pl.ds(pl.multiple_of(i * strip, strip), strip)
            keys = lax.broadcasted_iota(jnp.int32, (strip, length), 1)
            rows = lax.broadcasted_iota(jnp.int32, (strip, length), 0) + i * strip
            allowed = (keys >= first_sc[here, 0:1]) & (keys <= rows)
            bias_sc[here, :] = jnp.where(allowed, 0.0, NEGATIVE)
            return carry

        lax.fori_loop(0, length // strip, bias, 0)
        own_x().wait()
        x_copy(0).wait_recv()
        weight().wait()

    @pl.when(step == 1)
    def _():
        for k in (1, 2):
            x_copy(k).wait()
        for k in (1, 2, 0):
            y_copy(k).start()
        save_x().start()

    @pl.when(step < 2)
    def _():
        first = near + (far - near) * step
        rows = x_sc[pl.ds(first, 2)].reshape(half, width).astype(f32)
        unit, _ = norm_stats(rows)
        normed = (unit * line(gain_ref) + line(shift_ref)).astype(bf16)
        here = pl.ds(pl.multiple_of(first * tile, tile), half)
        normed_sc[here, :] = normed
        low_q = dg(normed, downq_ref[...], NT).astype(bf16)
        low_v = dg(normed, downv_ref[...], NT).astype(bf16)
        scale = size**-0.5 * LOG2E
        wide = 512
        for at in range(0, 3 * width, wide):
            cols = slice(at, at + wide)
            part = dg(normed, w_sc[:, cols], NN)
            if at < width:
                part = (part + ADAPTER_SCALE * dg(low_q, upq_ref[:, cols], NN)) * scale
            if at >= 2 * width:
                part = part + ADAPTER_SCALE * dg(low_v, upv_ref[:, at - 2 * width : at - 2 * width + wide], NN)
            qkv_sc[here, cols] = part.astype(bf16)

    @pl.when(step == 1)
    def _():
        save_normed().start()
        save_qkv().start()

    @pl.when(step >= 2)
    def _():
        g = step - 2

        def part(third):
            return qkv_sc.at[:, pl.ds(pl.multiple_of(third * width + g * GROUP, GROUP), GROUP)]

        attention_group(part(0), part(1), part(2), ctx_ref, p_ref, s_sc, bias_sc, size, strip)

    @pl.when(step == groups + 1)
    def _():
        x_copy(0).wait_send()
        for k in range(3):
            y_copy(k).wait()
            m_copy(k).wait()
        own_m().wait()
        own_y().wait()
        save_x().wait()
        save_normed().wait()
        save_qkv().wait()


def opening(x, dy, w, mask, start, gain, shift, downq, downv, upq, upv, size):
    slots, tile, width = x.shape
    length = slots * tile
    groups = width // GROUP
    per = GROUP // size
    dma = pltpu.SemaphoreType.DMA
    small = [mask, start, gain, shift, downq, downv, upq, upv]
    masks = (slots, 8, tile)
    return pl.pallas_call(
        functools.partial(open_kernel, size=size, strip=32),
        grid=(groups + 2,),
        in_specs=[ANY] * 3 + [resident(a.shape) for a in small],
        out_specs=[ANY] * 5 + [
            pl.BlockSpec((length, GROUP), lambda t: (0, jnp.maximum(t - 2, 0))),
            pl.BlockSpec((per, length, length), lambda t: (jnp.maximum(t - 2, 0), 0, 0)),
        ],
        out_shape=[
            jax.ShapeDtypeStruct(x.shape, bf16),
            jax.ShapeDtypeStruct(x.shape, bf16),
            jax.ShapeDtypeStruct(masks, f32),
            jax.ShapeDtypeStruct((length, width), bf16),
            jax.ShapeDtypeStruct((length, 3 * width), bf16),
            jax.ShapeDtypeStruct((length, width), bf16),
            jax.ShapeDtypeStruct((per * groups, length, length), bf16),
        ],
        scratch_shapes=[
            pltpu.VMEM(x.shape, bf16),
            pltpu.VMEM(w.shape, bf16),
            pltpu.VMEM(masks, f32),
            pltpu.VMEM((length, width), bf16),
            pltpu.VMEM((length, 3 * width), bf16),
            pltpu.VMEM((2, per * TILE, length), f32),
            pltpu.VMEM((length, length), f32),
            pltpu.VMEM((length, 128), jnp.int32),
            dma((3,)), dma((3,)), dma((3,)), dma((3,)), dma((3,)), dma((3,)), dma((7,)),
        ],
        compiler_params=pltpu.CompilerParams(
            collective_id=0, has_side_effects=True, vmem_limit_bytes=60 * MIB, dimension_semantics=("arbitrary",)
        ),
        name="opening",
    )(x, dy, w, *small)


def feed_kernel(
    x_ref, y_ref, ctx_ref, mask_ref, wo_hbm, wi_hbm, wf_hbm, gain_ref, shift_ref, bias_ref,
    out_ref, hg_ref, cg_ref, sums_ref, wo_ref, wi_ref, wf_ref, feed_sc, grad_sc, normed_sc, v_sc, g_sc, sem,
    *, step,
):
    blocks, tile, width = x_ref.shape
    rows = blocks * tile
    chunks = wi_ref.shape[1] // step
    first = pl.program_id(0) == 0

    def cols_of(c):
        return pl.ds(c * step if isinstance(c, int) else pl.multiple_of(c * step, step), step)

    def load_o():
        return pltpu.make_async_copy(wo_hbm, wo_ref, sem.at[2 * chunks])

    def load_i(c):
        return pltpu.make_async_copy(wi_hbm.at[:, cols_of(c)], wi_ref.at[:, cols_of(c)], sem.at[2 * c])

    def load_f(c):
        return pltpu.make_async_copy(wf_hbm.at[cols_of(c), :], wf_ref.at[cols_of(c), :], sem.at[2 * c + 1])

    @pl.when(first)
    def _():
        load_o().start()
        for c in range(chunks):
            load_i(c).start()
            load_f(c).start()
        load_o().wait()

    branch = dg(ctx_ref[...], wo_ref[...], NN)
    hidden = x_ref[...].reshape(rows, width).astype(f32) + branch
    unit, rs = norm_stats(hidden)
    gain = line(gain_ref)
    normed_sc[...] = (unit * gain + line(shift_ref)).astype(bf16)
    c0 = 0.7978845608028654
    c1 = c0 * 0.044715

    def enter(c, slot):
        @pl.when(first)
        def _():
            load_i(c).wait()
            load_f(c).wait()

        cols = cols_of(c)
        v_sc[slot] = dg(normed_sc[...], wi_ref[:, cols], NN) + bias_ref[cols].astype(f32).reshape(1, step)
        g_sc[slot] = dg(y_ref[...].reshape(rows, width), wf_ref[cols, :], NT)

    def leave(c, slot):
        v = v_sc[slot]
        square = v * v
        half = 0.5 * jnp.tanh(v * (c0 + c1 * square)) + 0.5
        act = v * half
        slope = half + act * (1.0 - half) * (2.0 * c0 + 6.0 * c1 * square)
        cols = cols_of(c)
        feed_sc[...] += dg(act.astype(bf16), wf_ref[cols, :], NN)
        grad_sc[...] += dg((slope * g_sc[slot]).astype(bf16), wi_ref[:, cols], NT)

    feed_sc[...] = jnp.zeros_like(feed_sc)
    grad_sc[...] = jnp.zeros_like(grad_sc)
    enter(0, 0)

    def pair(i, carry):
        enter(2 * i + 1, 1)
        leave(2 * i, 0)
        enter(2 * i + 2, 0)
        leave(2 * i + 1, 1)
        return carry

    lax.fori_loop(0, chunks // 2 - 1, pair, 0)
    enter(chunks - 1, 1)
    leave(chunks - 2, 0)
    leave(chunks - 1, 1)
    feed = feed_sc[...]
    result = hidden + feed
    out_ref[...] = result.astype(bf16).reshape(out_ref.shape)
    valid = jnp.concatenate([column(mask_ref[b, 0:1, :])[:, 0:1] for b in range(blocks)], 0)
    one = jnp.sum(valid * jnp.sum(result * result, axis=1, keepdims=True))
    two = jnp.sum(valid * jnp.sum(branch * branch + feed * feed, axis=1, keepdims=True))
    count = jnp.sum(valid)
    row = lax.broadcasted_iota(jnp.int32, sums_ref.shape, 0)
    col = lax.broadcasted_iota(jnp.int32, sums_ref.shape, 1)
    mine = jnp.where(col == 0, one, jnp.where(col == 1, two, jnp.where(col == 2, count, 0.0)))
    mine = jnp.where(row == 0, mine, 0.0)

    @pl.when(first)
    def _():
        sums_ref[...] = mine

    @pl.when(jnp.logical_not(first))
    def _():
        sums_ref[...] += mine

    dy = y_ref[...].reshape(rows, width).astype(f32)
    low = (dy + norm_grad(unit, rs, gain, grad_sc[...])).astype(bf16)
    hg_ref[...] = low
    cg_ref[...] = dg(low, wo_ref[...], NT).astype(bf16)


def feed(x, dy, context, mask, wo, gain, shift, wi, bias, wf):
    slots, tile, width = x.shape
    rows = slots * tile
    units = wi.shape[1]
    each = 2
    step = 512
    slab = pl.BlockSpec((each, tile, width), lambda i: (i, 0, 0))
    flat = pl.BlockSpec((each * tile, width), lambda i: (i, 0))
    return pl.pallas_call(
        functools.partial(feed_kernel, step=step),
        grid=(slots // each,),
        in_specs=[
            slab, slab, flat,
            pl.BlockSpec((each,) + mask.shape[1:], lambda i: (i, 0, 0)),
            ANY, ANY, ANY, resident(gain.shape), resident(shift.shape), resident(bias.shape),
        ],
        out_specs=[slab, flat, flat, pl.BlockSpec((8, width), lambda i: (0, 0))],
        out_shape=[
            jax.ShapeDtypeStruct(x.shape, bf16),
            jax.ShapeDtypeStruct((rows, width), bf16),
            jax.ShapeDtypeStruct((rows, width), bf16),
            jax.ShapeDtypeStruct((8, width), f32),
        ],
        scratch_shapes=[
            pltpu.VMEM(wo.shape, bf16), pltpu.VMEM(wi.shape, bf16), pltpu.VMEM(wf.shape, bf16),
            pltpu.VMEM((each * tile, width), f32), pltpu.VMEM((each * tile, width), f32),
            pltpu.VMEM((each * tile, width), bf16),
            pltpu.VMEM((2, each * tile, step), f32), pltpu.VMEM((2, each * tile, step), f32),
            pltpu.SemaphoreType.DMA((2 * (units // step) + 1,)),
        ],
        compiler_params=params(62),
        name="feed",
    )(x, dy, context, mask, wo, wi, wf, gain, shift, bias)


def attend_back_kernel(
    q_ref, k_ref, v_ref, g_ref, o_ref, p_ref, res_ref,
    dq_ref, dk_ref, dv_ref, out_ref,
    dp_sc, ds_sc, dk_sc, dv_sc, send, recv, local_sem,
    *, size, strip,
):
    length = q_ref.shape[0]
    heads = q_ref.shape[1] // size
    blocks = length // TILE
    scale = size**-0.5
    slots = res_ref.shape[0]
    group, me = lax.axis_index("dp"), lax.axis_index("head")
    peers = [(group, lax.rem(me + k, slots)) for k in range(1, slots)]
    grid_step = pl.program_id(0)

    def copy(k):
        return remote(res_ref.at[peers[k][1]], out_ref.at[me], send.at[k], recv.at[k], peers[k])

    def own():
        return pltpu.make_async_copy(res_ref.at[me], out_ref.at[me], local_sem)

    @pl.when(grid_step == 0)
    def _():
        entry_signal(peers)
        own().start()

    @pl.when(grid_step == 1)
    def _():
        entry_wait(len(peers))
        for k in range(len(peers)):
            copy(k).start()

    def stack(ref, i):
        return jnp.concatenate(head_masks(ref[i * TILE : (i + 1) * TILE, :], heads, size), 0)

    def prob_grads(i):
        masked = stack(g_ref, i)
        for j in range(i + 1):
            dp_sc[i % 2, :, j * TILE : (j + 1) * TILE] = dg(masked, v_ref[j * TILE : (j + 1) * TILE, :], NT)

    def score_grads(i):
        n = (i + 1) * TILE
        both = g_ref[i * TILE : n, :].astype(f32) * o_ref[i * TILE : n, :].astype(f32)
        for h in range(heads):
            for r in range(0, TILE, strip):
                at = h * TILE + r
                inner = jnp.sum(both[r : r + strip, size * h : size * (h + 1)], axis=1, keepdims=True)
                prob = p_ref[h, i * TILE + r : i * TILE + r + strip, 0:n].astype(f32)
                ds_sc[i % 2, at : at + strip, 0:n] = (prob * (dp_sc[i % 2, at : at + strip, 0:n] - inner)).astype(bf16)

    def products(i):
        n = (i + 1) * TILE
        dq = merge_heads(dg(ds_sc[i % 2, :, 0:n], k_ref[0:n, :], NN), heads, size)
        dq_ref[i * TILE : n, :] = (dq * scale).astype(bf16)
        grad4 = stack(g_ref, i)
        query4 = stack(q_ref, i)
        for j in range(i + 1):
            at = slice(j * TILE, (j + 1) * TILE)
            dv = dg(p_ref[:, i * TILE : n, at].reshape(heads * TILE, TILE), grad4, TN)
            dk = dg(ds_sc[i % 2, :, at], query4, TN)
            if i == j:
                dv_sc[at] = dv
                dk_sc[at] = dk
            else:
                dv_sc[at] += dv
                dk_sc[at] += dk

    for t in range(blocks + 2):
        if t < blocks:
            prob_grads(t)
        if 0 <= t - 1 < blocks:
            score_grads(t - 1)
        if 0 <= t - 2 < blocks:
            products(t - 2)
    dk_ref[...] = (dk_sc[...] * LN2).astype(bf16)
    dv_ref[...] = dv_sc[...].astype(bf16)

    @pl.when(grid_step == pl.num_programs(0) - 1)
    def _():
        own().wait()
        for k in range(len(peers)):
            copy(k).wait()


def attend_back_slot(qkv, grad, context, probs, result, size):
    length, wide = qkv.shape
    width = wide // 3
    groups = width // GROUP
    per = GROUP // size
    slots = result.shape[0]
    part = pl.BlockSpec((length, GROUP), lambda g: (0, g))
    dma = pltpu.SemaphoreType.DMA
    return pl.pallas_call(
        functools.partial(attend_back_kernel, size=size, strip=32),
        grid=(groups,),
        in_specs=[
            part,
            pl.BlockSpec((length, GROUP), lambda g: (0, g + groups)),
            pl.BlockSpec((length, GROUP), lambda g: (0, g + 2 * groups)),
            part,
            part,
            pl.BlockSpec((per, length, length), lambda g: (g, 0, 0)),
            ANY,
        ],
        out_specs=[part] * 3 + [ANY],
        out_shape=[jax.ShapeDtypeStruct((length, width), bf16)] * 3 + [jax.ShapeDtypeStruct(result.shape, bf16)],
        scratch_shapes=[
            pltpu.VMEM((2, per * TILE, length), f32),
            pltpu.VMEM((2, per * TILE, length), bf16),
            pltpu.VMEM((length, GROUP), f32),
            pltpu.VMEM((length, GROUP), f32),
            dma((slots - 1,)), dma((slots - 1,)), dma,
        ],
        compiler_params=pltpu.CompilerParams(
            collective_id=1, has_side_effects=True, vmem_limit_bytes=60 * MIB, dimension_semantics=("arbitrary",)
        ),
        name="attend_back",
    )(qkv, qkv, qkv, grad, context, probs, result)


def close_kernel(
    x_hbm, hg_hbm, dq_hbm, dk_hbm, dv_hbm, normed_hbm, w_hbm,
    gain_ref, downq_ref, downv_ref, upq_ref, upv_ref, sums_ref,
    out_ref, total_ref,
    x_sc, hg_sc, dq_sc, dk_sc, dv_sc, normed_sc, w_sc, low_sc, res_sc, sums, heard, parts, mean,
    load_sem, send, recv, local_sem, pair_send, pair_recv, part_send, part_recv, mean_send, mean_recv,
    *, sizes,
):
    slots, tile, width = x_sc.shape
    half = slots // 2 * tile
    rank = downq_ref.shape[0]
    group, me = lax.axis_index("dp"), lax.axis_index("head")
    mine = lax.rem(me, 2)
    near = me - mine
    far = slots // 2 - near
    beside = near + 1 - mine
    peers = [(group, p) for p in (far + mine, far + 1 - mine, beside)]
    rest = [(lax.rem(group + k, sizes[0]), me) for k in range(1, sizes[0])]
    lanes = width // sizes[0]
    arrays = [
        (dq_hbm, dq_sc), (dv_hbm, dv_sc), (normed_hbm, normed_sc), (dk_hbm, dk_sc), (x_hbm, x_sc), (hg_hbm, hg_sc)
    ]
    entry_signal(peers + rest)

    def load(a):
        src, dst = arrays[a]
        return pltpu.make_async_copy(src, dst, load_sem.at[a])

    def weight():
        return pltpu.make_async_copy(w_hbm, w_sc, local_sem.at[0])

    for a in range(len(arrays)):
        load(a).start()
    weight().start()
    for a in range(3):
        load(a).wait()

    def adapters(t, carry):
        at = pl.ds(2 * t, 2)
        dq = dq_sc[at].reshape(half, width)
        dv = dv_sc[at].reshape(half, width)
        normed = normed_sc[at].reshape(half, width)
        low_gq = (ADAPTER_SCALE * dg(dq, upq_ref[...], NT)).astype(bf16)
        low_gv = (ADAPTER_SCALE * dg(dv, upv_ref[...], NT)).astype(bf16)
        low_q = dg(normed, downq_ref[...], NT).astype(bf16)
        low_v = dg(normed, downv_ref[...], NT).astype(bf16)
        here = pl.ds(pl.multiple_of(t * half, half), half)
        low_sc[0, here, :] = low_gq
        low_sc[1, here, :] = low_gv
        sums[0, 0:rank] += dg(low_gq, normed, TN)
        sums[0, rank : 2 * rank] += dg(low_gv, normed, TN)
        sums[0, 2 * rank : 3 * rank] += ADAPTER_SCALE * dg(low_q, dq, TN)
        sums[0, 3 * rank : 4 * rank] += ADAPTER_SCALE * dg(low_v, dv, TN)
        return carry

    sums[0, 0 : 4 * rank] = jnp.zeros((4 * rank, width), f32)
    sums[0, 4 * rank :] = sums_ref[...]
    lax.fori_loop(0, 2, adapters, 0)

    def pair(at, peer):
        return remote(sums.at[at], heard.at[at], pair_send.at[at], pair_recv.at[at], peer)

    def block_of(d):
        return pl.ds(pl.multiple_of(d * lanes, lanes), lanes)

    def scatter(k):
        to = rest[k][0]
        return remote(
            sums.at[2, :, block_of(to)], parts.at[k], part_send.at[k], part_recv.at[k], rest[k]
        )

    def gather(k):
        return remote(
            mean, total_ref.at[:, block_of(group)], mean_send.at[k], mean_recv.at[k], rest[k]
        )

    def give(k):
        return remote(res_sc.at[peers[k][1]], out_ref.at[me], send.at[k], recv.at[k], peers[k])

    def keep():
        return pltpu.make_async_copy(res_sc.at[me], out_ref.at[me], local_sem.at[1])

    entry_wait(len(peers) + len(rest))
    pair(0, peers[0]).start()
    for a in range(3, len(arrays)):
        load(a).wait()
    weight().wait()

    def rows_back(t, carry):
        first = far + (near - far) * t
        at = pl.ds(first, 2)
        here = pl.ds(pl.multiple_of(first * tile, tile), half)
        normed_grad = (
            dg(dq_sc[at].reshape(half, width), w_sc[:, :width], NT)
            + dg(dk_sc[at].reshape(half, width), w_sc[:, width : 2 * width], NT)
            + dg(dv_sc[at].reshape(half, width), w_sc[:, 2 * width :], NT)
            + dg(low_sc[0, here, :], downq_ref[...], NN)
            + dg(low_sc[1, here, :], downv_ref[...], NN)
        )
        unit, rs = norm_stats(x_sc[at].reshape(half, width).astype(f32))
        grad = hg_sc[at].reshape(half, width).astype(f32) + norm_grad(unit, rs, line(gain_ref), normed_grad)
        res_sc[at] = grad.astype(bf16).reshape(2, tile, width)

        @pl.when(t == 0)
        def _():
            give(0).start()
            give(1).start()
            pair(0, peers[0]).wait()
            sums[1] = sums[0] + heard[0]
            pair(1, peers[2]).start()

        return carry

    lax.fori_loop(0, 2, rows_back, 0)
    give(2).start()
    keep().start()
    pair(1, peers[2]).wait()
    sums[2] = sums[1] + heard[1]
    for k in range(len(rest)):
        scatter(k).start()
    for k in range(len(rest)):
        scatter(k).wait()
    whole = sums[2, :, block_of(group)]
    for k in range(len(rest)):
        whole = whole + parts[k]
    mean[...] = whole
    total_ref[:, block_of(group)] = whole
    for k in range(len(rest)):
        gather(k).start()
    for k in range(len(rest)):
        gather(k).wait()
    keep().wait()
    for k in range(3):
        give(k).wait()


def closing(x, hidden_grad, dq, dk, dv, normed, w, gain, downq, downv, upq, upv, sums, sizes):
    slots, tile, width = x.shape
    rank = downq.shape[0]
    total = (4 * rank + 8, width)
    rest = sizes[0] - 1
    lanes = width // sizes[0]
    dma = pltpu.SemaphoreType.DMA

    def fold(a):
        return a.reshape(x.shape)

    return pl.pallas_call(
        functools.partial(close_kernel, sizes=sizes),
        in_specs=[ANY] * 7 + [VMEM] * 6,
        out_specs=[ANY, VMEM],
        out_shape=[jax.ShapeDtypeStruct(x.shape, bf16), jax.ShapeDtypeStruct(total, f32)],
        scratch_shapes=[pltpu.VMEM(x.shape, bf16)] * 6 + [
            pltpu.VMEM(w.shape, bf16),
            pltpu.VMEM((2, slots * tile, rank), bf16),
            pltpu.VMEM(x.shape, bf16),
            pltpu.VMEM((3,) + total, f32),
            pltpu.VMEM((2,) + total, f32),
            pltpu.VMEM((rest, total[0], lanes), f32),
            pltpu.VMEM((total[0], lanes), f32),
            dma((6,)), dma((3,)), dma((3,)), dma((2,)), dma((2,)), dma((2,)),
            dma((rest,)), dma((rest,)), dma((rest,)), dma((rest,)),
        ],
        compiler_params=pltpu.CompilerParams(collective_id=2, has_side_effects=True, vmem_limit_bytes=60 * MIB),
        name="closing",
    )(x, fold(hidden_grad), fold(dq), fold(dk), fold(dv), fold(normed), w, gain, downq, downv, upq, upv, sums)


def finish_kernel(total_ref, aq_ref, bq_ref, av_ref, bv_ref, rms_ref):
    rank, width = aq_ref.shape
    aq_ref[...] = total_ref[0:rank]
    av_ref[...] = total_ref[rank : 2 * rank]
    bq_ref[...] = total_ref[2 * rank : 3 * rank]
    bv_ref[...] = total_ref[3 * rank : 4 * rank]
    line = total_ref[4 * rank : 4 * rank + 1, 0:128]
    lane = lax.broadcasted_iota(jnp.int32, line.shape, 1)
    count = jnp.maximum(jnp.sum(jnp.where(lane == 2, line, 0.0)), 1.0)
    rms_ref[...] = jnp.sqrt(line / (jnp.where(lane == 0, 1.0, 2.0) * count * width))


def finish(total, rank):
    width = total.shape[1]
    small = jax.ShapeDtypeStruct((rank, width), f32)
    return pl.pallas_call(
        finish_kernel,
        in_specs=[VMEM],
        out_specs=[VMEM] * 5,
        out_shape=[small] * 4 + [jax.ShapeDtypeStruct((1, 128), f32)],
        name="finish",
    )(total)


def whole_slots(
    block_input_rows,
    document_starts,
    counted_mask,
    output_gradient,
    first_norm_gain,
    first_norm_bias,
    query_key_value_weight,
    query_down_weight,
    query_up_weight,
    value_down_weight,
    value_up_weight,
    attention_out_weight,
    second_norm_gain,
    second_norm_bias,
    feed_input_weight,
    feed_input_bias,
    feed_output_weight,
):
    sizes = (lax.axis_size("dp"), lax.axis_size("head"))
    size = block_input_rows.shape[-1] // H
    rank = query_down_weight.shape[1]
    downq = query_down_weight.T
    downv = value_down_weight.T
    x, dy, mask, normed, qkv, context, probs = opening(
        block_input_rows, output_gradient, query_key_value_weight, counted_mask, document_starts,
        first_norm_gain, first_norm_bias, downq, downv, query_up_weight, value_up_weight, size,
    )
    out, hidden_grad, context_grad, sums = feed(
        x, dy, context, mask, attention_out_weight, second_norm_gain, second_norm_bias,
        feed_input_weight, feed_input_bias, feed_output_weight,
    )
    dq, dk, dv, output = attend_back_slot(qkv, context_grad, context, probs, out, size)
    input_grad, total = closing(
        x, hidden_grad, dq, dk, dv, normed, query_key_value_weight, first_norm_gain, downq, downv,
        query_up_weight, value_up_weight, sums, sizes,
    )
    grad_aq, grad_bq, grad_av, grad_bv, rms = finish(total, rank)
    return output, input_grad, grad_aq.T, grad_bq, grad_av.T, grad_bv, rms[0, :2]


def body(*args):
    same = args[0].shape[0] == lax.axis_size("head")
    return whole_slots(*args) if same else shards(*args)


def solution(mesh):
    return jax.shard_map(
        body,
        mesh=mesh,
        in_specs=(
            P("dp", "head", None),
            P("dp", None),
            P("dp", "head"),
            P("dp", "head", None),
            P(),
            P(),
            P(),
            P(),
            P(),
            P(),
            P(),
            P(),
            P(),
            P(),
            P(),
            P(),
            P(),
        ),
        out_specs=(P("dp", "head", None), P("dp", "head", None), P(), P(), P(), P(), P()),
        check_vma=False,
    )
```

```python
import functools

import jax
import jax.numpy as jnp
from jax import lax
from jax.experimental import pallas as pl
from jax.experimental.pallas import tpu as pltpu
from jax.sharding import PartitionSpec as P

H = 16


EPSILON = 1e-05
ADAPTER_SCALE = 8.0
NEGATIVE = -1e30


def as_sent(x):

    def short(part):
        return part.astype(jnp.bfloat16) if part.dtype == jnp.float32 else part

    return jax.tree.map(short, x)


def norm_rows(matrix, gain_vec, shift_vec):
    center = matrix - jnp.mean(matrix, axis=-1, keepdims=True)
    variance = jnp.mean(center * center, axis=-1, keepdims=True)
    return center * lax.rsqrt(variance + EPSILON) * gain_vec + shift_vec


def norm_back(matrix, gain_vec, shift_vec, incoming):
    pullback = jax.vjp(lambda element_item: norm_rows(element_item, gain_vec, shift_vec), matrix)[1]
    return pullback(incoming)[0]


def gelu_tanh(matrix):
    return jax.nn.gelu(matrix, approximate=True)


def plain_product(left, right):
    return jnp.dot(left, right, preferred_element_type=jnp.float32)


def last_product(left, right):
    return lax.dot_general(
        left, right, (((1,), (1,)), ((), ())), preferred_element_type=jnp.float32
    )


def first_product(left, right):
    return lax.dot_general(
        left, right, (((0,), (0,)), ((), ())), preferred_element_type=jnp.float32
    )


def masked_scores(query_block, key_slot, segments, row_start, row_end, score_scale):
    places = jnp.arange(row_end)
    allowed = (segments[row_start:row_end, None] == segments[None, :row_end]) & (
        places[None, :] <= places[row_start:row_end, None]
    )
    scores = (
        jnp.einsum(
            "qhd,khd->hqk", query_block, key_slot[:row_end], preferred_element_type=jnp.float32
        )
        * score_scale
    )
    return jnp.where(allowed[None], scores, NEGATIVE)


def attend_slot(query_slot, key_slot, value_slot, segments, block_rows, score_scale):
    length = query_slot.shape[0]
    outputs_list = []
    logsum_list = []
    for block_index in range(length // block_rows):
        row_start = block_index * block_rows
        row_end = row_start + block_rows
        scores = masked_scores(
            query_slot[row_start:row_end], key_slot, segments, row_start, row_end, score_scale
        )
        row_max = jnp.max(scores, axis=-1, keepdims=True)
        exponent = jnp.exp(scores - row_max)
        row_total = jnp.sum(exponent, axis=-1, keepdims=True)
        probability = (exponent / row_total).astype(jnp.bfloat16)
        context = jnp.einsum(
            "hqk,khd->qhd", probability, value_slot[:row_end], preferred_element_type=jnp.float32
        )
        outputs_list.append(context.astype(jnp.bfloat16))
        logsum_list.append((row_max + jnp.log(row_total))[..., 0])
    return (jnp.concatenate(outputs_list, 0), jnp.concatenate(logsum_list, 1))


def attend_back(
    query_slot, key_slot, value_slot, grad_slot, logsum, segments, block_rows, score_scale
):
    length = query_slot.shape[0]
    key_grad = jnp.zeros(key_slot.shape, jnp.float32)
    value_gradient = jnp.zeros(value_slot.shape, jnp.float32)
    query_parts = []
    for block_index in range(length // block_rows):
        row_start = block_index * block_rows
        row_end = row_start + block_rows
        query_block = query_slot[row_start:row_end]
        grad_block = grad_slot[row_start:row_end]
        scores = masked_scores(query_block, key_slot, segments, row_start, row_end, score_scale)
        probability = jnp.exp(scores - logsum[:, row_start:row_end, None])
        prob_grad = jnp.einsum(
            "qhd,khd->hqk", grad_block, value_slot[:row_end], preferred_element_type=jnp.float32
        )
        inner_sum = jnp.sum(probability * prob_grad, axis=-1, keepdims=True)
        score_grad = (probability * (prob_grad - inner_sum)).astype(jnp.bfloat16)
        query_parts.append(
            jnp.einsum(
                "hqk,khd->qhd", score_grad, key_slot[:row_end], preferred_element_type=jnp.float32
            )
            * score_scale
        )
        key_grad = key_grad.at[:row_end].add(
            jnp.einsum("hqk,qhd->khd", score_grad, query_block, preferred_element_type=jnp.float32)
            * score_scale
        )
        value_gradient = value_gradient.at[:row_end].add(
            jnp.einsum(
                "hqk,qhd->khd",
                probability.astype(jnp.bfloat16),
                grad_block,
                preferred_element_type=jnp.float32,
            )
        )
    query_gradient = jnp.concatenate(query_parts, 0)
    return (
        query_gradient.astype(jnp.bfloat16),
        key_grad.astype(jnp.bfloat16),
        value_gradient.astype(jnp.bfloat16),
    )


def shards(
    block_input_rows,
    document_starts,
    counted_mask,
    output_gradient,
    first_norm_gain,
    first_norm_bias,
    query_key_value_weight,
    query_down_weight,
    query_up_weight,
    value_down_weight,
    value_up_weight,
    attention_out_weight,
    second_norm_gain,
    second_norm_bias,
    feed_input_weight,
    feed_input_bias,
    feed_output_weight,
):
    slot_count, local_len, row_width = block_input_rows.shape
    groups = lax.axis_size("head")
    full_len = local_len * groups
    head_size = row_width // H
    heads_here = H // groups
    row_count = slot_count * local_len
    block_rows = min(512, full_len)
    score_scale = head_size ** (-0.5)
    gain_one = first_norm_gain.astype(jnp.float32)
    shift_one = first_norm_bias.astype(jnp.float32)
    gain_two = second_norm_gain.astype(jnp.float32)
    shift_two = second_norm_bias.astype(jnp.float32)
    fc_bias = feed_input_bias.astype(jnp.float32)
    local_shape = (slot_count, local_len, row_width)
    split_shape = (slot_count, full_len, heads_here, head_size)
    merged_shape = (slot_count, full_len, heads_here * head_size)
    flat_in = block_input_rows.reshape(row_count, row_width).astype(jnp.float32)
    normed_rows = norm_rows(flat_in, gain_one, shift_one).astype(jnp.bfloat16)
    query_low_rank = plain_product(normed_rows, query_down_weight).astype(jnp.bfloat16)
    value_low_rank = plain_product(normed_rows, value_down_weight).astype(jnp.bfloat16)
    projected_rows = plain_product(normed_rows, query_key_value_weight)
    query_rows = (
        projected_rows[:, :row_width]
        + ADAPTER_SCALE * plain_product(query_low_rank, query_up_weight)
    ).astype(jnp.bfloat16)
    key_rows = projected_rows[:, row_width : 2 * row_width].astype(jnp.bfloat16)
    value_matrix = (
        projected_rows[:, 2 * row_width :]
        + ADAPTER_SCALE * plain_product(value_low_rank, value_up_weight)
    ).astype(jnp.bfloat16)
    head_query, head_key, head_value = (
        lax.all_to_all(
            query_rows.reshape(local_shape), "head", split_axis=2, concat_axis=1, tiled=True
        ),
        lax.all_to_all(
            key_rows.reshape(local_shape), "head", split_axis=2, concat_axis=1, tiled=True
        ),
        lax.all_to_all(
            value_matrix.reshape(local_shape), "head", split_axis=2, concat_axis=1, tiled=True
        ),
    )
    head_query = head_query.reshape(split_shape)
    head_key = head_key.reshape(split_shape)
    head_value = head_value.reshape(split_shape)

    def slot_fn(packed):
        return attend_slot(packed[0], packed[1], packed[2], packed[3], block_rows, score_scale)

    context_heads, logsum = lax.map(slot_fn, (head_query, head_key, head_value, document_starts))
    context_local = lax.all_to_all(
        as_sent(context_heads.reshape(merged_shape)),
        "head",
        split_axis=1,
        concat_axis=2,
        tiled=True,
    )
    context_flat = context_local.reshape(row_count, row_width)
    branch = plain_product(context_flat, attention_out_weight)
    hidden_state = flat_in + branch
    normed_two = norm_rows(hidden_state, gain_two, shift_two).astype(jnp.bfloat16)
    before = plain_product(normed_two, feed_input_weight) + fc_bias
    activated = gelu_tanh(before).astype(jnp.bfloat16)
    feed_out = plain_product(activated, feed_output_weight)
    result = hidden_state + feed_out
    output = result.astype(jnp.bfloat16).reshape(block_input_rows.shape)
    valid_rows = counted_mask.reshape(row_count).astype(jnp.float32)[:, None]
    square_sums = jnp.stack(
        [
            jnp.sum(valid_rows * result * result),
            jnp.sum(valid_rows * (branch * branch + feed_out * feed_out)),
            jnp.sum(valid_rows),
        ]
    )
    grad_flat = output_gradient.reshape(row_count, row_width)
    act_grad = last_product(grad_flat, feed_output_weight)
    gelu_pull = jax.vjp(gelu_tanh, before)[1]
    before_grad = gelu_pull(act_grad)[0].astype(jnp.bfloat16)
    normed_two_grad = last_product(before_grad, feed_input_weight)
    hidden_grad = grad_flat.astype(jnp.float32) + norm_back(
        hidden_state, gain_two, shift_two, normed_two_grad
    )
    branch_grad = hidden_grad.astype(jnp.bfloat16)
    context_grad = last_product(branch_grad, attention_out_weight).astype(jnp.bfloat16)
    grad_heads = lax.all_to_all(
        context_grad.reshape(local_shape), "head", split_axis=2, concat_axis=1, tiled=True
    ).reshape(split_shape)

    def back_fn(packed):
        return attend_back(
            packed[0],
            packed[1],
            packed[2],
            packed[3],
            packed[4],
            packed[5],
            block_rows,
            score_scale,
        )

    query_gradient, key_grad, value_gradient = lax.map(
        back_fn, (head_query, head_key, head_value, grad_heads, logsum, document_starts)
    )
    query_gradient, key_grad, value_gradient = (
        lax.all_to_all(
            as_sent(query_gradient.reshape(merged_shape)),
            "head",
            split_axis=1,
            concat_axis=2,
            tiled=True,
        ),
        lax.all_to_all(
            as_sent(key_grad.reshape(merged_shape)), "head", split_axis=1, concat_axis=2, tiled=True
        ),
        lax.all_to_all(
            as_sent(value_gradient.reshape(merged_shape)),
            "head",
            split_axis=1,
            concat_axis=2,
            tiled=True,
        ),
    )
    query_gradient = query_gradient.reshape(row_count, row_width)
    key_grad = key_grad.reshape(row_count, row_width)
    value_gradient = value_gradient.reshape(row_count, row_width)
    query_low_gradient = (ADAPTER_SCALE * last_product(query_gradient, query_up_weight)).astype(
        jnp.bfloat16
    )
    value_low_gradient = (ADAPTER_SCALE * last_product(value_gradient, value_up_weight)).astype(
        jnp.bfloat16
    )
    joined_grads = jnp.concatenate([query_gradient, key_grad, value_gradient], axis=1)
    normed_grad = (
        last_product(joined_grads, query_key_value_weight)
        + last_product(query_low_gradient, query_down_weight)
        + last_product(value_low_gradient, value_down_weight)
    )
    input_grad = hidden_grad + norm_back(flat_in, gain_one, shift_one, normed_grad)
    down_query = first_product(normed_rows, query_low_gradient)
    lifted_query = ADAPTER_SCALE * first_product(query_low_rank, query_gradient)
    down_value = first_product(normed_rows, value_low_gradient)
    lifted_value = ADAPTER_SCALE * first_product(value_low_rank, value_gradient)
    totals = lax.psum(
        (down_query, lifted_query, down_value, lifted_value, square_sums), ("dp", "head")
    )
    token_count = jnp.maximum(totals[4][2], 1.0)
    rms_values = jnp.stack(
        [
            jnp.sqrt(totals[4][0] / (token_count * row_width)),
            jnp.sqrt(totals[4][1] / (2.0 * token_count * row_width)),
        ]
    )
    return (
        output,
        input_grad.astype(jnp.bfloat16).reshape(block_input_rows.shape),
        totals[0],
        totals[1],
        totals[2],
        totals[3],
        rms_values,
    )


LOG2E = 1.4426950408889634
LN2 = 0.6931471805599453
TILE = 256
GROUP = 256
bf16 = jnp.bfloat16
f32 = jnp.float32
NT = (((1,), (1,)), ((), ()))
NN = (((1,), (0,)), ((), ()))
TN = (((0,), (0,)), ((), ()))
MESH = pl.DeviceIdType.MESH
MIB = 2**20


def dg(left, right, dims):
    return lax.dot_general(left, right, dims, preferred_element_type=f32)


def resident(shape):
    zeros = (0,) * len(shape)
    return pl.BlockSpec(shape, lambda *_: zeros, pipeline_mode=pl.Buffered(1))


def params(mib):
    return pltpu.CompilerParams(
        vmem_limit_bytes=mib * MIB, dimension_semantics=("arbitrary",)
    )


def norm_stats(rows):
    center = rows - jnp.mean(rows, axis=-1, keepdims=True)
    rs = lax.rsqrt(jnp.mean(center * center, axis=-1, keepdims=True) + EPSILON)
    return center * rs, rs


def norm_grad(unit, rs, gain, incoming):
    t = incoming * gain
    return (
        t - jnp.mean(t, axis=-1, keepdims=True) - unit * jnp.mean(t * unit, axis=-1, keepdims=True)
    ) * rs


def head_masks(x, heads, size):
    lane = lax.broadcasted_iota(jnp.int32, x.shape, 1)
    return [
        jnp.where((lane >= size * h) & (lane < size * (h + 1)), x, jnp.zeros_like(x))
        for h in range(heads)
    ]


def merge_heads(stacked, heads, size):
    rows = stacked.shape[0] // heads
    out = stacked[:rows]
    lane = lax.broadcasted_iota(jnp.int32, out.shape, 1)
    for h in range(1, heads):
        out = jnp.where(lane >= size * h, stacked[h * rows : (h + 1) * rows], out)
    return out


def column(line):
    return jnp.broadcast_to(line, (128, line.shape[1])).T


def entry_signal(peers):
    barrier = pltpu.get_barrier_semaphore()
    for peer in peers:
        pl.semaphore_signal(barrier, inc=1, device_id=peer, device_id_type=MESH)


def entry_wait(count):
    pl.semaphore_wait(pltpu.get_barrier_semaphore(), count)


def remote(src, dst, send_sem, recv_sem, peer):
    return pltpu.make_async_remote_copy(
        src_ref=src, dst_ref=dst, send_sem=send_sem, recv_sem=recv_sem, device_id=peer, device_id_type=MESH
    )


ANY = pl.BlockSpec(memory_space=pl.ANY)
VMEM = pl.BlockSpec(memory_space=pltpu.VMEM)


def line(ref):
    return ref[...].astype(f32).reshape(1, -1)


def rows_at(base, offset, count):
    return pl.ds(pl.multiple_of(base + offset, TILE), count)


def lanes_of(columns, width):
    size = width // len(columns)
    shape = (columns[0].shape[0], width)
    lane = lax.broadcasted_iota(jnp.int32, shape, 1)
    out = jnp.broadcast_to(columns[0], shape)
    for h in range(1, len(columns)):
        out = jnp.where(lane >= size * h, columns[h], out)
    return out


def pipelined(units, stages):
    for t in range(len(units) + len(stages) - 1):
        for b, stage in enumerate(stages):
            if 0 <= t - b < len(units):
                stage(t - b, units[t - b])


def open_kernel(
    x_ref, dy_ref, w_ref, mask_ref, start_ref, gain_ref, shift_ref, downq_ref, downv_ref, upq_ref, upv_ref,
    xs_ref, dys_ref, masks_ref, normed_ref, qkv_ref, ctx_ref, pd_ref, pc_ref, cd_ref, cc_ref,
    x_sc, w_sc, mask_sc, normed_sc, qkv_sc, s_sc, diag_sc, cross_sc, first_sc, state, part,
    x_send, x_recv, y_send, y_recv, m_send, m_recv, local_sem,
    *, size, strip,
):
    slots, tile, width = x_ref.shape
    length = slots * tile
    half = length // 2
    groups = width // GROUP
    heads = GROUP // size
    step = pl.program_id(0)
    group, me = lax.axis_index("dp"), lax.axis_index("head")
    mine = lax.rem(me, 2)
    near = me - mine
    far = slots // 2 - near
    beside = near + 1 - mine
    across = (far + mine, far + 1 - mine)
    peers = [(group, p) for p in (beside,) + across]

    def x_copy(k):
        return remote(x_ref.at[peers[k][1]], x_sc.at[me], x_send.at[k], x_recv.at[k], peers[k])

    def y_copy(k):
        return remote(dy_ref.at[peers[k][1]], dys_ref.at[me], y_send.at[k], y_recv.at[k], peers[k])

    def m_copy(k):
        return remote(mask_sc.at[peers[k][1]], masks_ref.at[me], m_send.at[k], m_recv.at[k], peers[k])

    def own_x():
        return pltpu.make_async_copy(x_ref.at[me], x_sc.at[me], local_sem.at[0])

    def own_y():
        return pltpu.make_async_copy(dy_ref.at[me], dys_ref.at[me], local_sem.at[1])

    def own_m():
        return pltpu.make_async_copy(mask_sc.at[me], masks_ref.at[me], local_sem.at[2])

    def weight():
        return pltpu.make_async_copy(w_ref, w_sc, local_sem.at[3])

    def save_x():
        return pltpu.make_async_copy(x_sc, xs_ref, local_sem.at[4])

    def save_normed():
        return pltpu.make_async_copy(normed_sc, normed_ref, local_sem.at[5])

    def save_qkv():
        return pltpu.make_async_copy(qkv_sc, qkv_ref, local_sem.at[6])

    @pl.when(step == 0)
    def _():
        entry_signal(peers)
        own_x().start()
        weight().start()
        own_y().start()
        for s in range(slots):
            mask_sc[s] = jnp.broadcast_to(mask_ref[s : s + 1, :].astype(f32), mask_sc.shape[1:])
        own_m().start()
        entry_wait(len(peers))
        for k in (1, 2, 0):
            x_copy(k).start()
        for k in range(3):
            m_copy(k).start()
        first_sc[...] = column(start_ref[pl.ds(me, 1), :])

        def bias(i, carry):
            here = pl.ds(pl.multiple_of(i * strip, strip), strip)
            base = half * lax.div(i * strip, half)
            keys = lax.broadcasted_iota(jnp.int32, (strip, half), 1) + base
            rows = lax.broadcasted_iota(jnp.int32, (strip, half), 0) + i * strip
            allowed = (keys >= first_sc[here, 0:1]) & (keys <= rows)
            diag_sc[here, :] = jnp.where(allowed, 0.0, NEGATIVE)
            return carry

        lax.fori_loop(0, length // strip, bias, 0)

        def cross_bias(i, carry):
            here = pl.ds(pl.multiple_of(i * strip, strip), strip)
            keys = lax.broadcasted_iota(jnp.int32, (strip, half), 1)
            rows = pl.ds(pl.multiple_of(half + i * strip, strip), strip)
            cross_sc[here, :] = jnp.where(keys >= first_sc[rows, 0:1], 0.0, NEGATIVE)
            return carry

        lax.fori_loop(0, half // strip, cross_bias, 0)
        own_x().wait()
        x_copy(0).wait_recv()
        weight().wait()

    @pl.when(step == groups + 1)
    def _():
        for k in (1, 2):
            x_copy(k).wait()
        for k in (1, 2, 0):
            y_copy(k).start()
        save_x().start()

    @pl.when(lax.rem(step, groups + 1) == 0)
    def _():
        first = near + (far - near) * lax.div(step, groups + 1)
        rows = x_sc[pl.ds(first, 2)].reshape(half, width).astype(f32)
        unit, _ = norm_stats(rows)
        normed = (unit * line(gain_ref) + line(shift_ref)).astype(bf16)
        here = pl.ds(pl.multiple_of(first * tile, tile), half)
        normed_sc[here, :] = normed
        low_q = dg(normed, downq_ref[...], NT).astype(bf16)
        low_v = dg(normed, downv_ref[...], NT).astype(bf16)
        scale = size**-0.5 * LOG2E
        wide = 512
        for at in range(0, 3 * width, wide):
            cols = slice(at, at + wide)
            piece = dg(normed, w_sc[:, cols], NN)
            if at < width:
                piece = (piece + ADAPTER_SCALE * dg(low_q, upq_ref[:, cols], NN)) * scale
            if at >= 2 * width:
                piece = piece + ADAPTER_SCALE * dg(low_v, upv_ref[:, at - 2 * width : at - 2 * width + wide], NN)
            qkv_sc[here, cols] = piece.astype(bf16)

    @pl.when(step == groups + 1)
    def _():
        save_normed().start()
        save_qkv().start()

    def attention(g, units):
        def third(k):
            return qkv_sc.at[:, pl.ds(pl.multiple_of(k * width + g * GROUP, GROUP), GROUP)]

        q_ref, k_ref, v_ref = third(0), third(1), third(2)

        def scores(at, unit):
            i, n, q_base, k_base = unit[:4]
            masked = jnp.concatenate(head_masks(q_ref[rows_at(q_base, i * TILE, TILE), :], heads, size), 0)
            for j in range(0, n, TILE):
                s_sc[at % 2, :, j : j + TILE] = dg(masked, k_ref[rows_at(k_base, j, TILE), :], NT)

        def soft(at, unit):
            i, n, q_base, _, bias, probs, (_, keep_m, keep_l, keep_row) = unit
            tops, sums = [], []
            for r in range(0, TILE, strip):
                tops.append([])
                sums.append([])
                for h in range(heads):
                    here = h * TILE + r
                    s = s_sc[at % 2, here : here + strip, 0:n] + bias(i * TILE + r, n)
                    top = jnp.max(s, axis=1, keepdims=True)
                    e = jnp.exp2(s - top)
                    tops[-1].append(top)
                    sums[-1].append(jnp.sum(e, axis=1, keepdims=True))
                    probs[h, i * TILE + r : i * TILE + r + strip, 0:n] = e.astype(bf16)
                where = pl.ds(pl.multiple_of(keep_row + i * TILE + r, strip), strip)
                keep_m[where, :] = lanes_of(tops[-1], GROUP)
                keep_l[where, :] = lanes_of(sums[-1], GROUP)

        def mix(at, unit):
            i, n, _, k_base, _, probs, (keep_o, _, _, keep_row) = unit
            stacked = probs[:, i * TILE : (i + 1) * TILE, 0:n].reshape(heads * TILE, n)
            merged = merge_heads(dg(stacked, v_ref[rows_at(k_base, 0, n), :], NN), heads, size)
            keep_o[rows_at(keep_row, i * TILE, TILE), :] = merged

        pipelined(units, (scores, soft, mix))

    def diag_units(g, base):
        def bias(r, n):
            return diag_sc[pl.ds(pl.multiple_of(base + r, strip), strip), 0:n]

        kept = tuple(state.at[a, :, pl.ds(pl.multiple_of(g * GROUP, GROUP), GROUP)] for a in range(3))
        return [
            (i, (i + 1) * TILE, base, base, bias, pd_ref.at[0], kept + (base,)) for i in range(half // TILE)
        ]

    def cross_units(g):
        def bias(r, n):
            return cross_sc[r : r + strip, 0:n]

        return [
            (i, half, half, 0, bias, pc_ref, (part.at[0], part.at[1], part.at[2], 0)) for i in range(half // TILE)
        ]

    @pl.when((step > 0) & (step <= groups))
    def _():
        attention(step - 1, diag_units(step - 1, near * tile))

    @pl.when(step > groups + 1)
    def _():
        g = step - groups - 2
        attention(g, diag_units(g, far * tile) + cross_units(g))
        cols = pl.ds(pl.multiple_of(g * GROUP, GROUP), GROUP)
        inverse = 1.0 / state[2, 0:half, cols]
        cd_ref[0:half] = inverse
        ctx_ref[0:half] = (state[0, 0:half, cols] * inverse).astype(bf16)
        for r in range(0, half, TILE):
            high = slice(half + r, half + r + TILE)
            here = slice(r, r + TILE)
            top = jnp.maximum(state[1, high, cols], part[1, here])
            weight_d = jnp.exp2(state[1, high, cols] - top)
            weight_c = jnp.exp2(part[1, here] - top)
            inverse = 1.0 / (weight_d * state[2, high, cols] + weight_c * part[2, here])
            weight_d = weight_d * inverse
            weight_c = weight_c * inverse
            cd_ref[high] = weight_d
            cc_ref[here] = weight_c
            ctx_ref[high] = (state[0, high, cols] * weight_d + part[0, here] * weight_c).astype(bf16)

    @pl.when(step == 2 * groups + 1)
    def _():
        x_copy(0).wait_send()
        for k in range(3):
            y_copy(k).wait()
            m_copy(k).wait()
        own_m().wait()
        own_y().wait()
        save_x().wait()
        save_normed().wait()
        save_qkv().wait()


def opening(x, dy, w, mask, start, gain, shift, downq, downv, upq, upv, size):
    slots, tile, width = x.shape
    length = slots * tile
    half = length // 2
    groups = width // GROUP
    per = GROUP // size
    dma = pltpu.SemaphoreType.DMA
    small = [mask, start, gain, shift, downq, downv, upq, upv]
    masks = (slots, 8, tile)

    def late(t):
        return jnp.maximum(t - groups - 2, 0)

    def diag_at(t):
        second = lax.div(t, groups + 2)
        return second, jnp.where(second == 1, t - groups - 2, jnp.clip(t - 1, 0, groups - 1)), 0, 0

    return pl.pallas_call(
        functools.partial(open_kernel, size=size, strip=32),
        grid=(2 * groups + 2,),
        in_specs=[ANY] * 3 + [resident(a.shape) for a in small],
        out_specs=[ANY] * 5 + [
            pl.BlockSpec((length, GROUP), lambda t: (0, late(t))),
            pl.BlockSpec((1, per, half, half), diag_at),
            pl.BlockSpec((per, half, half), lambda t: (late(t), 0, 0)),
            pl.BlockSpec((length, GROUP), lambda t: (0, late(t))),
            pl.BlockSpec((half, GROUP), lambda t: (0, late(t))),
        ],
        out_shape=[
            jax.ShapeDtypeStruct(x.shape, bf16),
            jax.ShapeDtypeStruct(x.shape, bf16),
            jax.ShapeDtypeStruct(masks, f32),
            jax.ShapeDtypeStruct((length, width), bf16),
            jax.ShapeDtypeStruct((length, 3 * width), bf16),
            jax.ShapeDtypeStruct((length, width), bf16),
            jax.ShapeDtypeStruct((2, per * groups, half, half), bf16),
            jax.ShapeDtypeStruct((per * groups, half, half), bf16),
            jax.ShapeDtypeStruct((length, width), f32),
            jax.ShapeDtypeStruct((half, width), f32),
        ],
        scratch_shapes=[
            pltpu.VMEM(x.shape, bf16),
            pltpu.VMEM(w.shape, bf16),
            pltpu.VMEM(masks, f32),
            pltpu.VMEM((length, width), bf16),
            pltpu.VMEM((length, 3 * width), bf16),
            pltpu.VMEM((2, per * TILE, half), f32),
            pltpu.VMEM((length, half), f32),
            pltpu.VMEM((half, half), f32),
            pltpu.VMEM((length, 128), jnp.int32),
            pltpu.VMEM((3, length, width), f32),
            pltpu.VMEM((3, half, GROUP), f32),
            dma((3,)), dma((3,)), dma((3,)), dma((3,)), dma((3,)), dma((3,)), dma((7,)),
        ],
        compiler_params=pltpu.CompilerParams(
            collective_id=0, has_side_effects=True, vmem_limit_bytes=62 * MIB, dimension_semantics=("arbitrary",)
        ),
        name="opening",
    )(x, dy, w, *small)


def feed_kernel(
    x_ref, y_ref, ctx_ref, mask_ref, wo_hbm, wi_hbm, wf_hbm, gain_ref, shift_ref, bias_ref,
    out_ref, hg_ref, cg_ref, sums_ref, wo_ref, wi_ref, wf_ref, feed_sc, grad_sc, normed_sc, v_sc, g_sc, sem,
    *, step,
):
    blocks, tile, width = x_ref.shape
    rows = blocks * tile
    chunks = wi_ref.shape[1] // step
    first = pl.program_id(0) == 0

    def cols_of(c):
        return pl.ds(c * step if isinstance(c, int) else pl.multiple_of(c * step, step), step)

    def load_o():
        return pltpu.make_async_copy(wo_hbm, wo_ref, sem.at[2 * chunks])

    def load_i(c):
        return pltpu.make_async_copy(wi_hbm.at[:, cols_of(c)], wi_ref.at[:, cols_of(c)], sem.at[2 * c])

    def load_f(c):
        return pltpu.make_async_copy(wf_hbm.at[cols_of(c), :], wf_ref.at[cols_of(c), :], sem.at[2 * c + 1])

    @pl.when(first)
    def _():
        load_o().start()
        for c in range(chunks):
            load_i(c).start()
            load_f(c).start()
        load_o().wait()

    branch = dg(ctx_ref[...], wo_ref[...], NN)
    hidden = x_ref[...].reshape(rows, width).astype(f32) + branch
    unit, rs = norm_stats(hidden)
    gain = line(gain_ref)
    normed_sc[...] = (unit * gain + line(shift_ref)).astype(bf16)
    c0 = 0.7978845608028654
    c1 = c0 * 0.044715

    def enter(c, slot):
        @pl.when(first)
        def _():
            load_i(c).wait()
            load_f(c).wait()

        cols = cols_of(c)
        v_sc[slot] = dg(normed_sc[...], wi_ref[:, cols], NN) + bias_ref[cols].astype(f32).reshape(1, step)
        g_sc[slot] = dg(y_ref[...].reshape(rows, width), wf_ref[cols, :], NT)

    def leave(c, slot):
        v = v_sc[slot]
        square = v * v
        half = 0.5 * jnp.tanh(v * (c0 + c1 * square)) + 0.5
        act = v * half
        slope = half + act * (1.0 - half) * (2.0 * c0 + 6.0 * c1 * square)
        cols = cols_of(c)
        feed_sc[...] += dg(act.astype(bf16), wf_ref[cols, :], NN)
        grad_sc[...] += dg((slope * g_sc[slot]).astype(bf16), wi_ref[:, cols], NT)

    feed_sc[...] = jnp.zeros_like(feed_sc)
    grad_sc[...] = jnp.zeros_like(grad_sc)
    enter(0, 0)

    def pair(i, carry):
        enter(2 * i + 1, 1)
        leave(2 * i, 0)
        enter(2 * i + 2, 0)
        leave(2 * i + 1, 1)
        return carry

    lax.fori_loop(0, chunks // 2 - 1, pair, 0)
    enter(chunks - 1, 1)
    leave(chunks - 2, 0)
    leave(chunks - 1, 1)
    feed = feed_sc[...]
    result = hidden + feed
    out_ref[...] = result.astype(bf16).reshape(out_ref.shape)
    valid = jnp.concatenate([column(mask_ref[b, 0:1, :])[:, 0:1] for b in range(blocks)], 0)
    one = jnp.sum(valid * jnp.sum(result * result, axis=1, keepdims=True))
    two = jnp.sum(valid * jnp.sum(branch * branch + feed * feed, axis=1, keepdims=True))
    count = jnp.sum(valid)
    row = lax.broadcasted_iota(jnp.int32, sums_ref.shape, 0)
    col = lax.broadcasted_iota(jnp.int32, sums_ref.shape, 1)
    mine = jnp.where(col == 0, one, jnp.where(col == 1, two, jnp.where(col == 2, count, 0.0)))
    mine = jnp.where(row == 0, mine, 0.0)

    @pl.when(first)
    def _():
        sums_ref[...] = mine

    @pl.when(jnp.logical_not(first))
    def _():
        sums_ref[...] += mine

    dy = y_ref[...].reshape(rows, width).astype(f32)
    low = (dy + norm_grad(unit, rs, gain, grad_sc[...])).astype(bf16)
    hg_ref[...] = low
    cg_ref[...] = dg(low, wo_ref[...], NT).astype(bf16)


def feed(x, dy, context, mask, wo, gain, shift, wi, bias, wf):
    slots, tile, width = x.shape
    rows = slots * tile
    units = wi.shape[1]
    each = 2
    step = 512
    slab = pl.BlockSpec((each, tile, width), lambda i: (i, 0, 0))
    flat = pl.BlockSpec((each * tile, width), lambda i: (i, 0))
    return pl.pallas_call(
        functools.partial(feed_kernel, step=step),
        grid=(slots // each,),
        in_specs=[
            slab, slab, flat,
            pl.BlockSpec((each,) + mask.shape[1:], lambda i: (i, 0, 0)),
            ANY, ANY, ANY, resident(gain.shape), resident(shift.shape), resident(bias.shape),
        ],
        out_specs=[slab, flat, flat, pl.BlockSpec((8, width), lambda i: (0, 0))],
        out_shape=[
            jax.ShapeDtypeStruct(x.shape, bf16),
            jax.ShapeDtypeStruct((rows, width), bf16),
            jax.ShapeDtypeStruct((rows, width), bf16),
            jax.ShapeDtypeStruct((8, width), f32),
        ],
        scratch_shapes=[
            pltpu.VMEM(wo.shape, bf16), pltpu.VMEM(wi.shape, bf16), pltpu.VMEM(wf.shape, bf16),
            pltpu.VMEM((each * tile, width), f32), pltpu.VMEM((each * tile, width), f32),
            pltpu.VMEM((each * tile, width), bf16),
            pltpu.VMEM((2, each * tile, step), f32), pltpu.VMEM((2, each * tile, step), f32),
            pltpu.SemaphoreType.DMA((2 * (units // step) + 1,)),
        ],
        compiler_params=params(62),
        name="feed",
    )(x, dy, context, mask, wo, wi, wf, gain, shift, bias)


def close_kernel(
    q_ref, k_ref, v_ref, g_ref, o_ref, cd_ref, cc_ref, pd_ref, pc_ref,
    res_hbm, x_hbm, hg_hbm, normed_hbm, w_hbm,
    gain_ref, downq_ref, downv_ref, upq_ref, upv_ref, sums_ref,
    result_ref, out_ref, total_ref,
    dp_sc, ds_sc, inner_sc, do_sc, loc, near_sc, grads, x_sc, hg_sc, normed_sc, w_sc, res_sc,
    sums, parts, chunk, heard, total_sc,
    r_send, r_recv, send, recv, local_sem, part_send, part_recv, pair_send, pair_recv, mean_send, mean_recv,
    *, size, strip, sizes,
):
    slots, tile, width = x_sc.shape
    length = slots * tile
    half = length // 2
    groups = width // GROUP
    heads = GROUP // size
    rank = downq_ref.shape[0]
    step = pl.program_id(0)
    last = 2 * groups + 1
    group, me = lax.axis_index("dp"), lax.axis_index("head")
    mine = lax.rem(me, 2)
    near = me - mine
    far = slots // 2 - near
    beside = near + 1 - mine
    peers = [(group, p) for p in (far + mine, far + 1 - mine, beside)]
    rest = [(lax.rem(group + k, sizes[0]), me) for k in range(1, sizes[0])]
    lanes = width // sizes[0]

    def own_result():
        return pltpu.make_async_copy(res_hbm.at[me], result_ref.at[me], local_sem.at[0])

    def result_copy(k):
        return remote(res_hbm.at[peers[k][1]], result_ref.at[me], r_send.at[k], r_recv.at[k], peers[k])

    def loads():
        return [
            pltpu.make_async_copy(src, dst, local_sem.at[1 + a])
            for a, (src, dst) in enumerate([(x_hbm, x_sc), (hg_hbm, hg_sc), (normed_hbm, normed_sc), (w_hbm, w_sc)])
        ]

    @pl.when(step == 0)
    def _():
        entry_signal(peers + rest)
        own_result().start()
        for copy in loads():
            copy.start()
        sums[...] = jnp.zeros_like(sums)
        sums[4 * rank :, :] = sums_ref[...]

    @pl.when(step == 1)
    def _():
        entry_wait(len(peers) + len(rest))
        for k in range(3):
            result_copy(k).start()

    def attention(units):
        def stack(x):
            return jnp.concatenate(head_masks(x, heads, size), 0)

        def prob_grads(at, unit):
            i, n, q_base, k_base, _, which, row = unit[:7]
            grad = do_sc[which, rows_at(row, i * TILE, TILE), :]
            masked = stack(grad)
            for j in range(0, n, TILE):
                dp_sc[at % 2, :, j : j + TILE] = dg(masked, v_ref[rows_at(k_base, j, TILE), :], NT)
            both = (grad.astype(f32) * o_ref[rows_at(q_base, i * TILE, TILE), :].astype(f32)).astype(bf16)
            inner_sc[at % 2] = dg(stack(both), jnp.ones((GROUP, 128), bf16), NN)

        def score_grads(at, unit):
            i, n, _, _, probs = unit[:5]
            for h in range(heads):
                for r in range(0, TILE, strip):
                    here = h * TILE + r
                    inner = jnp.concatenate([inner_sc[at % 2, here : here + strip, :]] * (n // 128), 1)
                    prob = probs[h, i * TILE + r : i * TILE + r + strip, 0:n].astype(f32)
                    ds = prob * (dp_sc[at % 2, here : here + strip, 0:n] - inner)
                    ds_sc[at % 2, here : here + strip, 0:n] = ds.astype(bf16)

        def products(at, unit):
            i, n, q_base, k_base, probs, which, row, add = unit
            query = rows_at(q_base, i * TILE, TILE)
            ds = ds_sc[at % 2, :, 0:n]
            dq = merge_heads(dg(ds, k_ref[rows_at(k_base, 0, n), :], NN), heads, size)
            stacked = probs[:, i * TILE : (i + 1) * TILE, 0:n].reshape(heads * TILE, n)
            dv = dg(stacked, stack(do_sc[which, rows_at(row, i * TILE, TILE), :]), TN)
            dk = dg(ds, stack(q_ref[query, :]), TN)
            if add:
                loc[0, query, :] += dq
                keys = rows_at(k_base, 0, n)
                loc[1, keys, :] += dk
                loc[2, keys, :] += dv
            else:
                loc[0, query, :] = dq
                if i:
                    keys = rows_at(k_base, 0, i * TILE)
                    loc[1, keys, :] += dk[: i * TILE]
                    loc[2, keys, :] += dv[: i * TILE]
                loc[1, query, :] = dk[i * TILE :]
                loc[2, query, :] = dv[i * TILE :]

        pipelined(units, (prob_grads, score_grads, products))

    def diag_units(base):
        here = rows_at(base, 0, half)
        do_sc[0] = (g_ref[here, :].astype(f32) * cd_ref[here, :]).astype(bf16)
        return [(i, (i + 1) * TILE, base, base, pd_ref.at[0], 0, 0, False) for i in range(half // TILE)]

    def cross_units():
        do_sc[1] = (g_ref[half:, :].astype(f32) * cc_ref[...]).astype(bf16)
        return [(i, half, half, 0, pc_ref, 1, 0, True) for i in range(half // TILE)]

    scales = (size**-0.5, LN2, 1.0)

    @pl.when(step < groups)
    def _():
        cols = pl.ds(pl.multiple_of(step * GROUP, GROUP), GROUP)
        far_rows = rows_at(far * tile, 0, half)
        near_rows = rows_at(near * tile, 0, half)
        for a in range(3):
            loc[a, near_rows, :] = jnp.zeros((half, GROUP), f32)
        attention(diag_units(far * tile) + cross_units())
        for a in range(3):
            grads[a, far_rows, cols] = (loc[a, far_rows, :] * scales[a]).astype(bf16)
            near_sc[a, :, cols] = loc[a, near_rows, :]

    @pl.when((step > groups) & (step < last))
    def _():
        cols = pl.ds(pl.multiple_of((step - groups - 1) * GROUP, GROUP), GROUP)
        near_rows = rows_at(near * tile, 0, half)
        attention(diag_units(near * tile))
        for a in range(3):
            both = loc[a, near_rows, :] + near_sc[a, :, cols]
            grads[a, near_rows, cols] = (both * scales[a]).astype(bf16)

    def give(k):
        return remote(res_sc.at[peers[k][1]], out_ref.at[me], send.at[k], recv.at[k], peers[k])

    def give_part(p):
        rows = pl.ds(p * (tile // 2), tile // 2)
        return remote(
            res_sc.at[peers[1][1], rows], out_ref.at[me, rows], send.at[1 + 2 * p], recv.at[1 + 2 * p], peers[1]
        )

    def keep():
        return pltpu.make_async_copy(res_sc.at[me], out_ref.at[me], local_sem.at[5])

    def block_of(d):
        return pl.ds(pl.multiple_of(d * lanes, lanes), lanes)

    def scatter(k):
        return remote(sums.at[:, block_of(rest[k][0])], parts.at[k], part_send.at[k], part_recv.at[k], rest[k])

    def pair(at, peer):
        return remote(chunk.at[at], heard.at[at], pair_send.at[at], pair_recv.at[at], peer)

    def gather(k):
        return remote(chunk.at[2], total_sc.at[:, block_of(group)], mean_send.at[k], mean_recv.at[k], rest[k])

    @pl.when(step == groups)
    def _():
        for copy in loads():
            copy.wait()

    @pl.when((step == groups) | (step == last))
    def _():
        first = far + (near - far) * lax.div(step, last)
        at = pl.ds(first, 2)
        here = pl.ds(pl.multiple_of(first * tile, tile), half)
        dq, dk, dv = grads[0, here, :], grads[1, here, :], grads[2, here, :]
        normed = normed_sc[at].reshape(half, width)
        low_gq = (ADAPTER_SCALE * dg(dq, upq_ref[...], NT)).astype(bf16)
        low_gv = (ADAPTER_SCALE * dg(dv, upv_ref[...], NT)).astype(bf16)
        low_q = dg(normed, downq_ref[...], NT).astype(bf16)
        low_v = dg(normed, downv_ref[...], NT).astype(bf16)
        sums[0:rank] += dg(low_gq, normed, TN)
        sums[rank : 2 * rank] += dg(low_gv, normed, TN)
        sums[2 * rank : 3 * rank] += ADAPTER_SCALE * dg(low_q, dq, TN)
        sums[3 * rank : 4 * rank] += ADAPTER_SCALE * dg(low_v, dv, TN)

        @pl.when(step == last)
        def _():
            for k in range(len(rest)):
                scatter(k).start()

        normed_grad = (
            dg(dq, w_sc[:, :width], NT)
            + dg(dk, w_sc[:, width : 2 * width], NT)
            + dg(dv, w_sc[:, 2 * width :], NT)
            + dg(low_gq, downq_ref[...], NN)
            + dg(low_gv, downv_ref[...], NN)
        )
        unit, rs = norm_stats(x_sc[at].reshape(half, width).astype(f32))
        grad = hg_sc[at].reshape(half, width).astype(f32) + norm_grad(unit, rs, line(gain_ref), normed_grad)
        res_sc[at] = grad.astype(bf16).reshape(2, tile, width)

    @pl.when(step == groups)
    def _():
        give(0).start()
        give_part(0).start()

    @pl.when(step == last)
    def _():
        give(2).start()
        keep().start()
        for k in range(len(rest)):
            scatter(k).wait()
        whole = sums[:, block_of(group)]
        for k in range(len(rest)):
            whole = whole + parts[k]
        chunk[0] = whole
        pair(0, peers[2]).start()
        pair(0, peers[2]).wait()
        chunk[1] = chunk[0] + heard[0]
        pair(1, peers[0]).start()
        give_part(1).start()
        pair(1, peers[0]).wait()
        whole = chunk[1] + heard[1]
        chunk[2] = whole
        total_sc[:, block_of(group)] = whole
        for k in range(len(rest)):
            gather(k).start()
        for k in range(len(rest)):
            gather(k).wait()
        total_ref[...] = total_sc[...]
        own_result().wait()
        keep().wait()
        for k in range(3):
            result_copy(k).wait()
        give(0).wait()
        give(2).wait()
        give_part(0).wait()
        give_part(1).wait()


def closing(
    qkv, grad, context, cd, cc, pd, pc, result, x, hidden_grad, normed, w,
    gain, downq, downv, upq, upv, sums, size, sizes,
):
    slots, tile, width = x.shape
    length = slots * tile
    half = length // 2
    groups = width // GROUP
    per = GROUP // size
    rank = downq.shape[0]
    total = (4 * rank + 8, width)
    rest = sizes[0] - 1
    lanes = width // sizes[0]
    dma = pltpu.SemaphoreType.DMA
    small = [gain, downq, downv, upq, upv, sums]

    def fold(a):
        return a.reshape(x.shape)

    def of(t):
        second = lax.div(t, groups + 1)
        return jnp.minimum(t - second * (groups + 1), groups - 1)

    def early(t):
        return jnp.minimum(t, groups - 1)

    def columns(third):
        return pl.BlockSpec((length, GROUP), lambda t: (0, of(t) + third * groups))

    return pl.pallas_call(
        functools.partial(close_kernel, size=size, strip=32, sizes=sizes),
        grid=(2 * groups + 2,),
        in_specs=[
            columns(0), columns(1), columns(2), columns(0), columns(0), columns(0),
            pl.BlockSpec((half, GROUP), lambda t: (0, early(t))),
            pl.BlockSpec((1, per, half, half), lambda t: (1 - lax.div(t, groups + 1), of(t), 0, 0)),
            pl.BlockSpec((per, half, half), lambda t: (early(t), 0, 0)),
        ]
        + [ANY] * 5
        + [resident(a.shape) for a in small],
        out_specs=[ANY, ANY, pl.BlockSpec(total, lambda t: (0, 0))],
        out_shape=[
            jax.ShapeDtypeStruct(x.shape, bf16),
            jax.ShapeDtypeStruct(x.shape, bf16),
            jax.ShapeDtypeStruct(total, f32),
        ],
        scratch_shapes=[
            pltpu.VMEM((2, per * TILE, half), f32),
            pltpu.VMEM((2, per * TILE, half), bf16),
            pltpu.VMEM((2, per * TILE, 128), f32),
            pltpu.VMEM((2, half, GROUP), bf16),
            pltpu.VMEM((3, length, GROUP), f32),
            pltpu.VMEM((3, half, width), f32),
            pltpu.VMEM((3, length, width), bf16),
            pltpu.VMEM(x.shape, bf16),
            pltpu.VMEM(x.shape, bf16),
            pltpu.VMEM(x.shape, bf16),
            pltpu.VMEM(w.shape, bf16),
            pltpu.VMEM(x.shape, bf16),
            pltpu.VMEM(total, f32),
            pltpu.VMEM((rest, total[0], lanes), f32),
            pltpu.VMEM((3, total[0], lanes), f32),
            pltpu.VMEM((2, total[0], lanes), f32),
            pltpu.VMEM(total, f32),
            dma((3,)), dma((3,)), dma((4,)), dma((4,)), dma((6,)),
            dma((rest,)), dma((rest,)), dma((2,)), dma((2,)), dma((rest,)), dma((rest,)),
        ],
        compiler_params=pltpu.CompilerParams(
            collective_id=1, has_side_effects=True, vmem_limit_bytes=62 * MIB, dimension_semantics=("arbitrary",)
        ),
        name="closing",
    )(qkv, qkv, qkv, grad, context, cd, cc, pd, pc, result, x, fold(hidden_grad), fold(normed), w, *small)


def finish_kernel(total_ref, aq_ref, bq_ref, av_ref, bv_ref, rms_ref):
    rank, width = aq_ref.shape
    aq_ref[...] = total_ref[0:rank]
    av_ref[...] = total_ref[rank : 2 * rank]
    bq_ref[...] = total_ref[2 * rank : 3 * rank]
    bv_ref[...] = total_ref[3 * rank : 4 * rank]
    line = total_ref[4 * rank : 4 * rank + 1, 0:128]
    lane = lax.broadcasted_iota(jnp.int32, line.shape, 1)
    count = jnp.maximum(jnp.sum(jnp.where(lane == 2, line, 0.0)), 1.0)
    rms_ref[...] = jnp.sqrt(line / (jnp.where(lane == 0, 1.0, 2.0) * count * width))


def finish(total, rank):
    width = total.shape[1]
    small = jax.ShapeDtypeStruct((rank, width), f32)
    return pl.pallas_call(
        finish_kernel,
        in_specs=[VMEM],
        out_specs=[VMEM] * 5,
        out_shape=[small] * 4 + [jax.ShapeDtypeStruct((1, 128), f32)],
        name="finish",
    )(total)


def whole_slots(
    block_input_rows,
    document_starts,
    counted_mask,
    output_gradient,
    first_norm_gain,
    first_norm_bias,
    query_key_value_weight,
    query_down_weight,
    query_up_weight,
    value_down_weight,
    value_up_weight,
    attention_out_weight,
    second_norm_gain,
    second_norm_bias,
    feed_input_weight,
    feed_input_bias,
    feed_output_weight,
):
    sizes = (lax.axis_size("dp"), lax.axis_size("head"))
    size = block_input_rows.shape[-1] // H
    rank = query_down_weight.shape[1]
    downq = query_down_weight.T
    downv = value_down_weight.T
    x, dy, mask, normed, qkv, context, pd, pc, cd, cc = opening(
        block_input_rows, output_gradient, query_key_value_weight, counted_mask, document_starts,
        first_norm_gain, first_norm_bias, downq, downv, query_up_weight, value_up_weight, size,
    )
    out, hidden_grad, context_grad, sums = feed(
        x, dy, context, mask, attention_out_weight, second_norm_gain, second_norm_bias,
        feed_input_weight, feed_input_bias, feed_output_weight,
    )
    output, input_grad, total = closing(
        qkv, context_grad, context, cd, cc, pd, pc, out, x, hidden_grad, normed, query_key_value_weight,
        first_norm_gain, downq, downv, query_up_weight, value_up_weight, sums, size, sizes,
    )
    grad_aq, grad_bq, grad_av, grad_bv, rms = finish(total, rank)
    return output, input_grad, grad_aq.T, grad_bq, grad_av.T, grad_bv, rms[0, :2]


def body(*args):
    same = args[0].shape[0] == lax.axis_size("head")
    return whole_slots(*args) if same else shards(*args)


def solution(mesh):
    return jax.shard_map(
        body,
        mesh=mesh,
        in_specs=(
            P("dp", "head", None),
            P("dp", None),
            P("dp", "head"),
            P("dp", "head", None),
            P(),
            P(),
            P(),
            P(),
            P(),
            P(),
            P(),
            P(),
            P(),
            P(),
            P(),
            P(),
            P(),
        ),
        out_specs=(P("dp", "head", None), P("dp", "head", None), P(), P(), P(), P(), P()),
        check_vma=False,
    )
```

```python
import functools

import jax
import jax.numpy as jnp
from jax import lax
from jax.experimental import pallas as pl
from jax.experimental.pallas import tpu as pltpu
from jax.sharding import PartitionSpec as P

H = 16


EPSILON = 1e-05
ADAPTER_SCALE = 8.0
NEGATIVE = -1e30


def as_sent(x):

    def short(part):
        return part.astype(jnp.bfloat16) if part.dtype == jnp.float32 else part

    return jax.tree.map(short, x)


def norm_rows(matrix, gain_vec, shift_vec):
    center = matrix - jnp.mean(matrix, axis=-1, keepdims=True)
    variance = jnp.mean(center * center, axis=-1, keepdims=True)
    return center * lax.rsqrt(variance + EPSILON) * gain_vec + shift_vec


def norm_back(matrix, gain_vec, shift_vec, incoming):
    pullback = jax.vjp(lambda element_item: norm_rows(element_item, gain_vec, shift_vec), matrix)[1]
    return pullback(incoming)[0]


def gelu_tanh(matrix):
    return jax.nn.gelu(matrix, approximate=True)


def plain_product(left, right):
    return jnp.dot(left, right, preferred_element_type=jnp.float32)


def last_product(left, right):
    return lax.dot_general(
        left, right, (((1,), (1,)), ((), ())), preferred_element_type=jnp.float32
    )


def first_product(left, right):
    return lax.dot_general(
        left, right, (((0,), (0,)), ((), ())), preferred_element_type=jnp.float32
    )


def masked_scores(query_block, key_slot, segments, row_start, row_end, score_scale):
    places = jnp.arange(row_end)
    allowed = (segments[row_start:row_end, None] == segments[None, :row_end]) & (
        places[None, :] <= places[row_start:row_end, None]
    )
    scores = (
        jnp.einsum(
            "qhd,khd->hqk", query_block, key_slot[:row_end], preferred_element_type=jnp.float32
        )
        * score_scale
    )
    return jnp.where(allowed[None], scores, NEGATIVE)


def attend_slot(query_slot, key_slot, value_slot, segments, block_rows, score_scale):
    length = query_slot.shape[0]
    outputs_list = []
    logsum_list = []
    for block_index in range(length // block_rows):
        row_start = block_index * block_rows
        row_end = row_start + block_rows
        scores = masked_scores(
            query_slot[row_start:row_end], key_slot, segments, row_start, row_end, score_scale
        )
        row_max = jnp.max(scores, axis=-1, keepdims=True)
        exponent = jnp.exp(scores - row_max)
        row_total = jnp.sum(exponent, axis=-1, keepdims=True)
        probability = (exponent / row_total).astype(jnp.bfloat16)
        context = jnp.einsum(
            "hqk,khd->qhd", probability, value_slot[:row_end], preferred_element_type=jnp.float32
        )
        outputs_list.append(context.astype(jnp.bfloat16))
        logsum_list.append((row_max + jnp.log(row_total))[..., 0])
    return (jnp.concatenate(outputs_list, 0), jnp.concatenate(logsum_list, 1))


def attend_back(
    query_slot, key_slot, value_slot, grad_slot, logsum, segments, block_rows, score_scale
):
    length = query_slot.shape[0]
    key_grad = jnp.zeros(key_slot.shape, jnp.float32)
    value_gradient = jnp.zeros(value_slot.shape, jnp.float32)
    query_parts = []
    for block_index in range(length // block_rows):
        row_start = block_index * block_rows
        row_end = row_start + block_rows
        query_block = query_slot[row_start:row_end]
        grad_block = grad_slot[row_start:row_end]
        scores = masked_scores(query_block, key_slot, segments, row_start, row_end, score_scale)
        probability = jnp.exp(scores - logsum[:, row_start:row_end, None])
        prob_grad = jnp.einsum(
            "qhd,khd->hqk", grad_block, value_slot[:row_end], preferred_element_type=jnp.float32
        )
        inner_sum = jnp.sum(probability * prob_grad, axis=-1, keepdims=True)
        score_grad = (probability * (prob_grad - inner_sum)).astype(jnp.bfloat16)
        query_parts.append(
            jnp.einsum(
                "hqk,khd->qhd", score_grad, key_slot[:row_end], preferred_element_type=jnp.float32
            )
            * score_scale
        )
        key_grad = key_grad.at[:row_end].add(
            jnp.einsum("hqk,qhd->khd", score_grad, query_block, preferred_element_type=jnp.float32)
            * score_scale
        )
        value_gradient = value_gradient.at[:row_end].add(
            jnp.einsum(
                "hqk,qhd->khd",
                probability.astype(jnp.bfloat16),
                grad_block,
                preferred_element_type=jnp.float32,
            )
        )
    query_gradient = jnp.concatenate(query_parts, 0)
    return (
        query_gradient.astype(jnp.bfloat16),
        key_grad.astype(jnp.bfloat16),
        value_gradient.astype(jnp.bfloat16),
    )


def shards(
    block_input_rows,
    document_starts,
    counted_mask,
    output_gradient,
    first_norm_gain,
    first_norm_bias,
    query_key_value_weight,
    query_down_weight,
    query_up_weight,
    value_down_weight,
    value_up_weight,
    attention_out_weight,
    second_norm_gain,
    second_norm_bias,
    feed_input_weight,
    feed_input_bias,
    feed_output_weight,
):
    slot_count, local_len, row_width = block_input_rows.shape
    groups = lax.axis_size("head")
    full_len = local_len * groups
    head_size = row_width // H
    heads_here = H // groups
    row_count = slot_count * local_len
    block_rows = min(512, full_len)
    score_scale = head_size ** (-0.5)
    gain_one = first_norm_gain.astype(jnp.float32)
    shift_one = first_norm_bias.astype(jnp.float32)
    gain_two = second_norm_gain.astype(jnp.float32)
    shift_two = second_norm_bias.astype(jnp.float32)
    fc_bias = feed_input_bias.astype(jnp.float32)
    local_shape = (slot_count, local_len, row_width)
    split_shape = (slot_count, full_len, heads_here, head_size)
    merged_shape = (slot_count, full_len, heads_here * head_size)
    flat_in = block_input_rows.reshape(row_count, row_width).astype(jnp.float32)
    normed_rows = norm_rows(flat_in, gain_one, shift_one).astype(jnp.bfloat16)
    query_low_rank = plain_product(normed_rows, query_down_weight).astype(jnp.bfloat16)
    value_low_rank = plain_product(normed_rows, value_down_weight).astype(jnp.bfloat16)
    projected_rows = plain_product(normed_rows, query_key_value_weight)
    query_rows = (
        projected_rows[:, :row_width]
        + ADAPTER_SCALE * plain_product(query_low_rank, query_up_weight)
    ).astype(jnp.bfloat16)
    key_rows = projected_rows[:, row_width : 2 * row_width].astype(jnp.bfloat16)
    value_matrix = (
        projected_rows[:, 2 * row_width :]
        + ADAPTER_SCALE * plain_product(value_low_rank, value_up_weight)
    ).astype(jnp.bfloat16)
    head_query, head_key, head_value = (
        lax.all_to_all(
            query_rows.reshape(local_shape), "head", split_axis=2, concat_axis=1, tiled=True
        ),
        lax.all_to_all(
            key_rows.reshape(local_shape), "head", split_axis=2, concat_axis=1, tiled=True
        ),
        lax.all_to_all(
            value_matrix.reshape(local_shape), "head", split_axis=2, concat_axis=1, tiled=True
        ),
    )
    head_query = head_query.reshape(split_shape)
    head_key = head_key.reshape(split_shape)
    head_value = head_value.reshape(split_shape)

    def slot_fn(packed):
        return attend_slot(packed[0], packed[1], packed[2], packed[3], block_rows, score_scale)

    context_heads, logsum = lax.map(slot_fn, (head_query, head_key, head_value, document_starts))
    context_local = lax.all_to_all(
        as_sent(context_heads.reshape(merged_shape)),
        "head",
        split_axis=1,
        concat_axis=2,
        tiled=True,
    )
    context_flat = context_local.reshape(row_count, row_width)
    branch = plain_product(context_flat, attention_out_weight)
    hidden_state = flat_in + branch
    normed_two = norm_rows(hidden_state, gain_two, shift_two).astype(jnp.bfloat16)
    before = plain_product(normed_two, feed_input_weight) + fc_bias
    activated = gelu_tanh(before).astype(jnp.bfloat16)
    feed_out = plain_product(activated, feed_output_weight)
    result = hidden_state + feed_out
    output = result.astype(jnp.bfloat16).reshape(block_input_rows.shape)
    valid_rows = counted_mask.reshape(row_count).astype(jnp.float32)[:, None]
    square_sums = jnp.stack(
        [
            jnp.sum(valid_rows * result * result),
            jnp.sum(valid_rows * (branch * branch + feed_out * feed_out)),
            jnp.sum(valid_rows),
        ]
    )
    grad_flat = output_gradient.reshape(row_count, row_width)
    act_grad = last_product(grad_flat, feed_output_weight)
    gelu_pull = jax.vjp(gelu_tanh, before)[1]
    before_grad = gelu_pull(act_grad)[0].astype(jnp.bfloat16)
    normed_two_grad = last_product(before_grad, feed_input_weight)
    hidden_grad = grad_flat.astype(jnp.float32) + norm_back(
        hidden_state, gain_two, shift_two, normed_two_grad
    )
    branch_grad = hidden_grad.astype(jnp.bfloat16)
    context_grad = last_product(branch_grad, attention_out_weight).astype(jnp.bfloat16)
    grad_heads = lax.all_to_all(
        context_grad.reshape(local_shape), "head", split_axis=2, concat_axis=1, tiled=True
    ).reshape(split_shape)

    def back_fn(packed):
        return attend_back(
            packed[0],
            packed[1],
            packed[2],
            packed[3],
            packed[4],
            packed[5],
            block_rows,
            score_scale,
        )

    query_gradient, key_grad, value_gradient = lax.map(
        back_fn, (head_query, head_key, head_value, grad_heads, logsum, document_starts)
    )
    query_gradient, key_grad, value_gradient = (
        lax.all_to_all(
            as_sent(query_gradient.reshape(merged_shape)),
            "head",
            split_axis=1,
            concat_axis=2,
            tiled=True,
        ),
        lax.all_to_all(
            as_sent(key_grad.reshape(merged_shape)), "head", split_axis=1, concat_axis=2, tiled=True
        ),
        lax.all_to_all(
            as_sent(value_gradient.reshape(merged_shape)),
            "head",
            split_axis=1,
            concat_axis=2,
            tiled=True,
        ),
    )
    query_gradient = query_gradient.reshape(row_count, row_width)
    key_grad = key_grad.reshape(row_count, row_width)
    value_gradient = value_gradient.reshape(row_count, row_width)
    query_low_gradient = (ADAPTER_SCALE * last_product(query_gradient, query_up_weight)).astype(
        jnp.bfloat16
    )
    value_low_gradient = (ADAPTER_SCALE * last_product(value_gradient, value_up_weight)).astype(
        jnp.bfloat16
    )
    joined_grads = jnp.concatenate([query_gradient, key_grad, value_gradient], axis=1)
    normed_grad = (
        last_product(joined_grads, query_key_value_weight)
        + last_product(query_low_gradient, query_down_weight)
        + last_product(value_low_gradient, value_down_weight)
    )
    input_grad = hidden_grad + norm_back(flat_in, gain_one, shift_one, normed_grad)
    down_query = first_product(normed_rows, query_low_gradient)
    lifted_query = ADAPTER_SCALE * first_product(query_low_rank, query_gradient)
    down_value = first_product(normed_rows, value_low_gradient)
    lifted_value = ADAPTER_SCALE * first_product(value_low_rank, value_gradient)
    totals = lax.psum(
        (down_query, lifted_query, down_value, lifted_value, square_sums), ("dp", "head")
    )
    token_count = jnp.maximum(totals[4][2], 1.0)
    rms_values = jnp.stack(
        [
            jnp.sqrt(totals[4][0] / (token_count * row_width)),
            jnp.sqrt(totals[4][1] / (2.0 * token_count * row_width)),
        ]
    )
    return (
        output,
        input_grad.astype(jnp.bfloat16).reshape(block_input_rows.shape),
        totals[0],
        totals[1],
        totals[2],
        totals[3],
        rms_values,
    )


LOG2E = 1.4426950408889634
LN2 = 0.6931471805599453
TILE = 256
GROUP = 256
bf16 = jnp.bfloat16
f32 = jnp.float32
NT = (((1,), (1,)), ((), ()))
NN = (((1,), (0,)), ((), ()))
TN = (((0,), (0,)), ((), ()))
MESH = pl.DeviceIdType.MESH
MIB = 2**20


def dg(left, right, dims):
    return lax.dot_general(left, right, dims, preferred_element_type=f32)


def resident(shape):
    zeros = (0,) * len(shape)
    return pl.BlockSpec(shape, lambda *_: zeros, pipeline_mode=pl.Buffered(1))


def params(mib):
    return pltpu.CompilerParams(
        vmem_limit_bytes=mib * MIB, dimension_semantics=("arbitrary",)
    )


def norm_stats(rows):
    center = rows - jnp.mean(rows, axis=-1, keepdims=True)
    rs = lax.rsqrt(jnp.mean(center * center, axis=-1, keepdims=True) + EPSILON)
    return center * rs, rs


def norm_grad(unit, rs, gain, incoming):
    t = incoming * gain
    return (
        t - jnp.mean(t, axis=-1, keepdims=True) - unit * jnp.mean(t * unit, axis=-1, keepdims=True)
    ) * rs


def head_masks(x, heads, size):
    lane = lax.broadcasted_iota(jnp.int32, x.shape, 1)
    return [
        jnp.where((lane >= size * h) & (lane < size * (h + 1)), x, jnp.zeros_like(x))
        for h in range(heads)
    ]


def merge_heads(stacked, heads, size):
    rows = stacked.shape[0] // heads
    out = stacked[:rows]
    lane = lax.broadcasted_iota(jnp.int32, out.shape, 1)
    for h in range(1, heads):
        out = jnp.where(lane >= size * h, stacked[h * rows : (h + 1) * rows], out)
    return out


def column(line):
    return jnp.broadcast_to(line, (128, line.shape[1])).T


def entry_signal(peers):
    barrier = pltpu.get_barrier_semaphore()
    for peer in peers:
        pl.semaphore_signal(barrier, inc=1, device_id=peer, device_id_type=MESH)


def entry_wait(count):
    pl.semaphore_wait(pltpu.get_barrier_semaphore(), count)


def remote(src, dst, send_sem, recv_sem, peer):
    return pltpu.make_async_remote_copy(
        src_ref=src, dst_ref=dst, send_sem=send_sem, recv_sem=recv_sem, device_id=peer, device_id_type=MESH
    )


ANY = pl.BlockSpec(memory_space=pl.ANY)
VMEM = pl.BlockSpec(memory_space=pltpu.VMEM)


def line(ref):
    return ref[...].astype(f32).reshape(1, -1)


def rows_at(base, offset, count):
    return pl.ds(pl.multiple_of(base + offset, TILE), count)


def lanes_of(columns, width):
    size = width // len(columns)
    shape = (columns[0].shape[0], width)
    lane = lax.broadcasted_iota(jnp.int32, shape, 1)
    out = jnp.broadcast_to(columns[0], shape)
    for h in range(1, len(columns)):
        out = jnp.where(lane >= size * h, columns[h], out)
    return out


def pipelined(units, stages):
    for t in range(len(units) + len(stages) - 1):
        for b, stage in enumerate(stages):
            if 0 <= t - b < len(units):
                stage(t - b, units[t - b])


def open_kernel(
    x_ref, dy_ref, w_ref, mask_ref, start_ref, gain_ref, shift_ref, downq_ref, downv_ref, upq_ref, upv_ref,
    xs_ref, dys_ref, masks_ref, normed_ref, qkv_ref, ctx_ref, pd_ref, pc_ref, cd_ref, cc_ref,
    x_sc, y_sc, w_sc, mask_sc, normed_sc, qkv_sc, s_sc, diag_sc, cross_sc, first_sc, near_sc, state, part,
    x_send, x_recv, y_send, y_recv, m_send, m_recv, local_sem,
    *, size, strip,
):
    slots, tile, width = x_ref.shape
    length = slots * tile
    half = length // 2
    groups = width // GROUP
    heads = GROUP // size
    step = pl.program_id(0)
    middle = groups + 1
    group, me = lax.axis_index("dp"), lax.axis_index("head")
    mine = lax.rem(me, 2)
    near = me - mine
    far = slots // 2 - near
    beside = near + 1 - mine
    across = (far + mine, far + 1 - mine)
    peers = [(group, p) for p in (beside,) + across]

    def x_copy(k):
        return remote(x_ref.at[peers[k][1]], x_sc.at[me], x_send.at[k], x_recv.at[k], peers[k])

    def y_copy(k):
        landing = y_sc.at[mine] if k == 0 else dys_ref.at[me]
        return remote(dy_ref.at[peers[k][1]], landing, y_send.at[k], y_recv.at[k], peers[k])

    def m_copy(k):
        return remote(mask_sc.at[peers[k][1]], masks_ref.at[me], m_send.at[k], m_recv.at[k], peers[k])

    def own_x():
        return pltpu.make_async_copy(x_ref.at[me], x_sc.at[me], local_sem.at[0])

    def own_y():
        return pltpu.make_async_copy(dy_ref.at[me], y_sc.at[mine], local_sem.at[1])

    def own_m():
        return pltpu.make_async_copy(mask_sc.at[me], masks_ref.at[me], local_sem.at[2])

    def weight():
        return pltpu.make_async_copy(w_ref, w_sc, local_sem.at[3])

    def save_x():
        return pltpu.make_async_copy(x_sc, xs_ref, local_sem.at[4])

    def save_y():
        return pltpu.make_async_copy(y_sc, dys_ref.at[pl.ds(near, 2)], local_sem.at[7])

    def save_normed():
        return pltpu.make_async_copy(normed_sc, normed_ref, local_sem.at[5])

    def save_qkv():
        return pltpu.make_async_copy(qkv_sc, qkv_ref, local_sem.at[6])

    @pl.when(step == 0)
    def _():
        entry_signal(peers)
        own_x().start()
        weight().start()
        own_y().start()
        for s in range(slots):
            mask_sc[s] = jnp.broadcast_to(mask_ref[s : s + 1, :].astype(f32), mask_sc.shape[1:])
        own_m().start()
        entry_wait(len(peers))
        for k in (1, 2, 0):
            x_copy(k).start()
        for k in range(3):
            m_copy(k).start()
        first_sc[...] = column(start_ref[pl.ds(me, 1), :])

        def bias(i, carry):
            here = pl.ds(pl.multiple_of(i * strip, strip), strip)
            base = half * lax.div(i * strip, half)
            keys = lax.broadcasted_iota(jnp.int32, (strip, half), 1) + base
            rows = lax.broadcasted_iota(jnp.int32, (strip, half), 0) + i * strip
            allowed = (keys >= first_sc[here, 0:1]) & (keys <= rows)
            diag_sc[here, :] = jnp.where(allowed, 0.0, NEGATIVE)
            return carry

        lax.fori_loop(0, length // strip, bias, 0)

        def cross_bias(i, carry):
            here = pl.ds(pl.multiple_of(i * strip, strip), strip)
            keys = lax.broadcasted_iota(jnp.int32, (strip, half), 1)
            rows = pl.ds(pl.multiple_of(half + i * strip, strip), strip)
            cross_sc[here, :] = jnp.where(keys >= first_sc[rows, 0:1], 0.0, NEGATIVE)
            return carry

        lax.fori_loop(0, half // strip, cross_bias, 0)
        y_copy(0).start()
        own_x().wait()
        x_copy(0).wait_recv()
        weight().wait()

    @pl.when(step == groups + 1)
    def _():
        own_y().wait()
        y_copy(0).wait_recv()
        save_y().start()
        x_copy(1).wait()
        x_copy(2).wait()
        y_copy(1).start()
        save_x().start()

    @pl.when(lax.rem(step, middle) == 0)
    def _():
        first = near + (far - near) * lax.div(step, middle)
        unit, _ = norm_stats(x_sc[pl.ds(first, 2)].reshape(half, width).astype(f32))
        normed = (unit * line(gain_ref) + line(shift_ref)).astype(bf16)
        here = pl.ds(pl.multiple_of(first * tile, tile), half)
        normed_sc[here, :] = normed
        low_q = dg(normed, downq_ref[...], NT).astype(bf16)
        low_v = dg(normed, downv_ref[...], NT).astype(bf16)
        scale = size**-0.5 * LOG2E
        wide = 512
        for at in range(0, 3 * width, wide):
            cols = slice(at, at + wide)
            piece = dg(normed, w_sc[:, cols], NN)
            if at < width:
                piece = (piece + ADAPTER_SCALE * dg(low_q, upq_ref[:, cols], NN)) * scale
            if at >= 2 * width:
                piece = piece + ADAPTER_SCALE * dg(low_v, upv_ref[:, at - 2 * width : at - 2 * width + wide], NN)
            qkv_sc[here, cols] = piece.astype(bf16)

    @pl.when(step == middle)
    def _():
        save_normed().start()
        save_qkv().start()

    def attention(g, units):
        def third(k):
            return qkv_sc.at[:, pl.ds(pl.multiple_of(k * width + g * GROUP, GROUP), GROUP)]

        q_ref, k_ref, v_ref = third(0), third(1), third(2)

        def scores(at, unit):
            i, n, q_base, k_base = unit[:4]
            masked = jnp.concatenate(head_masks(q_ref[rows_at(q_base, i * TILE, TILE), :], heads, size), 0)
            for j in range(0, n, TILE):
                s_sc[at % 2, :, j : j + TILE] = dg(masked, k_ref[rows_at(k_base, j, TILE), :], NT)

        def soft(at, unit):
            i, n, q_base, _, bias, probs, (_, keep_m, keep_l, keep_row) = unit
            tops, sums = [], []
            for r in range(0, TILE, strip):
                tops.append([])
                sums.append([])
                for h in range(heads):
                    here = h * TILE + r
                    s = s_sc[at % 2, here : here + strip, 0:n] + bias(i * TILE + r, n)
                    top = jnp.max(s, axis=1, keepdims=True)
                    e = jnp.exp2(s - top)
                    tops[-1].append(top)
                    sums[-1].append(jnp.sum(e, axis=1, keepdims=True))
                    probs[h, i * TILE + r : i * TILE + r + strip, 0:n] = e.astype(bf16)
                where = pl.ds(pl.multiple_of(keep_row + i * TILE + r, strip), strip)
                keep_m[where, :] = lanes_of(tops[-1], GROUP)
                keep_l[where, :] = lanes_of(sums[-1], GROUP)

        def mix(at, unit):
            i, n, _, k_base, _, probs, (keep_o, _, _, keep_row) = unit
            stacked = probs[:, i * TILE : (i + 1) * TILE, 0:n].reshape(heads * TILE, n)
            merged = merge_heads(dg(stacked, v_ref[rows_at(k_base, 0, n), :], NN), heads, size)
            keep_o[rows_at(keep_row, i * TILE, TILE), :] = merged

        pipelined(units, (scores, soft, mix))

    def diag_units(base, keep, keep_row):
        def bias(r, n):
            return diag_sc[pl.ds(pl.multiple_of(base + r, strip), strip), 0:n]

        kept = (*keep, keep_row)
        return [(i, (i + 1) * TILE, base, base, bias, pd_ref.at[0], kept) for i in range(half // TILE)]

    def cross_units():
        def bias(r, n):
            return cross_sc[r : r + strip, 0:n]

        return [
            (i, half, half, 0, bias, pc_ref, (part.at[0], part.at[1], part.at[2], 0)) for i in range(half // TILE)
        ]

    @pl.when((step > 0) & (step <= groups))
    def _():
        cols = pl.ds(pl.multiple_of((step - 1) * GROUP, GROUP), GROUP)
        attention(step - 1, diag_units(near * tile, [near_sc.at[a, :, cols] for a in range(3)], 0))

    @pl.when(step > middle)
    def _():
        g = step - middle - 1
        cols = pl.ds(pl.multiple_of(g * GROUP, GROUP), GROUP)
        near_rows = rows_at(near * tile, 0, half)
        for a in range(3):
            state[a, near_rows, :] = near_sc[a, :, cols]
        far_units = diag_units(far * tile, [state.at[a] for a in range(3)], far * tile)
        attention(g, far_units + cross_units())
        inverse = 1.0 / state[2, 0:half]
        cd_ref[0:half] = inverse
        ctx_ref[0:half] = (state[0, 0:half] * inverse).astype(bf16)
        for r in range(0, half, TILE):
            high = slice(half + r, half + r + TILE)
            here = slice(r, r + TILE)
            top = jnp.maximum(state[1, high], part[1, here])
            weight_d = jnp.exp2(state[1, high] - top)
            weight_c = jnp.exp2(part[1, here] - top)
            inverse = 1.0 / (weight_d * state[2, high] + weight_c * part[2, here])
            weight_d = weight_d * inverse
            weight_c = weight_c * inverse
            cd_ref[high] = weight_d
            cc_ref[here] = weight_c
            ctx_ref[high] = (state[0, high] * weight_d + part[0, here] * weight_c).astype(bf16)

    @pl.when(step == middle + groups)
    def _():
        x_copy(0).wait_send()
        y_copy(0).wait_send()
        y_copy(1).wait()
        for k in range(3):
            m_copy(k).wait()
        own_m().wait()
        save_x().wait()
        save_y().wait()
        save_normed().wait()
        save_qkv().wait()


def opening(x, dy, w, mask, start, gain, shift, downq, downv, upq, upv, size):
    slots, tile, width = x.shape
    length = slots * tile
    half = length // 2
    groups = width // GROUP
    per = GROUP // size
    dma = pltpu.SemaphoreType.DMA
    small = [mask, start, gain, shift, downq, downv, upq, upv]
    masks = (slots, 8, tile)

    middle = groups + 1

    def late(t):
        return jnp.maximum(t - middle - 1, 0)

    def diag_at(t):
        second = lax.div(t, middle + 1)
        return second, jnp.where(second == 1, t - middle - 1, jnp.clip(t - 1, 0, groups - 1)), 0, 0

    return pl.pallas_call(
        functools.partial(open_kernel, size=size, strip=32),
        grid=(middle + groups + 1,),
        in_specs=[ANY] * 3 + [resident(a.shape) for a in small],
        out_specs=[ANY] * 5 + [
            pl.BlockSpec((length, GROUP), lambda t: (0, late(t))),
            pl.BlockSpec((1, per, half, half), diag_at),
            pl.BlockSpec((per, half, half), lambda t: (late(t), 0, 0)),
            pl.BlockSpec((length, GROUP), lambda t: (0, late(t))),
            pl.BlockSpec((half, GROUP), lambda t: (0, late(t))),
        ],
        out_shape=[
            jax.ShapeDtypeStruct(x.shape, bf16),
            jax.ShapeDtypeStruct(x.shape, bf16),
            jax.ShapeDtypeStruct(masks, f32),
            jax.ShapeDtypeStruct((length, width), bf16),
            jax.ShapeDtypeStruct((length, 3 * width), bf16),
            jax.ShapeDtypeStruct((length, width), bf16),
            jax.ShapeDtypeStruct((2, per * groups, half, half), bf16),
            jax.ShapeDtypeStruct((per * groups, half, half), bf16),
            jax.ShapeDtypeStruct((length, width), f32),
            jax.ShapeDtypeStruct((half, width), f32),
        ],
        scratch_shapes=[
            pltpu.VMEM(x.shape, bf16),
            pltpu.VMEM((2, tile, width), bf16),
            pltpu.VMEM(w.shape, bf16),
            pltpu.VMEM(masks, f32),
            pltpu.VMEM((length, width), bf16),
            pltpu.VMEM((length, 3 * width), bf16),
            pltpu.VMEM((2, per * TILE, half), f32),
            pltpu.VMEM((length, half), f32),
            pltpu.VMEM((half, half), f32),
            pltpu.VMEM((length, 128), jnp.int32),
            pltpu.VMEM((3, half, width), f32),
            pltpu.VMEM((3, length, GROUP), f32),
            pltpu.VMEM((3, half, GROUP), f32),
            dma((3,)), dma((3,)), dma((3,)), dma((3,)), dma((3,)), dma((3,)), dma((8,)),
        ],
        compiler_params=pltpu.CompilerParams(
            collective_id=0, has_side_effects=True, vmem_limit_bytes=62 * MIB, dimension_semantics=("arbitrary",)
        ),
        name="opening",
    )(x, dy, w, *small)


def feed_kernel(
    x_hbm, y_hbm, dy_hbm, ctx_hbm, wo_hbm, wi_hbm, wf_hbm, mask_ref, gain_ref, shift_ref, bias_ref,
    out_hbm, hg_hbm, cg_hbm, sums_ref,
    x_sc, y_sc, ctx_sc, wo_ref, wi_ref, wf_ref, normed, feed_sc, grad_sc, v_sc, g_sc,
    out_sc, hg_sc, cg_sc, load_sem, chunk_sem, save_sem, y_send, y_recv,
    *, step,
):
    slots, tile, width = x_hbm.shape
    rows = slots // 2 * tile
    chunks = wi_ref.shape[1] // step
    group, me = lax.axis_index("dp"), lax.axis_index("head")
    mine = lax.rem(me, 2)
    near = me - mine
    far = slots // 2 - near
    across = (far + mine, far + 1 - mine)
    peer = (group, across[1])
    half = pl.program_id(0)
    first = half == 0

    def base(h):
        return near + (far - near) * h

    def slabs(ref, h):
        return ref.at[pl.ds(base(h), 2)]

    def load_x(h):
        return pltpu.make_async_copy(slabs(x_hbm, h), x_sc.at[h], load_sem.at[h, 0])

    def load_ctx(h):
        return pltpu.make_async_copy(slabs(ctx_hbm, h), ctx_sc.at[h], load_sem.at[h, 1])

    def load_y(h):
        if h == 0:
            return pltpu.make_async_copy(slabs(y_hbm, 0), y_sc.at[0], load_sem.at[0, 2])
        return pltpu.make_async_copy(y_hbm.at[across[0]], y_sc.at[1, mine], load_sem.at[1, 2])

    def take_y():
        return remote(dy_hbm.at[across[1]], y_sc.at[1, mine], y_send, y_recv, peer)

    def load_o():
        return pltpu.make_async_copy(wo_hbm, wo_ref, load_sem.at[0, 3])

    def cols_of(c):
        return pl.ds(c * step if isinstance(c, int) else pl.multiple_of(c * step, step), step)

    def load_i(c):
        return pltpu.make_async_copy(wi_hbm.at[:, cols_of(c)], wi_ref.at[:, cols_of(c)], chunk_sem.at[0, c])

    def load_f(c):
        return pltpu.make_async_copy(wf_hbm.at[cols_of(c), :], wf_ref.at[cols_of(c), :], chunk_sem.at[1, c])

    @pl.when(first)
    def _():
        entry_signal([peer])
        load_o().start()
        load_ctx(0).start()
        load_x(0).start()
        for c in range(chunks):
            load_i(c).start()
            load_f(c).start()
            if c == 1:
                load_y(0).start()
                load_y(1).start()
                load_ctx(1).start()
                load_x(1).start()
        sums_ref[...] = jnp.zeros_like(sums_ref)
        load_o().wait()
        load_ctx(0).wait()
        load_x(0).wait()

    gain = line(gain_ref)
    c0 = 0.7978845608028654
    c1 = c0 * 0.044715
    branch = dg(ctx_sc[half].reshape(rows, width), wo_ref[...], NN)
    whole = x_sc[half].reshape(rows, width).astype(f32) + branch
    unit, rs = norm_stats(whole)
    normed[...] = (unit * gain + line(shift_ref)).astype(bf16)

    def enter(c, slot):
        cols = cols_of(c)
        v_sc[slot] = dg(normed[...], wi_ref[:, cols], NN) + bias_ref[cols].astype(f32).reshape(1, step)
        g_sc[slot] = dg(y_sc[half].reshape(rows, width), wf_ref[cols, :], NT)

    def leave(c, slot):
        cols = cols_of(c)
        v = v_sc[slot]
        square = v * v
        side = 0.5 * jnp.tanh(v * (c0 + c1 * square)) + 0.5
        act = v * side
        slope = side + act * (1.0 - side) * (2.0 * c0 + 6.0 * c1 * square)
        feed_sc[...] += dg(act.astype(bf16), wf_ref[cols, :], NN)
        grad_sc[...] += dg((slope * g_sc[slot]).astype(bf16), wi_ref[:, cols], NT)

    def wait_weights(*which):
        @pl.when(first)
        def _():
            for c in which:
                load_i(c).wait()
                load_f(c).wait()

    @pl.when(first)
    def _():
        load_y(0).wait()
        load_i(0).wait()
        load_f(0).wait()

    @pl.when(half == 1)
    def _():
        take_y().wait()

    feed_sc[...] = jnp.zeros_like(feed_sc)
    grad_sc[...] = jnp.zeros_like(grad_sc)
    enter(0, 0)

    @pl.when(first)
    def _():
        entry_wait(1)
        take_y().start()

    def pair(i, carry):
        wait_weights(2 * i + 1, 2 * i + 2)
        enter(2 * i + 1, 1)
        leave(2 * i, 0)
        enter(2 * i + 2, 0)
        leave(2 * i + 1, 1)
        return carry

    lax.fori_loop(0, chunks // 2 - 1, pair, 0)
    wait_weights(chunks - 1)
    enter(chunks - 1, 1)
    leave(chunks - 2, 0)
    leave(chunks - 1, 1)
    feed = feed_sc[...]
    result = whole + feed
    out_sc[half] = result.astype(bf16).reshape(out_sc.shape[1:])
    valid = jnp.concatenate([column(mask_ref[base(half) + b, 0:1, :])[:, 0:1] for b in range(2)], 0)
    one = jnp.sum(valid * jnp.sum(result * result, axis=1, keepdims=True))
    two = jnp.sum(valid * jnp.sum(branch * branch + feed * feed, axis=1, keepdims=True))
    count = jnp.sum(valid)
    row = lax.broadcasted_iota(jnp.int32, sums_ref.shape, 0)
    col = lax.broadcasted_iota(jnp.int32, sums_ref.shape, 1)
    total = jnp.where(col == 0, one, jnp.where(col == 1, two, jnp.where(col == 2, count, 0.0)))
    sums_ref[...] += jnp.where(row == 0, total, 0.0)
    dy = y_sc[half].reshape(rows, width).astype(f32)
    low = (dy + norm_grad(unit, rs, gain, grad_sc[...])).astype(bf16)
    hg_sc[half] = low.reshape(hg_sc.shape[1:])
    cg_sc[half] = dg(low, wo_ref[...], NT).astype(bf16)

    def saves(h):
        flat = pl.ds(pl.multiple_of(base(h) * tile, tile), rows)
        return [
            pltpu.make_async_copy(out_sc.at[h], slabs(out_hbm, h), save_sem.at[h, 0]),
            pltpu.make_async_copy(hg_sc.at[h], slabs(hg_hbm, h), save_sem.at[h, 1]),
            pltpu.make_async_copy(cg_sc.at[h], cg_hbm.at[flat, :], save_sem.at[h, 2]),
        ]

    for copy in saves(half):
        copy.start()

    @pl.when(first)
    def _():
        load_y(1).wait()
        load_ctx(1).wait()
        load_x(1).wait()

    @pl.when(half == 1)
    def _():
        for copy in saves(0) + saves(1):
            copy.wait()


def feed(x, y, dy, context, mask, wo, gain, shift, wi, bias, wf):
    slots, tile, width = x.shape
    rows = slots // 2 * tile
    units = wi.shape[1]
    step = 512
    chunks = units // step
    pair = (2, 2, tile, width)
    dma = pltpu.SemaphoreType.DMA
    return pl.pallas_call(
        functools.partial(feed_kernel, step=step),
        grid=(2,),
        in_specs=[ANY] * 7 + [resident(a.shape) for a in (mask, gain, shift, bias)],
        out_specs=[ANY] * 3 + [pl.BlockSpec((8, width), lambda h: (0, 0))],
        out_shape=[jax.ShapeDtypeStruct(x.shape, bf16)] * 2 + [
            jax.ShapeDtypeStruct((2 * rows, width), bf16), jax.ShapeDtypeStruct((8, width), f32)
        ],
        scratch_shapes=[pltpu.VMEM(pair, bf16)] * 3 + [
            pltpu.VMEM(wo.shape, bf16), pltpu.VMEM(wi.shape, bf16), pltpu.VMEM(wf.shape, bf16),
            pltpu.VMEM((rows, width), bf16),
            pltpu.VMEM((rows, width), f32), pltpu.VMEM((rows, width), f32),
            pltpu.VMEM((2, rows, step), f32), pltpu.VMEM((2, rows, step), f32),
            pltpu.VMEM(pair, bf16), pltpu.VMEM(pair, bf16), pltpu.VMEM((2, rows, width), bf16),
            dma((2, 4)), dma((2, chunks)), dma((2, 3)), dma, dma,
        ],
        compiler_params=pltpu.CompilerParams(
            collective_id=2, has_side_effects=True, vmem_limit_bytes=62 * MIB, dimension_semantics=("arbitrary",)
        ),
        name="feed",
    )(x, y, dy, context.reshape(x.shape), wo, wi, wf, mask, gain, shift, bias)


def close_kernel(
    q_ref, k_ref, v_ref, g_ref, o_ref, cd_ref, cc_ref, pd_ref, pc_ref,
    res_hbm, x_hbm, hg_hbm, normed_hbm, w_hbm,
    gain_ref, downq_ref, downv_ref, upq_ref, upv_ref, sums_ref,
    result_ref, out_ref, total_ref,
    dp_sc, ds_sc, inner_sc, do_sc, loc, near_sc, grads, x_sc, hg_sc, normed_sc, w_sc, res_sc,
    sums, parts, chunk, heard, total_sc,
    r_send, r_recv, send, recv, local_sem, part_send, part_recv, pair_send, pair_recv, mean_send, mean_recv,
    *, size, strip, sizes,
):
    slots, tile, width = x_sc.shape
    length = slots * tile
    half = length // 2
    groups = width // GROUP
    heads = GROUP // size
    rank = downq_ref.shape[0]
    step = pl.program_id(0)
    last = 2 * groups + 5
    group, me = lax.axis_index("dp"), lax.axis_index("head")
    mine = lax.rem(me, 2)
    near = me - mine
    far = slots // 2 - near
    beside = near + 1 - mine
    peers = [(group, p) for p in (far + mine, far + 1 - mine, beside)]
    rest = [(lax.rem(group + k, sizes[0]), me) for k in range(1, sizes[0])]
    lanes = width // sizes[0]

    def own_result():
        return pltpu.make_async_copy(res_hbm.at[me], result_ref.at[me], local_sem.at[0])

    def result_copy(k):
        return remote(res_hbm.at[peers[k][1]], result_ref.at[me], r_send.at[k], r_recv.at[k], peers[k])

    def loads():
        return [
            pltpu.make_async_copy(src, dst, local_sem.at[1 + a])
            for a, (src, dst) in enumerate([(x_hbm, x_sc), (hg_hbm, hg_sc), (normed_hbm, normed_sc), (w_hbm, w_sc)])
        ]

    @pl.when(step == 0)
    def _():
        entry_signal(peers + rest)
        own_result().start()
        for copy in loads():
            copy.start()
        sums[...] = jnp.zeros_like(sums)
        sums[4 * rank :, :] = sums_ref[...]

    @pl.when(step == 1)
    def _():
        entry_wait(len(peers) + len(rest))
        for k in range(3):
            result_copy(k).start()

    def attention(units):
        def stack(x):
            return jnp.concatenate(head_masks(x, heads, size), 0)

        def prob_grads(at, unit):
            i, n, q_base, k_base, _, which, row = unit[:7]
            grad = do_sc[which, rows_at(row, i * TILE, TILE), :]
            masked = stack(grad)
            for j in range(0, n, TILE):
                dp_sc[at % 2, :, j : j + TILE] = dg(masked, v_ref[rows_at(k_base, j, TILE), :], NT)
            both = (grad.astype(f32) * o_ref[rows_at(q_base, i * TILE, TILE), :].astype(f32)).astype(bf16)
            inner_sc[at % 2] = dg(stack(both), jnp.ones((GROUP, 128), bf16), NN)

        def score_grads(at, unit):
            i, n, _, _, probs = unit[:5]
            for h in range(heads):
                for r in range(0, TILE, strip):
                    here = h * TILE + r
                    inner = jnp.concatenate([inner_sc[at % 2, here : here + strip, :]] * (n // 128), 1)
                    prob = probs[h, i * TILE + r : i * TILE + r + strip, 0:n].astype(f32)
                    ds = prob * (dp_sc[at % 2, here : here + strip, 0:n] - inner)
                    ds_sc[at % 2, here : here + strip, 0:n] = ds.astype(bf16)

        def products(at, unit):
            i, n, q_base, k_base, probs, which, row, add = unit
            query = rows_at(q_base, i * TILE, TILE)
            ds = ds_sc[at % 2, :, 0:n]
            dq = merge_heads(dg(ds, k_ref[rows_at(k_base, 0, n), :], NN), heads, size)
            stacked = probs[:, i * TILE : (i + 1) * TILE, 0:n].reshape(heads * TILE, n)
            dv = dg(stacked, stack(do_sc[which, rows_at(row, i * TILE, TILE), :]), TN)
            dk = dg(ds, stack(q_ref[query, :]), TN)
            if add:
                loc[0, query, :] += dq
                keys = rows_at(k_base, 0, n)
                loc[1, keys, :] += dk
                loc[2, keys, :] += dv
            else:
                loc[0, query, :] = dq
                if i:
                    keys = rows_at(k_base, 0, i * TILE)
                    loc[1, keys, :] += dk[: i * TILE]
                    loc[2, keys, :] += dv[: i * TILE]
                loc[1, query, :] = dk[i * TILE :]
                loc[2, query, :] = dv[i * TILE :]

        pipelined(units, (prob_grads, score_grads, products))

    def diag_units(base):
        here = rows_at(base, 0, half)
        do_sc[0] = (g_ref[here, :].astype(f32) * cd_ref[here, :]).astype(bf16)
        return [(i, (i + 1) * TILE, base, base, pd_ref.at[0], 0, 0, False) for i in range(half // TILE)]

    def cross_units():
        do_sc[1] = (g_ref[half:, :].astype(f32) * cc_ref[...]).astype(bf16)
        return [(i, half, half, 0, pc_ref, 1, 0, True) for i in range(half // TILE)]

    scales = (size**-0.5, LN2, 1.0)

    @pl.when(step < groups)
    def _():
        cols = pl.ds(pl.multiple_of(step * GROUP, GROUP), GROUP)
        far_rows = rows_at(far * tile, 0, half)
        near_rows = rows_at(near * tile, 0, half)
        for a in range(3):
            loc[a, near_rows, :] = jnp.zeros((half, GROUP), f32)
        attention(diag_units(far * tile) + cross_units())
        for a in range(3):
            grads[a, far_rows, cols] = (loc[a, far_rows, :] * scales[a]).astype(bf16)
            near_sc[a, :, cols] = loc[a, near_rows, :]

    @pl.when((step > groups + 2) & (step < 2 * groups + 3))
    def _():
        cols = pl.ds(pl.multiple_of((step - groups - 3) * GROUP, GROUP), GROUP)
        near_rows = rows_at(near * tile, 0, half)
        attention(diag_units(near * tile))
        for a in range(3):
            both = loc[a, near_rows, :] + near_sc[a, :, cols]
            grads[a, near_rows, cols] = (both * scales[a]).astype(bf16)

    held = tile // 4

    def give(k):
        return remote(res_sc.at[peers[k][1]], out_ref.at[me], send.at[k], recv.at[k], peers[k])

    def give_part(p):
        rows = pl.ds(0, tile - held) if p == 0 else pl.ds(tile - held, held)
        return remote(
            res_sc.at[peers[1][1], rows], out_ref.at[me, rows], send.at[1 + 2 * p], recv.at[1 + 2 * p], peers[1]
        )

    def keep():
        return pltpu.make_async_copy(res_sc.at[me], out_ref.at[me], local_sem.at[5])

    def block_of(d):
        return pl.ds(pl.multiple_of(d * lanes, lanes), lanes)

    def scatter(k):
        return remote(sums.at[:, block_of(rest[k][0])], parts.at[k], part_send.at[k], part_recv.at[k], rest[k])

    def pair(at, peer):
        return remote(chunk.at[at], heard.at[at], pair_send.at[at], pair_recv.at[at], peer)

    def gather(k):
        return remote(chunk.at[2], total_sc.at[:, block_of(group)], mean_send.at[k], mean_recv.at[k], rest[k])

    @pl.when(step == groups)
    def _():
        for copy in loads():
            copy.wait()

    @pl.when((step == groups + 2) | (step == 2 * groups + 3))
    def _():
        first = far + (near - far) * lax.div(step, 2 * groups + 3)
        here = pl.ds(pl.multiple_of(first * tile, tile), half)
        dq, dv = grads[0, here, :], grads[2, here, :]
        normed = normed_sc[pl.ds(first, 2)].reshape(half, width)
        low_gq = (ADAPTER_SCALE * dg(dq, upq_ref[...], NT)).astype(bf16)
        low_gv = (ADAPTER_SCALE * dg(dv, upv_ref[...], NT)).astype(bf16)
        low_q = dg(normed, downq_ref[...], NT).astype(bf16)
        low_v = dg(normed, downv_ref[...], NT).astype(bf16)
        sums[0:rank] += dg(low_gq, normed, TN)
        sums[rank : 2 * rank] += dg(low_gv, normed, TN)
        sums[2 * rank : 3 * rank] += ADAPTER_SCALE * dg(low_q, dq, TN)
        sums[3 * rank : 4 * rank] += ADAPTER_SCALE * dg(low_v, dv, TN)

    @pl.when(step == 2 * groups + 3)
    def _():
        for k in range(len(rest)):
            scatter(k).start()

    @pl.when(step == last)
    def _():
        pair(0, peers[2]).wait()
        chunk[1] = chunk[0] + heard[0]
        pair(1, peers[0]).start()
        give_part(1).start()

    early = (step == groups) | (step == groups + 1)

    @pl.when(early | (step > 2 * groups + 3))
    def _():
        late = lax.div(step, 2 * groups + 4)
        second = lax.rem(step, 2)
        slab = late * (beside + second * (me - beside)) + (1 - late) * (
            peers[0][1] + second * (peers[1][1] - peers[0][1])
        )
        here = pl.ds(pl.multiple_of(slab * tile, tile), tile)
        dq, dk, dv = grads[0, here, :], grads[1, here, :], grads[2, here, :]
        low_gq = (ADAPTER_SCALE * dg(dq, upq_ref[...], NT)).astype(bf16)
        low_gv = (ADAPTER_SCALE * dg(dv, upv_ref[...], NT)).astype(bf16)
        normed_grad = (
            dg(dq, w_sc[:, :width], NT)
            + dg(dk, w_sc[:, width : 2 * width], NT)
            + dg(dv, w_sc[:, 2 * width :], NT)
            + dg(low_gq, downq_ref[...], NN)
            + dg(low_gv, downv_ref[...], NN)
        )
        unit, rs = norm_stats(x_sc[slab].astype(f32))
        grad = hg_sc[slab].astype(f32) + norm_grad(unit, rs, line(gain_ref), normed_grad)
        res_sc[slab] = grad.astype(bf16)

    @pl.when(step == groups)
    def _():
        give(0).start()

    @pl.when(step == groups + 1)
    def _():
        give_part(0).start()

    @pl.when(step == 2 * groups + 4)
    def _():
        give(2).start()
        for k in range(len(rest)):
            scatter(k).wait()
        whole = sums[:, block_of(group)]
        for k in range(len(rest)):
            whole = whole + parts[k]
        chunk[0] = whole
        pair(0, peers[2]).start()

    @pl.when(step == last)
    def _():
        keep().start()
        pair(1, peers[0]).wait()
        whole = chunk[1] + heard[1]
        chunk[2] = whole
        total_sc[:, block_of(group)] = whole
        for k in range(len(rest)):
            gather(k).start()
        for k in range(len(rest)):
            gather(k).wait()
        total_ref[...] = total_sc[...]
        own_result().wait()
        keep().wait()
        for k in range(3):
            result_copy(k).wait()
        give(0).wait()
        give(2).wait()
        give_part(0).wait()
        give_part(1).wait()


def closing(
    qkv, grad, context, cd, cc, pd, pc, result, x, hidden_grad, normed, w,
    gain, downq, downv, upq, upv, sums, size, sizes,
):
    slots, tile, width = x.shape
    length = slots * tile
    half = length // 2
    groups = width // GROUP
    per = GROUP // size
    rank = downq.shape[0]
    total = (4 * rank + 8, width)
    rest = sizes[0] - 1
    lanes = width // sizes[0]
    dma = pltpu.SemaphoreType.DMA
    small = [gain, downq, downv, upq, upv, sums]

    def fold(a):
        return a.reshape(x.shape)

    def of(t):
        second = lax.div(t, groups + 3)
        return jnp.minimum(t - second * (groups + 3), groups - 1)

    def early(t):
        return jnp.minimum(t, groups - 1)

    def columns(third):
        return pl.BlockSpec((length, GROUP), lambda t: (0, of(t) + third * groups))

    return pl.pallas_call(
        functools.partial(close_kernel, size=size, strip=32, sizes=sizes),
        grid=(2 * groups + 6,),
        in_specs=[
            columns(0), columns(1), columns(2), columns(0), columns(0), columns(0),
            pl.BlockSpec((half, GROUP), lambda t: (0, early(t))),
            pl.BlockSpec((1, per, half, half), lambda t: (1 - jnp.minimum(lax.div(t, groups + 3), 1), of(t), 0, 0)),
            pl.BlockSpec((per, half, half), lambda t: (early(t), 0, 0)),
        ]
        + [ANY] * 5
        + [resident(a.shape) for a in small],
        out_specs=[ANY, ANY, pl.BlockSpec(total, lambda t: (0, 0))],
        out_shape=[
            jax.ShapeDtypeStruct(x.shape, bf16),
            jax.ShapeDtypeStruct(x.shape, bf16),
            jax.ShapeDtypeStruct(total, f32),
        ],
        scratch_shapes=[
            pltpu.VMEM((2, per * TILE, half), f32),
            pltpu.VMEM((2, per * TILE, half), bf16),
            pltpu.VMEM((2, per * TILE, 128), f32),
            pltpu.VMEM((2, half, GROUP), bf16),
            pltpu.VMEM((3, length, GROUP), f32),
            pltpu.VMEM((3, half, width), f32),
            pltpu.VMEM((3, length, width), bf16),
            pltpu.VMEM(x.shape, bf16),
            pltpu.VMEM(x.shape, bf16),
            pltpu.VMEM(x.shape, bf16),
            pltpu.VMEM(w.shape, bf16),
            pltpu.VMEM(x.shape, bf16),
            pltpu.VMEM(total, f32),
            pltpu.VMEM((rest, total[0], lanes), f32),
            pltpu.VMEM((3, total[0], lanes), f32),
            pltpu.VMEM((2, total[0], lanes), f32),
            pltpu.VMEM(total, f32),
            dma((3,)), dma((3,)), dma((4,)), dma((4,)), dma((6,)),
            dma((rest,)), dma((rest,)), dma((2,)), dma((2,)), dma((rest,)), dma((rest,)),
        ],
        compiler_params=pltpu.CompilerParams(
            collective_id=1, has_side_effects=True, vmem_limit_bytes=62 * MIB, dimension_semantics=("arbitrary",)
        ),
        name="closing",
    )(qkv, qkv, qkv, grad, context, cd, cc, pd, pc, result, x, fold(hidden_grad), fold(normed), w, *small)


def finish_kernel(total_ref, a_hbm, b_hbm, aq_ref, bq_ref, av_ref, bv_ref, rms_ref, a_out, b_out, a_sc, b_sc, sem):
    rank, width = aq_ref.shape
    loads, saves = [], []
    for k, (src, kept, dst) in enumerate(((a_hbm, a_sc, a_out), (b_hbm, b_sc, b_out))):
        for s in range(src.shape[0]):
            loads.append(pltpu.make_async_copy(src.at[s], kept.at[s], sem.at[k, s, 0]))
            saves.append(pltpu.make_async_copy(kept.at[s], dst.at[s], sem.at[k, s, 1]))
    for load in loads:
        load.start()
    aq_ref[...] = total_ref[0:rank]
    av_ref[...] = total_ref[rank : 2 * rank]
    bq_ref[...] = total_ref[2 * rank : 3 * rank]
    bv_ref[...] = total_ref[3 * rank : 4 * rank]
    line = total_ref[4 * rank : 4 * rank + 1, 0:128]
    lane = lax.broadcasted_iota(jnp.int32, line.shape, 1)
    count = jnp.maximum(jnp.sum(jnp.where(lane == 2, line, 0.0)), 1.0)
    values = jnp.sqrt(line / (jnp.where(lane == 0, 1.0, 2.0) * count * width))
    for k in range(2):
        rms_ref[k] = jnp.sum(jnp.where(lane == k, values, 0.0))
    for load, save in zip(loads, saves):
        load.wait()
        save.start()
    for save in saves:
        save.wait()


def finish(total, a, b, rank):
    width = total.shape[1]
    small = jax.ShapeDtypeStruct((rank, width), f32)
    return pl.pallas_call(
        finish_kernel,
        in_specs=[VMEM, ANY, ANY],
        out_specs=[VMEM] * 4 + [pl.BlockSpec(memory_space=pltpu.SMEM), ANY, ANY],
        out_shape=[small] * 4 + [
            jax.ShapeDtypeStruct((2,), f32),
            jax.ShapeDtypeStruct(a.shape, a.dtype),
            jax.ShapeDtypeStruct(b.shape, b.dtype),
        ],
        scratch_shapes=[
            pltpu.VMEM(a.shape, a.dtype), pltpu.VMEM(b.shape, b.dtype), pltpu.SemaphoreType.DMA((2, a.shape[0], 2))
        ],
        name="finish",
    )(total, a, b)


def whole_slots(
    block_input_rows,
    document_starts,
    counted_mask,
    output_gradient,
    first_norm_gain,
    first_norm_bias,
    query_key_value_weight,
    query_down_weight,
    query_up_weight,
    value_down_weight,
    value_up_weight,
    attention_out_weight,
    second_norm_gain,
    second_norm_bias,
    feed_input_weight,
    feed_input_bias,
    feed_output_weight,
):
    sizes = (lax.axis_size("dp"), lax.axis_size("head"))
    size = block_input_rows.shape[-1] // H
    rank = query_down_weight.shape[1]
    downq = query_down_weight.T
    downv = value_down_weight.T
    x, dy, mask, normed, qkv, context, pd, pc, cd, cc = opening(
        block_input_rows, output_gradient, query_key_value_weight, counted_mask, document_starts,
        first_norm_gain, first_norm_bias, downq, downv, query_up_weight, value_up_weight, size,
    )
    out, hidden_grad, context_grad, sums = feed(
        x, dy, output_gradient, context, mask, attention_out_weight, second_norm_gain, second_norm_bias,
        feed_input_weight, feed_input_bias, feed_output_weight,
    )
    output, input_grad, total = closing(
        qkv, context_grad, context, cd, cc, pd, pc, out, x, hidden_grad, normed, query_key_value_weight,
        first_norm_gain, downq, downv, query_up_weight, value_up_weight, sums, size, sizes,
    )
    grad_aq, grad_bq, grad_av, grad_bv, rms, output, input_grad = finish(total, output, input_grad, rank)
    return output, input_grad, grad_aq.T, grad_bq, grad_av.T, grad_bv, rms


def body(*args):
    same = args[0].shape[0] == lax.axis_size("head")
    return whole_slots(*args) if same else shards(*args)


def solution(mesh):
    return jax.shard_map(
        body,
        mesh=mesh,
        in_specs=(
            P("dp", "head", None),
            P("dp", None),
            P("dp", "head"),
            P("dp", "head", None),
            P(),
            P(),
            P(),
            P(),
            P(),
            P(),
            P(),
            P(),
            P(),
            P(),
            P(),
            P(),
            P(),
        ),
        out_specs=(P("dp", "head", None), P("dp", "head", None), P(), P(), P(), P(), P()),
        check_vma=False,
    )
```

```python
import functools

import jax
import jax.numpy as jnp
from jax import lax
from jax.experimental import pallas as pl
from jax.experimental.pallas import tpu as pltpu
from jax.sharding import PartitionSpec as P

H = 16


EPSILON = 1e-05
ADAPTER_SCALE = 8.0
NEGATIVE = -1e30


def as_sent(x):

    def short(part):
        return part.astype(jnp.bfloat16) if part.dtype == jnp.float32 else part

    return jax.tree.map(short, x)


def norm_rows(matrix, gain_vec, shift_vec):
    center = matrix - jnp.mean(matrix, axis=-1, keepdims=True)
    variance = jnp.mean(center * center, axis=-1, keepdims=True)
    return center * lax.rsqrt(variance + EPSILON) * gain_vec + shift_vec


def norm_back(matrix, gain_vec, shift_vec, incoming):
    pullback = jax.vjp(lambda element_item: norm_rows(element_item, gain_vec, shift_vec), matrix)[1]
    return pullback(incoming)[0]


def gelu_tanh(matrix):
    return jax.nn.gelu(matrix, approximate=True)


def plain_product(left, right):
    return jnp.dot(left, right, preferred_element_type=jnp.float32)


def last_product(left, right):
    return lax.dot_general(
        left, right, (((1,), (1,)), ((), ())), preferred_element_type=jnp.float32
    )


def first_product(left, right):
    return lax.dot_general(
        left, right, (((0,), (0,)), ((), ())), preferred_element_type=jnp.float32
    )


def masked_scores(query_block, key_slot, segments, row_start, row_end, score_scale):
    places = jnp.arange(row_end)
    allowed = (segments[row_start:row_end, None] == segments[None, :row_end]) & (
        places[None, :] <= places[row_start:row_end, None]
    )
    scores = (
        jnp.einsum(
            "qhd,khd->hqk", query_block, key_slot[:row_end], preferred_element_type=jnp.float32
        )
        * score_scale
    )
    return jnp.where(allowed[None], scores, NEGATIVE)


def attend_slot(query_slot, key_slot, value_slot, segments, block_rows, score_scale):
    length = query_slot.shape[0]
    outputs_list = []
    logsum_list = []
    for block_index in range(length // block_rows):
        row_start = block_index * block_rows
        row_end = row_start + block_rows
        scores = masked_scores(
            query_slot[row_start:row_end], key_slot, segments, row_start, row_end, score_scale
        )
        row_max = jnp.max(scores, axis=-1, keepdims=True)
        exponent = jnp.exp(scores - row_max)
        row_total = jnp.sum(exponent, axis=-1, keepdims=True)
        probability = (exponent / row_total).astype(jnp.bfloat16)
        context = jnp.einsum(
            "hqk,khd->qhd", probability, value_slot[:row_end], preferred_element_type=jnp.float32
        )
        outputs_list.append(context.astype(jnp.bfloat16))
        logsum_list.append((row_max + jnp.log(row_total))[..., 0])
    return (jnp.concatenate(outputs_list, 0), jnp.concatenate(logsum_list, 1))


def attend_back(
    query_slot, key_slot, value_slot, grad_slot, logsum, segments, block_rows, score_scale
):
    length = query_slot.shape[0]
    key_grad = jnp.zeros(key_slot.shape, jnp.float32)
    value_gradient = jnp.zeros(value_slot.shape, jnp.float32)
    query_parts = []
    for block_index in range(length // block_rows):
        row_start = block_index * block_rows
        row_end = row_start + block_rows
        query_block = query_slot[row_start:row_end]
        grad_block = grad_slot[row_start:row_end]
        scores = masked_scores(query_block, key_slot, segments, row_start, row_end, score_scale)
        probability = jnp.exp(scores - logsum[:, row_start:row_end, None])
        prob_grad = jnp.einsum(
            "qhd,khd->hqk", grad_block, value_slot[:row_end], preferred_element_type=jnp.float32
        )
        inner_sum = jnp.sum(probability * prob_grad, axis=-1, keepdims=True)
        score_grad = (probability * (prob_grad - inner_sum)).astype(jnp.bfloat16)
        query_parts.append(
            jnp.einsum(
                "hqk,khd->qhd", score_grad, key_slot[:row_end], preferred_element_type=jnp.float32
            )
            * score_scale
        )
        key_grad = key_grad.at[:row_end].add(
            jnp.einsum("hqk,qhd->khd", score_grad, query_block, preferred_element_type=jnp.float32)
            * score_scale
        )
        value_gradient = value_gradient.at[:row_end].add(
            jnp.einsum(
                "hqk,qhd->khd",
                probability.astype(jnp.bfloat16),
                grad_block,
                preferred_element_type=jnp.float32,
            )
        )
    query_gradient = jnp.concatenate(query_parts, 0)
    return (
        query_gradient.astype(jnp.bfloat16),
        key_grad.astype(jnp.bfloat16),
        value_gradient.astype(jnp.bfloat16),
    )


def shards(
    block_input_rows,
    document_starts,
    counted_mask,
    output_gradient,
    first_norm_gain,
    first_norm_bias,
    query_key_value_weight,
    query_down_weight,
    query_up_weight,
    value_down_weight,
    value_up_weight,
    attention_out_weight,
    second_norm_gain,
    second_norm_bias,
    feed_input_weight,
    feed_input_bias,
    feed_output_weight,
):
    slot_count, local_len, row_width = block_input_rows.shape
    groups = lax.axis_size("head")
    full_len = local_len * groups
    head_size = row_width // H
    heads_here = H // groups
    row_count = slot_count * local_len
    block_rows = min(512, full_len)
    score_scale = head_size ** (-0.5)
    gain_one = first_norm_gain.astype(jnp.float32)
    shift_one = first_norm_bias.astype(jnp.float32)
    gain_two = second_norm_gain.astype(jnp.float32)
    shift_two = second_norm_bias.astype(jnp.float32)
    fc_bias = feed_input_bias.astype(jnp.float32)
    local_shape = (slot_count, local_len, row_width)
    split_shape = (slot_count, full_len, heads_here, head_size)
    merged_shape = (slot_count, full_len, heads_here * head_size)
    flat_in = block_input_rows.reshape(row_count, row_width).astype(jnp.float32)
    normed_rows = norm_rows(flat_in, gain_one, shift_one).astype(jnp.bfloat16)
    query_low_rank = plain_product(normed_rows, query_down_weight).astype(jnp.bfloat16)
    value_low_rank = plain_product(normed_rows, value_down_weight).astype(jnp.bfloat16)
    projected_rows = plain_product(normed_rows, query_key_value_weight)
    query_rows = (
        projected_rows[:, :row_width]
        + ADAPTER_SCALE * plain_product(query_low_rank, query_up_weight)
    ).astype(jnp.bfloat16)
    key_rows = projected_rows[:, row_width : 2 * row_width].astype(jnp.bfloat16)
    value_matrix = (
        projected_rows[:, 2 * row_width :]
        + ADAPTER_SCALE * plain_product(value_low_rank, value_up_weight)
    ).astype(jnp.bfloat16)
    head_query, head_key, head_value = (
        lax.all_to_all(
            query_rows.reshape(local_shape), "head", split_axis=2, concat_axis=1, tiled=True
        ),
        lax.all_to_all(
            key_rows.reshape(local_shape), "head", split_axis=2, concat_axis=1, tiled=True
        ),
        lax.all_to_all(
            value_matrix.reshape(local_shape), "head", split_axis=2, concat_axis=1, tiled=True
        ),
    )
    head_query = head_query.reshape(split_shape)
    head_key = head_key.reshape(split_shape)
    head_value = head_value.reshape(split_shape)

    def slot_fn(packed):
        return attend_slot(packed[0], packed[1], packed[2], packed[3], block_rows, score_scale)

    context_heads, logsum = lax.map(slot_fn, (head_query, head_key, head_value, document_starts))
    context_local = lax.all_to_all(
        as_sent(context_heads.reshape(merged_shape)),
        "head",
        split_axis=1,
        concat_axis=2,
        tiled=True,
    )
    context_flat = context_local.reshape(row_count, row_width)
    branch = plain_product(context_flat, attention_out_weight)
    hidden_state = flat_in + branch
    normed_two = norm_rows(hidden_state, gain_two, shift_two).astype(jnp.bfloat16)
    before = plain_product(normed_two, feed_input_weight) + fc_bias
    activated = gelu_tanh(before).astype(jnp.bfloat16)
    feed_out = plain_product(activated, feed_output_weight)
    result = hidden_state + feed_out
    output = result.astype(jnp.bfloat16).reshape(block_input_rows.shape)
    valid_rows = counted_mask.reshape(row_count).astype(jnp.float32)[:, None]
    square_sums = jnp.stack(
        [
            jnp.sum(valid_rows * result * result),
            jnp.sum(valid_rows * (branch * branch + feed_out * feed_out)),
            jnp.sum(valid_rows),
        ]
    )
    grad_flat = output_gradient.reshape(row_count, row_width)
    act_grad = last_product(grad_flat, feed_output_weight)
    gelu_pull = jax.vjp(gelu_tanh, before)[1]
    before_grad = gelu_pull(act_grad)[0].astype(jnp.bfloat16)
    normed_two_grad = last_product(before_grad, feed_input_weight)
    hidden_grad = grad_flat.astype(jnp.float32) + norm_back(
        hidden_state, gain_two, shift_two, normed_two_grad
    )
    branch_grad = hidden_grad.astype(jnp.bfloat16)
    context_grad = last_product(branch_grad, attention_out_weight).astype(jnp.bfloat16)
    grad_heads = lax.all_to_all(
        context_grad.reshape(local_shape), "head", split_axis=2, concat_axis=1, tiled=True
    ).reshape(split_shape)

    def back_fn(packed):
        return attend_back(
            packed[0],
            packed[1],
            packed[2],
            packed[3],
            packed[4],
            packed[5],
            block_rows,
            score_scale,
        )

    query_gradient, key_grad, value_gradient = lax.map(
        back_fn, (head_query, head_key, head_value, grad_heads, logsum, document_starts)
    )
    query_gradient, key_grad, value_gradient = (
        lax.all_to_all(
            as_sent(query_gradient.reshape(merged_shape)),
            "head",
            split_axis=1,
            concat_axis=2,
            tiled=True,
        ),
        lax.all_to_all(
            as_sent(key_grad.reshape(merged_shape)), "head", split_axis=1, concat_axis=2, tiled=True
        ),
        lax.all_to_all(
            as_sent(value_gradient.reshape(merged_shape)),
            "head",
            split_axis=1,
            concat_axis=2,
            tiled=True,
        ),
    )
    query_gradient = query_gradient.reshape(row_count, row_width)
    key_grad = key_grad.reshape(row_count, row_width)
    value_gradient = value_gradient.reshape(row_count, row_width)
    query_low_gradient = (ADAPTER_SCALE * last_product(query_gradient, query_up_weight)).astype(
        jnp.bfloat16
    )
    value_low_gradient = (ADAPTER_SCALE * last_product(value_gradient, value_up_weight)).astype(
        jnp.bfloat16
    )
    joined_grads = jnp.concatenate([query_gradient, key_grad, value_gradient], axis=1)
    normed_grad = (
        last_product(joined_grads, query_key_value_weight)
        + last_product(query_low_gradient, query_down_weight)
        + last_product(value_low_gradient, value_down_weight)
    )
    input_grad = hidden_grad + norm_back(flat_in, gain_one, shift_one, normed_grad)
    down_query = first_product(normed_rows, query_low_gradient)
    lifted_query = ADAPTER_SCALE * first_product(query_low_rank, query_gradient)
    down_value = first_product(normed_rows, value_low_gradient)
    lifted_value = ADAPTER_SCALE * first_product(value_low_rank, value_gradient)
    totals = lax.psum(
        (down_query, lifted_query, down_value, lifted_value, square_sums), ("dp", "head")
    )
    token_count = jnp.maximum(totals[4][2], 1.0)
    rms_values = jnp.stack(
        [
            jnp.sqrt(totals[4][0] / (token_count * row_width)),
            jnp.sqrt(totals[4][1] / (2.0 * token_count * row_width)),
        ]
    )
    return (
        output,
        input_grad.astype(jnp.bfloat16).reshape(block_input_rows.shape),
        totals[0],
        totals[1],
        totals[2],
        totals[3],
        rms_values,
    )


LOG2E = 1.4426950408889634
LN2 = 0.6931471805599453
TILE = 256
GROUP = 256
bf16 = jnp.bfloat16
f32 = jnp.float32
NT = (((1,), (1,)), ((), ()))
NN = (((1,), (0,)), ((), ()))
TN = (((0,), (0,)), ((), ()))
MESH = pl.DeviceIdType.MESH
MIB = 2**20


def dg(left, right, dims):
    return lax.dot_general(left, right, dims, preferred_element_type=f32)


def resident(shape):
    zeros = (0,) * len(shape)
    return pl.BlockSpec(shape, lambda *_: zeros, pipeline_mode=pl.Buffered(1))


def params(mib):
    return pltpu.CompilerParams(
        vmem_limit_bytes=mib * MIB, dimension_semantics=("arbitrary",)
    )


def norm_stats(rows):
    center = rows - jnp.mean(rows, axis=-1, keepdims=True)
    rs = lax.rsqrt(jnp.mean(center * center, axis=-1, keepdims=True) + EPSILON)
    return center * rs, rs


def norm_grad(unit, rs, gain, incoming):
    t = incoming * gain
    return (
        t - jnp.mean(t, axis=-1, keepdims=True) - unit * jnp.mean(t * unit, axis=-1, keepdims=True)
    ) * rs


def head_masks(x, heads, size):
    lane = lax.broadcasted_iota(jnp.int32, x.shape, 1)
    return [
        jnp.where((lane >= size * h) & (lane < size * (h + 1)), x, jnp.zeros_like(x))
        for h in range(heads)
    ]


def merge_heads(stacked, heads, size):
    rows = stacked.shape[0] // heads
    out = stacked[:rows]
    lane = lax.broadcasted_iota(jnp.int32, out.shape, 1)
    for h in range(1, heads):
        out = jnp.where(lane >= size * h, stacked[h * rows : (h + 1) * rows], out)
    return out


def column(line):
    return jnp.broadcast_to(line, (128, line.shape[1])).T


def entry_signal(peers):
    barrier = pltpu.get_barrier_semaphore()
    for peer in peers:
        pl.semaphore_signal(barrier, inc=1, device_id=peer, device_id_type=MESH)


def entry_wait(count):
    pl.semaphore_wait(pltpu.get_barrier_semaphore(), count)


def remote(src, dst, send_sem, recv_sem, peer):
    return pltpu.make_async_remote_copy(
        src_ref=src, dst_ref=dst, send_sem=send_sem, recv_sem=recv_sem, device_id=peer, device_id_type=MESH
    )


ANY = pl.BlockSpec(memory_space=pl.ANY)
VMEM = pl.BlockSpec(memory_space=pltpu.VMEM)


def line(ref):
    return ref[...].astype(f32).reshape(1, -1)


def rows_at(base, offset, count):
    return pl.ds(pl.multiple_of(base + offset, TILE), count)


def lanes_of(columns, width):
    size = width // len(columns)
    shape = (columns[0].shape[0], width)
    lane = lax.broadcasted_iota(jnp.int32, shape, 1)
    out = jnp.broadcast_to(columns[0], shape)
    for h in range(1, len(columns)):
        out = jnp.where(lane >= size * h, columns[h], out)
    return out


def pipelined(units, stages):
    for t in range(len(units) + len(stages) - 1):
        for b, stage in enumerate(stages):
            if 0 <= t - b < len(units):
                stage(t - b, units[t - b])


def open_kernel(
    x_ref, dy_ref, w_ref, mask_ref, start_ref, gain_ref, shift_ref, downq_ref, downv_ref, upq_ref, upv_ref,
    xs_ref, dys_ref, masks_ref, normed_ref, low_ref, qkv_ref, ctx_ref, pd_ref, pc_ref, cd_ref, cc_ref,
    x_sc, y_sc, w_sc, mask_sc, normed_sc, low_sc, qkv_sc, s_sc, diag_sc, cross_sc, first_sc, near_sc, state, part,
    x_send, x_recv, y_send, y_recv, m_send, m_recv, local_sem,
    *, size, strip,
):
    slots, tile, width = x_ref.shape
    length = slots * tile
    half = length // 2
    groups = width // GROUP
    heads = GROUP // size
    step = pl.program_id(0)
    middle = groups + 1
    group, me = lax.axis_index("dp"), lax.axis_index("head")
    mine = lax.rem(me, 2)
    near = me - mine
    far = slots // 2 - near
    beside = near + 1 - mine
    across = (far + mine, far + 1 - mine)
    peers = [(group, p) for p in (beside,) + across]

    def x_copy(k):
        return remote(x_ref.at[peers[k][1]], x_sc.at[me], x_send.at[k], x_recv.at[k], peers[k])

    def y_copy(k):
        landing = y_sc.at[mine] if k == 0 else dys_ref.at[me]
        return remote(dy_ref.at[peers[k][1]], landing, y_send.at[k], y_recv.at[k], peers[k])

    def m_copy(k):
        return remote(mask_sc.at[peers[k][1]], masks_ref.at[me], m_send.at[k], m_recv.at[k], peers[k])

    def own_x():
        return pltpu.make_async_copy(x_ref.at[me], x_sc.at[me], local_sem.at[0])

    def own_y():
        return pltpu.make_async_copy(dy_ref.at[me], y_sc.at[mine], local_sem.at[1])

    def own_m():
        return pltpu.make_async_copy(mask_sc.at[me], masks_ref.at[me], local_sem.at[2])

    def weight():
        return pltpu.make_async_copy(w_ref, w_sc, local_sem.at[3])

    def save_x():
        return pltpu.make_async_copy(x_sc, xs_ref, local_sem.at[4])

    def save_y():
        return pltpu.make_async_copy(y_sc, dys_ref.at[pl.ds(near, 2)], local_sem.at[7])

    def save_normed():
        return pltpu.make_async_copy(normed_sc, normed_ref, local_sem.at[5])

    def save_low():
        return pltpu.make_async_copy(low_sc, low_ref, local_sem.at[8])

    def save_qkv():
        return pltpu.make_async_copy(qkv_sc, qkv_ref, local_sem.at[6])

    @pl.when(step == 0)
    def _():
        entry_signal(peers)
        own_x().start()
        weight().start()
        own_y().start()
        for s in range(slots):
            mask_sc[s] = jnp.broadcast_to(mask_ref[s : s + 1, :].astype(f32), mask_sc.shape[1:])
        own_m().start()
        entry_wait(len(peers))
        for k in (1, 2, 0):
            x_copy(k).start()
        for k in range(3):
            m_copy(k).start()
        first_sc[...] = column(start_ref[pl.ds(me, 1), :])

        def bias(i, carry):
            here = pl.ds(pl.multiple_of(i * strip, strip), strip)
            base = half * lax.div(i * strip, half)
            keys = lax.broadcasted_iota(jnp.int32, (strip, half), 1) + base
            rows = lax.broadcasted_iota(jnp.int32, (strip, half), 0) + i * strip
            allowed = (keys >= first_sc[here, 0:1]) & (keys <= rows)
            diag_sc[here, :] = jnp.where(allowed, 0.0, NEGATIVE)
            return carry

        lax.fori_loop(0, length // strip, bias, 0)

        def cross_bias(i, carry):
            here = pl.ds(pl.multiple_of(i * strip, strip), strip)
            keys = lax.broadcasted_iota(jnp.int32, (strip, half), 1)
            rows = pl.ds(pl.multiple_of(half + i * strip, strip), strip)
            cross_sc[here, :] = jnp.where(keys >= first_sc[rows, 0:1], 0.0, NEGATIVE)
            return carry

        lax.fori_loop(0, half // strip, cross_bias, 0)
        y_copy(0).start()
        own_x().wait()
        x_copy(0).wait_recv()
        weight().wait()

    @pl.when(step == groups + 1)
    def _():
        own_y().wait()
        y_copy(0).wait_recv()
        save_y().start()
        x_copy(1).wait()
        x_copy(2).wait()
        y_copy(1).start()
        save_x().start()

    @pl.when(lax.rem(step, middle) == 0)
    def _():
        first = near + (far - near) * lax.div(step, middle)
        unit, _ = norm_stats(x_sc[pl.ds(first, 2)].reshape(half, width).astype(f32))
        normed = (unit * line(gain_ref) + line(shift_ref)).astype(bf16)
        here = pl.ds(pl.multiple_of(first * tile, tile), half)
        normed_sc[here, :] = normed
        low_q = dg(normed, downq_ref[...], NT).astype(bf16)
        low_v = dg(normed, downv_ref[...], NT).astype(bf16)
        low_sc[0, here, :] = low_q
        low_sc[1, here, :] = low_v
        scale = size**-0.5 * LOG2E
        wide = 512
        for at in range(0, 3 * width, wide):
            cols = slice(at, at + wide)
            piece = dg(normed, w_sc[:, cols], NN)
            if at < width:
                piece = (piece + ADAPTER_SCALE * dg(low_q, upq_ref[:, cols], NN)) * scale
            if at >= 2 * width:
                piece = piece + ADAPTER_SCALE * dg(low_v, upv_ref[:, at - 2 * width : at - 2 * width + wide], NN)
            qkv_sc[here, cols] = piece.astype(bf16)

    @pl.when(step == middle)
    def _():
        save_normed().start()
        save_low().start()
        save_qkv().start()

    def attention(g, units):
        def third(k):
            return qkv_sc.at[:, pl.ds(pl.multiple_of(k * width + g * GROUP, GROUP), GROUP)]

        q_ref, k_ref, v_ref = third(0), third(1), third(2)

        def scores(at, unit):
            i, n, q_base, k_base = unit[:4]
            masked = jnp.concatenate(head_masks(q_ref[rows_at(q_base, i * TILE, TILE), :], heads, size), 0)
            for j in range(0, n, TILE):
                s_sc[at % 2, :, j : j + TILE] = dg(masked, k_ref[rows_at(k_base, j, TILE), :], NT)

        def soft(at, unit):
            i, n, q_base, _, bias, probs, (_, keep_m, keep_l, keep_row) = unit
            tops, sums = [], []
            for r in range(0, TILE, strip):
                tops.append([])
                sums.append([])
                for h in range(heads):
                    here = h * TILE + r
                    s = s_sc[at % 2, here : here + strip, 0:n] + bias(i * TILE + r, n)
                    top = jnp.max(s, axis=1, keepdims=True)
                    e = jnp.exp2(s - top)
                    tops[-1].append(top)
                    sums[-1].append(jnp.sum(e, axis=1, keepdims=True))
                    probs[h, i * TILE + r : i * TILE + r + strip, 0:n] = e.astype(bf16)
                where = pl.ds(pl.multiple_of(keep_row + i * TILE + r, strip), strip)
                keep_m[where, :] = lanes_of(tops[-1], GROUP)
                keep_l[where, :] = lanes_of(sums[-1], GROUP)

        def mix(at, unit):
            i, n, _, k_base, _, probs, (keep_o, _, _, keep_row) = unit
            stacked = probs[:, i * TILE : (i + 1) * TILE, 0:n].reshape(heads * TILE, n)
            merged = merge_heads(dg(stacked, v_ref[rows_at(k_base, 0, n), :], NN), heads, size)
            keep_o[rows_at(keep_row, i * TILE, TILE), :] = merged

        pipelined(units, (scores, soft, mix))

    def diag_units(base, keep, keep_row):
        def bias(r, n):
            return diag_sc[pl.ds(pl.multiple_of(base + r, strip), strip), 0:n]

        kept = (*keep, keep_row)
        return [(i, (i + 1) * TILE, base, base, bias, pd_ref.at[0], kept) for i in range(half // TILE)]

    def cross_units():
        def bias(r, n):
            return cross_sc[r : r + strip, 0:n]

        return [
            (i, half, half, 0, bias, pc_ref, (part.at[0], part.at[1], part.at[2], 0)) for i in range(half // TILE)
        ]

    @pl.when((step > 0) & (step <= groups))
    def _():
        cols = pl.ds(pl.multiple_of((step - 1) * GROUP, GROUP), GROUP)
        attention(step - 1, diag_units(near * tile, [near_sc.at[a, :, cols] for a in range(3)], 0))

    @pl.when(step > middle)
    def _():
        g = step - middle - 1
        cols = pl.ds(pl.multiple_of(g * GROUP, GROUP), GROUP)
        near_rows = rows_at(near * tile, 0, half)
        for a in range(3):
            state[a, near_rows, :] = near_sc[a, :, cols]
        far_units = diag_units(far * tile, [state.at[a] for a in range(3)], far * tile)
        attention(g, far_units + cross_units())
        inverse = 1.0 / state[2, 0:half]
        cd_ref[0:half] = inverse
        ctx_ref[0:half] = (state[0, 0:half] * inverse).astype(bf16)
        for r in range(0, half, TILE):
            high = slice(half + r, half + r + TILE)
            here = slice(r, r + TILE)
            top = jnp.maximum(state[1, high], part[1, here])
            weight_d = jnp.exp2(state[1, high] - top)
            weight_c = jnp.exp2(part[1, here] - top)
            inverse = 1.0 / (weight_d * state[2, high] + weight_c * part[2, here])
            weight_d = weight_d * inverse
            weight_c = weight_c * inverse
            cd_ref[high] = weight_d
            cc_ref[here] = weight_c
            ctx_ref[high] = (state[0, high] * weight_d + part[0, here] * weight_c).astype(bf16)

    @pl.when(step == middle + groups)
    def _():
        x_copy(0).wait_send()
        y_copy(0).wait_send()
        y_copy(1).wait()
        for k in range(3):
            m_copy(k).wait()
        own_m().wait()
        save_x().wait()
        save_y().wait()
        save_normed().wait()
        save_low().wait()
        save_qkv().wait()


def opening(x, dy, w, mask, start, gain, shift, downq, downv, upq, upv, size):
    slots, tile, width = x.shape
    length = slots * tile
    half = length // 2
    groups = width // GROUP
    per = GROUP // size
    dma = pltpu.SemaphoreType.DMA
    small = [mask, start, gain, shift, downq, downv, upq, upv]
    masks = (slots, 8, tile)

    middle = groups + 1

    def late(t):
        return jnp.maximum(t - middle - 1, 0)

    def diag_at(t):
        second = lax.div(t, middle + 1)
        return second, jnp.where(second == 1, t - middle - 1, jnp.clip(t - 1, 0, groups - 1)), 0, 0

    return pl.pallas_call(
        functools.partial(open_kernel, size=size, strip=32),
        grid=(middle + groups + 1,),
        in_specs=[ANY] * 3 + [resident(a.shape) for a in small],
        out_specs=[ANY] * 6 + [
            pl.BlockSpec((length, GROUP), lambda t: (0, late(t))),
            pl.BlockSpec((1, per, half, half), diag_at),
            pl.BlockSpec((per, half, half), lambda t: (late(t), 0, 0)),
            pl.BlockSpec((length, GROUP), lambda t: (0, late(t))),
            pl.BlockSpec((half, GROUP), lambda t: (0, late(t))),
        ],
        out_shape=[
            jax.ShapeDtypeStruct(x.shape, bf16),
            jax.ShapeDtypeStruct(x.shape, bf16),
            jax.ShapeDtypeStruct(masks, f32),
            jax.ShapeDtypeStruct((length, width), bf16),
            jax.ShapeDtypeStruct((2, length, downq.shape[0]), bf16),
            jax.ShapeDtypeStruct((length, 3 * width), bf16),
            jax.ShapeDtypeStruct((length, width), bf16),
            jax.ShapeDtypeStruct((2, per * groups, half, half), bf16),
            jax.ShapeDtypeStruct((per * groups, half, half), bf16),
            jax.ShapeDtypeStruct((length, width), f32),
            jax.ShapeDtypeStruct((half, width), f32),
        ],
        scratch_shapes=[
            pltpu.VMEM(x.shape, bf16),
            pltpu.VMEM((2, tile, width), bf16),
            pltpu.VMEM(w.shape, bf16),
            pltpu.VMEM(masks, f32),
            pltpu.VMEM((length, width), bf16),
            pltpu.VMEM((2, length, downq.shape[0]), bf16),
            pltpu.VMEM((length, 3 * width), bf16),
            pltpu.VMEM((2, per * TILE, half), f32),
            pltpu.VMEM((length, half), f32),
            pltpu.VMEM((half, half), f32),
            pltpu.VMEM((length, 128), jnp.int32),
            pltpu.VMEM((3, half, width), f32),
            pltpu.VMEM((3, length, GROUP), f32),
            pltpu.VMEM((3, half, GROUP), f32),
            dma((3,)), dma((3,)), dma((3,)), dma((3,)), dma((3,)), dma((3,)), dma((9,)),
        ],
        compiler_params=pltpu.CompilerParams(
            collective_id=0, has_side_effects=True, vmem_limit_bytes=62 * MIB, dimension_semantics=("arbitrary",)
        ),
        name="opening",
    )(x, dy, w, *small)


def feed_kernel(
    x_hbm, y_hbm, dy_hbm, ctx_hbm, wo_hbm, wi_hbm, wf_hbm, mask_ref, gain_ref, shift_ref, bias_ref,
    out_hbm, hg_hbm, cg_hbm, sums_ref,
    x_sc, y_sc, ctx_sc, wo_ref, wi_ref, wf_ref, normed, feed_sc, grad_sc, v_sc, g_sc,
    out_sc, hg_sc, cg_sc, load_sem, chunk_sem, save_sem, y_send, y_recv,
    *, step,
):
    slots, tile, width = x_hbm.shape
    rows = slots // 2 * tile
    chunks = wi_ref.shape[1] // step
    group, me = lax.axis_index("dp"), lax.axis_index("head")
    mine = lax.rem(me, 2)
    near = me - mine
    far = slots // 2 - near
    across = (far + mine, far + 1 - mine)
    peer = (group, across[1])
    half = pl.program_id(0)
    first = half == 0

    def base(h):
        return near + (far - near) * h

    def slabs(ref, h):
        return ref.at[pl.ds(base(h), 2)]

    def load_x(h):
        return pltpu.make_async_copy(slabs(x_hbm, h), x_sc.at[h], load_sem.at[h, 0])

    def load_ctx(h):
        return pltpu.make_async_copy(slabs(ctx_hbm, h), ctx_sc.at[h], load_sem.at[h, 1])

    def load_y(h):
        if h == 0:
            return pltpu.make_async_copy(slabs(y_hbm, 0), y_sc.at[0], load_sem.at[0, 2])
        return pltpu.make_async_copy(y_hbm.at[across[0]], y_sc.at[1, mine], load_sem.at[1, 2])

    def take_y():
        return remote(dy_hbm.at[across[1]], y_sc.at[1, mine], y_send, y_recv, peer)

    def load_o():
        return pltpu.make_async_copy(wo_hbm, wo_ref, load_sem.at[0, 3])

    def cols_of(c):
        return pl.ds(c * step if isinstance(c, int) else pl.multiple_of(c * step, step), step)

    def twice(c):
        return pl.ds(2 * c * step if isinstance(c, int) else pl.multiple_of(2 * c * step, 2 * step), 2 * step)

    def load_i(c):
        return pltpu.make_async_copy(wi_hbm.at[:, twice(c)], wi_ref.at[:, twice(c)], chunk_sem.at[0, c])

    def load_f(c):
        return pltpu.make_async_copy(wf_hbm.at[twice(c), :], wf_ref.at[twice(c), :], chunk_sem.at[1, c])

    @pl.when(first)
    def _():
        entry_signal([peer])
        load_o().start()
        load_ctx(0).start()
        load_x(0).start()
        load_y(0).start()
        for c in range(chunks // 2):
            load_i(c).start()
            load_f(c).start()
        load_y(1).start()
        load_ctx(1).start()
        load_x(1).start()
        sums_ref[...] = jnp.zeros_like(sums_ref)
        load_o().wait()
        load_ctx(0).wait()
        load_x(0).wait()

    gain = line(gain_ref)
    c0 = 0.7978845608028654
    c1 = c0 * 0.044715
    branch = dg(ctx_sc[half].reshape(rows, width), wo_ref[...], NN)
    whole = x_sc[half].reshape(rows, width).astype(f32) + branch
    unit, rs = norm_stats(whole)
    normed[...] = (unit * gain + line(shift_ref)).astype(bf16)

    def enter(c, slot):
        cols = cols_of(c)
        v_sc[slot] = dg(normed[...], wi_ref[:, cols], NN) + bias_ref[cols].astype(f32).reshape(1, step)
        g_sc[slot] = dg(y_sc[half].reshape(rows, width), wf_ref[cols, :], NT)

    def leave(c, slot):
        cols = cols_of(c)
        v = v_sc[slot]
        square = v * v
        side = 0.5 * jnp.tanh(v * (c0 + c1 * square)) + 0.5
        act = v * side
        slope = side + act * (1.0 - side) * (2.0 * c0 + 6.0 * c1 * square)
        feed_sc[...] += dg(act.astype(bf16), wf_ref[cols, :], NN)
        grad_sc[...] += dg((slope * g_sc[slot]).astype(bf16), wi_ref[:, cols], NT)

    def wait_weights(c):
        @pl.when(first)
        def _():
            load_i(c).wait()
            load_f(c).wait()

    @pl.when(first)
    def _():
        load_y(0).wait()
        load_i(0).wait()
        load_f(0).wait()

    @pl.when(half == 1)
    def _():
        take_y().wait()

    feed_sc[...] = jnp.zeros_like(feed_sc)
    grad_sc[...] = jnp.zeros_like(grad_sc)
    enter(0, 0)

    @pl.when(first)
    def _():
        entry_wait(1)
        take_y().start()

    def pair(i, carry):
        wait_weights(i + 1)
        enter(2 * i + 1, 1)
        leave(2 * i, 0)
        enter(2 * i + 2, 0)
        leave(2 * i + 1, 1)
        return carry

    lax.fori_loop(0, chunks // 2 - 1, pair, 0)
    enter(chunks - 1, 1)
    leave(chunks - 2, 0)
    leave(chunks - 1, 1)
    feed = feed_sc[...]
    result = whole + feed
    out_sc[half] = result.astype(bf16).reshape(out_sc.shape[1:])
    valid = jnp.concatenate([column(mask_ref[base(half) + b, 0:1, :])[:, 0:1] for b in range(2)], 0)
    one = jnp.sum(valid * jnp.sum(result * result, axis=1, keepdims=True))
    two = jnp.sum(valid * jnp.sum(branch * branch + feed * feed, axis=1, keepdims=True))
    count = jnp.sum(valid)
    row = lax.broadcasted_iota(jnp.int32, sums_ref.shape, 0)
    col = lax.broadcasted_iota(jnp.int32, sums_ref.shape, 1)
    total = jnp.where(col == 0, one, jnp.where(col == 1, two, jnp.where(col == 2, count, 0.0)))
    sums_ref[...] += jnp.where(row == 0, total, 0.0)
    dy = y_sc[half].reshape(rows, width).astype(f32)
    low = (dy + norm_grad(unit, rs, gain, grad_sc[...])).astype(bf16)
    hg_sc[half] = low.reshape(hg_sc.shape[1:])
    cg_sc[half] = dg(low, wo_ref[...], NT).astype(bf16)

    def saves(h):
        flat = pl.ds(pl.multiple_of(base(h) * tile, tile), rows)
        return [
            pltpu.make_async_copy(out_sc.at[h], slabs(out_hbm, h), save_sem.at[h, 0]),
            pltpu.make_async_copy(hg_sc.at[h], slabs(hg_hbm, h), save_sem.at[h, 1]),
            pltpu.make_async_copy(cg_sc.at[h], cg_hbm.at[flat, :], save_sem.at[h, 2]),
        ]

    for copy in saves(half):
        copy.start()

    @pl.when(first)
    def _():
        load_y(1).wait()
        load_ctx(1).wait()
        load_x(1).wait()

    @pl.when(half == 1)
    def _():
        for copy in saves(0) + saves(1):
            copy.wait()


def feed(x, y, dy, context, mask, wo, gain, shift, wi, bias, wf):
    slots, tile, width = x.shape
    rows = slots // 2 * tile
    units = wi.shape[1]
    step = 512
    chunks = units // step
    pair = (2, 2, tile, width)
    dma = pltpu.SemaphoreType.DMA
    return pl.pallas_call(
        functools.partial(feed_kernel, step=step),
        grid=(2,),
        in_specs=[ANY] * 7 + [resident(a.shape) for a in (mask, gain, shift, bias)],
        out_specs=[ANY] * 3 + [pl.BlockSpec((8, width), lambda h: (0, 0))],
        out_shape=[jax.ShapeDtypeStruct(x.shape, bf16)] * 2 + [
            jax.ShapeDtypeStruct((2 * rows, width), bf16), jax.ShapeDtypeStruct((8, width), f32)
        ],
        scratch_shapes=[pltpu.VMEM(pair, bf16)] * 3 + [
            pltpu.VMEM(wo.shape, bf16), pltpu.VMEM(wi.shape, bf16), pltpu.VMEM(wf.shape, bf16),
            pltpu.VMEM((rows, width), bf16),
            pltpu.VMEM((rows, width), f32), pltpu.VMEM((rows, width), f32),
            pltpu.VMEM((2, rows, step), f32), pltpu.VMEM((2, rows, step), f32),
            pltpu.VMEM(pair, bf16), pltpu.VMEM(pair, bf16), pltpu.VMEM((2, rows, width), bf16),
            dma((2, 4)), dma((2, chunks // 2)), dma((2, 3)), dma, dma,
        ],
        compiler_params=pltpu.CompilerParams(
            collective_id=2, has_side_effects=True, vmem_limit_bytes=62 * MIB, dimension_semantics=("arbitrary",)
        ),
        name="feed",
    )(x, y, dy, context.reshape(x.shape), wo, wi, wf, mask, gain, shift, bias)


def close_kernel(
    q_ref, k_ref, v_ref, g_ref, o_ref, cd_ref, cc_ref, pd_ref, pc_ref,
    res_hbm, x_hbm, hg_hbm, normed_hbm, w_hbm, low_hbm,
    gain_ref, downq_ref, downv_ref, upq_ref, upv_ref, sums_ref,
    result_ref, out_ref, total_ref,
    dp_sc, ds_sc, inner_sc, ones_sc, do_sc, loc, near_sc, grads, x_sc, hg_sc, normed_sc, w_sc, low_sc, res_sc,
    sums, parts, chunk, heard, total_sc,
    r_send, r_recv, send, recv, local_sem, part_send, part_recv, pair_send, pair_recv, mean_send, mean_recv,
    *, size, strip, sizes,
):
    slots, tile, width = x_sc.shape
    length = slots * tile
    half = length // 2
    groups = width // GROUP
    heads = GROUP // size
    rank = downq_ref.shape[0]
    step = pl.program_id(0)
    last = 2 * groups + 5
    group, me = lax.axis_index("dp"), lax.axis_index("head")
    mine = lax.rem(me, 2)
    near = me - mine
    far = slots // 2 - near
    beside = near + 1 - mine
    peers = [(group, p) for p in (far + mine, far + 1 - mine, beside)]
    rest = [(lax.rem(group + k, sizes[0]), me) for k in range(1, sizes[0])]
    lanes = width // sizes[0]

    def own_result():
        return pltpu.make_async_copy(res_hbm.at[me], result_ref.at[me], local_sem.at[0])

    def result_copy(k):
        return remote(res_hbm.at[peers[k][1]], result_ref.at[me], r_send.at[k], r_recv.at[k], peers[k])

    def loads():
        return [
            pltpu.make_async_copy(src, dst, local_sem.at[1 + a])
            for a, (src, dst) in enumerate(
                [(x_hbm, x_sc), (hg_hbm, hg_sc), (normed_hbm, normed_sc), (w_hbm, w_sc), (low_hbm, low_sc.at[0:2])]
            )
        ]

    @pl.when(step == 0)
    def _():
        entry_signal(peers + rest)
        own_result().start()
        for copy in loads():
            copy.start()
        sums[...] = jnp.zeros_like(sums)
        sums[4 * rank :, :] = sums_ref[...]
        lane_head = lax.div(lax.broadcasted_iota(jnp.int32, ones_sc.shape, 0), size)
        spot_head = lax.div(lax.broadcasted_iota(jnp.int32, ones_sc.shape, 1), 128)
        ones_sc[...] = jnp.where(lane_head == spot_head, 1.0, 0.0).astype(bf16)

    @pl.when(step == 1)
    def _():
        entry_wait(len(peers) + len(rest))
        for k in range(3):
            result_copy(k).start()

    def attention(units):
        def stack(x):
            return jnp.concatenate(head_masks(x, heads, size), 0)

        def prob_grads(at, unit):
            i, n, q_base, k_base, _, which, row = unit[:7]
            grad = do_sc[which, rows_at(row, i * TILE, TILE), :]
            masked = stack(grad)
            for j in range(0, n, TILE):
                dp_sc[at % 2, :, j : j + TILE] = dg(masked, v_ref[rows_at(k_base, j, TILE), :], NT)
            both = (grad.astype(f32) * o_ref[rows_at(q_base, i * TILE, TILE), :].astype(f32)).astype(bf16)
            inner_sc[at % 2] = dg(both, ones_sc[...], NN)

        def score_grads(at, unit):
            i, n, _, _, probs = unit[:5]
            for h in range(heads):
                for r in range(0, TILE, strip):
                    here = h * TILE + r
                    inner = inner_sc[at % 2, r : r + strip, 128 * h : 128 * (h + 1)]
                    inner = jnp.concatenate([inner] * (n // 128), 1)
                    prob = probs[h, i * TILE + r : i * TILE + r + strip, 0:n].astype(f32)
                    ds = prob * (dp_sc[at % 2, here : here + strip, 0:n] - inner)
                    ds_sc[at % 2, here : here + strip, 0:n] = ds.astype(bf16)

        def products(at, unit):
            i, n, q_base, k_base, probs, which, row, add = unit
            query = rows_at(q_base, i * TILE, TILE)
            ds = ds_sc[at % 2, :, 0:n]
            dq = merge_heads(dg(ds, k_ref[rows_at(k_base, 0, n), :], NN), heads, size)
            stacked = probs[:, i * TILE : (i + 1) * TILE, 0:n].reshape(heads * TILE, n)
            dv = dg(stacked, stack(do_sc[which, rows_at(row, i * TILE, TILE), :]), TN)
            dk = dg(ds, stack(q_ref[query, :]), TN)
            if add:
                loc[0, query, :] += dq
                keys = rows_at(k_base, 0, n)
                loc[1, keys, :] += dk
                loc[2, keys, :] += dv
            else:
                loc[0, query, :] = dq
                if i:
                    keys = rows_at(k_base, 0, i * TILE)
                    loc[1, keys, :] += dk[: i * TILE]
                    loc[2, keys, :] += dv[: i * TILE]
                loc[1, query, :] = dk[i * TILE :]
                loc[2, query, :] = dv[i * TILE :]

        pipelined(units, (prob_grads, score_grads, products))

    def diag_units(base):
        here = rows_at(base, 0, half)
        do_sc[0] = (g_ref[here, :].astype(f32) * cd_ref[here, :]).astype(bf16)
        return [(i, (i + 1) * TILE, base, base, pd_ref.at[0], 0, 0, False) for i in range(half // TILE)]

    def cross_units():
        do_sc[1] = (g_ref[half:, :].astype(f32) * cc_ref[...]).astype(bf16)
        return [(i, half, half, 0, pc_ref, 1, 0, True) for i in range(half // TILE)]

    scales = (size**-0.5, LN2, 1.0)

    @pl.when(step < groups)
    def _():
        cols = pl.ds(pl.multiple_of(step * GROUP, GROUP), GROUP)
        far_rows = rows_at(far * tile, 0, half)
        near_rows = rows_at(near * tile, 0, half)
        for a in range(3):
            loc[a, near_rows, :] = jnp.zeros((half, GROUP), f32)
        attention(diag_units(far * tile) + cross_units())
        for a in range(3):
            grads[a, far_rows, cols] = (loc[a, far_rows, :] * scales[a]).astype(bf16)
            near_sc[a, :, cols] = loc[a, near_rows, :]

    @pl.when((step > groups + 2) & (step < 2 * groups + 3))
    def _():
        cols = pl.ds(pl.multiple_of((step - groups - 3) * GROUP, GROUP), GROUP)
        near_rows = rows_at(near * tile, 0, half)
        attention(diag_units(near * tile))
        for a in range(3):
            both = loc[a, near_rows, :] + near_sc[a, :, cols]
            grads[a, near_rows, cols] = (both * scales[a]).astype(bf16)

    held = tile // 4

    def give(k):
        return remote(res_sc.at[peers[k][1]], out_ref.at[me], send.at[k], recv.at[k], peers[k])

    def give_part(p):
        rows = pl.ds(0, tile - held) if p == 0 else pl.ds(tile - held, held)
        return remote(
            res_sc.at[peers[1][1], rows], out_ref.at[me, rows], send.at[1 + 2 * p], recv.at[1 + 2 * p], peers[1]
        )

    def keep():
        return pltpu.make_async_copy(res_sc.at[me], out_ref.at[me], local_sem.at[6])

    def block_of(d):
        return pl.ds(pl.multiple_of(d * lanes, lanes), lanes)

    def scatter(k):
        return remote(sums.at[:, block_of(rest[k][0])], parts.at[k], part_send.at[k], part_recv.at[k], rest[k])

    def pair(at, peer):
        return remote(chunk.at[at], heard.at[at], pair_send.at[at], pair_recv.at[at], peer)

    def gather(k):
        return remote(chunk.at[2], total_sc.at[:, block_of(group)], mean_send.at[k], mean_recv.at[k], rest[k])

    @pl.when(step == groups)
    def _():
        for copy in loads():
            copy.wait()

    @pl.when((step == groups) | (step == 2 * groups + 3))
    def _():
        first = far + (near - far) * lax.div(step, 2 * groups + 3)
        here = pl.ds(pl.multiple_of(first * tile, tile), half)
        low_sc[2, here, :] = (ADAPTER_SCALE * dg(grads[0, here, :], upq_ref[...], NT)).astype(bf16)
        low_sc[3, here, :] = (ADAPTER_SCALE * dg(grads[2, here, :], upv_ref[...], NT)).astype(bf16)

    @pl.when((step == groups + 2) | (step == 2 * groups + 3))
    def _():
        first = far + (near - far) * lax.div(step, 2 * groups + 3)
        here = pl.ds(pl.multiple_of(first * tile, tile), half)
        dq, dv = grads[0, here, :], grads[2, here, :]
        normed = normed_sc[pl.ds(first, 2)].reshape(half, width)
        low_q, low_v, low_gq, low_gv = (low_sc[a, here, :] for a in range(4))
        sums[0:rank] += dg(low_gq, normed, TN)
        sums[rank : 2 * rank] += dg(low_gv, normed, TN)
        sums[2 * rank : 3 * rank] += ADAPTER_SCALE * dg(low_q, dq, TN)
        sums[3 * rank : 4 * rank] += ADAPTER_SCALE * dg(low_v, dv, TN)

    @pl.when(step == 2 * groups + 3)
    def _():
        for k in range(len(rest)):
            scatter(k).start()

    @pl.when(step == last)
    def _():
        pair(0, peers[2]).wait()
        chunk[1] = chunk[0] + heard[0]
        pair(1, peers[0]).start()
        give_part(1).start()

    early = (step == groups) | (step == groups + 1)

    @pl.when(early | (step > 2 * groups + 3))
    def _():
        late = lax.div(step, 2 * groups + 4)
        second = lax.rem(step, 2)
        slab = late * (beside + second * (me - beside)) + (1 - late) * (
            peers[0][1] + second * (peers[1][1] - peers[0][1])
        )
        here = pl.ds(pl.multiple_of(slab * tile, tile), tile)
        dq, dk, dv = grads[0, here, :], grads[1, here, :], grads[2, here, :]
        low_gq, low_gv = low_sc[2, here, :], low_sc[3, here, :]
        normed_grad = (
            dg(dq, w_sc[:, :width], NT)
            + dg(dk, w_sc[:, width : 2 * width], NT)
            + dg(dv, w_sc[:, 2 * width :], NT)
            + dg(low_gq, downq_ref[...], NN)
            + dg(low_gv, downv_ref[...], NN)
        )
        unit, rs = norm_stats(x_sc[slab].astype(f32))
        grad = hg_sc[slab].astype(f32) + norm_grad(unit, rs, line(gain_ref), normed_grad)
        res_sc[slab] = grad.astype(bf16)

    @pl.when(step == groups)
    def _():
        give(0).start()

    @pl.when(step == groups + 1)
    def _():
        give_part(0).start()

    @pl.when(step == 2 * groups + 4)
    def _():
        give(2).start()
        for k in range(len(rest)):
            scatter(k).wait()
        whole = sums[:, block_of(group)]
        for k in range(len(rest)):
            whole = whole + parts[k]
        chunk[0] = whole
        pair(0, peers[2]).start()

    @pl.when(step == last)
    def _():
        keep().start()
        pair(1, peers[0]).wait()
        whole = chunk[1] + heard[1]
        chunk[2] = whole
        total_sc[:, block_of(group)] = whole
        for k in range(len(rest)):
            gather(k).start()
        for k in range(len(rest)):
            gather(k).wait()
        total_ref[...] = total_sc[...]
        own_result().wait()
        keep().wait()
        for k in range(3):
            result_copy(k).wait()
        give(0).wait()
        give(2).wait()
        give_part(0).wait()
        give_part(1).wait()


def closing(
    qkv, grad, context, cd, cc, pd, pc, result, x, hidden_grad, normed, w, low,
    gain, downq, downv, upq, upv, sums, size, sizes,
):
    slots, tile, width = x.shape
    length = slots * tile
    half = length // 2
    groups = width // GROUP
    per = GROUP // size
    rank = downq.shape[0]
    total = (4 * rank + 8, width)
    rest = sizes[0] - 1
    lanes = width // sizes[0]
    dma = pltpu.SemaphoreType.DMA
    small = [gain, downq, downv, upq, upv, sums]

    def fold(a):
        return a.reshape(x.shape)

    def of(t):
        second = lax.div(t, groups + 3)
        return jnp.minimum(t - second * (groups + 3), groups - 1)

    def early(t):
        return jnp.minimum(t, groups - 1)

    def columns(third):
        return pl.BlockSpec((length, GROUP), lambda t: (0, of(t) + third * groups))

    return pl.pallas_call(
        functools.partial(close_kernel, size=size, strip=32, sizes=sizes),
        grid=(2 * groups + 6,),
        in_specs=[
            columns(0), columns(1), columns(2), columns(0), columns(0), columns(0),
            pl.BlockSpec((half, GROUP), lambda t: (0, early(t))),
            pl.BlockSpec((1, per, half, half), lambda t: (1 - jnp.minimum(lax.div(t, groups + 3), 1), of(t), 0, 0)),
            pl.BlockSpec((per, half, half), lambda t: (early(t), 0, 0)),
        ]
        + [ANY] * 6
        + [resident(a.shape) for a in small],
        out_specs=[ANY, ANY, pl.BlockSpec(total, lambda t: (0, 0))],
        out_shape=[
            jax.ShapeDtypeStruct(x.shape, bf16),
            jax.ShapeDtypeStruct(x.shape, bf16),
            jax.ShapeDtypeStruct(total, f32),
        ],
        scratch_shapes=[
            pltpu.VMEM((2, per * TILE, half), f32),
            pltpu.VMEM((2, per * TILE, half), bf16),
            pltpu.VMEM((2, TILE, per * 128), f32),
            pltpu.VMEM((GROUP, per * 128), bf16),
            pltpu.VMEM((2, half, GROUP), bf16),
            pltpu.VMEM((3, length, GROUP), f32),
            pltpu.VMEM((3, half, width), f32),
            pltpu.VMEM((3, length, width), bf16),
            pltpu.VMEM(x.shape, bf16),
            pltpu.VMEM(x.shape, bf16),
            pltpu.VMEM(x.shape, bf16),
            pltpu.VMEM(w.shape, bf16),
            pltpu.VMEM((4, length, rank), bf16),
            pltpu.VMEM(x.shape, bf16),
            pltpu.VMEM(total, f32),
            pltpu.VMEM((rest, total[0], lanes), f32),
            pltpu.VMEM((3, total[0], lanes), f32),
            pltpu.VMEM((2, total[0], lanes), f32),
            pltpu.VMEM(total, f32),
            dma((3,)), dma((3,)), dma((4,)), dma((4,)), dma((7,)),
            dma((rest,)), dma((rest,)), dma((2,)), dma((2,)), dma((rest,)), dma((rest,)),
        ],
        compiler_params=pltpu.CompilerParams(
            collective_id=1, has_side_effects=True, vmem_limit_bytes=62 * MIB, dimension_semantics=("arbitrary",)
        ),
        name="closing",
    )(qkv, qkv, qkv, grad, context, cd, cc, pd, pc, result, x, fold(hidden_grad), fold(normed), w, low, *small)


def finish_kernel(total_ref, a_hbm, b_hbm, aq_ref, bq_ref, av_ref, bv_ref, rms_ref, a_out, b_out, a_sc, b_sc, sem):
    rank, width = aq_ref.shape
    loads, saves = [], []
    for k, (src, kept, dst) in enumerate(((a_hbm, a_sc, a_out), (b_hbm, b_sc, b_out))):
        for s in range(src.shape[0]):
            loads.append(pltpu.make_async_copy(src.at[s], kept.at[s], sem.at[k, s, 0]))
            saves.append(pltpu.make_async_copy(kept.at[s], dst.at[s], sem.at[k, s, 1]))
    for load in loads:
        load.start()
    aq_ref[...] = total_ref[0:rank]
    av_ref[...] = total_ref[rank : 2 * rank]
    bq_ref[...] = total_ref[2 * rank : 3 * rank]
    bv_ref[...] = total_ref[3 * rank : 4 * rank]
    line = total_ref[4 * rank : 4 * rank + 1, 0:128]
    lane = lax.broadcasted_iota(jnp.int32, line.shape, 1)
    count = jnp.maximum(jnp.sum(jnp.where(lane == 2, line, 0.0)), 1.0)
    values = jnp.sqrt(line / (jnp.where(lane == 0, 1.0, 2.0) * count * width))
    for k in range(2):
        rms_ref[k] = jnp.sum(jnp.where(lane == k, values, 0.0))
    for load, save in zip(loads, saves):
        load.wait()
        save.start()
    for save in saves:
        save.wait()


def finish(total, a, b, rank):
    width = total.shape[1]
    small = jax.ShapeDtypeStruct((rank, width), f32)
    return pl.pallas_call(
        finish_kernel,
        in_specs=[VMEM, ANY, ANY],
        out_specs=[VMEM] * 4 + [pl.BlockSpec(memory_space=pltpu.SMEM), ANY, ANY],
        out_shape=[small] * 4 + [
            jax.ShapeDtypeStruct((2,), f32),
            jax.ShapeDtypeStruct(a.shape, a.dtype),
            jax.ShapeDtypeStruct(b.shape, b.dtype),
        ],
        scratch_shapes=[
            pltpu.VMEM(a.shape, a.dtype), pltpu.VMEM(b.shape, b.dtype), pltpu.SemaphoreType.DMA((2, a.shape[0], 2))
        ],
        name="finish",
    )(total, a, b)


def whole_slots(
    block_input_rows,
    document_starts,
    counted_mask,
    output_gradient,
    first_norm_gain,
    first_norm_bias,
    query_key_value_weight,
    query_down_weight,
    query_up_weight,
    value_down_weight,
    value_up_weight,
    attention_out_weight,
    second_norm_gain,
    second_norm_bias,
    feed_input_weight,
    feed_input_bias,
    feed_output_weight,
):
    sizes = (lax.axis_size("dp"), lax.axis_size("head"))
    size = block_input_rows.shape[-1] // H
    rank = query_down_weight.shape[1]
    downq = query_down_weight.T
    downv = value_down_weight.T
    x, dy, mask, normed, low, qkv, context, pd, pc, cd, cc = opening(
        block_input_rows, output_gradient, query_key_value_weight, counted_mask, document_starts,
        first_norm_gain, first_norm_bias, downq, downv, query_up_weight, value_up_weight, size,
    )
    out, hidden_grad, context_grad, sums = feed(
        x, dy, output_gradient, context, mask, attention_out_weight, second_norm_gain, second_norm_bias,
        feed_input_weight, feed_input_bias, feed_output_weight,
    )
    output, input_grad, total = closing(
        qkv, context_grad, context, cd, cc, pd, pc, out, x, hidden_grad, normed, query_key_value_weight, low,
        first_norm_gain, downq, downv, query_up_weight, value_up_weight, sums, size, sizes,
    )
    grad_aq, grad_bq, grad_av, grad_bv, rms, output, input_grad = finish(total, output, input_grad, rank)
    return output, input_grad, grad_aq.T, grad_bq, grad_av.T, grad_bv, rms


def body(*args):
    same = args[0].shape[0] == lax.axis_size("head")
    return whole_slots(*args) if same else shards(*args)


def solution(mesh):
    return jax.shard_map(
        body,
        mesh=mesh,
        in_specs=(
            P("dp", "head", None),
            P("dp", None),
            P("dp", "head"),
            P("dp", "head", None),
            P(),
            P(),
            P(),
            P(),
            P(),
            P(),
            P(),
            P(),
            P(),
            P(),
            P(),
            P(),
            P(),
        ),
        out_specs=(P("dp", "head", None), P("dp", "head", None), P(), P(), P(), P(), P()),
        check_vma=False,
    )
```

```python
import functools

import jax
import jax.numpy as jnp
from jax import lax
from jax.experimental import pallas as pl
from jax.experimental.pallas import tpu as pltpu
from jax.sharding import PartitionSpec as P

H = 16


EPSILON = 1e-05
ADAPTER_SCALE = 8.0
NEGATIVE = -1e30


def as_sent(x):

    def short(part):
        return part.astype(jnp.bfloat16) if part.dtype == jnp.float32 else part

    return jax.tree.map(short, x)


def norm_rows(matrix, gain_vec, shift_vec):
    center = matrix - jnp.mean(matrix, axis=-1, keepdims=True)
    variance = jnp.mean(center * center, axis=-1, keepdims=True)
    return center * lax.rsqrt(variance + EPSILON) * gain_vec + shift_vec


def norm_back(matrix, gain_vec, shift_vec, incoming):
    pullback = jax.vjp(lambda element_item: norm_rows(element_item, gain_vec, shift_vec), matrix)[1]
    return pullback(incoming)[0]


def gelu_tanh(matrix):
    return jax.nn.gelu(matrix, approximate=True)


def plain_product(left, right):
    return jnp.dot(left, right, preferred_element_type=jnp.float32)


def last_product(left, right):
    return lax.dot_general(
        left, right, (((1,), (1,)), ((), ())), preferred_element_type=jnp.float32
    )


def first_product(left, right):
    return lax.dot_general(
        left, right, (((0,), (0,)), ((), ())), preferred_element_type=jnp.float32
    )


def masked_scores(query_block, key_slot, segments, row_start, row_end, score_scale):
    places = jnp.arange(row_end)
    allowed = (segments[row_start:row_end, None] == segments[None, :row_end]) & (
        places[None, :] <= places[row_start:row_end, None]
    )
    scores = (
        jnp.einsum(
            "qhd,khd->hqk", query_block, key_slot[:row_end], preferred_element_type=jnp.float32
        )
        * score_scale
    )
    return jnp.where(allowed[None], scores, NEGATIVE)


def attend_slot(query_slot, key_slot, value_slot, segments, block_rows, score_scale):
    length = query_slot.shape[0]
    outputs_list = []
    logsum_list = []
    for block_index in range(length // block_rows):
        row_start = block_index * block_rows
        row_end = row_start + block_rows
        scores = masked_scores(
            query_slot[row_start:row_end], key_slot, segments, row_start, row_end, score_scale
        )
        row_max = jnp.max(scores, axis=-1, keepdims=True)
        exponent = jnp.exp(scores - row_max)
        row_total = jnp.sum(exponent, axis=-1, keepdims=True)
        probability = (exponent / row_total).astype(jnp.bfloat16)
        context = jnp.einsum(
            "hqk,khd->qhd", probability, value_slot[:row_end], preferred_element_type=jnp.float32
        )
        outputs_list.append(context.astype(jnp.bfloat16))
        logsum_list.append((row_max + jnp.log(row_total))[..., 0])
    return (jnp.concatenate(outputs_list, 0), jnp.concatenate(logsum_list, 1))


def attend_back(
    query_slot, key_slot, value_slot, grad_slot, logsum, segments, block_rows, score_scale
):
    length = query_slot.shape[0]
    key_grad = jnp.zeros(key_slot.shape, jnp.float32)
    value_gradient = jnp.zeros(value_slot.shape, jnp.float32)
    query_parts = []
    for block_index in range(length // block_rows):
        row_start = block_index * block_rows
        row_end = row_start + block_rows
        query_block = query_slot[row_start:row_end]
        grad_block = grad_slot[row_start:row_end]
        scores = masked_scores(query_block, key_slot, segments, row_start, row_end, score_scale)
        probability = jnp.exp(scores - logsum[:, row_start:row_end, None])
        prob_grad = jnp.einsum(
            "qhd,khd->hqk", grad_block, value_slot[:row_end], preferred_element_type=jnp.float32
        )
        inner_sum = jnp.sum(probability * prob_grad, axis=-1, keepdims=True)
        score_grad = (probability * (prob_grad - inner_sum)).astype(jnp.bfloat16)
        query_parts.append(
            jnp.einsum(
                "hqk,khd->qhd", score_grad, key_slot[:row_end], preferred_element_type=jnp.float32
            )
            * score_scale
        )
        key_grad = key_grad.at[:row_end].add(
            jnp.einsum("hqk,qhd->khd", score_grad, query_block, preferred_element_type=jnp.float32)
            * score_scale
        )
        value_gradient = value_gradient.at[:row_end].add(
            jnp.einsum(
                "hqk,qhd->khd",
                probability.astype(jnp.bfloat16),
                grad_block,
                preferred_element_type=jnp.float32,
            )
        )
    query_gradient = jnp.concatenate(query_parts, 0)
    return (
        query_gradient.astype(jnp.bfloat16),
        key_grad.astype(jnp.bfloat16),
        value_gradient.astype(jnp.bfloat16),
    )


def shards(
    block_input_rows,
    document_starts,
    counted_mask,
    output_gradient,
    first_norm_gain,
    first_norm_bias,
    query_key_value_weight,
    query_down_weight,
    query_up_weight,
    value_down_weight,
    value_up_weight,
    attention_out_weight,
    second_norm_gain,
    second_norm_bias,
    feed_input_weight,
    feed_input_bias,
    feed_output_weight,
):
    slot_count, local_len, row_width = block_input_rows.shape
    groups = lax.axis_size("head")
    full_len = local_len * groups
    head_size = row_width // H
    heads_here = H // groups
    row_count = slot_count * local_len
    block_rows = min(512, full_len)
    score_scale = head_size ** (-0.5)
    gain_one = first_norm_gain.astype(jnp.float32)
    shift_one = first_norm_bias.astype(jnp.float32)
    gain_two = second_norm_gain.astype(jnp.float32)
    shift_two = second_norm_bias.astype(jnp.float32)
    fc_bias = feed_input_bias.astype(jnp.float32)
    local_shape = (slot_count, local_len, row_width)
    split_shape = (slot_count, full_len, heads_here, head_size)
    merged_shape = (slot_count, full_len, heads_here * head_size)
    flat_in = block_input_rows.reshape(row_count, row_width).astype(jnp.float32)
    normed_rows = norm_rows(flat_in, gain_one, shift_one).astype(jnp.bfloat16)
    query_low_rank = plain_product(normed_rows, query_down_weight).astype(jnp.bfloat16)
    value_low_rank = plain_product(normed_rows, value_down_weight).astype(jnp.bfloat16)
    projected_rows = plain_product(normed_rows, query_key_value_weight)
    query_rows = (
        projected_rows[:, :row_width]
        + ADAPTER_SCALE * plain_product(query_low_rank, query_up_weight)
    ).astype(jnp.bfloat16)
    key_rows = projected_rows[:, row_width : 2 * row_width].astype(jnp.bfloat16)
    value_matrix = (
        projected_rows[:, 2 * row_width :]
        + ADAPTER_SCALE * plain_product(value_low_rank, value_up_weight)
    ).astype(jnp.bfloat16)
    head_query, head_key, head_value = (
        lax.all_to_all(
            query_rows.reshape(local_shape), "head", split_axis=2, concat_axis=1, tiled=True
        ),
        lax.all_to_all(
            key_rows.reshape(local_shape), "head", split_axis=2, concat_axis=1, tiled=True
        ),
        lax.all_to_all(
            value_matrix.reshape(local_shape), "head", split_axis=2, concat_axis=1, tiled=True
        ),
    )
    head_query = head_query.reshape(split_shape)
    head_key = head_key.reshape(split_shape)
    head_value = head_value.reshape(split_shape)

    def slot_fn(packed):
        return attend_slot(packed[0], packed[1], packed[2], packed[3], block_rows, score_scale)

    context_heads, logsum = lax.map(slot_fn, (head_query, head_key, head_value, document_starts))
    context_local = lax.all_to_all(
        as_sent(context_heads.reshape(merged_shape)),
        "head",
        split_axis=1,
        concat_axis=2,
        tiled=True,
    )
    context_flat = context_local.reshape(row_count, row_width)
    branch = plain_product(context_flat, attention_out_weight)
    hidden_state = flat_in + branch
    normed_two = norm_rows(hidden_state, gain_two, shift_two).astype(jnp.bfloat16)
    before = plain_product(normed_two, feed_input_weight) + fc_bias
    activated = gelu_tanh(before).astype(jnp.bfloat16)
    feed_out = plain_product(activated, feed_output_weight)
    result = hidden_state + feed_out
    output = result.astype(jnp.bfloat16).reshape(block_input_rows.shape)
    valid_rows = counted_mask.reshape(row_count).astype(jnp.float32)[:, None]
    square_sums = jnp.stack(
        [
            jnp.sum(valid_rows * result * result),
            jnp.sum(valid_rows * (branch * branch + feed_out * feed_out)),
            jnp.sum(valid_rows),
        ]
    )
    grad_flat = output_gradient.reshape(row_count, row_width)
    act_grad = last_product(grad_flat, feed_output_weight)
    gelu_pull = jax.vjp(gelu_tanh, before)[1]
    before_grad = gelu_pull(act_grad)[0].astype(jnp.bfloat16)
    normed_two_grad = last_product(before_grad, feed_input_weight)
    hidden_grad = grad_flat.astype(jnp.float32) + norm_back(
        hidden_state, gain_two, shift_two, normed_two_grad
    )
    branch_grad = hidden_grad.astype(jnp.bfloat16)
    context_grad = last_product(branch_grad, attention_out_weight).astype(jnp.bfloat16)
    grad_heads = lax.all_to_all(
        context_grad.reshape(local_shape), "head", split_axis=2, concat_axis=1, tiled=True
    ).reshape(split_shape)

    def back_fn(packed):
        return attend_back(
            packed[0],
            packed[1],
            packed[2],
            packed[3],
            packed[4],
            packed[5],
            block_rows,
            score_scale,
        )

    query_gradient, key_grad, value_gradient = lax.map(
        back_fn, (head_query, head_key, head_value, grad_heads, logsum, document_starts)
    )
    query_gradient, key_grad, value_gradient = (
        lax.all_to_all(
            as_sent(query_gradient.reshape(merged_shape)),
            "head",
            split_axis=1,
            concat_axis=2,
            tiled=True,
        ),
        lax.all_to_all(
            as_sent(key_grad.reshape(merged_shape)), "head", split_axis=1, concat_axis=2, tiled=True
        ),
        lax.all_to_all(
            as_sent(value_gradient.reshape(merged_shape)),
            "head",
            split_axis=1,
            concat_axis=2,
            tiled=True,
        ),
    )
    query_gradient = query_gradient.reshape(row_count, row_width)
    key_grad = key_grad.reshape(row_count, row_width)
    value_gradient = value_gradient.reshape(row_count, row_width)
    query_low_gradient = (ADAPTER_SCALE * last_product(query_gradient, query_up_weight)).astype(
        jnp.bfloat16
    )
    value_low_gradient = (ADAPTER_SCALE * last_product(value_gradient, value_up_weight)).astype(
        jnp.bfloat16
    )
    joined_grads = jnp.concatenate([query_gradient, key_grad, value_gradient], axis=1)
    normed_grad = (
        last_product(joined_grads, query_key_value_weight)
        + last_product(query_low_gradient, query_down_weight)
        + last_product(value_low_gradient, value_down_weight)
    )
    input_grad = hidden_grad + norm_back(flat_in, gain_one, shift_one, normed_grad)
    down_query = first_product(normed_rows, query_low_gradient)
    lifted_query = ADAPTER_SCALE * first_product(query_low_rank, query_gradient)
    down_value = first_product(normed_rows, value_low_gradient)
    lifted_value = ADAPTER_SCALE * first_product(value_low_rank, value_gradient)
    totals = lax.psum(
        (down_query, lifted_query, down_value, lifted_value, square_sums), ("dp", "head")
    )
    token_count = jnp.maximum(totals[4][2], 1.0)
    rms_values = jnp.stack(
        [
            jnp.sqrt(totals[4][0] / (token_count * row_width)),
            jnp.sqrt(totals[4][1] / (2.0 * token_count * row_width)),
        ]
    )
    return (
        output,
        input_grad.astype(jnp.bfloat16).reshape(block_input_rows.shape),
        totals[0],
        totals[1],
        totals[2],
        totals[3],
        rms_values,
    )


LOG2E = 1.4426950408889634
TILE = 256
GROUP = 256
bf16 = jnp.bfloat16
f32 = jnp.float32
NT = (((1,), (1,)), ((), ()))
NN = (((1,), (0,)), ((), ()))
TN = (((0,), (0,)), ((), ()))
MESH = pl.DeviceIdType.MESH
MIB = 2**20


def dg(left, right, dims):
    return lax.dot_general(left, right, dims, preferred_element_type=f32)


def resident(shape):
    zeros = (0,) * len(shape)
    return pl.BlockSpec(shape, lambda *_: zeros, pipeline_mode=pl.Buffered(1))


def params(mib):
    return pltpu.CompilerParams(
        vmem_limit_bytes=mib * MIB, dimension_semantics=("arbitrary",)
    )


def norm_stats(rows):
    center = rows - jnp.mean(rows, axis=-1, keepdims=True)
    rs = lax.rsqrt(jnp.mean(center * center, axis=-1, keepdims=True) + EPSILON)
    return center * rs, rs


def norm_grad(unit, rs, gain, incoming):
    t = incoming * gain
    return (
        t - jnp.mean(t, axis=-1, keepdims=True) - unit * jnp.mean(t * unit, axis=-1, keepdims=True)
    ) * rs


def head_masks(x, heads, size):
    lane = lax.broadcasted_iota(jnp.int32, x.shape, 1)
    return [
        jnp.where((lane >= size * h) & (lane < size * (h + 1)), x, jnp.zeros_like(x))
        for h in range(heads)
    ]


def merge_heads(stacked, heads, size):
    rows = stacked.shape[0] // heads
    out = stacked[:rows]
    lane = lax.broadcasted_iota(jnp.int32, out.shape, 1)
    for h in range(1, heads):
        out = jnp.where(lane >= size * h, stacked[h * rows : (h + 1) * rows], out)
    return out


def column(line):
    return jnp.broadcast_to(line, (128, line.shape[1])).T


def entry_signal(peers):
    barrier = pltpu.get_barrier_semaphore()
    for peer in peers:
        pl.semaphore_signal(barrier, inc=1, device_id=peer, device_id_type=MESH)


def entry_wait(count):
    pl.semaphore_wait(pltpu.get_barrier_semaphore(), count)


def remote(src, dst, send_sem, recv_sem, peer):
    return pltpu.make_async_remote_copy(
        src_ref=src, dst_ref=dst, send_sem=send_sem, recv_sem=recv_sem, device_id=peer, device_id_type=MESH
    )


ANY = pl.BlockSpec(memory_space=pl.ANY)
VMEM = pl.BlockSpec(memory_space=pltpu.VMEM)


def line(ref):
    return ref[...].astype(f32).reshape(1, -1)


def rows_at(base, offset, count):
    return pl.ds(pl.multiple_of(base + offset, TILE), count)


def lanes_of(columns, width):
    size = width // len(columns)
    shape = (columns[0].shape[0], width)
    lane = lax.broadcasted_iota(jnp.int32, shape, 1)
    out = jnp.broadcast_to(columns[0], shape)
    for h in range(1, len(columns)):
        out = jnp.where(lane >= size * h, columns[h], out)
    return out


def pipelined(units, stages):
    for t in range(len(units) + len(stages) - 1):
        for b, stage in enumerate(stages):
            if 0 <= t - b < len(units):
                stage(t - b, units[t - b])


def open_kernel(
    x_ref, dy_ref, w_ref, mask_ref, start_ref, gain_ref, shift_ref, downq_ref, downv_ref, upq_ref, upv_ref,
    xs_ref, dys_ref, masks_ref, normed_ref, low_ref, qkv_ref, ctx_ref, pd_ref, pc_ref, cd_ref, cc_ref,
    x_sc, y_sc, w_sc, mask_sc, normed_sc, low_sc, qkv_sc, s_sc, diag_sc, cross_sc, first_sc, near_sc, state, part,
    x_send, x_recv, y_send, y_recv, m_send, m_recv, local_sem,
    *, size, strip,
):
    slots, tile, width = x_ref.shape
    length = slots * tile
    half = length // 2
    groups = width // GROUP
    heads = GROUP // size
    step = pl.program_id(0)
    middle = groups + 1
    group, me = lax.axis_index("dp"), lax.axis_index("head")
    mine = lax.rem(me, 2)
    near = me - mine
    far = slots // 2 - near
    beside = near + 1 - mine
    across = (far + mine, far + 1 - mine)
    peers = [(group, p) for p in (beside,) + across]

    def x_copy(k):
        return remote(x_ref.at[peers[k][1]], x_sc.at[me], x_send.at[k], x_recv.at[k], peers[k])

    def y_copy(k):
        landing = y_sc.at[mine] if k == 0 else dys_ref.at[me]
        return remote(dy_ref.at[peers[k][1]], landing, y_send.at[k], y_recv.at[k], peers[k])

    def m_copy(k):
        return remote(mask_sc.at[peers[k][1]], masks_ref.at[me], m_send.at[k], m_recv.at[k], peers[k])

    def own_x():
        return pltpu.make_async_copy(x_ref.at[me], x_sc.at[me], local_sem.at[0])

    def own_y():
        return pltpu.make_async_copy(dy_ref.at[me], y_sc.at[mine], local_sem.at[1])

    def own_m():
        return pltpu.make_async_copy(mask_sc.at[me], masks_ref.at[me], local_sem.at[2])

    def weight():
        return pltpu.make_async_copy(w_ref, w_sc, local_sem.at[3])

    def save_x():
        return pltpu.make_async_copy(x_sc, xs_ref, local_sem.at[4])

    def save_y():
        return pltpu.make_async_copy(y_sc, dys_ref.at[pl.ds(near, 2)], local_sem.at[7])

    def save_normed():
        return pltpu.make_async_copy(normed_sc, normed_ref, local_sem.at[5])

    def save_low():
        return pltpu.make_async_copy(low_sc, low_ref, local_sem.at[8])

    def save_qkv():
        return pltpu.make_async_copy(qkv_sc, qkv_ref, local_sem.at[6])

    @pl.when(step == 0)
    def _():
        entry_signal(peers)
        own_x().start()
        weight().start()
        own_y().start()
        for s in range(slots):
            mask_sc[s] = jnp.broadcast_to(mask_ref[s : s + 1, :].astype(f32), mask_sc.shape[1:])
        own_m().start()
        entry_wait(len(peers))
        for k in (1, 2, 0):
            x_copy(k).start()
        for k in range(3):
            m_copy(k).start()
        first_sc[...] = column(start_ref[pl.ds(me, 1), :])

        def bias(i, carry):
            here = pl.ds(pl.multiple_of(i * strip, strip), strip)
            base = half * lax.div(i * strip, half)
            keys = lax.broadcasted_iota(jnp.int32, (strip, half), 1) + base
            rows = lax.broadcasted_iota(jnp.int32, (strip, half), 0) + i * strip
            allowed = (keys >= first_sc[here, 0:1]) & (keys <= rows)
            diag_sc[here, :] = jnp.where(allowed, 0.0, NEGATIVE)
            return carry

        lax.fori_loop(0, length // strip, bias, 0)

        def cross_bias(i, carry):
            here = pl.ds(pl.multiple_of(i * strip, strip), strip)
            keys = lax.broadcasted_iota(jnp.int32, (strip, half), 1)
            rows = pl.ds(pl.multiple_of(half + i * strip, strip), strip)
            cross_sc[here, :] = jnp.where(keys >= first_sc[rows, 0:1], 0.0, NEGATIVE)
            return carry

        lax.fori_loop(0, half // strip, cross_bias, 0)
        y_copy(0).start()
        own_x().wait()
        x_copy(0).wait_recv()
        weight().wait()

    @pl.when(step == groups + 1)
    def _():
        own_y().wait()
        y_copy(0).wait_recv()
        save_y().start()
        x_copy(1).wait()
        x_copy(2).wait()
        y_copy(1).start()
        save_x().start()

    @pl.when(lax.rem(step, middle) == 0)
    def _():
        first = near + (far - near) * lax.div(step, middle)
        unit, _ = norm_stats(x_sc[pl.ds(first, 2)].reshape(half, width).astype(f32))
        normed = (unit * line(gain_ref) + line(shift_ref)).astype(bf16)
        here = pl.ds(pl.multiple_of(first * tile, tile), half)
        normed_sc[here, :] = normed
        low_q = dg(normed, downq_ref[...], NT).astype(bf16)
        low_v = dg(normed, downv_ref[...], NT).astype(bf16)
        low_sc[0, here, :] = low_q
        low_sc[1, here, :] = low_v
        scale = size**-0.5
        wide = 512
        for at in range(0, 3 * width, wide):
            cols = slice(at, at + wide)
            piece = dg(normed, w_sc[:, cols], NN)
            if at < width:
                piece = (piece + ADAPTER_SCALE * dg(low_q, upq_ref[:, cols], NN)) * scale
            if at >= 2 * width:
                piece = piece + ADAPTER_SCALE * dg(low_v, upv_ref[:, at - 2 * width : at - 2 * width + wide], NN)
            qkv_sc[here, cols] = piece.astype(bf16)

    @pl.when(step == middle)
    def _():
        save_normed().start()
        save_low().start()
        save_qkv().start()

    def attention(g, units):
        def third(k):
            return qkv_sc.at[:, pl.ds(pl.multiple_of(k * width + g * GROUP, GROUP), GROUP)]

        q_ref, k_ref, v_ref = third(0), third(1), third(2)

        def scores(at, unit):
            i, n, q_base, k_base = unit[:4]
            masked = jnp.concatenate(head_masks(q_ref[rows_at(q_base, i * TILE, TILE), :], heads, size), 0)
            for j in range(0, n, TILE):
                s_sc[at % 2, :, j : j + TILE] = dg(masked, k_ref[rows_at(k_base, j, TILE), :], NT)

        def soft(at, unit):
            i, n, q_base, _, bias, probs, (_, keep_m, keep_l, keep_row) = unit
            tops, sums = [], []
            for r in range(0, TILE, strip):
                tops.append([])
                sums.append([])
                for h in range(heads):
                    here = h * TILE + r
                    s = s_sc[at % 2, here : here + strip, 0:n] * LOG2E + bias(i * TILE + r, n)
                    top = jnp.max(s, axis=1, keepdims=True)
                    e = jnp.exp2(s - top)
                    tops[-1].append(top)
                    sums[-1].append(jnp.sum(e, axis=1, keepdims=True))
                    probs[h, i * TILE + r : i * TILE + r + strip, 0:n] = e.astype(bf16)
                where = pl.ds(pl.multiple_of(keep_row + i * TILE + r, strip), strip)
                keep_m[where, :] = lanes_of(tops[-1], GROUP)
                keep_l[where, :] = lanes_of(sums[-1], GROUP)

        def mix(at, unit):
            i, n, _, k_base, _, probs, (keep_o, _, _, keep_row) = unit
            stacked = probs[:, i * TILE : (i + 1) * TILE, 0:n].reshape(heads * TILE, n)
            merged = merge_heads(dg(stacked, v_ref[rows_at(k_base, 0, n), :], NN), heads, size)
            keep_o[rows_at(keep_row, i * TILE, TILE), :] = merged

        pipelined(units, (scores, soft, mix))

    def diag_units(base, keep, keep_row):
        def bias(r, n):
            return diag_sc[pl.ds(pl.multiple_of(base + r, strip), strip), 0:n]

        kept = (*keep, keep_row)
        return [(i, (i + 1) * TILE, base, base, bias, pd_ref.at[0], kept) for i in range(half // TILE)]

    def cross_units():
        def bias(r, n):
            return cross_sc[r : r + strip, 0:n]

        return [
            (i, half, half, 0, bias, pc_ref, (part.at[0], part.at[1], part.at[2], 0)) for i in range(half // TILE)
        ]

    @pl.when((step > 0) & (step <= groups))
    def _():
        cols = pl.ds(pl.multiple_of((step - 1) * GROUP, GROUP), GROUP)
        attention(step - 1, diag_units(near * tile, [near_sc.at[a, :, cols] for a in range(3)], 0))

    @pl.when(step > middle)
    def _():
        g = step - middle - 1
        cols = pl.ds(pl.multiple_of(g * GROUP, GROUP), GROUP)
        near_rows = rows_at(near * tile, 0, half)
        for a in range(3):
            state[a, near_rows, :] = near_sc[a, :, cols]
        far_units = diag_units(far * tile, [state.at[a] for a in range(3)], far * tile)
        attention(g, far_units + cross_units())
        inverse = 1.0 / state[2, 0:half]
        cd_ref[0:half] = inverse
        ctx_ref[0:half] = (state[0, 0:half] * inverse).astype(bf16)
        for r in range(0, half, TILE):
            high = slice(half + r, half + r + TILE)
            here = slice(r, r + TILE)
            top = jnp.maximum(state[1, high], part[1, here])
            weight_d = jnp.exp2(state[1, high] - top)
            weight_c = jnp.exp2(part[1, here] - top)
            inverse = 1.0 / (weight_d * state[2, high] + weight_c * part[2, here])
            weight_d = weight_d * inverse
            weight_c = weight_c * inverse
            cd_ref[high] = weight_d
            cc_ref[here] = weight_c
            ctx_ref[high] = (state[0, high] * weight_d + part[0, here] * weight_c).astype(bf16)

    @pl.when(step == middle + groups)
    def _():
        x_copy(0).wait_send()
        y_copy(0).wait_send()
        y_copy(1).wait()
        for k in range(3):
            m_copy(k).wait()
        own_m().wait()
        save_x().wait()
        save_y().wait()
        save_normed().wait()
        save_low().wait()
        save_qkv().wait()


def opening(x, dy, w, mask, start, gain, shift, downq, downv, upq, upv, size):
    slots, tile, width = x.shape
    length = slots * tile
    half = length // 2
    groups = width // GROUP
    per = GROUP // size
    dma = pltpu.SemaphoreType.DMA
    small = [mask, start, gain, shift, downq, downv, upq, upv]
    masks = (slots, 8, tile)

    middle = groups + 1

    def late(t):
        return jnp.maximum(t - middle - 1, 0)

    def diag_at(t):
        second = lax.div(t, middle + 1)
        return second, jnp.where(second == 1, t - middle - 1, jnp.clip(t - 1, 0, groups - 1)), 0, 0

    return pl.pallas_call(
        functools.partial(open_kernel, size=size, strip=32),
        grid=(middle + groups + 1,),
        in_specs=[ANY] * 3 + [resident(a.shape) for a in small],
        out_specs=[ANY] * 6 + [
            pl.BlockSpec((length, GROUP), lambda t: (0, late(t))),
            pl.BlockSpec((1, per, half, half), diag_at),
            pl.BlockSpec((per, half, half), lambda t: (late(t), 0, 0)),
            pl.BlockSpec((length, GROUP), lambda t: (0, late(t))),
            pl.BlockSpec((half, GROUP), lambda t: (0, late(t))),
        ],
        out_shape=[
            jax.ShapeDtypeStruct(x.shape, bf16),
            jax.ShapeDtypeStruct(x.shape, bf16),
            jax.ShapeDtypeStruct(masks, f32),
            jax.ShapeDtypeStruct((length, width), bf16),
            jax.ShapeDtypeStruct((2, length, downq.shape[0]), bf16),
            jax.ShapeDtypeStruct((length, 3 * width), bf16),
            jax.ShapeDtypeStruct((length, width), bf16),
            jax.ShapeDtypeStruct((2, per * groups, half, half), bf16),
            jax.ShapeDtypeStruct((per * groups, half, half), bf16),
            jax.ShapeDtypeStruct((length, width), f32),
            jax.ShapeDtypeStruct((half, width), f32),
        ],
        scratch_shapes=[
            pltpu.VMEM(x.shape, bf16),
            pltpu.VMEM((2, tile, width), bf16),
            pltpu.VMEM(w.shape, bf16),
            pltpu.VMEM(masks, f32),
            pltpu.VMEM((length, width), bf16),
            pltpu.VMEM((2, length, downq.shape[0]), bf16),
            pltpu.VMEM((length, 3 * width), bf16),
            pltpu.VMEM((2, per * TILE, half), f32),
            pltpu.VMEM((length, half), f32),
            pltpu.VMEM((half, half), f32),
            pltpu.VMEM((length, 128), jnp.int32),
            pltpu.VMEM((3, half, width), f32),
            pltpu.VMEM((3, length, GROUP), f32),
            pltpu.VMEM((3, half, GROUP), f32),
            dma((3,)), dma((3,)), dma((3,)), dma((3,)), dma((3,)), dma((3,)), dma((9,)),
        ],
        compiler_params=pltpu.CompilerParams(
            collective_id=0, has_side_effects=True, vmem_limit_bytes=62 * MIB, dimension_semantics=("arbitrary",)
        ),
        name="opening",
    )(x, dy, w, *small)


def feed_kernel(
    x_hbm, y_hbm, dy_hbm, ctx_hbm, wo_hbm, wi_hbm, wf_hbm, mask_ref, gain_ref, shift_ref, bias_ref,
    out_hbm, hg_hbm, cg_hbm, sums_ref,
    x_sc, y_sc, ctx_sc, wo_ref, wi_ref, wf_ref, normed, feed_sc, grad_sc, v_sc, g_sc,
    out_sc, hg_sc, cg_sc, load_sem, chunk_sem, save_sem, y_send, y_recv,
    *, step,
):
    slots, tile, width = x_hbm.shape
    rows = slots // 2 * tile
    chunks = wi_ref.shape[1] // step
    group, me = lax.axis_index("dp"), lax.axis_index("head")
    mine = lax.rem(me, 2)
    near = me - mine
    far = slots // 2 - near
    across = (far + mine, far + 1 - mine)
    peer = (group, across[1])
    half = pl.program_id(0)
    first = half == 0

    def base(h):
        return near + (far - near) * h

    def slabs(ref, h):
        return ref.at[pl.ds(base(h), 2)]

    def load_x(h):
        return pltpu.make_async_copy(slabs(x_hbm, h), x_sc.at[h], load_sem.at[h, 0])

    def load_ctx(h):
        return pltpu.make_async_copy(slabs(ctx_hbm, h), ctx_sc.at[h], load_sem.at[h, 1])

    def load_y(h):
        if h == 0:
            return pltpu.make_async_copy(slabs(y_hbm, 0), y_sc.at[0], load_sem.at[0, 2])
        return pltpu.make_async_copy(y_hbm.at[across[0]], y_sc.at[1, mine], load_sem.at[1, 2])

    def take_y():
        return remote(dy_hbm.at[across[1]], y_sc.at[1, mine], y_send, y_recv, peer)

    def load_o():
        return pltpu.make_async_copy(wo_hbm, wo_ref, load_sem.at[0, 3])

    def cols_of(c):
        return pl.ds(c * step if isinstance(c, int) else pl.multiple_of(c * step, step), step)

    def twice(c):
        return pl.ds(2 * c * step if isinstance(c, int) else pl.multiple_of(2 * c * step, 2 * step), 2 * step)

    def load_i(c):
        return pltpu.make_async_copy(wi_hbm.at[:, twice(c)], wi_ref.at[:, twice(c)], chunk_sem.at[0, c])

    def load_f(c):
        return pltpu.make_async_copy(wf_hbm.at[twice(c), :], wf_ref.at[twice(c), :], chunk_sem.at[1, c])

    @pl.when(first)
    def _():
        entry_signal([peer])
        load_o().start()
        load_ctx(0).start()
        load_x(0).start()
        load_y(0).start()
        for c in range(chunks // 2):
            load_i(c).start()
            load_f(c).start()
        load_y(1).start()
        load_ctx(1).start()
        load_x(1).start()
        sums_ref[...] = jnp.zeros_like(sums_ref)
        load_o().wait()
        load_ctx(0).wait()
        load_x(0).wait()

    gain = line(gain_ref)
    c0 = 0.7978845608028654
    c1 = c0 * 0.044715
    branch = dg(ctx_sc[half].reshape(rows, width), wo_ref[...], NN)
    whole = x_sc[half].reshape(rows, width).astype(f32) + branch
    unit, rs = norm_stats(whole)
    normed[...] = (unit * gain + line(shift_ref)).astype(bf16)

    def enter(c, slot):
        cols = cols_of(c)
        v_sc[slot] = dg(normed[...], wi_ref[:, cols], NN) + bias_ref[cols].astype(f32).reshape(1, step)
        g_sc[slot] = dg(y_sc[half].reshape(rows, width), wf_ref[cols, :], NT)

    def leave(c, slot):
        cols = cols_of(c)
        v = v_sc[slot]
        square = v * v
        side = 0.5 * jnp.tanh(v * (c0 + c1 * square)) + 0.5
        act = v * side
        slope = side + act * (1.0 - side) * (2.0 * c0 + 6.0 * c1 * square)
        feed_sc[...] += dg(act.astype(bf16), wf_ref[cols, :], NN)
        grad_sc[...] += dg((slope * g_sc[slot]).astype(bf16), wi_ref[:, cols], NT)

    def wait_weights(c):
        @pl.when(first)
        def _():
            load_i(c).wait()
            load_f(c).wait()

    @pl.when(first)
    def _():
        load_y(0).wait()
        load_i(0).wait()
        load_f(0).wait()

    @pl.when(half == 1)
    def _():
        take_y().wait()

    feed_sc[...] = jnp.zeros_like(feed_sc)
    grad_sc[...] = jnp.zeros_like(grad_sc)
    enter(0, 0)

    @pl.when(first)
    def _():
        entry_wait(1)
        take_y().start()

    def pair(i, carry):
        wait_weights(i + 1)
        enter(2 * i + 1, 1)
        leave(2 * i, 0)
        enter(2 * i + 2, 0)
        leave(2 * i + 1, 1)
        return carry

    lax.fori_loop(0, chunks // 2 - 1, pair, 0)
    enter(chunks - 1, 1)
    leave(chunks - 2, 0)
    leave(chunks - 1, 1)
    feed = feed_sc[...]
    result = whole + feed
    out_sc[half] = result.astype(bf16).reshape(out_sc.shape[1:])
    valid = jnp.concatenate([column(mask_ref[base(half) + b, 0:1, :])[:, 0:1] for b in range(2)], 0)
    one = jnp.sum(valid * jnp.sum(result * result, axis=1, keepdims=True))
    two = jnp.sum(valid * jnp.sum(branch * branch + feed * feed, axis=1, keepdims=True))
    count = jnp.sum(valid)
    row = lax.broadcasted_iota(jnp.int32, sums_ref.shape, 0)
    col = lax.broadcasted_iota(jnp.int32, sums_ref.shape, 1)
    total = jnp.where(col == 0, one, jnp.where(col == 1, two, jnp.where(col == 2, count, 0.0)))
    sums_ref[...] += jnp.where(row == 0, total, 0.0)
    dy = y_sc[half].reshape(rows, width).astype(f32)
    low = (dy + norm_grad(unit, rs, gain, grad_sc[...])).astype(bf16)
    hg_sc[half] = low.reshape(hg_sc.shape[1:])
    cg_sc[half] = dg(low, wo_ref[...], NT).astype(bf16)

    def saves(h):
        flat = pl.ds(pl.multiple_of(base(h) * tile, tile), rows)
        return [
            pltpu.make_async_copy(out_sc.at[h], slabs(out_hbm, h), save_sem.at[h, 0]),
            pltpu.make_async_copy(hg_sc.at[h], slabs(hg_hbm, h), save_sem.at[h, 1]),
            pltpu.make_async_copy(cg_sc.at[h], cg_hbm.at[flat, :], save_sem.at[h, 2]),
        ]

    for copy in saves(half):
        copy.start()

    @pl.when(first)
    def _():
        load_y(1).wait()
        load_ctx(1).wait()
        load_x(1).wait()

    @pl.when(half == 1)
    def _():
        for copy in saves(0) + saves(1):
            copy.wait()


def feed(x, y, dy, context, mask, wo, gain, shift, wi, bias, wf):
    slots, tile, width = x.shape
    rows = slots // 2 * tile
    units = wi.shape[1]
    step = 512
    chunks = units // step
    pair = (2, 2, tile, width)
    dma = pltpu.SemaphoreType.DMA
    return pl.pallas_call(
        functools.partial(feed_kernel, step=step),
        grid=(2,),
        in_specs=[ANY] * 7 + [resident(a.shape) for a in (mask, gain, shift, bias)],
        out_specs=[ANY] * 3 + [pl.BlockSpec((8, width), lambda h: (0, 0))],
        out_shape=[jax.ShapeDtypeStruct(x.shape, bf16)] * 2 + [
            jax.ShapeDtypeStruct((2 * rows, width), bf16), jax.ShapeDtypeStruct((8, width), f32)
        ],
        scratch_shapes=[pltpu.VMEM(pair, bf16)] * 3 + [
            pltpu.VMEM(wo.shape, bf16), pltpu.VMEM(wi.shape, bf16), pltpu.VMEM(wf.shape, bf16),
            pltpu.VMEM((rows, width), bf16),
            pltpu.VMEM((rows, width), f32), pltpu.VMEM((rows, width), f32),
            pltpu.VMEM((2, rows, step), f32), pltpu.VMEM((2, rows, step), f32),
            pltpu.VMEM(pair, bf16), pltpu.VMEM(pair, bf16), pltpu.VMEM((2, rows, width), bf16),
            dma((2, 4)), dma((2, chunks // 2)), dma((2, 3)), dma, dma,
        ],
        compiler_params=pltpu.CompilerParams(
            collective_id=2, has_side_effects=True, vmem_limit_bytes=62 * MIB, dimension_semantics=("arbitrary",)
        ),
        name="feed",
    )(x, y, dy, context.reshape(x.shape), wo, wi, wf, mask, gain, shift, bias)


def close_kernel(
    q_ref, k_ref, v_ref, g_ref, o_ref, cd_ref, cc_ref, pd_ref, pc_ref,
    res_hbm, x_hbm, hg_hbm, normed_hbm, w_hbm, low_hbm,
    gain_ref, downq_ref, downv_ref, upq_ref, upv_ref, sums_ref,
    result_ref, out_ref, total_ref,
    dp_sc, ds_sc, inner_sc, ones_sc, do_sc, loc, near_sc, grads, x_sc, hg_sc, normed_sc, w_sc, low_sc, res_sc,
    sums, parts, chunk, heard, total_sc,
    r_send, r_recv, send, recv, local_sem, part_send, part_recv, pair_send, pair_recv, mean_send, mean_recv,
    *, size, strip, sizes,
):
    slots, tile, width = x_sc.shape
    length = slots * tile
    half = length // 2
    groups = width // GROUP
    heads = GROUP // size
    rank = downq_ref.shape[0]
    step = pl.program_id(0)
    last = 2 * groups + 5
    group, me = lax.axis_index("dp"), lax.axis_index("head")
    mine = lax.rem(me, 2)
    near = me - mine
    far = slots // 2 - near
    beside = near + 1 - mine
    peers = [(group, p) for p in (far + mine, far + 1 - mine, beside)]
    rest = [(lax.rem(group + k, sizes[0]), me) for k in range(1, sizes[0])]
    lanes = width // sizes[0]

    def own_result():
        return pltpu.make_async_copy(res_hbm.at[me], result_ref.at[me], local_sem.at[0])

    def result_copy(k):
        return remote(res_hbm.at[peers[k][1]], result_ref.at[me], r_send.at[k], r_recv.at[k], peers[k])

    def loads():
        return [
            pltpu.make_async_copy(src, dst, local_sem.at[1 + a])
            for a, (src, dst) in enumerate(
                [(x_hbm, x_sc), (hg_hbm, hg_sc), (normed_hbm, normed_sc), (w_hbm, w_sc), (low_hbm, low_sc.at[0:2])]
            )
        ]

    @pl.when(step == 0)
    def _():
        entry_signal(peers + rest)
        own_result().start()
        for copy in loads():
            copy.start()
        sums[...] = jnp.zeros_like(sums)
        sums[4 * rank :, :] = sums_ref[...]
        lane_head = lax.div(lax.broadcasted_iota(jnp.int32, ones_sc.shape, 0), size)
        spot_head = lax.div(lax.broadcasted_iota(jnp.int32, ones_sc.shape, 1), 128)
        ones_sc[...] = jnp.where(lane_head == spot_head, 1.0, 0.0).astype(bf16)

    @pl.when(step == 1)
    def _():
        entry_wait(len(peers) + len(rest))
        for k in range(3):
            result_copy(k).start()

    def attention(units):
        def stack(x):
            return jnp.concatenate(head_masks(x, heads, size), 0)

        def prob_grads(at, unit):
            i, n, q_base, k_base, _, which, row = unit[:7]
            grad = do_sc[which, rows_at(row, i * TILE, TILE), :]
            masked = stack(grad)
            for j in range(0, n, TILE):
                dp_sc[at % 2, :, j : j + TILE] = dg(masked, v_ref[rows_at(k_base, j, TILE), :], NT)
            both = grad.astype(f32) * o_ref[rows_at(q_base, i * TILE, TILE), :].astype(f32)
            high = both.astype(bf16)
            rest_of = (both - high.astype(f32)).astype(bf16)
            inner_sc[at % 2] = dg(high, ones_sc[...], NN) + dg(rest_of, ones_sc[...], NN)

        def score_grads(at, unit):
            i, n, _, _, probs = unit[:5]
            for h in range(heads):
                for r in range(0, TILE, strip):
                    here = h * TILE + r
                    inner = inner_sc[at % 2, r : r + strip, 128 * h : 128 * (h + 1)]
                    inner = jnp.concatenate([inner] * (n // 128), 1)
                    prob = probs[h, i * TILE + r : i * TILE + r + strip, 0:n].astype(f32)
                    ds = prob * (dp_sc[at % 2, here : here + strip, 0:n] - inner)
                    ds_sc[at % 2, here : here + strip, 0:n] = ds.astype(bf16)

        def products(at, unit):
            i, n, q_base, k_base, probs, which, row, add = unit
            query = rows_at(q_base, i * TILE, TILE)
            ds = ds_sc[at % 2, :, 0:n]
            dq = merge_heads(dg(ds, k_ref[rows_at(k_base, 0, n), :], NN), heads, size)
            stacked = probs[:, i * TILE : (i + 1) * TILE, 0:n].reshape(heads * TILE, n)
            dv = dg(stacked, stack(do_sc[which, rows_at(row, i * TILE, TILE), :]), TN)
            dk = dg(ds, stack(q_ref[query, :]), TN)
            if add:
                loc[0, query, :] += dq
                keys = rows_at(k_base, 0, n)
                loc[1, keys, :] += dk
                loc[2, keys, :] += dv
            else:
                loc[0, query, :] = dq
                if i:
                    keys = rows_at(k_base, 0, i * TILE)
                    loc[1, keys, :] += dk[: i * TILE]
                    loc[2, keys, :] += dv[: i * TILE]
                loc[1, query, :] = dk[i * TILE :]
                loc[2, query, :] = dv[i * TILE :]

        pipelined(units, (prob_grads, score_grads, products))

    def diag_units(base):
        here = rows_at(base, 0, half)
        do_sc[0] = (g_ref[here, :].astype(f32) * cd_ref[here, :]).astype(bf16)
        return [(i, (i + 1) * TILE, base, base, pd_ref.at[0], 0, 0, False) for i in range(half // TILE)]

    def cross_units():
        do_sc[1] = (g_ref[half:, :].astype(f32) * cc_ref[...]).astype(bf16)
        return [(i, half, half, 0, pc_ref, 1, 0, True) for i in range(half // TILE)]

    scales = (size**-0.5, 1.0, 1.0)

    @pl.when(step < groups)
    def _():
        cols = pl.ds(pl.multiple_of(step * GROUP, GROUP), GROUP)
        far_rows = rows_at(far * tile, 0, half)
        near_rows = rows_at(near * tile, 0, half)
        for a in range(3):
            loc[a, near_rows, :] = jnp.zeros((half, GROUP), f32)
        attention(diag_units(far * tile) + cross_units())
        for a in range(3):
            grads[a, far_rows, cols] = (loc[a, far_rows, :] * scales[a]).astype(bf16)
            near_sc[a, :, cols] = loc[a, near_rows, :]

    @pl.when((step > groups + 2) & (step < 2 * groups + 3))
    def _():
        cols = pl.ds(pl.multiple_of((step - groups - 3) * GROUP, GROUP), GROUP)
        near_rows = rows_at(near * tile, 0, half)
        attention(diag_units(near * tile))
        for a in range(3):
            both = loc[a, near_rows, :] + near_sc[a, :, cols]
            grads[a, near_rows, cols] = (both * scales[a]).astype(bf16)

    held = tile // 4

    def give(k):
        return remote(res_sc.at[peers[k][1]], out_ref.at[me], send.at[k], recv.at[k], peers[k])

    def give_part(p):
        rows = pl.ds(0, tile - held) if p == 0 else pl.ds(tile - held, held)
        return remote(
            res_sc.at[peers[1][1], rows], out_ref.at[me, rows], send.at[1 + 2 * p], recv.at[1 + 2 * p], peers[1]
        )

    def keep():
        return pltpu.make_async_copy(res_sc.at[me], out_ref.at[me], local_sem.at[6])

    def block_of(d):
        return pl.ds(pl.multiple_of(d * lanes, lanes), lanes)

    def scatter(k):
        return remote(sums.at[:, block_of(rest[k][0])], parts.at[k], part_send.at[k], part_recv.at[k], rest[k])

    def pair(at, peer):
        return remote(chunk.at[at], heard.at[at], pair_send.at[at], pair_recv.at[at], peer)

    def gather(k):
        return remote(chunk.at[2], total_sc.at[:, block_of(group)], mean_send.at[k], mean_recv.at[k], rest[k])

    @pl.when(step == groups)
    def _():
        for copy in loads():
            copy.wait()

    @pl.when((step == groups) | (step == 2 * groups + 3))
    def _():
        first = far + (near - far) * lax.div(step, 2 * groups + 3)
        here = pl.ds(pl.multiple_of(first * tile, tile), half)
        low_sc[2, here, :] = (ADAPTER_SCALE * dg(grads[0, here, :], upq_ref[...], NT)).astype(bf16)
        low_sc[3, here, :] = (ADAPTER_SCALE * dg(grads[2, here, :], upv_ref[...], NT)).astype(bf16)

    @pl.when((step == groups + 2) | (step == 2 * groups + 3))
    def _():
        first = far + (near - far) * lax.div(step, 2 * groups + 3)
        here = pl.ds(pl.multiple_of(first * tile, tile), half)
        dq, dv = grads[0, here, :], grads[2, here, :]
        normed = normed_sc[pl.ds(first, 2)].reshape(half, width)
        low_q, low_v, low_gq, low_gv = (low_sc[a, here, :] for a in range(4))
        sums[0:rank] += dg(low_gq, normed, TN)
        sums[rank : 2 * rank] += dg(low_gv, normed, TN)
        sums[2 * rank : 3 * rank] += ADAPTER_SCALE * dg(low_q, dq, TN)
        sums[3 * rank : 4 * rank] += ADAPTER_SCALE * dg(low_v, dv, TN)

    @pl.when(step == 2 * groups + 3)
    def _():
        for k in range(len(rest)):
            scatter(k).start()

    @pl.when(step == last)
    def _():
        pair(0, peers[2]).wait()
        chunk[1] = chunk[0] + heard[0]
        pair(1, peers[0]).start()
        give_part(1).start()

    early = (step == groups) | (step == groups + 1)

    @pl.when(early | (step > 2 * groups + 3))
    def _():
        late = lax.div(step, 2 * groups + 4)
        second = lax.rem(step, 2)
        slab = late * (beside + second * (me - beside)) + (1 - late) * (
            peers[0][1] + second * (peers[1][1] - peers[0][1])
        )
        here = pl.ds(pl.multiple_of(slab * tile, tile), tile)
        dq, dk, dv = grads[0, here, :], grads[1, here, :], grads[2, here, :]
        low_gq, low_gv = low_sc[2, here, :], low_sc[3, here, :]
        normed_grad = (
            dg(dq, w_sc[:, :width], NT)
            + dg(dk, w_sc[:, width : 2 * width], NT)
            + dg(dv, w_sc[:, 2 * width :], NT)
            + dg(low_gq, downq_ref[...], NN)
            + dg(low_gv, downv_ref[...], NN)
        )
        unit, rs = norm_stats(x_sc[slab].astype(f32))
        grad = hg_sc[slab].astype(f32) + norm_grad(unit, rs, line(gain_ref), normed_grad)
        res_sc[slab] = grad.astype(bf16)

    @pl.when(step == groups)
    def _():
        give(0).start()

    @pl.when(step == groups + 1)
    def _():
        give_part(0).start()

    @pl.when(step == 2 * groups + 4)
    def _():
        give(2).start()
        for k in range(len(rest)):
            scatter(k).wait()
        whole = sums[:, block_of(group)]
        for k in range(len(rest)):
            whole = whole + parts[k]
        chunk[0] = whole
        pair(0, peers[2]).start()

    @pl.when(step == last)
    def _():
        keep().start()
        pair(1, peers[0]).wait()
        whole = chunk[1] + heard[1]
        chunk[2] = whole
        total_sc[:, block_of(group)] = whole
        for k in range(len(rest)):
            gather(k).start()
        for k in range(len(rest)):
            gather(k).wait()
        total_ref[...] = total_sc[...]
        own_result().wait()
        keep().wait()
        for k in range(3):
            result_copy(k).wait()
        give(0).wait()
        give(2).wait()
        give_part(0).wait()
        give_part(1).wait()


def closing(
    qkv, grad, context, cd, cc, pd, pc, result, x, hidden_grad, normed, w, low,
    gain, downq, downv, upq, upv, sums, size, sizes,
):
    slots, tile, width = x.shape
    length = slots * tile
    half = length // 2
    groups = width // GROUP
    per = GROUP // size
    rank = downq.shape[0]
    total = (4 * rank + 8, width)
    rest = sizes[0] - 1
    lanes = width // sizes[0]
    dma = pltpu.SemaphoreType.DMA
    small = [gain, downq, downv, upq, upv, sums]

    def fold(a):
        return a.reshape(x.shape)

    def of(t):
        second = lax.div(t, groups + 3)
        return jnp.minimum(t - second * (groups + 3), groups - 1)

    def early(t):
        return jnp.minimum(t, groups - 1)

    def columns(third):
        return pl.BlockSpec((length, GROUP), lambda t: (0, of(t) + third * groups))

    return pl.pallas_call(
        functools.partial(close_kernel, size=size, strip=32, sizes=sizes),
        grid=(2 * groups + 6,),
        in_specs=[
            columns(0), columns(1), columns(2), columns(0), columns(0), columns(0),
            pl.BlockSpec((half, GROUP), lambda t: (0, early(t))),
            pl.BlockSpec((1, per, half, half), lambda t: (1 - jnp.minimum(lax.div(t, groups + 3), 1), of(t), 0, 0)),
            pl.BlockSpec((per, half, half), lambda t: (early(t), 0, 0)),
        ]
        + [ANY] * 6
        + [resident(a.shape) for a in small],
        out_specs=[ANY, ANY, pl.BlockSpec(total, lambda t: (0, 0))],
        out_shape=[
            jax.ShapeDtypeStruct(x.shape, bf16),
            jax.ShapeDtypeStruct(x.shape, bf16),
            jax.ShapeDtypeStruct(total, f32),
        ],
        scratch_shapes=[
            pltpu.VMEM((2, per * TILE, half), f32),
            pltpu.VMEM((2, per * TILE, half), bf16),
            pltpu.VMEM((2, TILE, per * 128), f32),
            pltpu.VMEM((GROUP, per * 128), bf16),
            pltpu.VMEM((2, half, GROUP), bf16),
            pltpu.VMEM((3, length, GROUP), f32),
            pltpu.VMEM((3, half, width), f32),
            pltpu.VMEM((3, length, width), bf16),
            pltpu.VMEM(x.shape, bf16),
            pltpu.VMEM(x.shape, bf16),
            pltpu.VMEM(x.shape, bf16),
            pltpu.VMEM(w.shape, bf16),
            pltpu.VMEM((4, length, rank), bf16),
            pltpu.VMEM(x.shape, bf16),
            pltpu.VMEM(total, f32),
            pltpu.VMEM((rest, total[0], lanes), f32),
            pltpu.VMEM((3, total[0], lanes), f32),
            pltpu.VMEM((2, total[0], lanes), f32),
            pltpu.VMEM(total, f32),
            dma((3,)), dma((3,)), dma((4,)), dma((4,)), dma((7,)),
            dma((rest,)), dma((rest,)), dma((2,)), dma((2,)), dma((rest,)), dma((rest,)),
        ],
        compiler_params=pltpu.CompilerParams(
            collective_id=1, has_side_effects=True, vmem_limit_bytes=62 * MIB, dimension_semantics=("arbitrary",)
        ),
        name="closing",
    )(qkv, qkv, qkv, grad, context, cd, cc, pd, pc, result, x, fold(hidden_grad), fold(normed), w, low, *small)


def finish_kernel(total_ref, a_hbm, b_hbm, aq_ref, bq_ref, av_ref, bv_ref, rms_ref, a_out, b_out, a_sc, b_sc, sem):
    rank, width = aq_ref.shape
    loads, saves = [], []
    for k, (src, kept, dst) in enumerate(((a_hbm, a_sc, a_out), (b_hbm, b_sc, b_out))):
        for s in range(src.shape[0]):
            loads.append(pltpu.make_async_copy(src.at[s], kept.at[s], sem.at[k, s, 0]))
            saves.append(pltpu.make_async_copy(kept.at[s], dst.at[s], sem.at[k, s, 1]))
    for load in loads:
        load.start()
    aq_ref[...] = total_ref[0:rank]
    av_ref[...] = total_ref[rank : 2 * rank]
    bq_ref[...] = total_ref[2 * rank : 3 * rank]
    bv_ref[...] = total_ref[3 * rank : 4 * rank]
    line = total_ref[4 * rank : 4 * rank + 1, 0:128]
    lane = lax.broadcasted_iota(jnp.int32, line.shape, 1)
    count = jnp.maximum(jnp.sum(jnp.where(lane == 2, line, 0.0)), 1.0)
    values = jnp.sqrt(line / (jnp.where(lane == 0, 1.0, 2.0) * count * width))
    for k in range(2):
        rms_ref[k] = jnp.sum(jnp.where(lane == k, values, 0.0))
    for load, save in zip(loads, saves):
        load.wait()
        save.start()
    for save in saves:
        save.wait()


def finish(total, a, b, rank):
    width = total.shape[1]
    small = jax.ShapeDtypeStruct((rank, width), f32)
    return pl.pallas_call(
        finish_kernel,
        in_specs=[VMEM, ANY, ANY],
        out_specs=[VMEM] * 4 + [pl.BlockSpec(memory_space=pltpu.SMEM), ANY, ANY],
        out_shape=[small] * 4 + [
            jax.ShapeDtypeStruct((2,), f32),
            jax.ShapeDtypeStruct(a.shape, a.dtype),
            jax.ShapeDtypeStruct(b.shape, b.dtype),
        ],
        scratch_shapes=[
            pltpu.VMEM(a.shape, a.dtype), pltpu.VMEM(b.shape, b.dtype), pltpu.SemaphoreType.DMA((2, a.shape[0], 2))
        ],
        name="finish",
    )(total, a, b)


def whole_slots(
    block_input_rows,
    document_starts,
    counted_mask,
    output_gradient,
    first_norm_gain,
    first_norm_bias,
    query_key_value_weight,
    query_down_weight,
    query_up_weight,
    value_down_weight,
    value_up_weight,
    attention_out_weight,
    second_norm_gain,
    second_norm_bias,
    feed_input_weight,
    feed_input_bias,
    feed_output_weight,
):
    sizes = (lax.axis_size("dp"), lax.axis_size("head"))
    size = block_input_rows.shape[-1] // H
    rank = query_down_weight.shape[1]
    downq = query_down_weight.T
    downv = value_down_weight.T
    x, dy, mask, normed, low, qkv, context, pd, pc, cd, cc = opening(
        block_input_rows, output_gradient, query_key_value_weight, counted_mask, document_starts,
        first_norm_gain, first_norm_bias, downq, downv, query_up_weight, value_up_weight, size,
    )
    out, hidden_grad, context_grad, sums = feed(
        x, dy, output_gradient, context, mask, attention_out_weight, second_norm_gain, second_norm_bias,
        feed_input_weight, feed_input_bias, feed_output_weight,
    )
    output, input_grad, total = closing(
        qkv, context_grad, context, cd, cc, pd, pc, out, x, hidden_grad, normed, query_key_value_weight, low,
        first_norm_gain, downq, downv, query_up_weight, value_up_weight, sums, size, sizes,
    )
    grad_aq, grad_bq, grad_av, grad_bv, rms, output, input_grad = finish(total, output, input_grad, rank)
    return output, input_grad, grad_aq.T, grad_bq, grad_av.T, grad_bv, rms


def body(*args):
    same = args[0].shape[0] == lax.axis_size("head")
    return whole_slots(*args) if same else shards(*args)


def solution(mesh):
    return jax.shard_map(
        body,
        mesh=mesh,
        in_specs=(
            P("dp", "head", None),
            P("dp", None),
            P("dp", "head"),
            P("dp", "head", None),
            P(),
            P(),
            P(),
            P(),
            P(),
            P(),
            P(),
            P(),
            P(),
            P(),
            P(),
            P(),
            P(),
        ),
        out_specs=(P("dp", "head", None), P("dp", "head", None), P(), P(), P(), P(), P()),
        check_vma=False,
    )
```

```python
import functools

import jax
import jax.numpy as jnp
from jax import lax
from jax.experimental import pallas as pl
from jax.experimental.pallas import tpu as pltpu
from jax.sharding import PartitionSpec as P

H = 16


EPSILON = 1e-05
ADAPTER_SCALE = 8.0
NEGATIVE = -1e30


def as_sent(x):

    def short(part):
        return part.astype(jnp.bfloat16) if part.dtype == jnp.float32 else part

    return jax.tree.map(short, x)


def norm_rows(matrix, gain_vec, shift_vec):
    center = matrix - jnp.mean(matrix, axis=-1, keepdims=True)
    variance = jnp.mean(center * center, axis=-1, keepdims=True)
    return center * lax.rsqrt(variance + EPSILON) * gain_vec + shift_vec


def norm_back(matrix, gain_vec, shift_vec, incoming):
    pullback = jax.vjp(lambda element_item: norm_rows(element_item, gain_vec, shift_vec), matrix)[1]
    return pullback(incoming)[0]


def gelu_tanh(matrix):
    return jax.nn.gelu(matrix, approximate=True)


def plain_product(left, right):
    return jnp.dot(left, right, preferred_element_type=jnp.float32)


def last_product(left, right):
    return lax.dot_general(
        left, right, (((1,), (1,)), ((), ())), preferred_element_type=jnp.float32
    )


def first_product(left, right):
    return lax.dot_general(
        left, right, (((0,), (0,)), ((), ())), preferred_element_type=jnp.float32
    )


def masked_scores(query_block, key_slot, segments, row_start, row_end, score_scale):
    places = jnp.arange(row_end)
    allowed = (segments[row_start:row_end, None] == segments[None, :row_end]) & (
        places[None, :] <= places[row_start:row_end, None]
    )
    scores = (
        jnp.einsum(
            "qhd,khd->hqk", query_block, key_slot[:row_end], preferred_element_type=jnp.float32
        )
        * score_scale
    )
    return jnp.where(allowed[None], scores, NEGATIVE)


def attend_slot(query_slot, key_slot, value_slot, segments, block_rows, score_scale):
    length = query_slot.shape[0]
    outputs_list = []
    logsum_list = []
    for block_index in range(length // block_rows):
        row_start = block_index * block_rows
        row_end = row_start + block_rows
        scores = masked_scores(
            query_slot[row_start:row_end], key_slot, segments, row_start, row_end, score_scale
        )
        row_max = jnp.max(scores, axis=-1, keepdims=True)
        exponent = jnp.exp(scores - row_max)
        row_total = jnp.sum(exponent, axis=-1, keepdims=True)
        probability = (exponent / row_total).astype(jnp.bfloat16)
        context = jnp.einsum(
            "hqk,khd->qhd", probability, value_slot[:row_end], preferred_element_type=jnp.float32
        )
        outputs_list.append(context.astype(jnp.bfloat16))
        logsum_list.append((row_max + jnp.log(row_total))[..., 0])
    return (jnp.concatenate(outputs_list, 0), jnp.concatenate(logsum_list, 1))


def attend_back(
    query_slot, key_slot, value_slot, grad_slot, logsum, segments, block_rows, score_scale
):
    length = query_slot.shape[0]
    key_grad = jnp.zeros(key_slot.shape, jnp.float32)
    value_gradient = jnp.zeros(value_slot.shape, jnp.float32)
    query_parts = []
    for block_index in range(length // block_rows):
        row_start = block_index * block_rows
        row_end = row_start + block_rows
        query_block = query_slot[row_start:row_end]
        grad_block = grad_slot[row_start:row_end]
        scores = masked_scores(query_block, key_slot, segments, row_start, row_end, score_scale)
        probability = jnp.exp(scores - logsum[:, row_start:row_end, None])
        prob_grad = jnp.einsum(
            "qhd,khd->hqk", grad_block, value_slot[:row_end], preferred_element_type=jnp.float32
        )
        inner_sum = jnp.sum(probability * prob_grad, axis=-1, keepdims=True)
        score_grad = (probability * (prob_grad - inner_sum)).astype(jnp.bfloat16)
        query_parts.append(
            jnp.einsum(
                "hqk,khd->qhd", score_grad, key_slot[:row_end], preferred_element_type=jnp.float32
            )
            * score_scale
        )
        key_grad = key_grad.at[:row_end].add(
            jnp.einsum("hqk,qhd->khd", score_grad, query_block, preferred_element_type=jnp.float32)
            * score_scale
        )
        value_gradient = value_gradient.at[:row_end].add(
            jnp.einsum(
                "hqk,qhd->khd",
                probability.astype(jnp.bfloat16),
                grad_block,
                preferred_element_type=jnp.float32,
            )
        )
    query_gradient = jnp.concatenate(query_parts, 0)
    return (
        query_gradient.astype(jnp.bfloat16),
        key_grad.astype(jnp.bfloat16),
        value_gradient.astype(jnp.bfloat16),
    )


def shards(
    block_input_rows,
    document_starts,
    counted_mask,
    output_gradient,
    first_norm_gain,
    first_norm_bias,
    query_key_value_weight,
    query_down_weight,
    query_up_weight,
    value_down_weight,
    value_up_weight,
    attention_out_weight,
    second_norm_gain,
    second_norm_bias,
    feed_input_weight,
    feed_input_bias,
    feed_output_weight,
):
    slot_count, local_len, row_width = block_input_rows.shape
    groups = lax.axis_size("head")
    full_len = local_len * groups
    head_size = row_width // H
    heads_here = H // groups
    row_count = slot_count * local_len
    block_rows = min(512, full_len)
    score_scale = head_size ** (-0.5)
    gain_one = first_norm_gain.astype(jnp.float32)
    shift_one = first_norm_bias.astype(jnp.float32)
    gain_two = second_norm_gain.astype(jnp.float32)
    shift_two = second_norm_bias.astype(jnp.float32)
    fc_bias = feed_input_bias.astype(jnp.float32)
    local_shape = (slot_count, local_len, row_width)
    split_shape = (slot_count, full_len, heads_here, head_size)
    merged_shape = (slot_count, full_len, heads_here * head_size)
    flat_in = block_input_rows.reshape(row_count, row_width).astype(jnp.float32)
    normed_rows = norm_rows(flat_in, gain_one, shift_one).astype(jnp.bfloat16)
    query_low_rank = plain_product(normed_rows, query_down_weight).astype(jnp.bfloat16)
    value_low_rank = plain_product(normed_rows, value_down_weight).astype(jnp.bfloat16)
    projected_rows = plain_product(normed_rows, query_key_value_weight)
    query_rows = (
        projected_rows[:, :row_width]
        + ADAPTER_SCALE * plain_product(query_low_rank, query_up_weight)
    ).astype(jnp.bfloat16)
    key_rows = projected_rows[:, row_width : 2 * row_width].astype(jnp.bfloat16)
    value_matrix = (
        projected_rows[:, 2 * row_width :]
        + ADAPTER_SCALE * plain_product(value_low_rank, value_up_weight)
    ).astype(jnp.bfloat16)
    head_query, head_key, head_value = (
        lax.all_to_all(
            query_rows.reshape(local_shape), "head", split_axis=2, concat_axis=1, tiled=True
        ),
        lax.all_to_all(
            key_rows.reshape(local_shape), "head", split_axis=2, concat_axis=1, tiled=True
        ),
        lax.all_to_all(
            value_matrix.reshape(local_shape), "head", split_axis=2, concat_axis=1, tiled=True
        ),
    )
    head_query = head_query.reshape(split_shape)
    head_key = head_key.reshape(split_shape)
    head_value = head_value.reshape(split_shape)

    def slot_fn(packed):
        return attend_slot(packed[0], packed[1], packed[2], packed[3], block_rows, score_scale)

    context_heads, logsum = lax.map(slot_fn, (head_query, head_key, head_value, document_starts))
    context_local = lax.all_to_all(
        as_sent(context_heads.reshape(merged_shape)),
        "head",
        split_axis=1,
        concat_axis=2,
        tiled=True,
    )
    context_flat = context_local.reshape(row_count, row_width)
    branch = plain_product(context_flat, attention_out_weight)
    hidden_state = flat_in + branch
    normed_two = norm_rows(hidden_state, gain_two, shift_two).astype(jnp.bfloat16)
    before = plain_product(normed_two, feed_input_weight) + fc_bias
    activated = gelu_tanh(before).astype(jnp.bfloat16)
    feed_out = plain_product(activated, feed_output_weight)
    result = hidden_state + feed_out
    output = result.astype(jnp.bfloat16).reshape(block_input_rows.shape)
    valid_rows = counted_mask.reshape(row_count).astype(jnp.float32)[:, None]
    square_sums = jnp.stack(
        [
            jnp.sum(valid_rows * result * result),
            jnp.sum(valid_rows * (branch * branch + feed_out * feed_out)),
            jnp.sum(valid_rows),
        ]
    )
    grad_flat = output_gradient.reshape(row_count, row_width)
    act_grad = last_product(grad_flat, feed_output_weight)
    gelu_pull = jax.vjp(gelu_tanh, before)[1]
    before_grad = gelu_pull(act_grad)[0].astype(jnp.bfloat16)
    normed_two_grad = last_product(before_grad, feed_input_weight)
    hidden_grad = grad_flat.astype(jnp.float32) + norm_back(
        hidden_state, gain_two, shift_two, normed_two_grad
    )
    branch_grad = hidden_grad.astype(jnp.bfloat16)
    context_grad = last_product(branch_grad, attention_out_weight).astype(jnp.bfloat16)
    grad_heads = lax.all_to_all(
        context_grad.reshape(local_shape), "head", split_axis=2, concat_axis=1, tiled=True
    ).reshape(split_shape)

    def back_fn(packed):
        return attend_back(
            packed[0],
            packed[1],
            packed[2],
            packed[3],
            packed[4],
            packed[5],
            block_rows,
            score_scale,
        )

    query_gradient, key_grad, value_gradient = lax.map(
        back_fn, (head_query, head_key, head_value, grad_heads, logsum, document_starts)
    )
    query_gradient, key_grad, value_gradient = (
        lax.all_to_all(
            as_sent(query_gradient.reshape(merged_shape)),
            "head",
            split_axis=1,
            concat_axis=2,
            tiled=True,
        ),
        lax.all_to_all(
            as_sent(key_grad.reshape(merged_shape)), "head", split_axis=1, concat_axis=2, tiled=True
        ),
        lax.all_to_all(
            as_sent(value_gradient.reshape(merged_shape)),
            "head",
            split_axis=1,
            concat_axis=2,
            tiled=True,
        ),
    )
    query_gradient = query_gradient.reshape(row_count, row_width)
    key_grad = key_grad.reshape(row_count, row_width)
    value_gradient = value_gradient.reshape(row_count, row_width)
    query_low_gradient = (ADAPTER_SCALE * last_product(query_gradient, query_up_weight)).astype(
        jnp.bfloat16
    )
    value_low_gradient = (ADAPTER_SCALE * last_product(value_gradient, value_up_weight)).astype(
        jnp.bfloat16
    )
    joined_grads = jnp.concatenate([query_gradient, key_grad, value_gradient], axis=1)
    normed_grad = (
        last_product(joined_grads, query_key_value_weight)
        + last_product(query_low_gradient, query_down_weight)
        + last_product(value_low_gradient, value_down_weight)
    )
    input_grad = hidden_grad + norm_back(flat_in, gain_one, shift_one, normed_grad)
    down_query = first_product(normed_rows, query_low_gradient)
    lifted_query = ADAPTER_SCALE * first_product(query_low_rank, query_gradient)
    down_value = first_product(normed_rows, value_low_gradient)
    lifted_value = ADAPTER_SCALE * first_product(value_low_rank, value_gradient)
    totals = lax.psum(
        (down_query, lifted_query, down_value, lifted_value, square_sums), ("dp", "head")
    )
    token_count = jnp.maximum(totals[4][2], 1.0)
    rms_values = jnp.stack(
        [
            jnp.sqrt(totals[4][0] / (token_count * row_width)),
            jnp.sqrt(totals[4][1] / (2.0 * token_count * row_width)),
        ]
    )
    return (
        output,
        input_grad.astype(jnp.bfloat16).reshape(block_input_rows.shape),
        totals[0],
        totals[1],
        totals[2],
        totals[3],
        rms_values,
    )


LOG2E = 1.4426950408889634
TILE = 256
GROUP = 256
bf16 = jnp.bfloat16
f32 = jnp.float32
NT = (((1,), (1,)), ((), ()))
NN = (((1,), (0,)), ((), ()))
TN = (((0,), (0,)), ((), ()))
MESH = pl.DeviceIdType.MESH
MIB = 2**20


def dg(left, right, dims):
    return lax.dot_general(left, right, dims, preferred_element_type=f32)


def resident(shape):
    zeros = (0,) * len(shape)
    return pl.BlockSpec(shape, lambda *_: zeros, pipeline_mode=pl.Buffered(1))


def params(mib):
    return pltpu.CompilerParams(
        vmem_limit_bytes=mib * MIB, dimension_semantics=("arbitrary",)
    )


def norm_stats(rows):
    center = rows - jnp.mean(rows, axis=-1, keepdims=True)
    rs = lax.rsqrt(jnp.mean(center * center, axis=-1, keepdims=True) + EPSILON)
    return center * rs, rs


def norm_grad(unit, rs, gain, incoming):
    t = incoming * gain
    return (
        t - jnp.mean(t, axis=-1, keepdims=True) - unit * jnp.mean(t * unit, axis=-1, keepdims=True)
    ) * rs


def head_masks(x, heads, size):
    lane = lax.broadcasted_iota(jnp.int32, x.shape, 1)
    return [
        jnp.where((lane >= size * h) & (lane < size * (h + 1)), x, jnp.zeros_like(x))
        for h in range(heads)
    ]


def merge_heads(stacked, heads, size):
    rows = stacked.shape[0] // heads
    out = stacked[:rows]
    lane = lax.broadcasted_iota(jnp.int32, out.shape, 1)
    for h in range(1, heads):
        out = jnp.where(lane >= size * h, stacked[h * rows : (h + 1) * rows], out)
    return out


def column(line):
    return jnp.broadcast_to(line, (128, line.shape[1])).T


def entry_signal(peers):
    barrier = pltpu.get_barrier_semaphore()
    for peer in peers:
        pl.semaphore_signal(barrier, inc=1, device_id=peer, device_id_type=MESH)


def entry_wait(count):
    pl.semaphore_wait(pltpu.get_barrier_semaphore(), count)


def remote(src, dst, send_sem, recv_sem, peer):
    return pltpu.make_async_remote_copy(
        src_ref=src, dst_ref=dst, send_sem=send_sem, recv_sem=recv_sem, device_id=peer, device_id_type=MESH
    )


ANY = pl.BlockSpec(memory_space=pl.ANY)
VMEM = pl.BlockSpec(memory_space=pltpu.VMEM)


def line(ref):
    return ref[...].astype(f32).reshape(1, -1)


def rows_at(base, offset, count):
    return pl.ds(pl.multiple_of(base + offset, TILE), count)


def lanes_of(columns, width):
    size = width // len(columns)
    shape = (columns[0].shape[0], width)
    lane = lax.broadcasted_iota(jnp.int32, shape, 1)
    out = jnp.broadcast_to(columns[0], shape)
    for h in range(1, len(columns)):
        out = jnp.where(lane >= size * h, columns[h], out)
    return out


def pipelined(units, stages):
    for t in range(len(units) + len(stages) - 1):
        for b, stage in enumerate(stages):
            if 0 <= t - b < len(units):
                stage(t - b, units[t - b])


def open_kernel(
    x_ref, dy_ref, w_ref, mask_ref, start_ref, gain_ref, shift_ref, downq_ref, downv_ref, upq_ref, upv_ref,
    xs_ref, dys_ref, masks_ref, normed_ref, low_ref, qkv_ref, ctx_ref, pd_ref, pc_ref, cd_ref, cc_ref,
    x_sc, y_sc, w_sc, mask_sc, normed_sc, low_sc, qkv_sc, s_sc, diag_sc, cross_sc, first_sc, near_sc, state, part,
    x_send, x_recv, y_send, y_recv, m_send, m_recv, local_sem,
    *, size, strip,
):
    slots, tile, width = x_ref.shape
    length = slots * tile
    half = length // 2
    groups = width // GROUP
    heads = GROUP // size
    step = pl.program_id(0)
    middle = groups + 1
    group, me = lax.axis_index("dp"), lax.axis_index("head")
    mine = lax.rem(me, 2)
    near = me - mine
    far = slots // 2 - near
    beside = near + 1 - mine
    across = (far + mine, far + 1 - mine)
    peers = [(group, p) for p in (beside,) + across]

    def x_copy(k):
        return remote(x_ref.at[peers[k][1]], x_sc.at[me], x_send.at[k], x_recv.at[k], peers[k])

    def y_copy(k):
        landing = y_sc.at[mine] if k == 0 else dys_ref.at[me]
        return remote(dy_ref.at[peers[k][1]], landing, y_send.at[k], y_recv.at[k], peers[k])

    def m_copy(k):
        return remote(mask_sc.at[peers[k][1]], masks_ref.at[me], m_send.at[k], m_recv.at[k], peers[k])

    def own_x():
        return pltpu.make_async_copy(x_ref.at[me], x_sc.at[me], local_sem.at[0])

    def own_y():
        return pltpu.make_async_copy(dy_ref.at[me], y_sc.at[mine], local_sem.at[1])

    def own_m():
        return pltpu.make_async_copy(mask_sc.at[me], masks_ref.at[me], local_sem.at[2])

    def weight():
        return pltpu.make_async_copy(w_ref, w_sc, local_sem.at[3])

    def save_x():
        return pltpu.make_async_copy(x_sc, xs_ref, local_sem.at[4])

    def save_y():
        return pltpu.make_async_copy(y_sc, dys_ref.at[pl.ds(near, 2)], local_sem.at[7])

    def save_normed():
        return pltpu.make_async_copy(normed_sc, normed_ref, local_sem.at[5])

    def save_low():
        return pltpu.make_async_copy(low_sc, low_ref, local_sem.at[8])

    def save_qkv():
        return pltpu.make_async_copy(qkv_sc, qkv_ref, local_sem.at[6])

    @pl.when(step == 0)
    def _():
        entry_signal(peers)
        own_x().start()
        weight().start()
        own_y().start()
        for s in range(slots):
            mask_sc[s] = jnp.broadcast_to(mask_ref[s : s + 1, :].astype(f32), mask_sc.shape[1:])
        own_m().start()
        entry_wait(len(peers))
        for k in (1, 2, 0):
            x_copy(k).start()
        for k in range(3):
            m_copy(k).start()
        first_sc[...] = column(start_ref[pl.ds(me, 1), :])

        def bias(i, carry):
            here = pl.ds(pl.multiple_of(i * strip, strip), strip)
            base = half * lax.div(i * strip, half)
            keys = lax.broadcasted_iota(jnp.int32, (strip, half), 1) + base
            rows = lax.broadcasted_iota(jnp.int32, (strip, half), 0) + i * strip
            allowed = (keys >= first_sc[here, 0:1]) & (keys <= rows)
            diag_sc[here, :] = jnp.where(allowed, 0.0, NEGATIVE)
            return carry

        lax.fori_loop(0, length // strip, bias, 0)

        def cross_bias(i, carry):
            here = pl.ds(pl.multiple_of(i * strip, strip), strip)
            keys = lax.broadcasted_iota(jnp.int32, (strip, half), 1)
            rows = pl.ds(pl.multiple_of(half + i * strip, strip), strip)
            cross_sc[here, :] = jnp.where(keys >= first_sc[rows, 0:1], 0.0, NEGATIVE)
            return carry

        lax.fori_loop(0, half // strip, cross_bias, 0)
        y_copy(0).start()
        own_x().wait()
        x_copy(0).wait_recv()
        weight().wait()

    @pl.when(step == groups + 1)
    def _():
        own_y().wait()
        y_copy(0).wait_recv()
        save_y().start()
        x_copy(1).wait()
        x_copy(2).wait()
        y_copy(1).start()
        save_x().start()

    @pl.when(lax.rem(step, middle) == 0)
    def _():
        first = near + (far - near) * lax.div(step, middle)
        unit, _ = norm_stats(x_sc[pl.ds(first, 2)].reshape(half, width).astype(f32))
        normed = (unit * line(gain_ref) + line(shift_ref)).astype(bf16)
        here = pl.ds(pl.multiple_of(first * tile, tile), half)
        normed_sc[here, :] = normed
        low_q = dg(normed, downq_ref[...], NT).astype(bf16)
        low_v = dg(normed, downv_ref[...], NT).astype(bf16)
        low_sc[0, here, :] = low_q
        low_sc[1, here, :] = low_v
        scale = size**-0.5
        wide = 512
        for at in range(0, 3 * width, wide):
            cols = slice(at, at + wide)
            piece = dg(normed, w_sc[:, cols], NN)
            if at < width:
                piece = (piece + ADAPTER_SCALE * dg(low_q, upq_ref[:, cols], NN)) * scale
            if at >= 2 * width:
                piece = piece + ADAPTER_SCALE * dg(low_v, upv_ref[:, at - 2 * width : at - 2 * width + wide], NN)
            qkv_sc[here, cols] = piece.astype(bf16)

    @pl.when(step == middle)
    def _():
        save_normed().start()
        save_low().start()
        save_qkv().start()

    def attention(g, units):
        def third(k):
            return qkv_sc.at[:, pl.ds(pl.multiple_of(k * width + g * GROUP, GROUP), GROUP)]

        q_ref, k_ref, v_ref = third(0), third(1), third(2)

        def scores(at, unit):
            i, n, q_base, k_base = unit[:4]
            masked = jnp.concatenate(head_masks(q_ref[rows_at(q_base, i * TILE, TILE), :], heads, size), 0)
            for j in range(0, n, TILE):
                s_sc[at % 2, :, j : j + TILE] = dg(masked, k_ref[rows_at(k_base, j, TILE), :], NT)

        def soft(at, unit):
            i, n, q_base, _, bias, probs, (_, keep_m, keep_l, keep_row) = unit
            tops, sums = [], []
            for r in range(0, TILE, strip):
                tops.append([])
                sums.append([])
                for h in range(heads):
                    here = h * TILE + r
                    s = s_sc[at % 2, here : here + strip, 0:n] * LOG2E + bias(i * TILE + r, n)
                    top = jnp.max(s, axis=1, keepdims=True)
                    e = jnp.exp2(s - top)
                    tops[-1].append(top)
                    sums[-1].append(jnp.sum(e, axis=1, keepdims=True))
                    probs[h, i * TILE + r : i * TILE + r + strip, 0:n] = e.astype(bf16)
                where = pl.ds(pl.multiple_of(keep_row + i * TILE + r, strip), strip)
                keep_m[where, :] = lanes_of(tops[-1], GROUP)
                keep_l[where, :] = lanes_of(sums[-1], GROUP)

        def mix(at, unit):
            i, n, _, k_base, _, probs, (keep_o, _, _, keep_row) = unit
            stacked = probs[:, i * TILE : (i + 1) * TILE, 0:n].reshape(heads * TILE, n)
            merged = merge_heads(dg(stacked, v_ref[rows_at(k_base, 0, n), :], NN), heads, size)
            keep_o[rows_at(keep_row, i * TILE, TILE), :] = merged

        pipelined(units, (scores, soft, mix))

    def diag_units(base, keep, keep_row):
        def bias(r, n):
            return diag_sc[pl.ds(pl.multiple_of(base + r, strip), strip), 0:n]

        kept = (*keep, keep_row)
        return [(i, (i + 1) * TILE, base, base, bias, pd_ref.at[0], kept) for i in range(half // TILE)]

    def cross_units():
        def bias(r, n):
            return cross_sc[r : r + strip, 0:n]

        return [
            (i, half, half, 0, bias, pc_ref, (part.at[0], part.at[1], part.at[2], 0)) for i in range(half // TILE)
        ]

    @pl.when((step > 0) & (step <= groups))
    def _():
        cols = pl.ds(pl.multiple_of((step - 1) * GROUP, GROUP), GROUP)
        attention(step - 1, diag_units(near * tile, [near_sc.at[a, :, cols] for a in range(3)], 0))

    @pl.when(step > middle)
    def _():
        g = step - middle - 1
        cols = pl.ds(pl.multiple_of(g * GROUP, GROUP), GROUP)
        near_rows = rows_at(near * tile, 0, half)
        for a in range(3):
            state[a, near_rows, :] = near_sc[a, :, cols]
        far_units = diag_units(far * tile, [state.at[a] for a in range(3)], far * tile)
        attention(g, far_units + cross_units())
        inverse = 1.0 / state[2, 0:half]
        cd_ref[0:half] = inverse
        ctx_ref[0:half] = (state[0, 0:half] * inverse).astype(bf16)
        for r in range(0, half, TILE):
            high = slice(half + r, half + r + TILE)
            here = slice(r, r + TILE)
            top = jnp.maximum(state[1, high], part[1, here])
            weight_d = jnp.exp2(state[1, high] - top)
            weight_c = jnp.exp2(part[1, here] - top)
            inverse = 1.0 / (weight_d * state[2, high] + weight_c * part[2, here])
            weight_d = weight_d * inverse
            weight_c = weight_c * inverse
            cd_ref[high] = weight_d
            cc_ref[here] = weight_c
            ctx_ref[high] = (state[0, high] * weight_d + part[0, here] * weight_c).astype(bf16)

    @pl.when(step == middle + groups)
    def _():
        x_copy(0).wait_send()
        y_copy(0).wait_send()
        y_copy(1).wait()
        for k in range(3):
            m_copy(k).wait()
        own_m().wait()
        save_x().wait()
        save_y().wait()
        save_normed().wait()
        save_low().wait()
        save_qkv().wait()


def opening(x, dy, w, mask, start, gain, shift, downq, downv, upq, upv, size):
    slots, tile, width = x.shape
    length = slots * tile
    half = length // 2
    groups = width // GROUP
    per = GROUP // size
    dma = pltpu.SemaphoreType.DMA
    small = [mask, start, gain, shift, downq, downv, upq, upv]
    masks = (slots, 8, tile)

    middle = groups + 1

    def late(t):
        return jnp.maximum(t - middle - 1, 0)

    def diag_at(t):
        second = lax.div(t, middle + 1)
        return second, jnp.where(second == 1, t - middle - 1, jnp.clip(t - 1, 0, groups - 1)), 0, 0

    return pl.pallas_call(
        functools.partial(open_kernel, size=size, strip=32),
        grid=(middle + groups + 1,),
        in_specs=[ANY] * 3 + [resident(a.shape) for a in small],
        out_specs=[ANY] * 6 + [
            pl.BlockSpec((length, GROUP), lambda t: (0, late(t))),
            pl.BlockSpec((1, per, half, half), diag_at),
            pl.BlockSpec((per, half, half), lambda t: (late(t), 0, 0)),
            pl.BlockSpec((length, GROUP), lambda t: (0, late(t))),
            pl.BlockSpec((half, GROUP), lambda t: (0, late(t))),
        ],
        out_shape=[
            jax.ShapeDtypeStruct(x.shape, bf16),
            jax.ShapeDtypeStruct(x.shape, bf16),
            jax.ShapeDtypeStruct(masks, f32),
            jax.ShapeDtypeStruct((length, width), bf16),
            jax.ShapeDtypeStruct((2, length, downq.shape[0]), bf16),
            jax.ShapeDtypeStruct((length, 3 * width), bf16),
            jax.ShapeDtypeStruct((length, width), bf16),
            jax.ShapeDtypeStruct((2, per * groups, half, half), bf16),
            jax.ShapeDtypeStruct((per * groups, half, half), bf16),
            jax.ShapeDtypeStruct((length, width), f32),
            jax.ShapeDtypeStruct((half, width), f32),
        ],
        scratch_shapes=[
            pltpu.VMEM(x.shape, bf16),
            pltpu.VMEM((2, tile, width), bf16),
            pltpu.VMEM(w.shape, bf16),
            pltpu.VMEM(masks, f32),
            pltpu.VMEM((length, width), bf16),
            pltpu.VMEM((2, length, downq.shape[0]), bf16),
            pltpu.VMEM((length, 3 * width), bf16),
            pltpu.VMEM((2, per * TILE, half), f32),
            pltpu.VMEM((length, half), f32),
            pltpu.VMEM((half, half), f32),
            pltpu.VMEM((length, 128), jnp.int32),
            pltpu.VMEM((3, half, width), f32),
            pltpu.VMEM((3, length, GROUP), f32),
            pltpu.VMEM((3, half, GROUP), f32),
            dma((3,)), dma((3,)), dma((3,)), dma((3,)), dma((3,)), dma((3,)), dma((9,)),
        ],
        compiler_params=pltpu.CompilerParams(
            collective_id=0, has_side_effects=True, vmem_limit_bytes=62 * MIB, dimension_semantics=("arbitrary",)
        ),
        name="opening",
    )(x, dy, w, *small)


def feed_kernel(
    x_hbm, y_hbm, dy_hbm, ctx_hbm, wo_hbm, wi_hbm, wf_hbm, mask_ref, gain_ref, shift_ref, bias_ref,
    out_hbm, hg_hbm, cg_hbm, sums_ref,
    x_sc, y_sc, ctx_sc, wo_ref, wi_ref, wf_ref, normed, feed_sc, grad_sc, v_sc, g_sc,
    out_sc, hg_sc, cg_sc, load_sem, chunk_sem, save_sem, y_send, y_recv,
    *, step,
):
    slots, tile, width = x_hbm.shape
    rows = slots // 2 * tile
    chunks = wi_ref.shape[1] // step
    group, me = lax.axis_index("dp"), lax.axis_index("head")
    mine = lax.rem(me, 2)
    near = me - mine
    far = slots // 2 - near
    across = (far + mine, far + 1 - mine)
    peer = (group, across[1])
    half = pl.program_id(0)
    first = half == 0

    def base(h):
        return near + (far - near) * h

    def slabs(ref, h):
        return ref.at[pl.ds(base(h), 2)]

    def load_x(h):
        return pltpu.make_async_copy(slabs(x_hbm, h), x_sc.at[h], load_sem.at[h, 0])

    def load_ctx(h):
        return pltpu.make_async_copy(slabs(ctx_hbm, h), ctx_sc.at[h], load_sem.at[h, 1])

    def load_y(h):
        if h == 0:
            return pltpu.make_async_copy(slabs(y_hbm, 0), y_sc.at[0], load_sem.at[0, 2])
        return pltpu.make_async_copy(y_hbm.at[across[0]], y_sc.at[1, mine], load_sem.at[1, 2])

    def take_y():
        return remote(dy_hbm.at[across[1]], y_sc.at[1, mine], y_send, y_recv, peer)

    def load_o():
        return pltpu.make_async_copy(wo_hbm, wo_ref, load_sem.at[0, 3])

    def cols_of(c):
        return pl.ds(c * step if isinstance(c, int) else pl.multiple_of(c * step, step), step)

    def twice(c):
        return pl.ds(2 * c * step if isinstance(c, int) else pl.multiple_of(2 * c * step, 2 * step), 2 * step)

    def load_i(c):
        return pltpu.make_async_copy(wi_hbm.at[:, twice(c)], wi_ref.at[:, twice(c)], chunk_sem.at[0, c])

    def load_f(c):
        return pltpu.make_async_copy(wf_hbm.at[twice(c), :], wf_ref.at[twice(c), :], chunk_sem.at[1, c])

    @pl.when(first)
    def _():
        entry_signal([peer])
        load_o().start()
        load_ctx(0).start()
        load_x(0).start()
        load_y(0).start()
        for c in range(chunks // 2):
            load_i(c).start()
            load_f(c).start()
        load_y(1).start()
        load_ctx(1).start()
        load_x(1).start()
        sums_ref[...] = jnp.zeros_like(sums_ref)
        load_o().wait()
        load_ctx(0).wait()
        load_x(0).wait()

    gain = line(gain_ref)
    c0 = 0.7978845608028654
    c1 = c0 * 0.044715
    branch = dg(ctx_sc[half].reshape(rows, width), wo_ref[...], NN)
    whole = x_sc[half].reshape(rows, width).astype(f32) + branch
    unit, rs = norm_stats(whole)
    normed[...] = (unit * gain + line(shift_ref)).astype(bf16)

    def enter(c, slot):
        cols = cols_of(c)
        v_sc[slot] = dg(normed[...], wi_ref[:, cols], NN) + bias_ref[cols].astype(f32).reshape(1, step)
        g_sc[slot] = dg(y_sc[half].reshape(rows, width), wf_ref[cols, :], NT)

    def leave(c, slot):
        cols = cols_of(c)
        v = v_sc[slot]
        square = v * v
        side = 0.5 * jnp.tanh(v * (c0 + c1 * square)) + 0.5
        act = v * side
        slope = side + act * (1.0 - side) * (2.0 * c0 + 6.0 * c1 * square)
        feed_sc[...] += dg(act.astype(bf16), wf_ref[cols, :], NN)
        grad_sc[...] += dg((slope * g_sc[slot]).astype(bf16), wi_ref[:, cols], NT)

    def wait_weights(c):
        @pl.when(first)
        def _():
            load_i(c).wait()
            load_f(c).wait()

    @pl.when(first)
    def _():
        load_y(0).wait()
        load_i(0).wait()
        load_f(0).wait()

    @pl.when(half == 1)
    def _():
        take_y().wait()

    feed_sc[...] = jnp.zeros_like(feed_sc)
    grad_sc[...] = jnp.zeros_like(grad_sc)
    enter(0, 0)

    @pl.when(first)
    def _():
        entry_wait(1)
        take_y().start()

    def pair(i, carry):
        wait_weights(i + 1)
        enter(2 * i + 1, 1)
        leave(2 * i, 0)
        enter(2 * i + 2, 0)
        leave(2 * i + 1, 1)
        return carry

    lax.fori_loop(0, chunks // 2 - 1, pair, 0)
    enter(chunks - 1, 1)
    leave(chunks - 2, 0)
    leave(chunks - 1, 1)
    feed = feed_sc[...]
    result = whole + feed
    out_sc[half] = result.astype(bf16).reshape(out_sc.shape[1:])
    valid = jnp.concatenate([column(mask_ref[base(half) + b, 0:1, :])[:, 0:1] for b in range(2)], 0)
    one = jnp.sum(valid * jnp.sum(result * result, axis=1, keepdims=True))
    two = jnp.sum(valid * jnp.sum(branch * branch + feed * feed, axis=1, keepdims=True))
    count = jnp.sum(valid)
    row = lax.broadcasted_iota(jnp.int32, sums_ref.shape, 0)
    col = lax.broadcasted_iota(jnp.int32, sums_ref.shape, 1)
    total = jnp.where(col == 0, one, jnp.where(col == 1, two, jnp.where(col == 2, count, 0.0)))
    sums_ref[...] += jnp.where(row == 0, total, 0.0)
    dy = y_sc[half].reshape(rows, width).astype(f32)
    low = (dy + norm_grad(unit, rs, gain, grad_sc[...])).astype(bf16)
    hg_sc[half] = low.reshape(hg_sc.shape[1:])
    cg_sc[half] = dg(low, wo_ref[...], NT).astype(bf16)

    def saves(h):
        flat = pl.ds(pl.multiple_of(base(h) * tile, tile), rows)
        return [
            pltpu.make_async_copy(out_sc.at[h], slabs(out_hbm, h), save_sem.at[h, 0]),
            pltpu.make_async_copy(hg_sc.at[h], slabs(hg_hbm, h), save_sem.at[h, 1]),
            pltpu.make_async_copy(cg_sc.at[h], cg_hbm.at[flat, :], save_sem.at[h, 2]),
        ]

    for copy in saves(half):
        copy.start()

    @pl.when(first)
    def _():
        load_y(1).wait()
        load_ctx(1).wait()
        load_x(1).wait()

    @pl.when(half == 1)
    def _():
        for copy in saves(0) + saves(1):
            copy.wait()


def feed(x, y, dy, context, mask, wo, gain, shift, wi, bias, wf):
    slots, tile, width = x.shape
    rows = slots // 2 * tile
    units = wi.shape[1]
    step = 512
    chunks = units // step
    pair = (2, 2, tile, width)
    dma = pltpu.SemaphoreType.DMA
    return pl.pallas_call(
        functools.partial(feed_kernel, step=step),
        grid=(2,),
        in_specs=[ANY] * 7 + [resident(a.shape) for a in (mask, gain, shift, bias)],
        out_specs=[ANY] * 3 + [pl.BlockSpec((8, width), lambda h: (0, 0))],
        out_shape=[jax.ShapeDtypeStruct(x.shape, bf16)] * 2 + [
            jax.ShapeDtypeStruct((2 * rows, width), bf16), jax.ShapeDtypeStruct((8, width), f32)
        ],
        scratch_shapes=[pltpu.VMEM(pair, bf16)] * 3 + [
            pltpu.VMEM(wo.shape, bf16), pltpu.VMEM(wi.shape, bf16), pltpu.VMEM(wf.shape, bf16),
            pltpu.VMEM((rows, width), bf16),
            pltpu.VMEM((rows, width), f32), pltpu.VMEM((rows, width), f32),
            pltpu.VMEM((2, rows, step), f32), pltpu.VMEM((2, rows, step), f32),
            pltpu.VMEM(pair, bf16), pltpu.VMEM(pair, bf16), pltpu.VMEM((2, rows, width), bf16),
            dma((2, 4)), dma((2, chunks // 2)), dma((2, 3)), dma, dma,
        ],
        compiler_params=pltpu.CompilerParams(
            collective_id=2, has_side_effects=True, vmem_limit_bytes=62 * MIB, dimension_semantics=("arbitrary",)
        ),
        name="feed",
    )(x, y, dy, context.reshape(x.shape), wo, wi, wf, mask, gain, shift, bias)


def close_kernel(
    q_ref, k_ref, v_ref, g_ref, o_ref, cd_ref, cc_ref, pd_ref, pc_ref,
    res_hbm, x_hbm, hg_hbm, normed_hbm, w_hbm, low_hbm,
    gain_ref, downq_ref, downv_ref, upq_ref, upv_ref, sums_ref,
    result_ref, out_ref, total_ref,
    dp_sc, ds_sc, inner_sc, ones_sc, do_sc, loc, near_sc, grads, x_sc, hg_sc, normed_sc, w_sc, low_sc, res_sc,
    sums, parts, chunk, heard, total_sc,
    r_send, r_recv, send, recv, local_sem, part_send, part_recv, pair_send, pair_recv, mean_send, mean_recv,
    *, size, strip, sizes,
):
    slots, tile, width = x_sc.shape
    length = slots * tile
    half = length // 2
    groups = width // GROUP
    heads = GROUP // size
    rank = downq_ref.shape[0]
    step = pl.program_id(0)
    last = 2 * groups + 5
    group, me = lax.axis_index("dp"), lax.axis_index("head")
    mine = lax.rem(me, 2)
    near = me - mine
    far = slots // 2 - near
    beside = near + 1 - mine
    peers = [(group, p) for p in (far + mine, far + 1 - mine, beside)]
    rest = [(lax.rem(group + k, sizes[0]), me) for k in range(1, sizes[0])]
    lanes = width // sizes[0]

    def own_result():
        return pltpu.make_async_copy(res_hbm.at[me], result_ref.at[me], local_sem.at[0])

    def result_copy(k):
        return remote(res_hbm.at[peers[k][1]], result_ref.at[me], r_send.at[k], r_recv.at[k], peers[k])

    def loads():
        return [
            pltpu.make_async_copy(src, dst, local_sem.at[1 + a])
            for a, (src, dst) in enumerate(
                [(x_hbm, x_sc), (hg_hbm, hg_sc), (normed_hbm, normed_sc), (w_hbm, w_sc), (low_hbm, low_sc.at[0:2])]
            )
        ]

    @pl.when(step == 0)
    def _():
        entry_signal(peers + rest)
        own_result().start()
        for copy in loads():
            copy.start()
        sums[...] = jnp.zeros_like(sums)
        sums[4 * rank :, :] = sums_ref[...]
        lane_head = lax.div(lax.broadcasted_iota(jnp.int32, ones_sc.shape, 0), size)
        spot_head = lax.div(lax.broadcasted_iota(jnp.int32, ones_sc.shape, 1), 128)
        ones_sc[...] = jnp.where(lane_head == spot_head, 1.0, 0.0).astype(bf16)

    @pl.when(step == 1)
    def _():
        entry_wait(len(peers) + len(rest))
        for k in range(3):
            result_copy(k).start()

    def attention(units):
        def stack(x):
            return jnp.concatenate(head_masks(x, heads, size), 0)

        def prob_grads(at, unit):
            i, n, q_base, k_base, _, which, row = unit[:7]
            grad = do_sc[which, rows_at(row, i * TILE, TILE), :]
            masked = stack(grad)
            for j in range(0, n, TILE):
                dp_sc[at % 2, :, j : j + TILE] = dg(masked, v_ref[rows_at(k_base, j, TILE), :], NT)
            both = grad.astype(f32) * o_ref[rows_at(q_base, i * TILE, TILE), :].astype(f32)
            high = both.astype(bf16)
            rest_of = (both - high.astype(f32)).astype(bf16)
            inner_sc[at % 2] = dg(high, ones_sc[...], NN) + dg(rest_of, ones_sc[...], NN)

        def score_grads(at, unit):
            i, n, _, _, probs = unit[:5]
            for h in range(heads):
                for r in range(0, TILE, strip):
                    here = h * TILE + r
                    inner = inner_sc[at % 2, r : r + strip, 128 * h : 128 * (h + 1)]
                    inner = jnp.concatenate([inner] * (n // 128), 1)
                    prob = probs[h, i * TILE + r : i * TILE + r + strip, 0:n].astype(f32)
                    ds = prob * (dp_sc[at % 2, here : here + strip, 0:n] - inner)
                    ds_sc[at % 2, here : here + strip, 0:n] = ds.astype(bf16)

        def products(at, unit):
            i, n, q_base, k_base, probs, which, row, add = unit
            query = rows_at(q_base, i * TILE, TILE)
            ds = ds_sc[at % 2, :, 0:n]
            dq = merge_heads(dg(ds, k_ref[rows_at(k_base, 0, n), :], NN), heads, size)
            stacked = probs[:, i * TILE : (i + 1) * TILE, 0:n].reshape(heads * TILE, n)
            dv = dg(stacked, stack(do_sc[which, rows_at(row, i * TILE, TILE), :]), TN)
            dk = dg(ds, stack(q_ref[query, :]), TN)
            if add:
                loc[0, query, :] += dq
                keys = rows_at(k_base, 0, n)
                loc[1, keys, :] += dk
                loc[2, keys, :] += dv
            else:
                loc[0, query, :] = dq
                if i:
                    keys = rows_at(k_base, 0, i * TILE)
                    loc[1, keys, :] += dk[: i * TILE]
                    loc[2, keys, :] += dv[: i * TILE]
                loc[1, query, :] = dk[i * TILE :]
                loc[2, query, :] = dv[i * TILE :]

        pipelined(units, (prob_grads, score_grads, products))

    def diag_units(base):
        here = rows_at(base, 0, half)
        do_sc[0] = (g_ref[here, :].astype(f32) * cd_ref[here, :]).astype(bf16)
        return [(i, (i + 1) * TILE, base, base, pd_ref.at[0], 0, 0, False) for i in range(half // TILE)]

    def cross_units():
        do_sc[1] = (g_ref[half:, :].astype(f32) * cc_ref[...]).astype(bf16)
        return [(i, half, half, 0, pc_ref, 1, 0, True) for i in range(half // TILE)]

    scales = (size**-0.5, 1.0, 1.0)

    @pl.when(step < groups)
    def _():
        cols = pl.ds(pl.multiple_of(step * GROUP, GROUP), GROUP)
        far_rows = rows_at(far * tile, 0, half)
        near_rows = rows_at(near * tile, 0, half)
        for a in range(3):
            loc[a, near_rows, :] = jnp.zeros((half, GROUP), f32)
        attention(diag_units(far * tile) + cross_units())
        for a in range(3):
            grads[a, far_rows, cols] = (loc[a, far_rows, :] * scales[a]).astype(bf16)
            near_sc[a, :, cols] = loc[a, near_rows, :]

    @pl.when((step > groups + 2) & (step < 2 * groups + 3))
    def _():
        cols = pl.ds(pl.multiple_of((step - groups - 3) * GROUP, GROUP), GROUP)
        near_rows = rows_at(near * tile, 0, half)
        attention(diag_units(near * tile))
        for a in range(3):
            both = loc[a, near_rows, :] + near_sc[a, :, cols]
            grads[a, near_rows, cols] = (both * scales[a]).astype(bf16)

    held = tile // 2

    def give(k):
        return remote(res_sc.at[peers[k][1]], out_ref.at[me], send.at[k], recv.at[k], peers[k])

    def give_part(p):
        rows = pl.ds(0, tile - held) if p == 0 else pl.ds(tile - held, held)
        return remote(
            res_sc.at[peers[1][1], rows], out_ref.at[me, rows], send.at[1 + 2 * p], recv.at[1 + 2 * p], peers[1]
        )

    def keep():
        return pltpu.make_async_copy(res_sc.at[me], out_ref.at[me], local_sem.at[6])

    def block_of(d):
        return pl.ds(pl.multiple_of(d * lanes, lanes), lanes)

    def scatter(k):
        return remote(sums.at[:, block_of(rest[k][0])], parts.at[k], part_send.at[k], part_recv.at[k], rest[k])

    def pair(at, peer):
        return remote(chunk.at[at], heard.at[at], pair_send.at[at], pair_recv.at[at], peer)

    def gather(k):
        return remote(chunk.at[2], total_sc.at[:, block_of(group)], mean_send.at[k], mean_recv.at[k], rest[k])

    @pl.when(step == groups)
    def _():
        for copy in loads():
            copy.wait()

    @pl.when((step == groups) | (step == 2 * groups + 3))
    def _():
        first = far + (near - far) * lax.div(step, 2 * groups + 3)
        here = pl.ds(pl.multiple_of(first * tile, tile), half)
        low_sc[2, here, :] = (ADAPTER_SCALE * dg(grads[0, here, :], upq_ref[...], NT)).astype(bf16)
        low_sc[3, here, :] = (ADAPTER_SCALE * dg(grads[2, here, :], upv_ref[...], NT)).astype(bf16)

    @pl.when((step == groups + 2) | (step == 2 * groups + 3))
    def _():
        first = far + (near - far) * lax.div(step, 2 * groups + 3)
        here = pl.ds(pl.multiple_of(first * tile, tile), half)
        dq, dv = grads[0, here, :], grads[2, here, :]
        normed = normed_sc[pl.ds(first, 2)].reshape(half, width)
        low_q, low_v, low_gq, low_gv = (low_sc[a, here, :] for a in range(4))
        sums[0:rank] += dg(low_gq, normed, TN)
        sums[rank : 2 * rank] += dg(low_gv, normed, TN)
        sums[2 * rank : 3 * rank] += ADAPTER_SCALE * dg(low_q, dq, TN)
        sums[3 * rank : 4 * rank] += ADAPTER_SCALE * dg(low_v, dv, TN)

    @pl.when(step == 2 * groups + 3)
    def _():
        for k in range(len(rest)):
            scatter(k).start()

    @pl.when(step == last)
    def _():
        pair(0, peers[2]).wait()
        chunk[1] = chunk[0] + heard[0]
        pair(1, peers[0]).start()
        give_part(1).start()

    early = (step == groups) | (step == groups + 1)

    @pl.when(early | (step > 2 * groups + 3))
    def _():
        late = lax.div(step, 2 * groups + 4)
        second = lax.rem(step, 2)
        slab = late * (beside + second * (me - beside)) + (1 - late) * (
            peers[0][1] + second * (peers[1][1] - peers[0][1])
        )
        here = pl.ds(pl.multiple_of(slab * tile, tile), tile)
        dq, dk, dv = grads[0, here, :], grads[1, here, :], grads[2, here, :]
        low_gq, low_gv = low_sc[2, here, :], low_sc[3, here, :]
        normed_grad = (
            dg(dq, w_sc[:, :width], NT)
            + dg(dk, w_sc[:, width : 2 * width], NT)
            + dg(dv, w_sc[:, 2 * width :], NT)
            + dg(low_gq, downq_ref[...], NN)
            + dg(low_gv, downv_ref[...], NN)
        )
        unit, rs = norm_stats(x_sc[slab].astype(f32))
        grad = hg_sc[slab].astype(f32) + norm_grad(unit, rs, line(gain_ref), normed_grad)
        res_sc[slab] = grad.astype(bf16)

    @pl.when(step == groups)
    def _():
        give(0).start()

    @pl.when(step == groups + 1)
    def _():
        give_part(0).start()

    @pl.when(step == 2 * groups + 4)
    def _():
        give(2).start()
        for k in range(len(rest)):
            scatter(k).wait()
        whole = sums[:, block_of(group)]
        for k in range(len(rest)):
            whole = whole + parts[k]
        chunk[0] = whole
        pair(0, peers[2]).start()

    @pl.when(step == last)
    def _():
        keep().start()
        pair(1, peers[0]).wait()
        whole = chunk[1] + heard[1]
        chunk[2] = whole
        total_sc[:, block_of(group)] = whole
        for k in range(len(rest)):
            gather(k).start()
        for k in range(len(rest)):
            gather(k).wait()
        total_ref[...] = total_sc[...]
        own_result().wait()
        keep().wait()
        for k in range(3):
            result_copy(k).wait()
        give(0).wait()
        give(2).wait()
        give_part(0).wait()
        give_part(1).wait()


def closing(
    qkv, grad, context, cd, cc, pd, pc, result, x, hidden_grad, normed, w, low,
    gain, downq, downv, upq, upv, sums, size, sizes,
):
    slots, tile, width = x.shape
    length = slots * tile
    half = length // 2
    groups = width // GROUP
    per = GROUP // size
    rank = downq.shape[0]
    total = (4 * rank + 8, width)
    rest = sizes[0] - 1
    lanes = width // sizes[0]
    dma = pltpu.SemaphoreType.DMA
    small = [gain, downq, downv, upq, upv, sums]

    def fold(a):
        return a.reshape(x.shape)

    def of(t):
        second = lax.div(t, groups + 3)
        return jnp.minimum(t - second * (groups + 3), groups - 1)

    def early(t):
        return jnp.minimum(t, groups - 1)

    def columns(third):
        return pl.BlockSpec((length, GROUP), lambda t: (0, of(t) + third * groups))

    return pl.pallas_call(
        functools.partial(close_kernel, size=size, strip=32, sizes=sizes),
        grid=(2 * groups + 6,),
        in_specs=[
            columns(0), columns(1), columns(2), columns(0), columns(0), columns(0),
            pl.BlockSpec((half, GROUP), lambda t: (0, early(t))),
            pl.BlockSpec((1, per, half, half), lambda t: (1 - jnp.minimum(lax.div(t, groups + 3), 1), of(t), 0, 0)),
            pl.BlockSpec((per, half, half), lambda t: (early(t), 0, 0)),
        ]
        + [ANY] * 6
        + [resident(a.shape) for a in small],
        out_specs=[ANY, ANY, pl.BlockSpec(total, lambda t: (0, 0))],
        out_shape=[
            jax.ShapeDtypeStruct(x.shape, bf16),
            jax.ShapeDtypeStruct(x.shape, bf16),
            jax.ShapeDtypeStruct(total, f32),
        ],
        scratch_shapes=[
            pltpu.VMEM((2, per * TILE, half), f32),
            pltpu.VMEM((2, per * TILE, half), bf16),
            pltpu.VMEM((2, TILE, per * 128), f32),
            pltpu.VMEM((GROUP, per * 128), bf16),
            pltpu.VMEM((2, half, GROUP), bf16),
            pltpu.VMEM((3, length, GROUP), f32),
            pltpu.VMEM((3, half, width), f32),
            pltpu.VMEM((3, length, width), bf16),
            pltpu.VMEM(x.shape, bf16),
            pltpu.VMEM(x.shape, bf16),
            pltpu.VMEM(x.shape, bf16),
            pltpu.VMEM(w.shape, bf16),
            pltpu.VMEM((4, length, rank), bf16),
            pltpu.VMEM(x.shape, bf16),
            pltpu.VMEM(total, f32),
            pltpu.VMEM((rest, total[0], lanes), f32),
            pltpu.VMEM((3, total[0], lanes), f32),
            pltpu.VMEM((2, total[0], lanes), f32),
            pltpu.VMEM(total, f32),
            dma((3,)), dma((3,)), dma((4,)), dma((4,)), dma((7,)),
            dma((rest,)), dma((rest,)), dma((2,)), dma((2,)), dma((rest,)), dma((rest,)),
        ],
        compiler_params=pltpu.CompilerParams(
            collective_id=1, has_side_effects=True, vmem_limit_bytes=62 * MIB, dimension_semantics=("arbitrary",)
        ),
        name="closing",
    )(qkv, qkv, qkv, grad, context, cd, cc, pd, pc, result, x, fold(hidden_grad), fold(normed), w, low, *small)


def finish_kernel(total_ref, a_hbm, b_hbm, aq_ref, bq_ref, av_ref, bv_ref, rms_ref, a_out, b_out, a_sc, b_sc, sem):
    rank, width = aq_ref.shape
    loads, saves = [], []
    for k, (src, kept, dst) in enumerate(((a_hbm, a_sc, a_out), (b_hbm, b_sc, b_out))):
        for s in range(src.shape[0]):
            loads.append(pltpu.make_async_copy(src.at[s], kept.at[s], sem.at[k, s, 0]))
            saves.append(pltpu.make_async_copy(kept.at[s], dst.at[s], sem.at[k, s, 1]))
    for load in loads:
        load.start()
    aq_ref[...] = total_ref[0:rank]
    av_ref[...] = total_ref[rank : 2 * rank]
    bq_ref[...] = total_ref[2 * rank : 3 * rank]
    bv_ref[...] = total_ref[3 * rank : 4 * rank]
    line = total_ref[4 * rank : 4 * rank + 1, 0:128]
    lane = lax.broadcasted_iota(jnp.int32, line.shape, 1)
    count = jnp.maximum(jnp.sum(jnp.where(lane == 2, line, 0.0)), 1.0)
    values = jnp.sqrt(line / (jnp.where(lane == 0, 1.0, 2.0) * count * width))
    for k in range(2):
        rms_ref[k] = jnp.sum(jnp.where(lane == k, values, 0.0))
    for load, save in zip(loads, saves):
        load.wait()
        save.start()
    for save in saves:
        save.wait()


def finish(total, a, b, rank):
    width = total.shape[1]
    small = jax.ShapeDtypeStruct((rank, width), f32)
    return pl.pallas_call(
        finish_kernel,
        in_specs=[VMEM, ANY, ANY],
        out_specs=[VMEM] * 4 + [pl.BlockSpec(memory_space=pltpu.SMEM), ANY, ANY],
        out_shape=[small] * 4 + [
            jax.ShapeDtypeStruct((2,), f32),
            jax.ShapeDtypeStruct(a.shape, a.dtype),
            jax.ShapeDtypeStruct(b.shape, b.dtype),
        ],
        scratch_shapes=[
            pltpu.VMEM(a.shape, a.dtype), pltpu.VMEM(b.shape, b.dtype), pltpu.SemaphoreType.DMA((2, a.shape[0], 2))
        ],
        name="finish",
    )(total, a, b)


def whole_slots(
    block_input_rows,
    document_starts,
    counted_mask,
    output_gradient,
    first_norm_gain,
    first_norm_bias,
    query_key_value_weight,
    query_down_weight,
    query_up_weight,
    value_down_weight,
    value_up_weight,
    attention_out_weight,
    second_norm_gain,
    second_norm_bias,
    feed_input_weight,
    feed_input_bias,
    feed_output_weight,
):
    sizes = (lax.axis_size("dp"), lax.axis_size("head"))
    size = block_input_rows.shape[-1] // H
    rank = query_down_weight.shape[1]
    downq = query_down_weight.T
    downv = value_down_weight.T
    x, dy, mask, normed, low, qkv, context, pd, pc, cd, cc = opening(
        block_input_rows, output_gradient, query_key_value_weight, counted_mask, document_starts,
        first_norm_gain, first_norm_bias, downq, downv, query_up_weight, value_up_weight, size,
    )
    out, hidden_grad, context_grad, sums = feed(
        x, dy, output_gradient, context, mask, attention_out_weight, second_norm_gain, second_norm_bias,
        feed_input_weight, feed_input_bias, feed_output_weight,
    )
    output, input_grad, total = closing(
        qkv, context_grad, context, cd, cc, pd, pc, out, x, hidden_grad, normed, query_key_value_weight, low,
        first_norm_gain, downq, downv, query_up_weight, value_up_weight, sums, size, sizes,
    )
    grad_aq, grad_bq, grad_av, grad_bv, rms, output, input_grad = finish(total, output, input_grad, rank)
    return output, input_grad, grad_aq.T, grad_bq, grad_av.T, grad_bv, rms


def body(*args):
    same = args[0].shape[0] == lax.axis_size("head")
    return whole_slots(*args) if same else shards(*args)


def solution(mesh):
    return jax.shard_map(
        body,
        mesh=mesh,
        in_specs=(
            P("dp", "head", None),
            P("dp", None),
            P("dp", "head"),
            P("dp", "head", None),
            P(),
            P(),
            P(),
            P(),
            P(),
            P(),
            P(),
            P(),
            P(),
            P(),
            P(),
            P(),
            P(),
        ),
        out_specs=(P("dp", "head", None), P("dp", "head", None), P(), P(), P(), P(), P()),
        check_vma=False,
    )
```
